32 devices in a mesh: dp: 4 (over z), expert: 4 (over y, x), tensor: 2 (over core).
Axes of the slice: x: 2, y: 2, z: 4, core: 2. Of those that a mesh axis runs over, the one named last changes fastest.
Arguments:
- tokens: bfloat16 [8192, 1536], P(('dp', 'expert')), may hold values from -6 to 6
- teacher: bfloat16 [8192, 1536], P(('dp', 'expert')), may hold values from -6 to 6
- routes: int32 [8192, 8], P(('dp', 'expert')), may hold values from 0 to 39, all different within a row; in each aligned block of 512 rows (0 to 511, 512 to 1023, ...) at most 128 rows name the same one
- valid: int32 [8192], P(('dp', 'expert')), may hold values from 0 to 1
- teacher_rows: int32 [16, 512], P(('dp', 'expert')), may hold values from 0 to 511, each once within a row
- norm_attn: float32 [1536], replicated, may hold values from 0.5 to 1.5
- norm_moe: float32 [1536], replicated, may hold values from 0.5 to 1.5
- w_query: bfloat16 [1536, 1536], P(None, 'tensor'), may hold values from -0.15625 to 0.15625
- key_projection_weight: bfloat16 [1536, 512], P(None, 'tensor'), may hold values from -0.15625 to 0.15625
- value_projection_weight: bfloat16 [1536, 512], P(None, 'tensor'), may hold values from -0.15625 to 0.15625
- w_out: bfloat16 [1536, 1536], P('tensor'), may hold values from -0.625 to 0.625
- w_router: bfloat16 [1536, 40], replicated, may hold values from -0.078125 to 0.078125
- w_gate: bfloat16 [40, 1536, 512], P('expert', None, 'tensor'), may hold values from -0.15625 to 0.15625
- w_up: bfloat16 [40, 1536, 512], P('expert', None, 'tensor'), may hold values from -0.15625 to 0.15625
- w_down: bfloat16 [40, 512, 1536], P('expert', 'tensor'), may hold values from -1 to 1
Outputs:
- block_out: bfloat16 [8192, 1536], P(('dp', 'expert'))
- grad_tokens: float32 [8192, 1536], P(('dp', 'expert'))
- grad_norm_attn: float32 [1536], P(('dp', 'expert'))
- grad_norm_moe: float32 [1536], P(('dp', 'expert'))
- grad_query: float32 [1536, 1536], P(('dp', 'expert'), 'tensor')
- grad_key: float32 [1536, 512], P(('dp', 'expert'), 'tensor')
- grad_value: float32 [1536, 512], P(('dp', 'expert'), 'tensor')
- grad_out: float32 [1536, 1536], P('tensor', ('dp', 'expert'))
- grad_router: float32 [1536, 40], P(('dp', 'expert'))
- grad_gate: float32 [40, 1536, 512], P('expert', 'dp', 'tensor')
- grad_up: float32 [40, 1536, 512], P('expert', 'dp', 'tensor')
- grad_down: float32 [40, 512, 1536], P('expert', 'tensor', 'dp')
The draws below stay inside these ranges and needn't reach their ends.
Inputs may be any that keep to these rules, and one draw needn't show every extreme that they name: `routes`: no expert is named by more than 128 of the 512 rows of one index of dp+expert, a bound that some block reaches of them. `teacher_rows`: each row is a permutation of 0 to 511.
All inputs are finite; a program needn't handle non-finite values.
Results may differ from the reference program's by a relative error of at most 0.017.
Values may be sent and summed in bfloat16 or wider, within the bound.
No kernel may reach another device: no remote copies, remote signals or barrier semaphores. Data moves between devices by JAX's collectives and lax.ppermute only.
A program may use at most 256 MiB of HBM per device.

```python
import math
import jax
import jax.numpy as jnp
import numpy as np
from jax import lax

MODEL_DIMENSION = 1536
QUERY_HEADS = 24
KEY_VALUE_HEADS = 8
HEAD_DIMENSION = 64
FF = 512
TOPK = 8
SEQUENCE_LENGTH = 512
ABLK = 256
SEQS = 1
TOK_DEV = 512
GROUPS = 16
TOKENS = 8192
EXPERTS = 40
CAP = 128
N_TENSOR = 2


def draw_valid(key, part):
    key = jax.random.fold_in(key, 11)
    position = jnp.arange(TOKENS, dtype=jnp.int32)
    ticket = jax.random.randint(key, (TOKENS,), 0, 2 * TOKENS, dtype=jnp.int32)
    return (ticket < TOKENS // 2 + position).astype(jnp.int32)


def level_of(own_key, shape, split, smallest, largest):
    def one(dim, blocks):
        draws = jax.random.uniform(jax.random.fold_in(jax.random.fold_in(own_key, 6), dim), (blocks,), jnp.float32, smallest / len(split), largest / len(split))
        return jnp.repeat(jnp.exp(draws), shape[dim] // blocks).reshape((-1,) + (1,) * (len(shape) - dim - 1))

    loudness = one(*split[0])
    for cut in split[1:]:
        loudness = loudness * one(*cut)
    return loudness


def assign_block(own_key, own, number, rows, count, top, reach, skew):
    order = jax.random.permutation(own_key, count)
    crowded, common = load_shares(count, rows * top, reach, skew, True), load_shares(count, rows * top, reach, skew, False)
    places = jnp.arange(count)

    def named(sizes, offset_by):
        used = int((sizes > 0).sum())
        fixed = max(1, used // 4)
        moved = fixed + (places - fixed + offset_by * (used - fixed)) % max(1, count - fixed)
        return jnp.zeros((count,), jnp.int32).at[order[jnp.where(places < fixed, places, moved)]].set(jnp.asarray(sizes, jnp.int32))

    sizes = jnp.where(number % 4 == 0, named(crowded, number // 4), named(common, number - number // 4 - 1))
    mixed = jax.random.permutation(jax.random.fold_in(own, 3), count)
    source_of, taker = mixed[0:count // 2 * 2:2], mixed[1:count // 2 * 2:2]
    margin = jnp.minimum(sizes[source_of] - 1, reach - sizes[taker]) // 2
    margin = jnp.where((source_of == order[0]) | (taker == order[0]) | (sizes[taker] == 0), 0, jnp.maximum(margin, 0))
    moved = jax.random.randint(jax.random.fold_in(own, 4), (count // 2,), 0, 1 << 20) % (margin + 1)
    sizes = sizes.at[source_of].add(-moved).at[taker].add(moved)
    labels = jnp.searchsorted(jnp.cumsum(sizes), jnp.arange(rows * top), side="right").astype(jnp.int32)
    listing = labels.reshape(top, rows).T
    listing = listing[jax.random.permutation(jax.random.fold_in(own, 1), rows)]
    offset_by = jax.random.randint(jax.random.fold_in(own, 2), (rows, 1), 0, top)
    return jnp.take_along_axis(listing, (jnp.arange(top)[None, :] + offset_by) % top, axis=1)


def load_shares(amount, total, most, skew, full):
    portions = [(1 << 20) // math.isqrt(grade ** skew) + 1 for grade in range(1, amount + 1)]
    largest = most if full else min(most, max(-(-total // amount), total * portions[0] // sum(portions)))
    least = 1 if total - largest >= amount - 1 else 0
    holding, spare = [largest] + [least] * (amount - 1), total - largest - least * (amount - 1)
    while spare > 0:
        free = [i for i in range(1, amount) if holding[i] < largest] or [i for i in range(1, amount) if holding[i] < most]
        mass, budget = sum([portions[i] for i in free]), spare
        for i in free:
            extra = min(most - holding[i], max(1, budget * portions[i] // mass), spare)
            holding[i] = holding[i] + extra
            spare = spare - extra
    return np.array(holding)


def scatter_about(stream_key, shape, spread, reach, cuts=(), kind=jnp.bfloat16):
    level = level_of(stream_key, shape, cuts, -0.22, 0.18) if cuts else 1.0
    array = jax.random.normal(stream_key, shape, jnp.float32) * spread * level
    return jnp.minimum(jnp.maximum(array, -reach), reach).astype(kind)


def setup_inputs(seed: int = 0) -> dict:
    key_list = jax.random.split(jax.random.key(seed), 16)
    tokens = scatter_about(key_list[0], (TOKENS, MODEL_DIMENSION), 1.0, 6.0, ((0, 16),))
    teacher = scatter_about(key_list[1], (TOKENS, MODEL_DIMENSION), 1.0, 6.0, ((0, 16),))
    routes_keys = jax.random.split(jax.random.fold_in(key_list[2], 1), TOKENS // TOK_DEV)
    routes_turns = jax.random.permutation(jax.random.fold_in(key_list[2], 3), TOKENS // TOK_DEV)
    routes = jax.vmap(lambda own, number: assign_block(jax.random.fold_in(key_list[2], 2), own, number, TOK_DEV, EXPERTS, TOPK, CAP, 1))(routes_keys, routes_turns).reshape((TOKENS, TOPK))
    valid = draw_valid(jax.random.fold_in(key_list[15], 71), 0)
    teacher_rows = jax.vmap(lambda own: jax.random.permutation(own, TOK_DEV))(jax.random.split(key_list[4], GROUPS)).reshape((GROUPS, TOK_DEV)).astype(jnp.int32)
    norm_attn = jnp.clip(1.0 + 0.1 * jax.random.normal(key_list[5], (MODEL_DIMENSION,), jnp.float32), 0.5, 1.5)
    norm_moe = jnp.clip(1.0 + 0.1 * jax.random.normal(key_list[6], (MODEL_DIMENSION,), jnp.float32), 0.5, 1.5)
    w_query = scatter_about(key_list[7], (MODEL_DIMENSION, QUERY_HEADS * HEAD_DIMENSION), MODEL_DIMENSION ** -0.5, 0.15625, ((1, 2),))
    key_projection_weight = scatter_about(key_list[8], (MODEL_DIMENSION, KEY_VALUE_HEADS * HEAD_DIMENSION), MODEL_DIMENSION ** -0.5, 0.15625, ((1, 2),))
    value_projection_weight = scatter_about(key_list[9], (MODEL_DIMENSION, KEY_VALUE_HEADS * HEAD_DIMENSION), MODEL_DIMENSION ** -0.5, 0.15625, ((1, 2),))
    w_out = scatter_about(key_list[10], (QUERY_HEADS * HEAD_DIMENSION, MODEL_DIMENSION), (QUERY_HEADS * HEAD_DIMENSION // 16) ** -0.5, 0.625, ((0, 2),))
    w_router = scatter_about(key_list[11], (MODEL_DIMENSION, EXPERTS), (4 * MODEL_DIMENSION) ** -0.5, 0.078125)
    w_gate = scatter_about(key_list[12], (EXPERTS, MODEL_DIMENSION, FF), MODEL_DIMENSION ** -0.5, 0.15625, ((0, 4), (2, 2)))
    w_up = scatter_about(key_list[13], (EXPERTS, MODEL_DIMENSION, FF), MODEL_DIMENSION ** -0.5, 0.15625, ((0, 4), (2, 2)))
    w_down = scatter_about(key_list[14], (EXPERTS, FF, MODEL_DIMENSION), (FF // 16) ** -0.5, 1.0, ((0, 4), (1, 2)))
    return dict(tokens=tokens, teacher=teacher, routes=routes, valid=valid, teacher_rows=teacher_rows, norm_attn=norm_attn, norm_moe=norm_moe, w_query=w_query, key_projection_weight=key_projection_weight, value_projection_weight=value_projection_weight, w_out=w_out, w_router=w_router, w_gate=w_gate, w_up=w_up, w_down=w_down)


EPS = 1e-06
THETA = 10000.0
HIGH = lax.Precision.HIGHEST

@jax.custom_vjp
def reduced_precision(v):
    return lax.optimization_barrier(v.astype(jnp.bfloat16)).astype(jnp.float32)

@jax.custom_vjp
def reduced_precision_backward(v):
    return v

def low_keep(v):
    return (reduced_precision(v), None)

def low_pass(kept, grad):
    return (grad,)

def back_keep(v):
    return (v, None)

def back_low(kept, grad):
    return (reduced_precision(grad),)
reduced_precision.defvjp(low_keep, low_pass)
reduced_precision_backward.defvjp(back_keep, back_low)

def matrix_product(left, right):
    return jnp.dot(left, right, precision=HIGH, preferred_element_type=jnp.float32)

def rope_tables():
    half_size = HEAD_DIMENSION // 2
    frequency = THETA ** (-jnp.arange(half_size, dtype=jnp.float32) * 2.0 / HEAD_DIMENSION)
    angles = jnp.arange(SEQUENCE_LENGTH, dtype=jnp.float32)[:, None] * frequency[None, :]
    return (jnp.cos(angles), jnp.sin(angles))

def apply_rotary(value_matrix, cosine_table, sine_table):
    half_size = value_matrix.shape[-1] // 2
    first_half = value_matrix[..., :half_size]
    second_half = value_matrix[..., half_size:]
    cosine_rows = cosine_table[:, None, :]
    sine_rows = sine_table[:, None, :]
    return jnp.concatenate([first_half * cosine_rows - second_half * sine_rows, second_half * cosine_rows + first_half * sine_rows], axis=-1)

def rms_norm(value_matrix, gain):
    inverse = lax.rsqrt(lax.optimization_barrier(jnp.mean(value_matrix * value_matrix, axis=-1, keepdims=True)) + EPS)
    return value_matrix * inverse * gain

def attend(attention_input, w_query, key_projection_weight, value_projection_weight, w_out):
    query_raw = reduced_precision_backward(matrix_product(attention_input, w_query)).reshape(SEQUENCE_LENGTH, QUERY_HEADS, HEAD_DIMENSION)
    key_unrotated = reduced_precision_backward(matrix_product(attention_input, key_projection_weight)).reshape(SEQUENCE_LENGTH, KEY_VALUE_HEADS, HEAD_DIMENSION)
    value_unprojected = reduced_precision_backward(matrix_product(attention_input, value_projection_weight)).reshape(SEQUENCE_LENGTH, KEY_VALUE_HEADS, HEAD_DIMENSION)
    cosine_table, sine_table = rope_tables()
    queries = reduced_precision(apply_rotary(query_raw, cosine_table, sine_table) * HEAD_DIMENSION ** (-0.5))
    key_matrix = jnp.repeat(reduced_precision(apply_rotary(key_unrotated, cosine_table, sine_table)), QUERY_HEADS // KEY_VALUE_HEADS, axis=1)
    value_matrix = jnp.repeat(reduced_precision(value_unprojected), QUERY_HEADS // KEY_VALUE_HEADS, axis=1)
    scores = reduced_precision_backward(jnp.einsum('qhe,khe->hqk', queries, key_matrix, precision=HIGH))
    block_ids = jnp.arange(SEQUENCE_LENGTH, dtype=jnp.int32) // ABLK
    allowed = block_ids[:, None] >= block_ids[None, :]
    scores = jnp.where(allowed[None, :, :], scores, -1e+30)
    row_peak = lax.optimization_barrier(jnp.max(scores, axis=-1, keepdims=True))
    weights = jnp.exp(scores - row_peak)
    probs_low = reduced_precision(weights / lax.optimization_barrier(jnp.sum(weights, axis=-1, keepdims=True)))
    mixed = jnp.einsum('hqk,khe->qhe', probs_low, value_matrix, precision=HIGH)
    mixed = reduced_precision(reduced_precision_backward(mixed)).reshape(SEQUENCE_LENGTH, QUERY_HEADS * HEAD_DIMENSION)
    return reduced_precision_backward(matrix_product(mixed, w_out))

def group_layer(inputs, target_block, group_routes, group_perm, group_valid, loss_scale, norm_attn, norm_moe, w_query, key_projection_weight, value_projection_weight, w_out, w_router, w_gate, w_up, w_down):
    attention_input = reduced_precision(rms_norm(inputs, norm_attn))
    attn = jax.vmap(attend, in_axes=(0, None, None, None, None))(attention_input.reshape(SEQS, SEQUENCE_LENGTH, MODEL_DIMENSION), w_query, key_projection_weight, value_projection_weight, w_out).reshape(TOK_DEV, MODEL_DIMENSION)
    hidden_first = inputs + attn
    moe_in = reduced_precision(rms_norm(hidden_first, norm_moe))
    logits = reduced_precision_backward(matrix_product(moe_in, w_router))
    chosen = jnp.take_along_axis(logits, group_routes, axis=1)
    chosen = chosen - lax.optimization_barrier(jnp.max(chosen, axis=1, keepdims=True))
    exponent = jnp.exp(chosen)
    gates = exponent / lax.optimization_barrier(jnp.sum(exponent, axis=1, keepdims=True))
    picked_mask = group_routes[:, :, None] == jnp.arange(EXPERTS, dtype=jnp.int32)[None, None, :]
    expert_loads = lax.optimization_barrier(jnp.sum(picked_mask.astype(jnp.int32), axis=1)).astype(jnp.int32)
    before = (jnp.cumsum(expert_loads, axis=0) - expert_loads).astype(jnp.int32)
    slot_index = jnp.take_along_axis(before, group_routes, axis=1).astype(jnp.int32)
    places = (group_routes * CAP + slot_index).reshape(-1).astype(jnp.int32)
    token_ids = (jnp.repeat(jnp.arange(TOK_DEV, dtype=jnp.int32), TOPK) + 1).astype(jnp.int32)
    owner_row = jnp.zeros((EXPERTS * CAP,), jnp.int32).at[places].set(token_ids)
    live_slot = (owner_row > 0)[:, None]
    source = jnp.maximum(owner_row - 1, 0).astype(jnp.int32)
    rows_all = jnp.where(live_slot, moe_in[source], 0.0).reshape(EXPERTS, CAP, MODEL_DIMENSION)
    span = FF // N_TENSOR
    combined = jnp.zeros((TOK_DEV, TOPK, MODEL_DIMENSION), jnp.float32)
    for half_index in range(N_TENSOR):
        lower = half_index * span
        rows_half = reduced_precision_backward(rows_all)
        gate_pre = reduced_precision_backward(jnp.einsum('ecd,edf->ecf', rows_half, w_gate[:, :, lower:lower + span], precision=HIGH))
        up_pre = reduced_precision_backward(jnp.einsum('ecd,edf->ecf', rows_half, w_up[:, :, lower:lower + span], precision=HIGH))
        hidden = reduced_precision(jax.nn.silu(gate_pre) * up_pre)
        expert_out = reduced_precision(reduced_precision_backward(jnp.einsum('ecf,efd->ecd', hidden, w_down[:, lower:lower + span, :], precision=HIGH)))
        combined = combined + expert_out.reshape(EXPERTS * CAP, MODEL_DIMENSION)[places].reshape(TOK_DEV, TOPK, MODEL_DIMENSION)
    moe = jnp.einsum('tk,tkd->td', gates, combined, precision=HIGH)
    layer_out = hidden_first + moe
    target = target_block[group_perm]
    diff = layer_out - target
    group_loss = loss_scale * 0.5 * jnp.sum(group_valid[:, None] * diff * diff)
    return (group_loss, layer_out)

def reference(tokens, teacher, routes, valid, teacher_rows, norm_attn, norm_moe, w_query, key_projection_weight, value_projection_weight, w_out, w_router, w_gate, w_up, w_down):
    valid_rows = valid.astype(jnp.float32)
    loss_scale = TOKENS / jnp.sum(valid_rows)
    inputs = tokens.astype(jnp.float32)
    targets = teacher.astype(jnp.float32).reshape(GROUPS, TOK_DEV, MODEL_DIMENSION)
    route_groups = routes.reshape(GROUPS, TOK_DEV, TOPK)
    valid_groups = valid_rows.reshape(GROUPS, TOK_DEV)
    weights = tuple((weight.astype(jnp.float32) for weight in (norm_attn, norm_moe, w_query, key_projection_weight, value_projection_weight, w_out, w_router, w_gate, w_up, w_down)))

    def whole_layer(layer_in, *params):

        def one_group(group_args):
            group_in, group_target, group_routes, group_perm, group_valid = group_args
            return group_layer(group_in, group_target, group_routes, group_perm, group_valid, loss_scale, *params)
        losses, outputs = lax.map(jax.checkpoint(one_group), (layer_in.reshape(GROUPS, TOK_DEV, MODEL_DIMENSION), targets, route_groups, teacher_rows, valid_groups))
        return (jnp.sum(losses), outputs.reshape(TOKENS, MODEL_DIMENSION))
    total_loss, pullback, layer_out = jax.vjp(whole_layer, inputs, *weights, has_aux=True)
    gradients = pullback(jnp.ones_like(total_loss))
    return (layer_out.astype(jnp.bfloat16), gradients[0], gradients[1], gradients[2], gradients[3], gradients[4], gradients[5], gradients[6], gradients[7], gradients[8], gradients[9], gradients[10])
```

```python
import functools

import jax
import jax.numpy as jnp
from jax import lax
from jax.experimental import pallas as pl
from jax.experimental.pallas import tpu as pltpu
from jax.sharding import PartitionSpec as P

HEAD_DIMENSION = 64
SEQUENCE_LENGTH = 512
ABLK = 256


EPS = 1e-06
THETA = 10000.0
VMEM_LIMIT = 60 * 1024 * 1024
bfloat = jnp.bfloat16
single = jnp.float32


def swap(value):
    return lax.ppermute(value, "tensor", [(0, 1), (1, 0)])


def to_peer(value, axis, step):
    return lax.ppermute(value, axis, [(i, i ^ step) for i in range(lax.axis_size(axis))])


def to_mirror(value):
    count = lax.axis_size("dp")
    return lax.ppermute(value, "dp", [(i, count - 1 - i) for i in range(count)])


def gather_groups(value):
    return [value] + [to_peer(value, "expert", s) for s in range(1, lax.axis_size("expert"))]


def sum_all(value, axes):
    for axis in axes:
        step = 1
        while step < lax.axis_size(axis):
            value = value + to_peer(value, axis, step)
            step *= 2
    return value


def scatter_dense(packed):
    count_dp, count_ex = lax.axis_size("dp"), lax.axis_size("expert")
    at_dp, at_ex = lax.axis_index("dp"), lax.axis_index("expert")
    rows, columns = packed.shape
    block = rows // (count_dp * count_ex)
    cut = packed.reshape(count_dp, count_ex, block, columns)

    def part(step):
        return lax.dynamic_index_in_dim(cut, at_ex ^ step, 1, keepdims=False)

    total = part(0).astype(single)
    for step in range(1, count_ex):
        total = total + to_peer(part(step).astype(bfloat), "expert", step).astype(single)

    def row(step):
        return lax.dynamic_index_in_dim(total, at_dp ^ step, 0, keepdims=False)

    result = row(0)
    for step in range(1, count_dp):
        result = result + to_peer(row(step).astype(bfloat), "dp", step).astype(single)
    return result


def dot(left, right):
    return lax.dot_general(left, right, (((1,), (0,)), ((), ())), preferred_element_type=single)


def dot_nt(left, right):
    return lax.dot_general(left, right, (((1,), (1,)), ((), ())), preferred_element_type=single)


def dot_tn(left, right):
    return lax.dot_general(left, right, (((0,), (0,)), ((), ())), preferred_element_type=single)


def picks(slots_ref, group, capacity):
    slot = slots_ref[0, group : group + 1, :]
    return slot == lax.broadcasted_iota(jnp.int32, (capacity, slot.shape[1]), 0)


def gather_rows(picked, mine, other, to_ref, group, capacity):
    span = mine.shape[0]
    low = picked.astype(bfloat)
    rows = dot(low[:, :span], mine[...]) + dot(low[:, span:], other[...])
    to_ref[group * capacity : (group + 1) * capacity, :] = rows.astype(bfloat)


def slot_gates(picked, gates_ref, group):
    return jnp.sum(jnp.where(picked, gates_ref[0, group : group + 1, :], 0.0), axis=1, keepdims=True)


def add_back(step, picked, rows, acc_mine, acc_other, group):
    back = dot_tn(picked.astype(bfloat), rows)
    span = acc_mine.shape[1]

    @pl.when(step == 0)
    def _():
        acc_mine[group] = back[:span]
        acc_other[group] = back[span:]

    @pl.when(step > 0)
    def _():
        acc_mine[group] += back[:span]
        acc_other[group] += back[span:]


def half_columns(half_ref, width):
    return pl.ds(pl.multiple_of(half_ref[0] * width, 128), width)


def forward_kernel(groups, with_out, half_ref, slots_ref, gates_ref, gate_w, up_w, *refs):
    step = pl.program_id(0)
    if with_out:
        down_w, refs = refs[0], refs[1:]
    x_refs, refs = refs[: 2 * groups], refs[2 * groups :]
    if with_out:
        half_rows, gate_ref, up_ref, out_mine, out_other, rows_ref, acc_mine, acc_other = refs
    else:
        half_rows, gate_ref, up_ref, rows_ref = refs
    capacity = rows_ref.shape[0] // groups
    picked = [picks(slots_ref, g, capacity) for g in range(groups)]
    for g in range(groups):
        gather_rows(picked[g], x_refs[2 * g], x_refs[2 * g + 1], rows_ref, g, capacity)
    rows = rows_ref[...]
    half_rows[0] = rows_ref[:, half_columns(half_ref, half_rows.shape[2])]
    gate_pre = dot(rows, gate_w[0])
    up_pre = dot(rows, up_w[0])
    gate_ref[0] = gate_pre
    up_ref[0] = up_pre
    if not with_out:
        return
    gates = jnp.concatenate([slot_gates(picked[g], gates_ref, g) for g in range(groups)], axis=0)
    hidden = (gate_pre * jax.nn.sigmoid(gate_pre) * up_pre * gates).astype(bfloat)
    out = dot(hidden, down_w[0]).astype(bfloat)
    for g in range(groups):
        add_back(step, picked[g], out[g * capacity : (g + 1) * capacity], acc_mine, acc_other, g)

    @pl.when(step == pl.num_programs(0) - 1)
    def _():
        out_mine[...] = acc_mine[...].astype(out_mine.dtype)
        out_other[...] = acc_other[...].astype(out_other.dtype)


def hidden_grads(gate_pre, up_pre, gates, grad_hidden):
    sig = jax.nn.sigmoid(gate_pre)
    silu = gate_pre * sig
    hidden = silu * up_pre
    grad_gates = jnp.sum(hidden * grad_hidden, axis=1, keepdims=True)
    scaled = grad_hidden * gates
    grad_gate_pre = (scaled * up_pre * sig * (1.0 + gate_pre * (1.0 - sig))).astype(bfloat)
    grad_up_pre = (scaled * silu).astype(bfloat)
    return (hidden * gates).astype(bfloat), grad_gate_pre, grad_up_pre, grad_gates


def backward_kernel(groups, half_ref, slots_ref, gates_ref, gate_w, up_w, down_w, *refs):
    step = pl.program_id(0)
    g_refs, refs = refs[: 2 * groups], refs[2 * groups :]
    gate_ref, up_ref = refs[:2]
    half_grad, hidden_ref, grad_gate_ref, grad_up_ref, gg_ref, out_mine, out_other = refs[2:9]
    rows_ref, acc_mine, acc_other = refs[9:]
    capacity = rows_ref.shape[0] // groups
    picked = [picks(slots_ref, g, capacity) for g in range(groups)]
    for g in range(groups):
        gather_rows(picked[g], g_refs[2 * g], g_refs[2 * g + 1], rows_ref, g, capacity)
    half_grad[0] = rows_ref[:, half_columns(half_ref, half_grad.shape[2])]
    gates = jnp.concatenate([slot_gates(picked[g], gates_ref, g) for g in range(groups)], axis=0)
    grad_hidden = dot_nt(rows_ref[...], down_w[0])
    hidden, grad_gate_pre, grad_up_pre, grad_gates = hidden_grads(
        gate_ref[0], up_ref[0], gates, grad_hidden
    )
    hidden_ref[0] = hidden
    grad_gate_ref[0] = grad_gate_pre
    grad_up_ref[0] = grad_up_pre
    for g in range(groups):
        own = grad_gates[g * capacity : (g + 1) * capacity]
        gg_ref[0, g : g + 1, :] = jnp.sum(jnp.where(picked[g], own, 0.0), axis=0, keepdims=True)
    back = (dot_nt(grad_gate_pre, gate_w[0]) + dot_nt(grad_up_pre, up_w[0])).astype(bfloat)
    for g in range(groups):
        add_back(step, picked[g], back[g * capacity : (g + 1) * capacity], acc_mine, acc_other, g)

    @pl.when(step == pl.num_programs(0) - 1)
    def _():
        out_mine[...] = acc_mine[...].astype(out_mine.dtype)
        out_other[...] = acc_other[...].astype(out_other.dtype)


def weights_kernel(groups, half_ref, slots_ref, gates_ref, down_w, *refs):
    g_refs, refs = refs[: 2 * groups], refs[2 * groups :]
    gate_ref, up_ref, rows_far, rows_near, grad_near, hidden_near, gate_near, up_near = refs[:8]
    d_gate, d_up, d_down, rows_ref = refs[8:]
    capacity = rows_ref.shape[0] // groups
    picked = [picks(slots_ref, g, capacity) for g in range(groups)]
    for g in range(groups):
        gather_rows(picked[g], g_refs[2 * g], g_refs[2 * g + 1], rows_ref, g, capacity)
    gates = jnp.concatenate([slot_gates(picked[g], gates_ref, g) for g in range(groups)], axis=0)
    grad_hidden = dot_nt(rows_ref[...], down_w[0])
    hidden, grad_gate_pre, grad_up_pre, _ = hidden_grads(gate_ref[0], up_ref[0], gates, grad_hidden)
    grad_far = rows_ref[:, half_columns(half_ref, d_gate.shape[1])]
    d_down[0] = (dot_tn(hidden, grad_far) + dot_tn(hidden_near[0], grad_near[0])).astype(bfloat)
    far, near = rows_far[0], rows_near[0]
    d_gate[0] = (dot_tn(far, grad_gate_pre) + dot_tn(near, gate_near[0])).astype(bfloat)
    d_up[0] = (dot_tn(far, grad_up_pre) + dot_tn(near, up_near[0])).astype(bfloat)


def per_expert(*shape):
    return pl.BlockSpec((1,) + shape, lambda e, half: (e,) + (0,) * len(shape))


def resident(*shape):
    return pl.BlockSpec(shape, lambda e, half: (0,) * len(shape))


def expert_call(kernel, name, experts, in_specs, out_specs, out_shape, scratch, flops, moved, args):
    return pl.pallas_call(
        kernel,
        name=name,
        grid_spec=pltpu.PrefetchScalarGridSpec(
            num_scalar_prefetch=1,
            grid=(experts,),
            in_specs=in_specs,
            out_specs=out_specs,
            scratch_shapes=scratch,
        ),
        out_shape=out_shape,
        compiler_params=pltpu.CompilerParams(
            dimension_semantics=("arbitrary",), vmem_limit_bytes=VMEM_LIMIT
        ),
        cost_estimate=pl.CostEstimate(flops=flops, bytes_accessed=moved, transcendentals=0),
    )(*args)


def expert_forward(half, slots, gates, weights, x_parts, capacity):
    experts, groups, tokens = slots.shape
    span, width = x_parts[0].shape
    with_out = len(weights) == 3
    rows = groups * capacity
    hidden = weights[0].shape[2]
    specs = [per_expert(groups, tokens)] * 2 + [per_expert(width, hidden)] * 2
    outs = [per_expert(rows, width // 2), per_expert(rows, hidden), per_expert(rows, hidden)]
    shapes = [
        jax.ShapeDtypeStruct((experts, rows, width // 2), bfloat),
        jax.ShapeDtypeStruct((experts, rows, hidden), single),
        jax.ShapeDtypeStruct((experts, rows, hidden), single),
    ]
    scratch = [pltpu.VMEM((rows, width), bfloat)]
    if with_out:
        specs += [per_expert(hidden, width)]
        outs += [resident(groups, span, width)] * 2
        shapes += [jax.ShapeDtypeStruct((groups, span, width), bfloat)] * 2
        scratch += [pltpu.VMEM((groups, span, width), single)] * 2
    specs += [resident(span, width)] * (2 * groups)
    once = 2 * experts * rows * width
    flops = once * (tokens + 2 * hidden) + (once * (tokens + hidden) if with_out else 0)
    moved = 2 * experts * (len(weights) * width * hidden + rows * width // 2 + 4 * rows * hidden)
    return expert_call(
        functools.partial(forward_kernel, groups, with_out),
        "expert_forward" if with_out else "expert_forward_far",
        experts, specs, outs, shapes, scratch, flops, moved,
        (half, slots, gates) + tuple(weights) + tuple(x_parts),
    )


def expert_backward(half, slots, gates, weights, g_parts, gate_pre, up_pre, capacity):
    experts, groups, tokens = slots.shape
    span, width = g_parts[0].shape
    rows = groups * capacity
    hidden = weights[0].shape[2]
    specs = [per_expert(groups, tokens)] * 2 + [per_expert(width, hidden)] * 2
    specs += [per_expert(hidden, width)] + [resident(span, width)] * (2 * groups)
    specs += [per_expert(rows, hidden)] * 2
    outs = [per_expert(rows, width // 2)] + [per_expert(rows, hidden)] * 3
    outs += [per_expert(groups, tokens)] + [resident(groups, span, width)] * 2
    shapes = [jax.ShapeDtypeStruct((experts, rows, width // 2), bfloat)]
    shapes += [jax.ShapeDtypeStruct((experts, rows, hidden), bfloat)] * 3
    shapes += [jax.ShapeDtypeStruct((experts, groups, tokens), single)]
    shapes += [jax.ShapeDtypeStruct((groups, span, width), bfloat)] * 2
    scratch = [pltpu.VMEM((rows, width), bfloat)]
    scratch += [pltpu.VMEM((groups, span, width), single)] * 2
    flops = 2 * experts * rows * width * (2 * tokens + 3 * hidden)
    moved = 2 * experts * (3 * width * hidden + rows * width // 2 + 7 * rows * hidden)
    return expert_call(
        functools.partial(backward_kernel, groups),
        "expert_backward",
        experts, specs, outs, shapes, scratch, flops, moved,
        (half, slots, gates) + tuple(weights) + tuple(g_parts) + (gate_pre, up_pre),
    )


def expert_weights(half, slots, gates, down_w, g_parts, far, near, capacity):
    experts, groups, tokens = slots.shape
    span, width = g_parts[0].shape
    rows = groups * capacity
    hidden = down_w.shape[1]
    wide, thin = per_expert(rows, width // 2), per_expert(rows, hidden)
    specs = [per_expert(groups, tokens)] * 2 + [per_expert(hidden, width)]
    specs += [resident(span, width)] * (2 * groups)
    specs += [thin, thin, wide, wide, wide, thin, thin, thin]
    outs = [per_expert(width // 2, hidden)] * 2 + [per_expert(hidden, width // 2)]
    shapes = [jax.ShapeDtypeStruct((experts, width // 2, hidden), bfloat)] * 2
    shapes += [jax.ShapeDtypeStruct((experts, hidden, width // 2), bfloat)]
    scratch = [pltpu.VMEM((rows, width), bfloat)]
    flops = 2 * experts * rows * width * (tokens + 4 * hidden)
    moved = 2 * experts * (3 * width * hidden + 3 * rows * width // 2 + 7 * rows * hidden)
    return expert_call(
        functools.partial(weights_kernel, groups),
        "expert_weights",
        experts, specs, outs, shapes, scratch, flops, moved,
        (half, slots, gates, down_w) + tuple(g_parts) + tuple(far) + tuple(near),
    )


def rope_tables(length, head_size):
    half_size = head_size // 2
    frequency = THETA ** (-jnp.arange(half_size, dtype=jnp.float32) * 2.0 / head_size)
    angles = jnp.arange(length, dtype=jnp.float32)[:, None] * frequency[None, :]
    return (jnp.cos(angles), jnp.sin(angles))


def apply_rotary(value_matrix, cosine_table, sine_table):
    half_size = value_matrix.shape[-1] // 2
    first_half = value_matrix[..., :half_size]
    second_half = value_matrix[..., half_size:]
    cosine_rows = cosine_table[:, None, :]
    sine_rows = sine_table[:, None, :]
    return jnp.concatenate(
        [
            first_half * cosine_rows - second_half * sine_rows,
            second_half * cosine_rows + first_half * sine_rows,
        ],
        axis=-1,
    )


def rotate_back(grads, cosine_table, sine_table):
    half_size = grads.shape[-1] // 2
    first_half = grads[..., :half_size]
    second_half = grads[..., half_size:]
    cosine_rows = cosine_table[:, None, :]
    sine_rows = sine_table[:, None, :]
    return jnp.concatenate(
        [
            first_half * cosine_rows + second_half * sine_rows,
            second_half * cosine_rows - first_half * sine_rows,
        ],
        axis=-1,
    )


def rms_forward(value_matrix, gain):
    inverse = lax.rsqrt(jnp.mean(value_matrix * value_matrix, axis=-1, keepdims=True) + EPS)
    return (value_matrix * inverse * gain, inverse)


def rms_backward(value_matrix, inverse, gain, grad_normed):
    scaled = grad_normed * gain
    grad_gain = jnp.sum(grad_normed * value_matrix * inverse, axis=0)
    grad_values = inverse * scaled - value_matrix * inverse**3 * jnp.mean(
        scaled * value_matrix, axis=-1, keepdims=True
    )
    return (grad_values, grad_gain)


def masked_scores(query_part, key_matrix, row_begin, length):
    scores = jnp.einsum(
        "qkge,tke->kgqt", query_part, key_matrix, preferred_element_type=jnp.float32
    )
    query_block = (row_begin + jnp.arange(query_part.shape[0], dtype=jnp.int32)) // ABLK
    key_block = jnp.arange(length, dtype=jnp.int32) // ABLK
    allowed = query_block[:, None] >= key_block[None, :]
    return jnp.where(allowed, scores, -1e30)


def attend_forward(args):
    queries, key_matrix, value_matrix = args
    length, kv_heads, head_size = key_matrix.shape
    group_size = queries.shape[1] // kv_heads
    rows_block = min(512, length)
    grouped = queries.reshape(length, kv_heads, group_size, head_size)

    def one_block(row_begin):
        scores = masked_scores(grouped, key_matrix, row_begin, length)
        row_peak = jnp.max(scores, axis=-1, keepdims=True)
        weights = jnp.exp(scores - row_peak)
        totals = jnp.sum(weights, axis=-1, keepdims=True)
        weights_low = (weights / totals).astype(jnp.bfloat16)
        outputs = jnp.einsum(
            "kgqt,tke->qkge", weights_low, value_matrix, preferred_element_type=jnp.float32
        )
        return (
            outputs.reshape(rows_block, kv_heads * group_size * head_size),
            (row_peak + jnp.log(totals))[..., 0],
        )

    outputs, log_sums = lax.map(one_block, jnp.arange(0, length, rows_block, dtype=jnp.int32))
    return (outputs.reshape(length, kv_heads * group_size * head_size), log_sums)


def attend_backward(args):
    queries, key_matrix, value_matrix, log_sums, grad_mixed = args
    length, kv_heads, head_size = key_matrix.shape
    group_size = queries.shape[1] // kv_heads
    rows_block = min(512, length)
    grouped = queries.reshape(length, kv_heads, group_size, head_size)
    grad_grouped = grad_mixed.reshape(length, kv_heads, group_size, head_size)

    def one_block(running, inputs):
        row_begin, block_sums = inputs
        scores = masked_scores(grouped, key_matrix, row_begin, length)
        probs = jnp.exp(scores - block_sums[..., None])
        grad_probs = jnp.einsum(
            "qkge,tke->kgqt", grad_grouped, value_matrix, preferred_element_type=jnp.float32
        )
        row_inner = jnp.sum(probs * grad_probs, axis=-1, keepdims=True)
        grad_scores = (probs * (grad_probs - row_inner)).astype(jnp.bfloat16)
        grad_query = jnp.einsum(
            "kgqt,tke->qkge", grad_scores, key_matrix, preferred_element_type=jnp.float32
        )
        grad_key = running[0] + jnp.einsum(
            "kgqt,qkge->tke", grad_scores, grouped, preferred_element_type=jnp.float32
        )
        grad_value = running[1] + jnp.einsum(
            "kgqt,qkge->tke",
            probs.astype(jnp.bfloat16),
            grad_grouped,
            preferred_element_type=jnp.float32,
        )
        return (
            (grad_key, grad_value),
            grad_query.reshape(rows_block, kv_heads * group_size, head_size),
        )

    zero_keys = jnp.zeros(key_matrix.shape, jnp.float32)
    starts = jnp.arange(0, length, rows_block, dtype=jnp.int32)
    (grad_key, grad_value), grad_query = lax.scan(
        one_block, (zero_keys, zero_keys), (starts, log_sums)
    )
    return (grad_query.reshape(length, kv_heads * group_size, head_size), grad_key, grad_value)


def assemble(mine, other):
    first = lax.axis_index("tensor") == 0
    return jnp.concatenate([jnp.where(first, mine, other), jnp.where(first, other, mine)], axis=0)


def both_halves(mine_groups):
    parts = []
    for mine in mine_groups:
        parts += [mine, swap(mine)]
    return parts


def combine_groups(mine, other):
    total = None
    for group in range(mine.shape[0]):
        part = mine[group].astype(single) + swap(other[group]).astype(single)
        if group:
            part = to_peer(part.astype(bfloat), "expert", group).astype(single)
        total = part if total is None else total + part
    return total


def on_device(
    tokens,
    teacher,
    routes,
    valid,
    teacher_rows,
    norm_attn,
    norm_moe,
    w_query,
    key_projection_weight,
    value_projection_weight,
    w_out,
    w_router,
    w_gate,
    w_up,
    w_down,
):
    rows_dev, model_width = tokens.shape
    seq_count = rows_dev // SEQUENCE_LENGTH
    heads_local = w_query.shape[1] // HEAD_DIMENSION
    kv_local = key_projection_weight.shape[1] // HEAD_DIMENSION
    query_width = w_query.shape[1]
    key_width = key_projection_weight.shape[1]
    experts_local = w_gate.shape[0]
    owners = lax.axis_size("expert")
    count_dp = lax.axis_size("dp")
    groups = count_dp * owners
    all_experts = experts_local * owners
    top_count = routes.shape[1]
    capacity = rows_dev * top_count * 5 // (4 * all_experts)
    at_dp, at_ex, core = lax.axis_index("dp"), lax.axis_index("expert"), lax.axis_index("tensor")
    span = rows_dev // 2
    shards = count_dp // 2
    half = (at_dp // shards).astype(jnp.int32).reshape(1)

    def mine_of(value, axis=0):
        return lax.dynamic_slice_in_dim(value, core * span, span, axis)

    def other_of(value, axis=0):
        return lax.dynamic_slice_in_dim(value, (1 - core) * span, span, axis)

    routes_t = routes.T
    routes_t = jnp.concatenate([mine_of(routes_t, 1), other_of(routes_t, 1)], axis=1)
    routes_two = jnp.stack([routes_t, to_mirror(routes_t)])
    all_routes = jnp.stack(gather_groups(routes_two), axis=1)
    expert_ids = jnp.arange(all_experts, dtype=jnp.int32)
    local_ids = at_ex * experts_local + jnp.arange(experts_local, dtype=jnp.int32)
    local_mask = jnp.any(all_routes[:, :, None] == local_ids[:, None, None], axis=3)
    earlier = jnp.triu(jnp.ones((rows_dev, rows_dev), bfloat), 1)
    before = jnp.dot(local_mask.astype(bfloat), earlier, preferred_element_type=single)
    slots = jnp.where(local_mask, before.astype(jnp.int32), -1).transpose(0, 2, 1, 3)
    mine_mask = jnp.any(routes_t[None, :, :span] == expert_ids[:, None, None], axis=1)

    valid_rows = valid.astype(single)
    valid_count = sum_all(jnp.full((8, 128), jnp.sum(valid_rows)), ("dp", "expert"))[0, 0]
    loss_scale = rows_dev * groups / valid_count
    inputs = tokens.astype(single)
    normed_first, inverse_first = rms_forward(inputs, norm_attn)
    attention_input = normed_first.astype(bfloat)
    cosine_table, sine_table = rope_tables(SEQUENCE_LENGTH, HEAD_DIMENSION)
    factor = HEAD_DIMENSION ** (-0.5)
    query_raw = jnp.dot(attention_input, w_query, preferred_element_type=single).reshape(
        seq_count, SEQUENCE_LENGTH, heads_local, HEAD_DIMENSION
    )
    key_unrotated = jnp.dot(
        attention_input, key_projection_weight, preferred_element_type=single
    ).reshape(seq_count, SEQUENCE_LENGTH, kv_local, HEAD_DIMENSION)
    value_unprojected = jnp.dot(
        attention_input, value_projection_weight, preferred_element_type=single
    ).reshape(seq_count, SEQUENCE_LENGTH, kv_local, HEAD_DIMENSION)
    queries = (apply_rotary(query_raw, cosine_table, sine_table) * factor).astype(bfloat)
    key_matrix = apply_rotary(key_unrotated, cosine_table, sine_table).astype(bfloat)
    value_matrix = value_unprojected.astype(bfloat)
    outputs, log_sums = lax.map(attend_forward, (queries, key_matrix, value_matrix))
    attn_low = outputs.reshape(rows_dev, heads_local * HEAD_DIMENSION).astype(bfloat)
    attn_part = jnp.dot(attn_low, w_out, preferred_element_type=single)

    hidden_first = mine_of(inputs) + mine_of(attn_part) + swap(other_of(attn_part))
    normed_second, inverse_second = rms_forward(hidden_first, norm_moe)
    moe_in = normed_second.astype(bfloat)
    logits = lax.dot_general(
        w_router, moe_in, (((0,), (1,)), ((), ())), preferred_element_type=single
    )
    peak = jnp.max(jnp.where(mine_mask, logits, -jnp.inf), axis=0, keepdims=True)
    exponent = jnp.where(mine_mask, jnp.exp(logits - peak), 0.0)
    gates = exponent / jnp.sum(exponent, axis=0, keepdims=True)

    def local_gates(gates_mine):
        stacked = jnp.stack(gather_groups(gates_mine))
        local = lax.dynamic_slice_in_dim(stacked, at_ex * experts_local, experts_local, 1)
        return jnp.concatenate([local, swap(local)], axis=2).transpose(1, 0, 2)

    near_gates = local_gates(gates)
    near_x = both_halves(gather_groups(moe_in))
    near_rows, gate_pre, up_pre, part_mine, part_other = expert_forward(
        half, slots[0], near_gates, (w_gate, w_up, w_down), near_x, capacity
    )
    far_gates = local_gates(to_mirror(gates))
    far_x = both_halves(gather_groups(to_mirror(moe_in)))
    far_rows, far_gate_pre, far_up_pre = expert_forward(
        half, slots[1], far_gates, (w_gate, w_up), far_x, capacity
    )

    layer_out = hidden_first + combine_groups(part_mine, part_other)
    rows_wanted = mine_of(teacher_rows[0])
    chooser = (rows_wanted[:, None] == jnp.arange(rows_dev, dtype=jnp.int32)).astype(bfloat)
    target = jnp.dot(chooser, teacher, preferred_element_type=single)
    grad_layer = loss_scale * mine_of(valid_rows)[:, None] * (layer_out - target)
    layer_low = layer_out.astype(bfloat)
    block_out = assemble(layer_low, swap(layer_low))

    grad_low = grad_layer.astype(bfloat)
    near_g = both_halves(gather_groups(grad_low))
    near_grad, hidden_low, grad_gate_pre, grad_up_pre, grad_gates, part_mine, part_other = (
        expert_backward(
            half, slots[0], near_gates, (w_gate, w_up, w_down), near_g, gate_pre, up_pre, capacity
        )
    )
    far_g = both_halves(gather_groups(to_mirror(grad_low)))
    d_gate, d_up, d_down = expert_weights(
        half,
        slots[1],
        far_gates,
        w_down,
        far_g,
        (far_gate_pre, far_up_pre, far_rows),
        (near_rows, near_grad, hidden_low, grad_gate_pre, grad_up_pre),
        capacity,
    )

    grad_gates = grad_gates.transpose(1, 0, 2)
    gate_parts = grad_gates[:, :, :span] + swap(grad_gates[:, :, span:])
    owner_ids = jnp.arange(owners, dtype=jnp.int32)[:, None, None]
    grad_gates = jnp.zeros((owners, experts_local, span), single)
    for step in range(owners):
        part = gate_parts[step]
        if step:
            part = to_peer(part, "expert", step)
        grad_gates = grad_gates + jnp.where(owner_ids == (at_ex ^ step), part[None], 0.0)
    grad_gates = grad_gates.reshape(all_experts, span)
    inner = jnp.sum(gates * grad_gates, axis=0, keepdims=True)
    grad_logits = (gates * (grad_gates - inner)).astype(bfloat)

    grad_moe_in = combine_groups(part_mine, part_other) + lax.dot_general(
        grad_logits, w_router, (((0,), (1,)), ((), ())), preferred_element_type=single
    )
    grad_router_part = lax.dot_general(
        moe_in, grad_logits, (((0,), (1,)), ((), ())), preferred_element_type=single
    )
    grad_second, grad_norm_moe_part = rms_backward(
        hidden_first, inverse_second, norm_moe, grad_moe_in
    )
    grad_hidden_mine = grad_layer + grad_second
    grad_attn_mine = grad_hidden_mine.astype(bfloat)
    grad_attn = assemble(grad_attn_mine, swap(grad_attn_mine))
    grad_hidden_first = assemble(grad_hidden_mine, swap(grad_hidden_mine))
    small = jnp.concatenate([grad_router_part, grad_norm_moe_part[:, None]], axis=1)
    small = small + swap(small)
    grad_out_t = lax.dot_general(
        grad_attn, attn_low, (((0,), (0,)), ((), ())), preferred_element_type=single
    )
    filler = jnp.zeros((model_width, 128 - small.shape[1]), single)
    first_pack = scatter_dense(
        jnp.concatenate([grad_out_t, small, filler], axis=1).astype(bfloat)
    )

    grad_mixed = jnp.dot(grad_attn, w_out.T, preferred_element_type=single).astype(bfloat)
    grad_mixed = grad_mixed.reshape(seq_count, SEQUENCE_LENGTH, heads_local * HEAD_DIMENSION)
    grad_queries, grad_keys, grad_values = lax.map(
        attend_backward, (queries, key_matrix, value_matrix, log_sums, grad_mixed)
    )
    grad_query_raw = (
        rotate_back(grad_queries * factor, cosine_table, sine_table)
        .astype(bfloat)
        .reshape(rows_dev, heads_local * HEAD_DIMENSION)
    )
    grad_key_raw = (
        rotate_back(grad_keys, cosine_table, sine_table)
        .astype(bfloat)
        .reshape(rows_dev, kv_local * HEAD_DIMENSION)
    )
    grad_value_raw = grad_values.astype(bfloat).reshape(rows_dev, kv_local * HEAD_DIMENSION)
    grad_attn_in = (
        jnp.dot(grad_query_raw, w_query.T, preferred_element_type=single)
        + jnp.dot(grad_key_raw, key_projection_weight.T, preferred_element_type=single)
        + jnp.dot(grad_value_raw, value_projection_weight.T, preferred_element_type=single)
    ).astype(bfloat)
    grad_raw = jnp.concatenate([grad_query_raw, grad_key_raw, grad_value_raw], axis=1)
    grad_qkv = jnp.dot(attention_input.T, grad_raw, preferred_element_type=single)
    grad_attn_in = grad_attn_in.astype(single) + swap(grad_attn_in).astype(single)
    grad_first, grad_norm_attn_part = rms_backward(inputs, inverse_first, norm_attn, grad_attn_in)
    grad_tokens = grad_hidden_first + grad_first
    tail = jnp.concatenate(
        [grad_norm_attn_part[:, None], jnp.zeros((model_width, 127), single)], axis=1
    )
    second_pack = scatter_dense(jnp.concatenate([grad_qkv, tail], axis=1).astype(bfloat))

    at_shard = at_dp % shards

    def scatter_experts(value, axis):
        size = value.shape[axis] // shards
        total = None
        for step in range(shards):
            part = lax.dynamic_slice_in_dim(value, (at_shard ^ step) * size, size, axis)
            if step:
                part = to_peer(part, "dp", step)
            part = part.astype(single)
            total = part if total is None else total + part
        return total

    return (
        block_out,
        grad_tokens,
        second_pack[:, query_width + 2 * key_width],
        first_pack[:, query_width + all_experts],
        second_pack[:, :query_width],
        second_pack[:, query_width : query_width + key_width],
        second_pack[:, query_width + key_width : query_width + 2 * key_width],
        first_pack[:, :query_width].T,
        first_pack[:, query_width : query_width + all_experts],
        scatter_experts(d_gate, 1),
        scatter_experts(d_up, 1),
        scatter_experts(d_down, 2),
    )


def solution(mesh):
    placed = (
        P(("dp", "expert"), None),
        P(("dp", "expert"), None),
        P(("dp", "expert"), None),
        P(("dp", "expert")),
        P(("dp", "expert"), None),
        P(),
        P(),
        P(None, "tensor"),
        P(None, "tensor"),
        P(None, "tensor"),
        P("tensor", None),
        P(),
        P("expert", None, "tensor"),
        P("expert", None, "tensor"),
        P("expert", "tensor", None),
    )
    return jax.shard_map(
        on_device,
        mesh=mesh,
        in_specs=placed,
        out_specs=(
            P(("dp", "expert"), None),
            P(("dp", "expert"), None),
            P(("dp", "expert")),
            P(("dp", "expert")),
            P(("dp", "expert"), "tensor"),
            P(("dp", "expert"), "tensor"),
            P(("dp", "expert"), "tensor"),
            P("tensor", ("dp", "expert")),
            P(("dp", "expert"), None),
            P("expert", "dp", "tensor"),
            P("expert", "dp", "tensor"),
            P("expert", "tensor", "dp"),
        ),
        check_vma=False,
    )
```

```python
import functools

import jax
import jax.numpy as jnp
from jax import lax
from jax.experimental import pallas as pl
from jax.experimental.pallas import tpu as pltpu
from jax.sharding import PartitionSpec as P

HEAD_DIMENSION = 64
SEQUENCE_LENGTH = 512
ABLK = 256


EPS = 1e-06
THETA = 10000.0
bfloat = jnp.bfloat16
single = jnp.float32


def swap(value):
    return lax.ppermute(value, "tensor", [(0, 1), (1, 0)])


def to_peer(value, axis, step):
    return lax.ppermute(value, axis, [(i, i ^ step) for i in range(lax.axis_size(axis))])


def to_mirror(value):
    count = lax.axis_size("dp")
    return lax.ppermute(value, "dp", [(i, count - 1 - i) for i in range(count)])


def after(value, *others):
    return lax.optimization_barrier((value,) + others)[0]


def gather_groups(value):
    return [value] + [to_peer(value, "expert", s) for s in range(1, lax.axis_size("expert"))]


def gather_tokens(value):
    if lax.axis_size("expert") != 4:
        return gather_groups(value)
    cut = value.shape[0] // 2
    first, second = to_peer(value, "expert", 1), to_peer(value, "expert", 2)
    low, high = to_peer(second[:cut], "expert", 1), to_peer(first[cut:], "expert", 2)
    return [value, first, second, jnp.concatenate([low, high], axis=0)]


def sum_all(value, axes):
    for axis in axes:
        step = 1
        while step < lax.axis_size(axis):
            value = value + to_peer(value, axis, step)
            step *= 2
    return value


def scatter_dense(packed, kind=bfloat):
    count_dp, count_ex = lax.axis_size("dp"), lax.axis_size("expert")
    at_dp, at_ex = lax.axis_index("dp"), lax.axis_index("expert")
    block = packed.shape[0] // (count_dp * count_ex)
    cut = packed.reshape((count_dp, count_ex, block) + packed.shape[1:])

    def part(step):
        return lax.dynamic_index_in_dim(cut, at_ex ^ step, 1, keepdims=False)

    sent = [part(step).astype(kind) for step in range(1, count_ex)]
    total = part(0).astype(single)
    for step in range(1, count_ex):
        total = total + to_peer(sent[step - 1], "expert", step).astype(single)

    def row(step):
        return lax.dynamic_index_in_dim(total, at_dp ^ step, 0, keepdims=False)

    result = row(0)
    for step in range(1, count_dp):
        result = result + to_peer(row(step).astype(kind), "dp", step).astype(single)
    return result, sent


def dot(left, right):
    return lax.dot_general(left, right, (((1,), (0,)), ((), ())), preferred_element_type=single)


def dot_nt(left, right):
    return lax.dot_general(left, right, (((1,), (1,)), ((), ())), preferred_element_type=single)


def dot_tn(left, right):
    return lax.dot_general(left, right, (((0,), (0,)), ((), ())), preferred_element_type=single)


def picks(slots_ref, expert, group, capacity):
    slot = slots_ref[expert, group : group + 1, :]
    return slot == lax.broadcasted_iota(jnp.int32, (capacity, slot.shape[1]), 0)


def gather_kernel(group, slots_ref, mine, other, rows_ref, picked_ref):
    experts, capacity, width = rows_ref.shape
    span = mine.shape[0]
    for e in range(experts):
        picked_ref[e * capacity : (e + 1) * capacity, :] = picks(
            slots_ref, e, group, capacity
        ).astype(bfloat)
    rows = dot(picked_ref[:, :span], mine[...]) + dot(picked_ref[:, span:], other[...])
    rows_ref[...] = rows.astype(bfloat).reshape(experts, capacity, width)


def return_kernel(group, slots_ref, rows_ref, mine, other, picked_ref):
    experts, capacity, width = rows_ref.shape
    span = mine.shape[0]

    @pl.when(pl.program_id(0) == 0)
    def _():
        for e in range(experts):
            picked_ref[e * capacity : (e + 1) * capacity, :] = picks(
                slots_ref, e, group, capacity
            ).astype(bfloat)

    back = dot_tn(picked_ref[...], rows_ref[...].reshape(experts * capacity, width)).astype(bfloat)
    mine[...] = back[:span]
    other[...] = back[span:]


def slot_gates(slots_ref, gates_ref, groups, capacity):
    parts = []
    for g in range(groups):
        picked = picks(slots_ref, 0, g, capacity)
        gate = gates_ref[0, g : g + 1, :]
        parts.append(jnp.sum(jnp.where(picked, gate, 0.0), axis=1, keepdims=True))
    return jnp.concatenate(parts, axis=0)


def joined(refs):
    return jnp.concatenate([ref[0] for ref in refs], axis=0)


def forward_kernel(groups, with_out, slots_ref, gates_ref, gate_w, up_w, *refs):
    if with_out:
        down_w, refs = refs[0], refs[1:]
    row_refs, refs = refs[:groups], refs[groups:]
    gate_ref, up_ref = refs[:2]
    rows = joined(row_refs)
    gate_pre = dot(rows, gate_w[0])
    up_pre = dot(rows, up_w[0])
    gate_ref[0] = gate_pre
    up_ref[0] = up_pre
    if with_out:
        gates = slot_gates(slots_ref, gates_ref, groups, row_refs[0].shape[1])
        hidden = (gate_pre * jax.nn.sigmoid(gate_pre) * up_pre * gates).astype(bfloat)
        refs[2][0] = dot(hidden, down_w[0]).astype(bfloat)


def hidden_grads(gate_pre, up_pre, gates, grad_hidden):
    sig = jax.nn.sigmoid(gate_pre)
    silu = gate_pre * sig
    hidden = silu * up_pre
    grad_gates = jnp.sum(hidden * grad_hidden, axis=1, keepdims=True)
    scaled = grad_hidden * gates
    grad_gate_pre = (scaled * up_pre * sig * (1.0 + gate_pre * (1.0 - sig))).astype(bfloat)
    grad_up_pre = (scaled * silu).astype(bfloat)
    return (hidden * gates).astype(bfloat), grad_gate_pre, grad_up_pre, grad_gates


def backward_kernel(groups, slots_ref, gates_ref, gate_w, up_w, down_w, gate_ref, up_ref, *refs):
    row_refs, refs = refs[:groups], refs[groups:]
    hidden_ref, grad_gate_ref, grad_up_ref, gg_ref, back_ref = refs
    capacity = row_refs[0].shape[1]
    gates = slot_gates(slots_ref, gates_ref, groups, capacity)
    grad_hidden = dot_nt(joined(row_refs), down_w[0])
    hidden, grad_gate_pre, grad_up_pre, grad_gates = hidden_grads(
        gate_ref[0], up_ref[0], gates, grad_hidden
    )
    hidden_ref[0] = hidden
    grad_gate_ref[0] = grad_gate_pre
    grad_up_ref[0] = grad_up_pre
    back = dot_nt(grad_gate_pre, gate_w[0]) + dot_nt(grad_up_pre, up_w[0])
    back_ref[0] = back.astype(bfloat)
    for g in range(groups):
        own = grad_gates[g * capacity : (g + 1) * capacity]
        picked = picks(slots_ref, 0, g, capacity)
        gg_ref[0, g : g + 1, :] = jnp.sum(jnp.where(picked, own, 0.0), axis=0, keepdims=True)


def weights_kernel(groups, half_ref, slots_ref, gates_ref, down_w, gate_ref, up_ref, *refs):
    hidden_near, gate_near, up_near = refs[:3]
    near_x, near_g, far_x, far_g = (refs[3 + i * groups : 3 + (i + 1) * groups] for i in range(4))
    d_gate, d_up, d_down, rows_ref = refs[3 + 4 * groups :]
    capacity = far_g[0].shape[1]
    width = d_gate.shape[1]
    for g in range(groups):
        rows_ref[g * capacity : (g + 1) * capacity, :] = far_g[g][0]
    gates = slot_gates(slots_ref, gates_ref, groups, capacity)
    grad_hidden = dot_nt(rows_ref[...], down_w[0])
    hidden, grad_gate_pre, grad_up_pre, _ = hidden_grads(gate_ref[0], up_ref[0], gates, grad_hidden)
    grad_far = rows_ref[:, pl.ds(pl.multiple_of(half_ref[0] * width, 128), width)]
    d_down[0] = (dot_tn(hidden, grad_far) + dot_tn(hidden_near[0], joined(near_g))).astype(bfloat)
    far, near = joined(far_x), joined(near_x)
    d_gate[0] = (dot_tn(far, grad_gate_pre) + dot_tn(near, gate_near[0])).astype(bfloat)
    d_up[0] = (dot_tn(far, grad_up_pre) + dot_tn(near, up_near[0])).astype(bfloat)


def kernel_call(kernel, name, grid, in_specs, out_specs, out_shape, scratch, flops, moved, vmem, args, prefetch=0):
    return pl.pallas_call(
        kernel,
        name=name,
        grid_spec=pltpu.PrefetchScalarGridSpec(
            num_scalar_prefetch=prefetch,
            grid=grid,
            in_specs=in_specs,
            out_specs=out_specs,
            scratch_shapes=scratch,
        ),
        out_shape=out_shape,
        compiler_params=pltpu.CompilerParams(
            dimension_semantics=("arbitrary",), vmem_limit_bytes=vmem * 1024 * 1024
        ),
        cost_estimate=pl.CostEstimate(flops=flops, bytes_accessed=moved, transcendentals=0),
    )(*args)


def per_expert(*shape):
    return pl.BlockSpec((1,) + shape, lambda e, *_: (e,) + (0,) * len(shape))


def half_wide(rows, width):
    return pl.BlockSpec((1, rows, width), lambda e, half: (e, 0, half[0]))


def gather_rows(slots, group, mine, other, capacity):
    experts, groups, tokens = slots.shape
    span, width = mine.shape
    chunk = experts // 2 if experts % 2 == 0 else experts
    whole = pl.BlockSpec((span, width), lambda i: (0, 0))
    return kernel_call(
        functools.partial(gather_kernel, group),
        "gather_rows",
        (experts // chunk,),
        [pl.BlockSpec((chunk, groups, tokens), lambda i: (i, 0, 0)), whole, whole],
        pl.BlockSpec((chunk, capacity, width), lambda i: (i, 0, 0)),
        jax.ShapeDtypeStruct((experts, capacity, width), bfloat),
        [pltpu.VMEM((chunk * capacity, tokens), bfloat)],
        2 * experts * capacity * tokens * width,
        2 * (experts * capacity + tokens) * width,
        24,
        (slots, mine, other),
    )


def return_rows(slots, group, rows, capacity, span):
    experts, groups, tokens = slots.shape
    width = rows.shape[2]
    cut = width // 3
    part = pl.BlockSpec((span, cut), lambda n: (0, n))
    return kernel_call(
        functools.partial(return_kernel, group),
        "return_rows",
        (3,),
        [
            pl.BlockSpec((experts, groups, tokens), lambda n: (0, 0, 0)),
            pl.BlockSpec((experts, capacity, cut), lambda n: (0, group, n)),
        ],
        [part, part],
        [jax.ShapeDtypeStruct((span, width), bfloat)] * 2,
        [pltpu.VMEM((experts * capacity, tokens), bfloat)],
        2 * experts * capacity * tokens * width,
        2 * (experts * capacity + tokens) * width,
        24,
        (slots, rows),
    )


def expert_forward(slots, gates, weights, rows):
    experts, groups, tokens = slots.shape
    capacity, width = rows[0].shape[1:]
    with_out = len(weights) == 3
    total = groups * capacity
    hidden = weights[0].shape[2]
    specs = [per_expert(groups, tokens)] * 2 + [per_expert(width, hidden)] * 2
    outs = [per_expert(total, hidden)] * 2
    shapes = [jax.ShapeDtypeStruct((experts, total, hidden), single)] * 2
    if with_out:
        specs += [per_expert(hidden, width)]
        outs += [per_expert(total, width)]
        shapes += [jax.ShapeDtypeStruct((experts, total, width), bfloat)]
    specs += [per_expert(capacity, width)] * groups
    return kernel_call(
        functools.partial(forward_kernel, groups, with_out),
        "expert_forward" if with_out else "expert_forward_far",
        (experts,), specs, outs, shapes, [],
        2 * experts * total * width * hidden * len(weights),
        2 * experts * (len(weights) * (width * hidden) + (len(weights) - 1) * total * width + 4 * total * hidden),
        32,
        (slots, gates) + tuple(weights) + tuple(rows),
    )


def expert_backward(slots, gates, weights, gate_pre, up_pre, rows):
    experts, groups, tokens = slots.shape
    capacity, width = rows[0].shape[1:]
    total = groups * capacity
    hidden = weights[0].shape[2]
    thin = per_expert(total, hidden)
    specs = [per_expert(groups, tokens)] * 2 + [per_expert(width, hidden)] * 2
    specs += [per_expert(hidden, width), thin, thin] + [per_expert(capacity, width)] * groups
    outs = [thin] * 3 + [per_expert(groups, tokens), per_expert(total, width)]
    shapes = [jax.ShapeDtypeStruct((experts, total, hidden), bfloat)] * 3
    shapes += [jax.ShapeDtypeStruct((experts, groups, tokens), single)]
    shapes += [jax.ShapeDtypeStruct((experts, total, width), bfloat)]
    return kernel_call(
        functools.partial(backward_kernel, groups),
        "expert_backward",
        (experts,), specs, outs, shapes, [],
        2 * experts * total * width * hidden * 3,
        2 * experts * (3 * width * hidden + 2 * total * width + 7 * total * hidden),
        36,
        (slots, gates) + tuple(weights) + (gate_pre, up_pre) + tuple(rows),
    )


def expert_weights(half, slots, gates, down_w, far, near, near_x, near_g, far_x, far_g):
    experts, groups, tokens = slots.shape
    capacity, width = far_g[0].shape[1:]
    total = groups * capacity
    hidden = down_w.shape[1]
    thin, wide = per_expert(total, hidden), half_wide(capacity, width // 2)
    specs = [per_expert(groups, tokens)] * 2 + [per_expert(hidden, width)] + [thin] * 5
    specs += [wide] * (3 * groups) + [per_expert(capacity, width)] * groups
    outs = [per_expert(width // 2, hidden)] * 2 + [per_expert(hidden, width // 2)]
    shapes = [jax.ShapeDtypeStruct((experts, width // 2, hidden), bfloat)] * 2
    shapes += [jax.ShapeDtypeStruct((experts, hidden, width // 2), bfloat)]
    return kernel_call(
        functools.partial(weights_kernel, groups),
        "expert_weights",
        (experts,), specs, outs, shapes, [pltpu.VMEM((total, width), bfloat)],
        2 * experts * total * width * hidden * 4,
        2 * experts * (5 * width * hidden // 2 + 5 * total * width // 2 + 7 * total * hidden),
        40,
        (half, slots, gates, down_w) + tuple(far) + tuple(near)
        + tuple(near_x) + tuple(near_g) + tuple(far_x) + tuple(far_g),
        prefetch=1,
    )


def rope_tables(length, head_size):
    half_size = head_size // 2
    frequency = THETA ** (-jnp.arange(half_size, dtype=jnp.float32) * 2.0 / head_size)
    angles = jnp.arange(length, dtype=jnp.float32)[:, None] * frequency[None, :]
    return (jnp.cos(angles), jnp.sin(angles))


def apply_rotary(value_matrix, cosine_table, sine_table):
    half_size = value_matrix.shape[-1] // 2
    first_half = value_matrix[..., :half_size]
    second_half = value_matrix[..., half_size:]
    cosine_rows = cosine_table[:, None, :]
    sine_rows = sine_table[:, None, :]
    return jnp.concatenate(
        [
            first_half * cosine_rows - second_half * sine_rows,
            second_half * cosine_rows + first_half * sine_rows,
        ],
        axis=-1,
    )


def rotate_back(grads, cosine_table, sine_table):
    half_size = grads.shape[-1] // 2
    first_half = grads[..., :half_size]
    second_half = grads[..., half_size:]
    cosine_rows = cosine_table[:, None, :]
    sine_rows = sine_table[:, None, :]
    return jnp.concatenate(
        [
            first_half * cosine_rows + second_half * sine_rows,
            second_half * cosine_rows - first_half * sine_rows,
        ],
        axis=-1,
    )


def rms_forward(value_matrix, gain):
    inverse = lax.rsqrt(jnp.mean(value_matrix * value_matrix, axis=-1, keepdims=True) + EPS)
    return (value_matrix * inverse * gain, inverse)


def rms_backward(value_matrix, inverse, gain, grad_normed):
    scaled = grad_normed * gain
    grad_gain = jnp.sum(grad_normed * value_matrix * inverse, axis=0)
    grad_values = inverse * scaled - value_matrix * inverse**3 * jnp.mean(
        scaled * value_matrix, axis=-1, keepdims=True
    )
    return (grad_values, grad_gain)


def masked_scores(query_part, key_matrix, row_begin, length):
    scores = jnp.einsum(
        "qkge,tke->kgqt", query_part, key_matrix, preferred_element_type=jnp.float32
    )
    query_block = (row_begin + jnp.arange(query_part.shape[0], dtype=jnp.int32)) // ABLK
    key_block = jnp.arange(length, dtype=jnp.int32) // ABLK
    allowed = query_block[:, None] >= key_block[None, :]
    return jnp.where(allowed, scores, -1e30)


def attend_forward(args):
    queries, key_matrix, value_matrix = args
    length, kv_heads, head_size = key_matrix.shape
    group_size = queries.shape[1] // kv_heads
    rows_block = min(512, length)
    grouped = queries.reshape(length, kv_heads, group_size, head_size)

    def one_block(row_begin):
        scores = masked_scores(grouped, key_matrix, row_begin, length)
        row_peak = jnp.max(scores, axis=-1, keepdims=True)
        weights = jnp.exp(scores - row_peak)
        totals = jnp.sum(weights, axis=-1, keepdims=True)
        weights_low = (weights / totals).astype(jnp.bfloat16)
        outputs = jnp.einsum(
            "kgqt,tke->qkge", weights_low, value_matrix, preferred_element_type=jnp.float32
        )
        return (
            outputs.reshape(rows_block, kv_heads * group_size * head_size),
            (row_peak + jnp.log(totals))[..., 0],
        )

    outputs, log_sums = lax.map(one_block, jnp.arange(0, length, rows_block, dtype=jnp.int32))
    return (outputs.reshape(length, kv_heads * group_size * head_size), log_sums)


def attend_backward(args):
    queries, key_matrix, value_matrix, log_sums, grad_mixed = args
    length, kv_heads, head_size = key_matrix.shape
    group_size = queries.shape[1] // kv_heads
    rows_block = min(512, length)
    grouped = queries.reshape(length, kv_heads, group_size, head_size)
    grad_grouped = grad_mixed.reshape(length, kv_heads, group_size, head_size)

    def one_block(running, inputs):
        row_begin, block_sums = inputs
        scores = masked_scores(grouped, key_matrix, row_begin, length)
        probs = jnp.exp(scores - block_sums[..., None])
        grad_probs = jnp.einsum(
            "qkge,tke->kgqt", grad_grouped, value_matrix, preferred_element_type=jnp.float32
        )
        row_inner = jnp.sum(probs * grad_probs, axis=-1, keepdims=True)
        grad_scores = (probs * (grad_probs - row_inner)).astype(jnp.bfloat16)
        grad_query = jnp.einsum(
            "kgqt,tke->qkge", grad_scores, key_matrix, preferred_element_type=jnp.float32
        )
        grad_key = running[0] + jnp.einsum(
            "kgqt,qkge->tke", grad_scores, grouped, preferred_element_type=jnp.float32
        )
        grad_value = running[1] + jnp.einsum(
            "kgqt,qkge->tke",
            probs.astype(jnp.bfloat16),
            grad_grouped,
            preferred_element_type=jnp.float32,
        )
        return (
            (grad_key, grad_value),
            grad_query.reshape(rows_block, kv_heads * group_size, head_size),
        )

    zero_keys = jnp.zeros(key_matrix.shape, jnp.float32)
    starts = jnp.arange(0, length, rows_block, dtype=jnp.int32)
    (grad_key, grad_value), grad_query = lax.scan(
        one_block, (zero_keys, zero_keys), (starts, log_sums)
    )
    return (grad_query.reshape(length, kv_heads * group_size, head_size), grad_key, grad_value)


def assemble(mine, other):
    first = lax.axis_index("tensor") == 0
    return jnp.concatenate([jnp.where(first, mine, other), jnp.where(first, other, mine)], axis=0)


def all_rows(slots, mine_groups, capacity):
    return [
        gather_rows(slots, g, mine, swap(mine), capacity) for g, mine in enumerate(mine_groups)
    ]


def combine_groups(slots, rows, capacity, span):
    owners = slots.shape[1]
    parts = {}
    for group in reversed(range(owners)):
        mine, other = return_rows(slots, group, rows, capacity, span)
        parts[group] = mine.astype(single) + swap(other).astype(single)
    if owners != 4:
        total = parts[0]
        for step in range(1, owners):
            total = total + to_peer(parts[step].astype(bfloat), "expert", step).astype(single)
        return total
    cut = span // 2
    far = parts[3].astype(bfloat)
    low = to_peer(far[:cut], "expert", 1).astype(single)
    high = to_peer(far[cut:], "expert", 2).astype(single)
    first = jnp.concatenate([parts[1][:cut], parts[1][cut:] + high], axis=0).astype(bfloat)
    second = jnp.concatenate([parts[2][:cut] + low, parts[2][cut:]], axis=0).astype(bfloat)
    first, second = to_peer(first, "expert", 1), to_peer(second, "expert", 2)
    return parts[0] + first.astype(single) + second.astype(single)


def on_device(
    tokens,
    teacher,
    routes,
    valid,
    teacher_rows,
    norm_attn,
    norm_moe,
    w_query,
    key_projection_weight,
    value_projection_weight,
    w_out,
    w_router,
    w_gate,
    w_up,
    w_down,
):
    rows_dev, model_width = tokens.shape
    seq_count = rows_dev // SEQUENCE_LENGTH
    heads_local = w_query.shape[1] // HEAD_DIMENSION
    kv_local = key_projection_weight.shape[1] // HEAD_DIMENSION
    query_width = w_query.shape[1]
    key_width = key_projection_weight.shape[1]
    experts_local = w_gate.shape[0]
    owners = lax.axis_size("expert")
    count_dp = lax.axis_size("dp")
    groups = count_dp * owners
    all_experts = experts_local * owners
    top_count = routes.shape[1]
    capacity = rows_dev * top_count * 5 // (4 * all_experts)
    at_dp, at_ex, core = lax.axis_index("dp"), lax.axis_index("expert"), lax.axis_index("tensor")
    span = rows_dev // 2
    shards = count_dp // 2
    half = (at_dp // shards).astype(jnp.int32).reshape(1)

    def mine_of(value, axis=0):
        return lax.dynamic_slice_in_dim(value, core * span, span, axis)

    def other_of(value, axis=0):
        return lax.dynamic_slice_in_dim(value, (1 - core) * span, span, axis)

    routes_t = routes.T
    routes_t = jnp.concatenate([mine_of(routes_t, 1), other_of(routes_t, 1)], axis=1)
    routes_two = jnp.stack([routes_t, to_mirror(routes_t)])
    all_routes = jnp.stack(gather_groups(routes_two), axis=1)
    expert_ids = jnp.arange(all_experts, dtype=jnp.int32)
    local_ids = at_ex * experts_local + jnp.arange(experts_local, dtype=jnp.int32)
    local_mask = jnp.any(all_routes[:, :, None] == local_ids[:, None, None], axis=3)
    earlier = jnp.triu(jnp.ones((rows_dev, rows_dev), bfloat), 1)
    before = jnp.dot(local_mask.astype(bfloat), earlier, preferred_element_type=single)
    slots = jnp.where(local_mask, before.astype(jnp.int32), -1).transpose(0, 2, 1, 3)
    mine_mask = jnp.any(routes_t[None, :, :span] == expert_ids[:, None, None], axis=1)

    valid_rows = valid.astype(single)
    valid_count = sum_all(jnp.full((8, 128), jnp.sum(valid_rows)), ("dp", "expert"))[0, 0]
    loss_scale = rows_dev * groups / valid_count
    inputs = tokens.astype(single)
    normed_first, inverse_first = rms_forward(inputs, norm_attn)
    attention_input = normed_first.astype(bfloat)
    cosine_table, sine_table = rope_tables(SEQUENCE_LENGTH, HEAD_DIMENSION)
    factor = HEAD_DIMENSION ** (-0.5)
    query_raw = jnp.dot(attention_input, w_query, preferred_element_type=single).reshape(
        seq_count, SEQUENCE_LENGTH, heads_local, HEAD_DIMENSION
    )
    key_unrotated = jnp.dot(
        attention_input, key_projection_weight, preferred_element_type=single
    ).reshape(seq_count, SEQUENCE_LENGTH, kv_local, HEAD_DIMENSION)
    value_unprojected = jnp.dot(
        attention_input, value_projection_weight, preferred_element_type=single
    ).reshape(seq_count, SEQUENCE_LENGTH, kv_local, HEAD_DIMENSION)
    queries = (apply_rotary(query_raw, cosine_table, sine_table) * factor).astype(bfloat)
    key_matrix = apply_rotary(key_unrotated, cosine_table, sine_table).astype(bfloat)
    value_matrix = value_unprojected.astype(bfloat)
    outputs, log_sums = lax.map(attend_forward, (queries, key_matrix, value_matrix))
    attn_low = outputs.reshape(rows_dev, heads_local * HEAD_DIMENSION).astype(bfloat)
    attn_low = after(attn_low, slots, valid_count)
    attn_part = jnp.dot(attn_low, w_out, preferred_element_type=single)

    hidden_first = mine_of(inputs) + mine_of(attn_part) + swap(other_of(attn_part))
    normed_second, inverse_second = rms_forward(hidden_first, norm_moe)
    moe_in = normed_second.astype(bfloat)
    logits = lax.dot_general(
        w_router, moe_in, (((0,), (1,)), ((), ())), preferred_element_type=single
    )
    peak = jnp.max(jnp.where(mine_mask, logits, -jnp.inf), axis=0, keepdims=True)
    exponent = jnp.where(mine_mask, jnp.exp(logits - peak), 0.0)
    gates = exponent / jnp.sum(exponent, axis=0, keepdims=True)

    def local_gates(gates_mine):
        stacked = jnp.stack(gather_groups(gates_mine))
        local = lax.dynamic_slice_in_dim(stacked, at_ex * experts_local, experts_local, 1)
        return jnp.concatenate([local, swap(local)], axis=2).transpose(1, 0, 2)

    near_tokens = gather_tokens(moe_in)
    near_gates = local_gates(gates)
    near_x = all_rows(slots[0], near_tokens, capacity)
    gate_pre, up_pre, expert_out = expert_forward(
        slots[0], near_gates, (w_gate, w_up, w_down), near_x
    )
    far_gates = local_gates(after(to_mirror(gates), near_gates))
    far_x = all_rows(
        slots[1], gather_tokens(after(to_mirror(moe_in), near_tokens[-1])), capacity
    )
    far_gate_pre, far_up_pre = expert_forward(slots[1], far_gates, (w_gate, w_up), far_x)

    layer_out = hidden_first + combine_groups(slots[0], expert_out, capacity, span)
    rows_wanted = mine_of(teacher_rows[0])
    chooser = (rows_wanted[:, None] == jnp.arange(rows_dev, dtype=jnp.int32)).astype(bfloat)
    target = jnp.dot(chooser, teacher, preferred_element_type=single)
    grad_layer = loss_scale * mine_of(valid_rows)[:, None] * (layer_out - target)
    layer_low = layer_out.astype(bfloat)
    block_out = assemble(layer_low, swap(layer_low))

    grad_low = grad_layer.astype(bfloat)
    near_grads = gather_tokens(grad_low)
    near_g = all_rows(slots[0], near_grads, capacity)
    hidden_low, grad_gate_pre, grad_up_pre, grad_gates, grad_rows = expert_backward(
        slots[0], near_gates, (w_gate, w_up, w_down), gate_pre, up_pre, near_g
    )
    far_g = all_rows(
        slots[1], gather_tokens(after(to_mirror(grad_low), near_grads[-1])), capacity
    )
    d_gate, d_up, d_down = expert_weights(
        half,
        slots[1],
        far_gates,
        w_down,
        (far_gate_pre, far_up_pre),
        (hidden_low, grad_gate_pre, grad_up_pre),
        near_x,
        near_g,
        far_x,
        far_g,
    )

    grad_gates = grad_gates.transpose(1, 0, 2)
    gate_parts = grad_gates[:, :, :span] + swap(grad_gates[:, :, span:])
    owner_ids = jnp.arange(owners, dtype=jnp.int32)[:, None, None]
    grad_gates = jnp.zeros((owners, experts_local, span), single)
    for step in range(owners):
        part = gate_parts[step]
        if step:
            part = to_peer(part, "expert", step)
        grad_gates = grad_gates + jnp.where(owner_ids == (at_ex ^ step), part[None], 0.0)
    grad_gates = grad_gates.reshape(all_experts, span)
    inner = jnp.sum(gates * grad_gates, axis=0, keepdims=True)
    grad_logits = (gates * (grad_gates - inner)).astype(bfloat)

    grad_moe_in = combine_groups(slots[0], grad_rows, capacity, span) + lax.dot_general(
        grad_logits, w_router, (((0,), (1,)), ((), ())), preferred_element_type=single
    )
    grad_router_part = lax.dot_general(
        moe_in, grad_logits, (((0,), (1,)), ((), ())), preferred_element_type=single
    )
    grad_second, grad_norm_moe_part = rms_backward(
        hidden_first, inverse_second, norm_moe, grad_moe_in
    )
    grad_hidden_mine = grad_layer + grad_second
    grad_attn_mine = grad_hidden_mine.astype(bfloat)
    grad_attn = assemble(grad_attn_mine, swap(grad_attn_mine))
    grad_hidden_first = assemble(grad_hidden_mine, swap(grad_hidden_mine))
    small = jnp.concatenate([grad_router_part, grad_norm_moe_part[:, None]], axis=1)
    small = small + swap(small)
    grad_out_t = lax.dot_general(
        grad_attn, attn_low, (((0,), (0,)), ((), ())), preferred_element_type=single
    )
    filler = jnp.zeros((model_width, 128 - small.shape[1]), single)
    first_pack, _ = scatter_dense(
        jnp.concatenate([grad_out_t, small, filler], axis=1).astype(bfloat)
    )

    grad_mixed = jnp.dot(grad_attn, w_out.T, preferred_element_type=single).astype(bfloat)
    grad_mixed = grad_mixed.reshape(seq_count, SEQUENCE_LENGTH, heads_local * HEAD_DIMENSION)
    grad_queries, grad_keys, grad_values = lax.map(
        attend_backward, (queries, key_matrix, value_matrix, log_sums, grad_mixed)
    )
    grad_query_raw = (
        rotate_back(grad_queries * factor, cosine_table, sine_table)
        .astype(bfloat)
        .reshape(rows_dev, heads_local * HEAD_DIMENSION)
    )
    grad_key_raw = (
        rotate_back(grad_keys, cosine_table, sine_table)
        .astype(bfloat)
        .reshape(rows_dev, kv_local * HEAD_DIMENSION)
    )
    grad_value_raw = grad_values.astype(bfloat).reshape(rows_dev, kv_local * HEAD_DIMENSION)
    grad_attn_in = (
        jnp.dot(grad_query_raw, w_query.T, preferred_element_type=single)
        + jnp.dot(grad_key_raw, key_projection_weight.T, preferred_element_type=single)
        + jnp.dot(grad_value_raw, value_projection_weight.T, preferred_element_type=single)
    ).astype(bfloat)
    grad_raw = jnp.concatenate([grad_query_raw, grad_key_raw, grad_value_raw], axis=1)
    grad_qkv = jnp.dot(attention_input.T, grad_raw, preferred_element_type=single)
    grad_attn_in = grad_attn_in.astype(single) + swap(grad_attn_in).astype(single)
    grad_first, grad_norm_attn_part = rms_backward(inputs, inverse_first, norm_attn, grad_attn_in)
    grad_tokens = grad_hidden_first + grad_first
    second_pack, sent = scatter_dense(grad_qkv.astype(bfloat))
    grad_norm_attn, _ = scatter_dense(grad_norm_attn_part, single)

    at_shard = at_dp % shards

    def scatter_experts(value, axis):
        size = value.shape[axis] // shards
        total = None
        for step in range(shards):
            part = lax.dynamic_slice_in_dim(value, (at_shard ^ step) * size, size, axis)
            if step:
                part = after(to_peer(part, "dp", step), *sent)
            part = part.astype(single)
            total = part if total is None else total + part
        return total

    return (
        block_out,
        grad_tokens,
        grad_norm_attn,
        first_pack[:, query_width + all_experts],
        second_pack[:, :query_width],
        second_pack[:, query_width : query_width + key_width],
        second_pack[:, query_width + key_width :],
        first_pack[:, :query_width].T,
        first_pack[:, query_width : query_width + all_experts],
        scatter_experts(d_gate, 1),
        scatter_experts(d_up, 1),
        scatter_experts(d_down, 2),
    )


def solution(mesh):
    placed = (
        P(("dp", "expert"), None),
        P(("dp", "expert"), None),
        P(("dp", "expert"), None),
        P(("dp", "expert")),
        P(("dp", "expert"), None),
        P(),
        P(),
        P(None, "tensor"),
        P(None, "tensor"),
        P(None, "tensor"),
        P("tensor", None),
        P(),
        P("expert", None, "tensor"),
        P("expert", None, "tensor"),
        P("expert", "tensor", None),
    )
    return jax.shard_map(
        on_device,
        mesh=mesh,
        in_specs=placed,
        out_specs=(
            P(("dp", "expert"), None),
            P(("dp", "expert"), None),
            P(("dp", "expert")),
            P(("dp", "expert")),
            P(("dp", "expert"), "tensor"),
            P(("dp", "expert"), "tensor"),
            P(("dp", "expert"), "tensor"),
            P("tensor", ("dp", "expert")),
            P(("dp", "expert"), None),
            P("expert", "dp", "tensor"),
            P("expert", "dp", "tensor"),
            P("expert", "tensor", "dp"),
        ),
        check_vma=False,
    )
```

```python
import functools

import jax
import jax.numpy as jnp
from jax import lax
from jax.experimental import pallas as pl
from jax.experimental.pallas import tpu as pltpu
from jax.sharding import PartitionSpec as P

HEAD_DIMENSION = 64
SEQUENCE_LENGTH = 512
ABLK = 256


EPS = 1e-06
VMEM_LIMIT = 56 * 1024 * 1024
THETA = 10000.0
bfloat = jnp.bfloat16
single = jnp.float32


def pass_kernel(*refs):
    pass


def after_all(values, *others):
    anywhere = pl.BlockSpec(memory_space=pl.ANY)
    return pl.pallas_call(
        pass_kernel,
        name="after",
        in_specs=[anywhere] * (len(values) + len(others)),
        out_specs=[anywhere] * len(values),
        out_shape=[jax.ShapeDtypeStruct(value.shape, value.dtype) for value in values],
        input_output_aliases={i: i for i in range(len(values))},
        cost_estimate=pl.CostEstimate(flops=0, bytes_accessed=0, transcendentals=0),
    )(*values, *others)


def after(value, *others):
    return after_all([value], *others)[0] if others else value


def hold_kernel(value_ref, out_ref):
    out_ref[...] = jnp.zeros_like(out_ref)


def hold(value):
    return pl.pallas_call(
        hold_kernel,
        name="hold",
        in_specs=[pl.BlockSpec(memory_space=pl.ANY)],
        out_shape=jax.ShapeDtypeStruct((8, 128), single),
        cost_estimate=pl.CostEstimate(flops=10**12, bytes_accessed=10**9, transcendentals=0),
    )(value)


def swap(value):
    return lax.ppermute(value, "tensor", [(0, 1), (1, 0)])


def to_peer(value, axis, step):
    return lax.ppermute(value, axis, [(i, i ^ step) for i in range(lax.axis_size(axis))])


def to_mirror(value):
    count = lax.axis_size("dp")
    return lax.ppermute(value, "dp", [(i, count - 1 - i) for i in range(count)])


def from_peers(value):
    return [to_peer(value, "expert", s) for s in range(1, lax.axis_size("expert"))]


def halves_kernel(low_ref, high_ref, *refs):
    refs[-2][...] = low_ref[...]
    refs[-1][...] = high_ref[...]


def low_and_high(low, high, *others):
    rows, width = low.shape
    half = jax.ShapeDtypeStruct((rows // 2, width), low.dtype)
    return pl.pallas_call(
        halves_kernel,
        name="halves",
        grid=(1,),
        in_specs=[
            pl.BlockSpec((rows // 2, width), lambda i: (0, 0)),
            pl.BlockSpec((rows // 2, width), lambda i: (1, 0)),
        ]
        + [pl.BlockSpec(memory_space=pl.ANY)] * len(others),
        out_specs=[pl.BlockSpec((rows // 2, width), lambda i: (0, 0))] * 2,
        out_shape=[half, half],
        cost_estimate=pl.CostEstimate(flops=0, bytes_accessed=2**20, transcendentals=0),
    )(low, high, *others)


def spread(value, pause=()):
    own_other = swap(value)
    if lax.axis_size("expert") != 4:
        near = from_peers(value)
        near[0] = after(near[0], own_other, hold(value), *pause)
        return [value, own_other] + [part for mine in near for part in (mine, swap(mine))]
    first, second = to_peer(value, "expert", 1), to_peer(value, "expert", 2)
    for_first, for_second = low_and_high(second, first, own_other, hold(value), *pause)
    low, high = to_peer(for_first, "expert", 1), to_peer(for_second, "expert", 2)
    first_other, second_other = swap(first), swap(second)
    low = after(low, hold(for_first), first_other, second_other)
    third = jnp.concatenate([low, high], axis=0)
    third_other = after(swap(third), hold(third))
    return [value, own_other, first, first_other, second, second_other, third, third_other]


def send_farthest(far):
    cut = far.shape[0] // 2
    low, high = far[:cut], far[cut:]
    return [to_peer(low, "expert", 1), to_peer(high, "expert", 2)], (low, high)


def send_nearer(first, second, came):
    cut = came[0].shape[0]
    low, high = came[0].astype(single), came[1].astype(single)
    first = jnp.concatenate([first[:cut], first[cut:] + high], axis=0).astype(bfloat)
    second = jnp.concatenate([second[:cut] + low, second[cut:]], axis=0).astype(bfloat)
    return [to_peer(first, "expert", 1), to_peer(second, "expert", 2)], (first, second)


def sum_at_owners(parts):
    if len(parts) != 4:
        arrived = [to_peer(part.astype(bfloat), "expert", i) for i, part in enumerate(parts[1:], 1)]
        return add_up(parts[0], arrived)
    came, sent = send_farthest(parts[3].astype(bfloat))
    came[0] = after(came[0], hold(sent[0]))
    came, sent = send_nearer(parts[1], parts[2], came)
    came[0] = after(came[0], hold(sent[0]))
    return add_up(parts[0], came)


def add_up(own, arrived):
    total = own.astype(single)
    for part in arrived:
        total = total + part.astype(single)
    return total


def sum_all(value, axes):
    for axis in axes:
        step = 1
        while step < lax.axis_size(axis):
            value = value + to_peer(value, axis, step)
            step *= 2
    return value


def over_owners(packed):
    count_dp, count_ex = lax.axis_size("dp"), lax.axis_size("expert")
    at_ex = lax.axis_index("expert")
    block = packed.shape[0] // (count_dp * count_ex)
    cut = packed.reshape(count_dp, count_ex, block, packed.shape[1])
    parts = [
        lax.dynamic_index_in_dim(cut, at_ex ^ step, 1, keepdims=False).astype(single)
        for step in range(count_ex)
    ]
    return sum_at_owners(parts)


def over_dp(total):
    at_dp, count = lax.axis_index("dp"), lax.axis_size("dp")
    parts = {r: lax.dynamic_index_in_dim(total, at_dp ^ r, 0, keepdims=False) for r in range(count)}
    step = 1
    while step < count:
        leaving = [r for r in parts if r & step]
        sent = jnp.concatenate([parts[r].astype(bfloat) for r in leaving], axis=0)
        came = to_peer(sent, "dp", step).astype(single)
        rows = came.shape[0] // len(leaving)
        for i, r in enumerate(leaving):
            parts[r ^ step] = parts[r ^ step] + came[i * rows : (i + 1) * rows]
            del parts[r]
        step *= 2
    return parts[0]


def dot(left, right):
    return lax.dot_general(left, right, (((1,), (0,)), ((), ())), preferred_element_type=single)


def dot_nt(left, right):
    return lax.dot_general(left, right, (((1,), (1,)), ((), ())), preferred_element_type=single)


def dot_tn(left, right):
    return lax.dot_general(left, right, (((0,), (0,)), ((), ())), preferred_element_type=single)


def picks(slot, capacity):
    return slot == lax.broadcasted_iota(jnp.int32, (capacity, slot.shape[1]), 0)


def gather_rows(slots_ref, expert, parts, rows_ref):
    capacity = 2 * rows_ref.shape[0] // len(parts)
    width = rows_ref.shape[1]
    for group in range(len(parts) // 2):
        mine, other = parts[2 * group], parts[2 * group + 1]
        span = mine.shape[0]
        slot = slots_ref[expert, group : group + 1, :]
        picked = picks(slot, capacity).astype(bfloat)
        rows = dot(picked[:, :span], mine[:, :width]) + dot(picked[:, span:], other[:, :width])
        rows_ref[group * capacity : (group + 1) * capacity, :] = rows.astype(bfloat)


def slot_gates(expert, tails, count):
    lane = lax.broadcasted_iota(jnp.int32, tails.shape, 1)
    chosen = (lane == expert) | (lane == expert + count) | (lane == expert + 2 * count)
    return jnp.sum(jnp.where(chosen, tails.astype(single), 0.0), axis=1, keepdims=True)


def half_columns(place_ref, width):
    return pl.ds(pl.multiple_of(place_ref[1] * width, 128), width)


def return_order(groups):
    rest = list(range(1, groups)) + [0]
    return [[3], [1, 2, 0]] if groups == 4 else [rest]


def forward_kernel(count, groups, start, with_out, place_ref, slots_ref, gate_w, up_w, *refs):
    if with_out:
        down_w, refs = refs[0], refs[1:]
    parts, refs = refs[: 2 * groups], refs[2 * groups :]
    gate_ref, up_ref, half_ref, tail_ref, refs = refs[0], refs[1], refs[2], refs[3], refs[4:]
    step = pl.program_id(0)
    rows_ref = refs[-1]
    width = gate_w.shape[1]
    gather_rows(slots_ref, start + step, parts, rows_ref)
    half_ref[0] = rows_ref[:, half_columns(place_ref, half_ref.shape[2])]
    tails = rows_ref[:, width:]
    tail_ref[0] = tails
    rows = rows_ref[:, :width]
    gate_pre = dot(rows, gate_w[0])
    up_pre = dot(rows, up_w[0])
    gate_ref[0] = gate_pre.astype(bfloat)
    up_ref[0] = up_pre.astype(bfloat)
    if with_out:
        gates = slot_gates(place_ref[0] + start + step, tails, count)
        hidden = (gate_pre * jax.nn.sigmoid(gate_pre) * up_pre * gates).astype(bfloat)
        refs[0][0] = dot(hidden, down_w[0]).astype(bfloat)


def hidden_grads(gate_pre, up_pre, gates, grad_hidden):
    sig = jax.nn.sigmoid(gate_pre)
    silu = gate_pre * sig
    hidden = silu * up_pre
    scaled = grad_hidden * gates
    grad_gate_pre = (scaled * up_pre * sig * (1.0 + gate_pre * (1.0 - sig))).astype(bfloat)
    grad_up_pre = (scaled * silu).astype(bfloat)
    return hidden, (hidden * gates).astype(bfloat), grad_gate_pre, grad_up_pre


def backward_kernel(count, groups, place_ref, slots_ref, gate_w, up_w, down_w, gate_ref, up_ref, tail_ref, *refs):
    parts, refs = refs[: 2 * groups], refs[2 * groups :]
    hidden_ref, grad_gate_ref, grad_up_ref, half_ref, refs = refs[0], refs[1], refs[2], refs[3], refs[4:]
    back_ref, rows_ref = refs
    width = gate_w.shape[1]
    step = pl.program_id(0)
    expert = place_ref[0] + step
    gather_rows(slots_ref, step, parts, rows_ref)
    half_ref[0] = rows_ref[:, half_columns(place_ref, half_ref.shape[2])]
    gates = slot_gates(expert, tail_ref[0], count)
    grad_hidden = dot_nt(rows_ref[:, :width], down_w[0])
    hidden, hidden_low, grad_gate_pre, grad_up_pre = hidden_grads(
        gate_ref[0].astype(single), up_ref[0].astype(single), gates, grad_hidden
    )
    hidden_ref[0] = hidden_low
    grad_gate_ref[0] = grad_gate_pre
    grad_up_ref[0] = grad_up_pre
    back = dot_nt(grad_gate_pre, gate_w[0]) + dot_nt(grad_up_pre, up_w[0])
    back_ref[0, :, :width] = back.astype(bfloat)
    tails = rows_ref[:, width:].astype(single)
    lane = lax.broadcasted_iota(jnp.int32, tails.shape, 1)
    inner = jnp.sum(jnp.where(lane < 3, tails, 0.0), axis=1, keepdims=True)
    inner = inner * (place_ref[2] == 0).astype(single)
    grad_logit = gates * (jnp.sum(hidden * grad_hidden, axis=1, keepdims=True) - inner)
    back_ref[0, :, width:] = jnp.where(lane == expert, grad_logit, 0.0).astype(bfloat)


def weights_kernel(count, groups, start, place_ref, slots_ref, down_w, gate_ref, up_ref, tail_ref, *refs):
    hidden_near, gate_near, up_near, near_x, near_g, far_x = refs[:6]
    parts, refs = refs[6 : 6 + 2 * groups], refs[6 + 2 * groups :]
    shards, (rows_ref, full_ref) = refs[:-2], refs[-2:]
    expert = start + pl.program_id(0)
    gather_rows(slots_ref, expert, parts, rows_ref)
    gates = slot_gates(place_ref[0] + expert, tail_ref[0], count)
    grad_hidden = dot_nt(rows_ref[...], down_w[0])
    _, hidden, grad_gate_pre, grad_up_pre = hidden_grads(
        gate_ref[0].astype(single), up_ref[0].astype(single), gates, grad_hidden
    )
    far_g = rows_ref[:, half_columns(place_ref, full_ref.shape[1])]
    far, near = far_x[0], near_x[0]
    sums = (
        dot_tn(far, grad_gate_pre) + dot_tn(near, gate_near[0]),
        dot_tn(far, grad_up_pre) + dot_tn(near, up_near[0]),
        dot_tn(far_g, hidden) + dot_tn(near_g[0], hidden_near[0]),
    )
    for i, value in enumerate(sums):
        full_ref[i] = value.astype(bfloat)
    size = shards[0].shape[2]
    for step, shard in enumerate(shards):
        at = pl.multiple_of((place_ref[3] ^ step) * size, size)
        for i in range(3):
            shard[0, i] = full_ref[i, pl.ds(at, size), :]


def finish_kernel(own_ref, *refs):
    arrived, (d_gate, d_up, d_down) = refs[:-3], refs[-3:]

    def total(i):
        value = own_ref[0, i].astype(single)
        for ref in arrived:
            value = value + ref[0, i].astype(single)
        return value

    d_gate[0] = total(0)
    d_up[0] = total(1)
    d_down[0] = total(2).T


def finish_more_kernel(gate_in, up_in, down_in, own_ref, *refs):
    finish_kernel(own_ref, *refs)


def return_kernel(first, cycle, slots_ref, rows_ref, mine, other, picked_ref):
    experts, capacity, width = rows_ref.shape
    span = mine.shape[1]
    group = (pl.program_id(0) + first) % cycle

    @pl.when(pl.program_id(1) == 0)
    def _():
        for e in range(experts):
            slot = slots_ref[e, pl.ds(group, 1), :]
            picked_ref[e * capacity : (e + 1) * capacity, :] = picks(slot, capacity).astype(bfloat)

    back = dot_tn(picked_ref[...], rows_ref[...].reshape(experts * capacity, width)).astype(bfloat)
    mine[0] = back[:span]
    other[0] = back[span:]


def pack_kernel(lane_at, left, right, left_tail, right_tail, value, base, inverse, out_ref):
    columns = right.shape[1]
    out_ref[:, :columns] = dot_tn(left[...], right[...]).astype(bfloat)
    product = value[...] * base[...].astype(single) * inverse[...]
    high = product.astype(bfloat)
    low = (product - high.astype(single)).astype(bfloat)
    lane = lax.broadcasted_iota(jnp.int32, (product.shape[0], 128), 1)
    chosen = (lane == lane_at).astype(bfloat)
    tail = dot_tn(high, chosen) + dot_tn(low, chosen)
    if lane_at:
        tail = tail + dot_tn(left_tail[...], right_tail[...])
    out_ref[:, columns:] = tail.astype(bfloat)


def kernel_call(kernel, name, grid, in_specs, out_specs, out_shape, scratch, flops, moved, args, prefetch=0, aliases=None):
    return pl.pallas_call(
        kernel,
        name=name,
        grid_spec=pltpu.PrefetchScalarGridSpec(
            num_scalar_prefetch=prefetch,
            grid=grid,
            in_specs=in_specs,
            out_specs=out_specs,
            scratch_shapes=scratch,
        ),
        out_shape=out_shape,
        input_output_aliases=aliases or {},
        compiler_params=pltpu.CompilerParams(
            dimension_semantics=("arbitrary",) * len(grid), vmem_limit_bytes=VMEM_LIMIT
        ),
        cost_estimate=pl.CostEstimate(flops=flops, bytes_accessed=moved, transcendentals=0),
    )(*args)


def per_expert(*shape, start=0):
    return pl.BlockSpec((1,) + shape, lambda e, *_: (e + start,) + (0,) * len(shape))


def once(*shape):
    return pl.BlockSpec(
        shape, lambda e, *_: (0,) * len(shape), pipeline_mode=pl.Buffered(buffer_count=1)
    )


def return_rows(slots, rows, order, capacity, span):
    experts, groups, tokens = slots.shape
    width = rows.shape[2]
    amount, first = len(order), order[0]
    cycle = amount if amount > 1 else groups
    cuts = 2 if width % 256 == 0 else 1
    cut = width // cuts
    part = pl.BlockSpec((1, span, cut), lambda g, n: (g, 0, n))
    return kernel_call(
        functools.partial(return_kernel, first, cycle),
        "return_rows",
        (amount, cuts),
        [
            pl.BlockSpec((experts, groups, tokens), lambda g, n: (0, 0, 0)),
            pl.BlockSpec((experts, capacity, cut), lambda g, n: (0, (g + first) % cycle, n)),
        ],
        [part, part],
        [jax.ShapeDtypeStruct((amount, span, width), bfloat)] * 2,
        [pltpu.VMEM((experts * capacity, tokens), bfloat)],
        2 * amount * experts * capacity * tokens * width,
        2 * amount * (experts * capacity + tokens) * width,
        (slots, rows),
    )


def expert_forward(place, count, slots, weights, parts, capacity, start, experts):
    _, groups, tokens = slots.shape
    span, whole = parts[0].shape
    width, hidden = weights[0].shape[1:]
    with_out = len(weights) == 3
    total = groups * capacity
    specs = [once(*slots.shape)] + [per_expert(width, hidden, start=start)] * 2
    outs = [per_expert(total, hidden)] * 2
    outs += [per_expert(total, width // 2), per_expert(total, whole - width)]
    shapes = [jax.ShapeDtypeStruct((experts, total, hidden), bfloat)] * 2
    shapes += [jax.ShapeDtypeStruct((experts, total, width // 2), bfloat)]
    shapes += [jax.ShapeDtypeStruct((experts, total, whole - width), bfloat)]
    scratch = [pltpu.VMEM((total, whole), bfloat)]
    if with_out:
        specs += [per_expert(hidden, width, start=start)]
        outs += [per_expert(total, width)]
        shapes += [jax.ShapeDtypeStruct((experts, total, width), bfloat)]
    return kernel_call(
        functools.partial(forward_kernel, count, groups, start, with_out),
        "expert_forward" if with_out else "expert_forward_far",
        (experts,), specs + [once(*part.shape) for part in parts], outs, shapes, scratch,
        2 * experts * total * (width * hidden * len(weights) + tokens * whole),
        2 * experts * (len(weights) * width * hidden + total * width + 4 * total * hidden),
        (place, slots) + tuple(weights) + tuple(parts),
        prefetch=1,
    )


def expert_backward(place, count, slots, weights, gate_pre, up_pre, tails, parts, capacity):
    experts, groups, tokens = slots.shape
    span, whole = parts[0].shape
    width, hidden = weights[0].shape[1:]
    total = groups * capacity
    thin = per_expert(total, hidden)
    specs = [once(*slots.shape)] + [per_expert(width, hidden)] * 2
    specs += [per_expert(hidden, width), thin, thin, per_expert(total, tails.shape[2])]
    outs = [thin] * 3 + [per_expert(total, width // 2), per_expert(total, whole)]
    shapes = [jax.ShapeDtypeStruct((experts, total, hidden), bfloat)] * 3
    shapes += [jax.ShapeDtypeStruct((experts, total, width // 2), bfloat)]
    shapes += [jax.ShapeDtypeStruct((experts, total, whole), bfloat)]
    return kernel_call(
        functools.partial(backward_kernel, count, groups),
        "expert_backward",
        (experts,), specs + [once(*part.shape) for part in parts], outs, shapes,
        [pltpu.VMEM((total, whole), bfloat)],
        2 * experts * total * width * (hidden * 3 + tokens),
        2 * experts * (3 * width * hidden + 3 * total * width // 2 + 7 * total * hidden),
        (place, slots) + tuple(weights) + (gate_pre, up_pre, tails) + tuple(parts),
        prefetch=1,
    )


def expert_weights(place, count, slots, down_w, far, near, parts, capacity, start, far_start, experts, shards):
    _, groups, tokens = slots.shape
    hidden, width = down_w.shape[1:]
    total = groups * capacity
    far_pre, (far_tails, far_half) = far[:2], far[2:]
    thin = per_expert(total, hidden, start=far_start)
    wide = per_expert(total, width // 2, start=far_start)
    thin_at = per_expert(total, hidden, start=start)
    wide_at = per_expert(total, width // 2, start=start)
    specs = [once(*slots.shape), per_expert(hidden, width, start=start)]
    specs += [thin, thin, per_expert(total, far_tails.shape[2], start=far_start)] + [thin_at] * 3
    specs += [wide_at, wide_at, wide]
    size = width // (2 * shards)
    return kernel_call(
        functools.partial(weights_kernel, count, groups, start),
        "expert_weights",
        (experts,), specs + [once(*part.shape) for part in parts],
        [per_expert(3, size, hidden)] * shards,
        [jax.ShapeDtypeStruct((experts, 3, size, hidden), bfloat)] * shards,
        [pltpu.VMEM((total, width), bfloat), pltpu.VMEM((3, width // 2, hidden), bfloat)],
        2 * experts * total * width * (hidden * 4 + tokens),
        2 * experts * (5 * width * hidden // 2 + 3 * total * width // 2 + 7 * total * hidden),
        (place, slots, down_w) + tuple(far_pre) + (far_tails,) + tuple(near) + (far_half,) + tuple(parts),
        prefetch=1,
    )


def pack_sums(left, right, tail, value, base, inverse, lane_at):
    tokens, width = left.shape
    columns = right.shape[1]
    left_tail, right_tail = tail if tail else (left, right)
    block = width // 4
    tall = lambda array: pl.BlockSpec((array.shape[0], block), lambda i: (0, i))
    whole = lambda array: pl.BlockSpec(array.shape, lambda i: (0, 0))
    return kernel_call(
        functools.partial(pack_kernel, lane_at),
        "pack_sums",
        (4,),
        [tall(left), whole(right), tall(left_tail), whole(right_tail), tall(value), tall(base), whole(inverse)],
        pl.BlockSpec((block, columns + 128), lambda i: (i, 0)),
        jax.ShapeDtypeStruct((width, columns + 128), bfloat),
        [],
        2 * tokens * width * (columns + 128),
        2 * (tokens * (4 * width + columns) + width * (columns + 128)),
        (left, right, left_tail, right_tail, value, base, inverse),
    )


def finish_weights(experts, start, own, arrived, before):
    some, _, size, hidden = own.shape
    ready = [per_expert(3, size, hidden)] * (1 + len(arrived))
    kernel = finish_kernel if before is None else finish_more_kernel
    kept = [] if before is None else [pl.BlockSpec(memory_space=pl.ANY)] * 3
    return kernel_call(
        kernel,
        "finish_weights",
        (some,),
        kept + ready,
        [per_expert(size, hidden, start=start)] * 2 + [per_expert(hidden, size, start=start)],
        [jax.ShapeDtypeStruct((experts, size, hidden), single)] * 2
        + [jax.ShapeDtypeStruct((experts, hidden, size), single)],
        [],
        3 * some * size * hidden,
        12 * some * size * hidden,
        tuple(before or ()) + (own,) + tuple(arrived),
        aliases={} if before is None else {0: 0, 1: 1, 2: 2},
    )


def rope_tables(length, head_size):
    half_size = head_size // 2
    frequency = THETA ** (-jnp.arange(half_size, dtype=jnp.float32) * 2.0 / head_size)
    angles = jnp.arange(length, dtype=jnp.float32)[:, None] * frequency[None, :]
    return (jnp.cos(angles), jnp.sin(angles))


def apply_rotary(value_matrix, cosine_table, sine_table):
    half_size = value_matrix.shape[-1] // 2
    first_half = value_matrix[..., :half_size]
    second_half = value_matrix[..., half_size:]
    cosine_rows = cosine_table[:, None, :]
    sine_rows = sine_table[:, None, :]
    return jnp.concatenate(
        [
            first_half * cosine_rows - second_half * sine_rows,
            second_half * cosine_rows + first_half * sine_rows,
        ],
        axis=-1,
    )


def rotate_back(grads, cosine_table, sine_table):
    half_size = grads.shape[-1] // 2
    first_half = grads[..., :half_size]
    second_half = grads[..., half_size:]
    cosine_rows = cosine_table[:, None, :]
    sine_rows = sine_table[:, None, :]
    return jnp.concatenate(
        [
            first_half * cosine_rows + second_half * sine_rows,
            second_half * cosine_rows - first_half * sine_rows,
        ],
        axis=-1,
    )


def rms_forward(value_matrix, gain):
    inverse = lax.rsqrt(jnp.mean(value_matrix * value_matrix, axis=-1, keepdims=True) + EPS)
    return (value_matrix * inverse * gain, inverse)


def rms_backward(value_matrix, inverse, gain, grad_normed):
    scaled = grad_normed * gain
    grad_gain = jnp.sum(grad_normed * value_matrix * inverse, axis=0)
    grad_values = inverse * scaled - value_matrix * inverse**3 * jnp.mean(
        scaled * value_matrix, axis=-1, keepdims=True
    )
    return (grad_values, grad_gain)


def masked_scores(query_part, key_matrix, row_begin, length):
    scores = jnp.einsum(
        "qkge,tke->kgqt", query_part, key_matrix, preferred_element_type=jnp.float32
    )
    query_block = (row_begin + jnp.arange(query_part.shape[0], dtype=jnp.int32)) // ABLK
    key_block = jnp.arange(length, dtype=jnp.int32) // ABLK
    allowed = query_block[:, None] >= key_block[None, :]
    return jnp.where(allowed, scores, -1e30)


def attend_forward(args):
    queries, key_matrix, value_matrix = args
    length, kv_heads, head_size = key_matrix.shape
    group_size = queries.shape[1] // kv_heads
    rows_block = min(512, length)
    grouped = queries.reshape(length, kv_heads, group_size, head_size)

    def one_block(row_begin):
        scores = masked_scores(grouped, key_matrix, row_begin, length)
        row_peak = jnp.max(scores, axis=-1, keepdims=True)
        weights = jnp.exp(scores - row_peak)
        totals = jnp.sum(weights, axis=-1, keepdims=True)
        weights_low = (weights / totals).astype(jnp.bfloat16)
        outputs = jnp.einsum(
            "kgqt,tke->qkge", weights_low, value_matrix, preferred_element_type=jnp.float32
        )
        return (
            outputs.reshape(rows_block, kv_heads * group_size * head_size),
            (row_peak + jnp.log(totals))[..., 0],
        )

    outputs, log_sums = lax.map(one_block, jnp.arange(0, length, rows_block, dtype=jnp.int32))
    return (outputs.reshape(length, kv_heads * group_size * head_size), log_sums)


def attend_backward(args):
    queries, key_matrix, value_matrix, log_sums, grad_mixed = args
    length, kv_heads, head_size = key_matrix.shape
    group_size = queries.shape[1] // kv_heads
    rows_block = min(512, length)
    grouped = queries.reshape(length, kv_heads, group_size, head_size)
    grad_grouped = grad_mixed.reshape(length, kv_heads, group_size, head_size)

    def one_block(running, inputs):
        row_begin, block_sums = inputs
        scores = masked_scores(grouped, key_matrix, row_begin, length)
        probs = jnp.exp(scores - block_sums[..., None])
        grad_probs = jnp.einsum(
            "qkge,tke->kgqt", grad_grouped, value_matrix, preferred_element_type=jnp.float32
        )
        row_inner = jnp.sum(probs * grad_probs, axis=-1, keepdims=True)
        grad_scores = (probs * (grad_probs - row_inner)).astype(jnp.bfloat16)
        grad_query = jnp.einsum(
            "kgqt,tke->qkge", grad_scores, key_matrix, preferred_element_type=jnp.float32
        )
        grad_key = running[0] + jnp.einsum(
            "kgqt,qkge->tke", grad_scores, grouped, preferred_element_type=jnp.float32
        )
        grad_value = running[1] + jnp.einsum(
            "kgqt,qkge->tke",
            probs.astype(jnp.bfloat16),
            grad_grouped,
            preferred_element_type=jnp.float32,
        )
        return (
            (grad_key, grad_value),
            grad_query.reshape(rows_block, kv_heads * group_size, head_size),
        )

    zero_keys = jnp.zeros(key_matrix.shape, jnp.float32)
    starts = jnp.arange(0, length, rows_block, dtype=jnp.int32)
    (grad_key, grad_value), grad_query = lax.scan(
        one_block, (zero_keys, zero_keys), (starts, log_sums)
    )
    return (grad_query.reshape(length, kv_heads * group_size, head_size), grad_key, grad_value)


def assemble(mine, other):
    first = lax.axis_index("tensor") == 0
    return jnp.concatenate([jnp.where(first, mine, other), jnp.where(first, other, mine)], axis=0)


def in_three(value):
    parts = []
    for _ in range(3):
        low = lax.reduce_precision(value, 8, 7)
        parts.append(low.astype(bfloat))
        value = value - low
    return parts


def widen(value, columns):
    filler = jnp.zeros((value.shape[0], -sum(c.shape[1] for c in [value] + columns) % 128), bfloat)
    return jnp.concatenate([value] + columns + [filler], axis=1)


def combine_groups(slots, rows, capacity, span, between):
    owners = slots.shape[1]
    parts = {}

    def to_tokens(rows, order):
        mine, other = return_rows(slots, rows, order, capacity, span)
        return mine, swap(other), other

    def add(order, mine, other):
        for i, group in enumerate(order):
            parts[group] = mine[i].astype(single) + other[i].astype(single)

    orders = return_order(owners)
    if len(orders) == 1:
        mine, other, _ = to_tokens(after(rows, *between(())), orders[0])
        add(orders[0], mine, other)
        sent = [parts[step].astype(bfloat) for step in range(1, owners)]
        return parts[0], [to_peer(part, "expert", i) for i, part in enumerate(sent, 1)], sent
    mine, other, leaving = to_tokens(rows, orders[0])
    add(orders[0], mine, after(other, hold(leaving)))
    came, sent = send_farthest(parts[3].astype(bfloat))
    mine, other, leaving = to_tokens(after(rows, *between(sent)), orders[1])
    add(orders[1], mine, after(other, hold(leaving)))
    came, sent = send_nearer(parts[1], parts[2], came)
    return parts[0], came, sent


def on_device(
    tokens,
    teacher,
    routes,
    valid,
    teacher_rows,
    norm_attn,
    norm_moe,
    w_query,
    key_projection_weight,
    value_projection_weight,
    w_out,
    w_router,
    w_gate,
    w_up,
    w_down,
):
    rows_dev, model_width = tokens.shape
    seq_count = rows_dev // SEQUENCE_LENGTH
    heads_local = w_query.shape[1] // HEAD_DIMENSION
    kv_local = key_projection_weight.shape[1] // HEAD_DIMENSION
    query_width = w_query.shape[1]
    key_width = key_projection_weight.shape[1]
    experts_local = w_gate.shape[0]
    owners = lax.axis_size("expert")
    count_dp = lax.axis_size("dp")
    groups = count_dp * owners
    all_experts = experts_local * owners
    top_count = routes.shape[1]
    capacity = rows_dev * top_count * 5 // (4 * all_experts)
    at_dp, at_ex, core = lax.axis_index("dp"), lax.axis_index("expert"), lax.axis_index("tensor")
    span = rows_dev // 2
    shards = count_dp // 2
    place = [at_ex * experts_local, at_dp // shards, core, at_dp % shards]
    place = jnp.stack(place).astype(jnp.int32)

    def mine_of(value, axis=0):
        return lax.dynamic_slice_in_dim(value, core * span, span, axis)

    def other_of(value, axis=0):
        return lax.dynamic_slice_in_dim(value, (1 - core) * span, span, axis)

    routes_t = routes.T
    routes_t = jnp.concatenate([mine_of(routes_t, 1), other_of(routes_t, 1)], axis=1)
    routes_two = jnp.stack([routes_t, to_mirror(routes_t)])
    all_routes = jnp.stack([routes_two] + from_peers(routes_two), axis=1)
    expert_ids = jnp.arange(all_experts, dtype=jnp.int32)
    local_ids = at_ex * experts_local + jnp.arange(experts_local, dtype=jnp.int32)
    local_mask = jnp.any(all_routes[:, :, None] == local_ids[:, None, None], axis=3)
    earlier = jnp.triu(jnp.ones((rows_dev, rows_dev), bfloat), 1)
    before = jnp.dot(local_mask.astype(bfloat), earlier, preferred_element_type=single)
    slots = jnp.where(local_mask, before.astype(jnp.int32), -1).transpose(0, 2, 1, 3)
    mine_mask = jnp.any(routes_t[None, :, :span] == expert_ids[:, None, None], axis=1)

    valid_rows = valid.astype(single)
    valid_count = sum_all(jnp.full((8, 128), jnp.sum(valid_rows)), ("dp", "expert"))
    loss_scale = rows_dev * groups / valid_count[0, 0]
    inputs = tokens.astype(single)
    normed_first, inverse_first = rms_forward(inputs, norm_attn)
    attention_input = normed_first.astype(bfloat)
    cosine_table, sine_table = rope_tables(SEQUENCE_LENGTH, HEAD_DIMENSION)
    factor = HEAD_DIMENSION ** (-0.5)
    query_raw = jnp.dot(attention_input, w_query, preferred_element_type=single).reshape(
        seq_count, SEQUENCE_LENGTH, heads_local, HEAD_DIMENSION
    )
    key_unrotated = jnp.dot(
        attention_input, key_projection_weight, preferred_element_type=single
    ).reshape(seq_count, SEQUENCE_LENGTH, kv_local, HEAD_DIMENSION)
    value_unprojected = jnp.dot(
        attention_input, value_projection_weight, preferred_element_type=single
    ).reshape(seq_count, SEQUENCE_LENGTH, kv_local, HEAD_DIMENSION)
    queries = (apply_rotary(query_raw, cosine_table, sine_table) * factor).astype(bfloat)
    key_matrix = apply_rotary(key_unrotated, cosine_table, sine_table).astype(bfloat)
    value_matrix = value_unprojected.astype(bfloat)
    outputs, log_sums = lax.map(attend_forward, (queries, key_matrix, value_matrix))
    attn_low = outputs.reshape(rows_dev, heads_local * HEAD_DIMENSION).astype(bfloat)
    attn_low = after(attn_low, slots, valid_count)
    attn_part = jnp.dot(attn_low, w_out, preferred_element_type=single)

    leaving = other_of(attn_part)
    hidden_first = mine_of(inputs) + mine_of(attn_part) + after(swap(leaving), hold(leaving))
    normed_second, inverse_second = rms_forward(hidden_first, norm_moe)
    moe_in = normed_second.astype(bfloat)
    logits = lax.dot_general(
        w_router, moe_in, (((0,), (1,)), ((), ())), preferred_element_type=single
    )
    peak = jnp.max(jnp.where(mine_mask, logits, -jnp.inf), axis=0, keepdims=True)
    exponent = jnp.where(mine_mask, jnp.exp(logits - peak), 0.0)
    gates = exponent / jnp.sum(exponent, axis=0, keepdims=True)
    token = widen(moe_in, in_three(gates.T))

    some = experts_local // 2
    pieces = ((0, some), (some, experts_local - some))
    few = max(1, experts_local // 5)

    def interleave(mine, other):
        return [part for pair in zip(mine, other) for part in pair]

    def far_forward(parts, start, amount):
        return expert_forward(
            place, all_experts, slots[1], (w_gate, w_up), parts, capacity, start, amount
        )

    mirror = to_mirror(token)
    near_parts = spread(token)
    mirror = after(mirror, *near_parts)
    peers = from_peers(mirror)
    mirror_other = swap(mirror)
    near_parts[0] = after(near_parts[0], mirror)
    gate_pre, up_pre, near_half, near_tails, results = expert_forward(
        place, all_experts, slots[0], (w_gate, w_up, w_down), near_parts, capacity, 0, experts_local
    )
    results = after(results, mirror_other, *peers)
    peers_other = []

    def swap_peers(sent):
        peers[:] = after_all(peers, *sent)
        peers_other.extend(swap(peer) for peer in peers)
        return sent

    own, arrived, sent = combine_groups(slots[0], results, capacity, span, swap_peers)
    far_tokens = interleave([mirror] + peers, [mirror_other] + peers_other)
    far_tokens[0] = after(far_tokens[0], *sent)
    far = [far_forward(far_tokens, *pieces[0])]
    arrived[0] = after(arrived[0], far[0][0], hold(sent[0]))
    moe = add_up(own, arrived)

    layer_out = hidden_first + moe
    rows_wanted = mine_of(teacher_rows[0])
    chooser = (rows_wanted[:, None] == jnp.arange(rows_dev, dtype=jnp.int32)).astype(bfloat)
    target = jnp.dot(chooser, teacher, preferred_element_type=single)
    grad_layer = loss_scale * mine_of(valid_rows)[:, None] * (layer_out - target)
    layer_low = layer_out.astype(bfloat)
    inner = jnp.sum(grad_layer * moe, axis=1, keepdims=True)
    token_grad = widen(grad_layer.astype(bfloat), in_three(inner))

    far_tokens[0] = after(far_tokens[0], token_grad)
    far.append(far_forward(far_tokens, *pieces[1]))
    mirror = to_mirror(token_grad)
    near_parts = spread(token_grad, (far[1][0],))
    mirror = after(mirror, *near_parts)
    peers = from_peers(mirror)
    mirror_other = swap(mirror)
    near_parts[0] = after(near_parts[0], mirror)
    hidden_low, grad_gate_pre, grad_up_pre, near_grad_half, results = expert_backward(
        place, all_experts, slots[0], (w_gate, w_up, w_down), gate_pre, up_pre, near_tails, near_parts, capacity
    )
    results = after(results, mirror_other, *peers)
    weight_parts, far_grads = [], []

    def weights_of(start, amount):
        piece = 0 if start < some else 1
        far_gate, far_up, far_half, far_tails = far[piece]
        values = expert_weights(
            place,
            all_experts,
            slots[1],
            w_down,
            (far_gate, far_up, far_tails, far_half),
            (hidden_low, grad_gate_pre, grad_up_pre, near_half, near_grad_half),
            far_grads,
            capacity,
            start,
            start - pieces[piece][0],
            amount,
            shards,
        )
        came = [to_peer(values[step], "dp", step) for step in range(1, shards)]
        weight_parts.append((start, values[0], came))
        return values

    def first_weights(sent):
        peers[:] = after_all(peers, *sent)
        peers_other = [swap(peer) for peer in peers]
        far_grads.extend(interleave([mirror] + peers, [mirror_other] + peers_other))
        return weights_of(0, few)

    own, arrived, sent = combine_groups(slots[0], results, capacity, span, first_weights)
    layer_other = swap(after(layer_low, *sent))
    block_out = assemble(layer_low, layer_other)
    far_grads[0] = after(far_grads[0], *sent)
    values = weights_of(few, some - few)
    arrived[0] = after(arrived[0], *values, layer_other, hold(sent[0]))
    grad_wide = add_up(own, arrived)
    grad_logits = grad_wide[:, model_width : model_width + all_experts].astype(bfloat)
    grad_moe_in = grad_wide[:, :model_width] + lax.dot_general(
        grad_logits, w_router, (((1,), (1,)), ((), ())), preferred_element_type=single
    )
    grad_second, _ = rms_backward(hidden_first, inverse_second, norm_moe, grad_moe_in)
    grad_hidden_mine = grad_layer + grad_second
    grad_attn_mine = grad_hidden_mine.astype(bfloat)
    far_grads[0] = after(far_grads[0], grad_attn_mine)
    values = weights_of(some, experts_local - some)
    grad_attn = assemble(
        grad_attn_mine, after(swap(grad_attn_mine), *values, *weight_parts[0][2])
    )
    first_pack = pack_sums(
        grad_attn,
        attn_low,
        (moe_in, widen(grad_logits, [])),
        grad_moe_in,
        hidden_first,
        inverse_second,
        all_experts,
    )
    first_total = over_owners(first_pack)

    grad_mixed = jnp.dot(grad_attn, w_out.T, preferred_element_type=single).astype(bfloat)
    grad_mixed = grad_mixed.reshape(seq_count, SEQUENCE_LENGTH, heads_local * HEAD_DIMENSION)
    grad_queries, grad_keys, grad_values = lax.map(
        attend_backward, (queries, key_matrix, value_matrix, log_sums, grad_mixed)
    )
    grad_query_raw = (
        rotate_back(grad_queries * factor, cosine_table, sine_table)
        .astype(bfloat)
        .reshape(rows_dev, heads_local * HEAD_DIMENSION)
    )
    grad_key_raw = (
        rotate_back(grad_keys, cosine_table, sine_table)
        .astype(bfloat)
        .reshape(rows_dev, kv_local * HEAD_DIMENSION)
    )
    grad_value_raw = grad_values.astype(bfloat).reshape(rows_dev, kv_local * HEAD_DIMENSION)
    grad_raw = jnp.concatenate([grad_query_raw, grad_key_raw, grad_value_raw], axis=1)
    grad_attn_in = (
        jnp.dot(grad_query_raw, w_query.T, preferred_element_type=single)
        + jnp.dot(grad_key_raw, key_projection_weight.T, preferred_element_type=single)
        + jnp.dot(grad_value_raw, value_projection_weight.T, preferred_element_type=single)
    )
    second_pack = pack_sums(
        attention_input, grad_raw, None, grad_attn_in, tokens, inverse_first, 0
    )
    second_pack = after(second_pack, first_total, *weight_parts[1][2])
    first_dense = over_dp(first_total)
    second_total = over_owners(second_pack)
    grad_attn_mine = mine_of(grad_attn_in) + swap(other_of(grad_attn_in).astype(bfloat)).astype(
        single
    )
    grad_first, _ = rms_backward(
        mine_of(inputs), mine_of(inverse_first), norm_attn, grad_attn_mine
    )
    grad_tokens_mine = grad_hidden_mine + grad_first
    grad_tokens = assemble(grad_tokens_mine, swap(grad_tokens_mine))

    second_dense = over_dp(after(second_total, grad_tokens, first_dense))
    shared = jnp.concatenate([first_dense[:, query_width:], second_dense[:, -128:]], axis=1)
    shared = shared + swap(shared)

    weight_grads = None
    for start, values, came in weight_parts:
        came = [after(part, second_total) for part in came]
        weight_grads = finish_weights(experts_local, start, values, came, weight_grads)

    key_at = query_width
    return (
        block_out,
        grad_tokens,
        shared[:, -128],
        shared[:, all_experts],
        second_dense[:, :key_at],
        second_dense[:, key_at : key_at + key_width],
        second_dense[:, key_at + key_width : key_at + 2 * key_width],
        first_dense[:, :query_width].T,
        shared[:, :all_experts],
        weight_grads[0],
        weight_grads[1],
        weight_grads[2],
    )


def solution(mesh):
    placed = (
        P(("dp", "expert"), None),
        P(("dp", "expert"), None),
        P(("dp", "expert"), None),
        P(("dp", "expert")),
        P(("dp", "expert"), None),
        P(),
        P(),
        P(None, "tensor"),
        P(None, "tensor"),
        P(None, "tensor"),
        P("tensor", None),
        P(),
        P("expert", None, "tensor"),
        P("expert", None, "tensor"),
        P("expert", "tensor", None),
    )
    return jax.shard_map(
        on_device,
        mesh=mesh,
        in_specs=placed,
        out_specs=(
            P(("dp", "expert"), None),
            P(("dp", "expert"), None),
            P(("dp", "expert")),
            P(("dp", "expert")),
            P(("dp", "expert"), "tensor"),
            P(("dp", "expert"), "tensor"),
            P(("dp", "expert"), "tensor"),
            P("tensor", ("dp", "expert")),
            P(("dp", "expert"), None),
            P("expert", "dp", "tensor"),
            P("expert", "dp", "tensor"),
            P("expert", "tensor", "dp"),
        ),
        check_vma=False,
    )
```

```python
import functools

import jax
import jax.numpy as jnp
from jax import lax
from jax.experimental import pallas as pl
from jax.experimental.pallas import tpu as pltpu
from jax.sharding import PartitionSpec as P

HEAD_DIMENSION = 64
SEQUENCE_LENGTH = 512
ABLK = 256


EPS = 1e-06
VMEM_LIMIT = 56 * 1024 * 1024
HOLDS = True
THETA = 10000.0
bfloat = jnp.bfloat16
single = jnp.float32


def pass_kernel(*refs):
    pass


def after_all(values, *others):
    anywhere = pl.BlockSpec(memory_space=pl.ANY)
    return pl.pallas_call(
        pass_kernel,
        name="after",
        in_specs=[anywhere] * (len(values) + len(others)),
        out_specs=[anywhere] * len(values),
        out_shape=[jax.ShapeDtypeStruct(value.shape, value.dtype) for value in values],
        input_output_aliases={i: i for i in range(len(values))},
        cost_estimate=pl.CostEstimate(flops=0, bytes_accessed=0, transcendentals=0),
    )(*values, *others)


def after(value, *others):
    return after_all([value], *others)[0] if others else value


def hold_kernel(value_ref, out_ref):
    out_ref[...] = jnp.zeros_like(out_ref)


def hold(value):
    if not HOLDS:
        return []
    return [
        pl.pallas_call(
            hold_kernel,
            name="hold",
            in_specs=[pl.BlockSpec(memory_space=pl.ANY)],
            out_shape=jax.ShapeDtypeStruct((8, 128), single),
            cost_estimate=pl.CostEstimate(flops=10**12, bytes_accessed=10**9, transcendentals=0),
        )(value)
    ]


def swap(value):
    return lax.ppermute(value, "tensor", [(0, 1), (1, 0)])


def to_peer(value, axis, step):
    return lax.ppermute(value, axis, [(i, i ^ step) for i in range(lax.axis_size(axis))])


def to_mirror(value):
    count = lax.axis_size("dp")
    return lax.ppermute(value, "dp", [(i, count - 1 - i) for i in range(count)])


def from_peers(value):
    return [to_peer(value, "expert", s) for s in range(1, lax.axis_size("expert"))]


def halves_kernel(low_ref, high_ref, *refs):
    refs[-2][...] = low_ref[...]
    refs[-1][...] = high_ref[...]


def low_and_high(low, high, *others):
    rows, width = low.shape
    half = jax.ShapeDtypeStruct((rows // 2, width), low.dtype)
    return pl.pallas_call(
        halves_kernel,
        name="halves",
        grid=(1,),
        in_specs=[
            pl.BlockSpec((rows // 2, width), lambda i: (0, 0)),
            pl.BlockSpec((rows // 2, width), lambda i: (1, 0)),
        ]
        + [pl.BlockSpec(memory_space=pl.ANY)] * len(others),
        out_specs=[pl.BlockSpec((rows // 2, width), lambda i: (0, 0))] * 2,
        out_shape=[half, half],
        cost_estimate=pl.CostEstimate(flops=0, bytes_accessed=2**20, transcendentals=0),
    )(low, high, *others)


def spread(value, pause=()):
    own_other = swap(value)
    if lax.axis_size("expert") != 4:
        near = from_peers(value)
        near[0] = after(near[0], own_other, *hold(value), *pause)
        return [value, own_other] + [part for mine in near for part in (mine, swap(mine))]
    first, second = to_peer(value, "expert", 1), to_peer(value, "expert", 2)
    for_first, for_second = low_and_high(second, first, own_other, *hold(value), *pause)
    low, high = to_peer(for_first, "expert", 1), to_peer(for_second, "expert", 2)
    first_other, second_other = swap(first), swap(second)
    low = after(low, *hold(for_first), first_other, second_other)
    return [value, own_other, first, first_other, second, second_other, low, high, swap(low), swap(high)]


def farther_kernel(mine_ref, other_ref, low_ref, high_ref):
    cut = low_ref.shape[0]
    total = (mine_ref[0].astype(single) + other_ref[0].astype(single)).astype(bfloat)
    low_ref[...] = total[:cut]
    high_ref[...] = total[cut:]


def nearer_kernel(mine_first, other_first, mine_second, other_second, low_ref, high_ref, first_ref, second_ref):
    step = pl.program_id(0)
    low = jnp.where(step == 0, low_ref[...].astype(single), 0.0)
    high = jnp.where(step == 0, 0.0, high_ref[...].astype(single))
    first = mine_first[0].astype(single) + other_first[0].astype(single) + high
    second = mine_second[0].astype(single) + other_second[0].astype(single) + low
    first_ref[...] = first.astype(bfloat)
    second_ref[...] = second.astype(bfloat)


def send_farthest(mine, other):
    _, span, width = mine.shape
    half = jax.ShapeDtypeStruct((span // 2, width), bfloat)
    low, high = pl.pallas_call(
        farther_kernel,
        name="farther",
        out_shape=[half, half],
        cost_estimate=pl.CostEstimate(flops=0, bytes_accessed=2**21, transcendentals=0),
    )(mine, other)
    return [to_peer(low, "expert", 1), to_peer(high, "expert", 2)], (low, high)


def send_nearer(mine, other, came):
    _, span, width = mine.shape
    half = pl.BlockSpec((span // 2, width), lambda i: (i, 0))
    only = pl.BlockSpec((span // 2, width), lambda i: (0, 0))
    stacked = lambda index: pl.BlockSpec((1, span // 2, width), lambda i: (index, i, 0))
    whole = jax.ShapeDtypeStruct((span, width), bfloat)
    first, second = pl.pallas_call(
        nearer_kernel,
        name="nearer",
        grid=(2,),
        in_specs=[stacked(0), stacked(0), stacked(1), stacked(1), only, only],
        out_specs=[half, half],
        out_shape=[whole, whole],
        cost_estimate=pl.CostEstimate(flops=0, bytes_accessed=2**22, transcendentals=0),
    )(mine, other, mine, other, *came)
    return [to_peer(first, "expert", 1), to_peer(second, "expert", 2)], (first, second)


def start_sum(parts):
    if len(parts) != 4:
        return parts, None
    low, high = parts[3]
    return parts, [to_peer(low, "expert", 1), to_peer(high, "expert", 2)]


def go_on(state, *others):
    parts, came = state
    if came is None:
        sent = [after(part, *others) for part in parts[1:]]
        return [parts[0]] + [to_peer(part, "expert", i) for i, part in enumerate(sent, 1)], sent
    low = after(came[0], *hold(parts[3][0]), *others).astype(single)
    high = came[1].astype(single)
    cut = low.shape[0]
    first, second = parts[1].astype(single), parts[2].astype(single)
    first = jnp.concatenate([first[:cut], first[cut:] + high], axis=0).astype(bfloat)
    second = jnp.concatenate([second[:cut] + low, second[cut:]], axis=0).astype(bfloat)
    return [parts[0], to_peer(first, "expert", 1), to_peer(second, "expert", 2)], [first, second]


def add_up(own, arrived):
    total = own.astype(single)
    for part in arrived:
        total = total + part.astype(single)
    return total


def sum_all(value, axes):
    for axis in axes:
        step = 1
        while step < lax.axis_size(axis):
            value = value + to_peer(value, axis, step)
            step *= 2
    return value


def over_dp(total):
    at_dp, count = lax.axis_index("dp"), lax.axis_size("dp")
    parts = {r: lax.dynamic_index_in_dim(total, at_dp ^ r, 0, keepdims=False) for r in range(count)}
    step = 1
    while step < count:
        leaving = [r for r in parts if r & step]
        sent = jnp.concatenate([parts[r].astype(bfloat) for r in leaving], axis=0)
        came = to_peer(sent, "dp", step).astype(single)
        rows = came.shape[0] // len(leaving)
        for i, r in enumerate(leaving):
            parts[r ^ step] = parts[r ^ step] + came[i * rows : (i + 1) * rows]
            del parts[r]
        step *= 2
    return parts[0]


def dot(left, right):
    return lax.dot_general(left, right, (((1,), (0,)), ((), ())), preferred_element_type=single)


def dot_nt(left, right):
    return lax.dot_general(left, right, (((1,), (1,)), ((), ())), preferred_element_type=single)


def dot_tn(left, right):
    return lax.dot_general(left, right, (((0,), (0,)), ((), ())), preferred_element_type=single)


def picks(slot, capacity):
    return slot == lax.broadcasted_iota(jnp.int32, (capacity, slot.shape[1]), 0)


def group_parts(parts, joined_ref):
    if joined_ref is None:
        return [(parts[i], parts[i + 1]) for i in range(0, len(parts), 2)]
    cut = parts[-1].shape[0]

    @pl.when(pl.program_id(0) == 0)
    def _():
        for i in range(2):
            for j in range(2):
                joined_ref[i, j * cut : (j + 1) * cut, :] = parts[-4 + 2 * i + j][...]

    pairs = [(parts[i], parts[i + 1]) for i in range(0, len(parts) - 4, 2)]
    return pairs + [(joined_ref.at[0], joined_ref.at[1])]


def find_slots(first_ref, top_count, pairs, slots_ref, count_ref):
    groups, experts, tokens = slots_ref.shape
    row = lax.broadcasted_iota(jnp.int32, (tokens, tokens), 0)
    earlier = (row < lax.broadcasted_iota(jnp.int32, (tokens, tokens), 1)).astype(bfloat)
    ids = lax.broadcasted_iota(jnp.int32, (experts, tokens), 0)
    ids = (ids + first_ref[0]).astype(single)
    total = None
    for group, pair in enumerate(pairs):
        tails = [part[:, part.shape[1] - 128 :].astype(single).T for part in pair]
        routes = jnp.concatenate(tails, axis=1)[128 - top_count :]
        valid = routes[:1] >= 64.0
        ahead = jnp.where(valid, 1.0, 0.0)
        total = ahead if total is None else total + ahead
        mask = ids == routes[:1] - 64.0 * ahead
        for k in range(1, top_count):
            mask = mask | (ids == routes[k : k + 1])
        before = dot(mask.astype(single).astype(bfloat), earlier)
        slots_ref[group] = jnp.where(mask, before, -1.0).astype(jnp.int32)
    count_ref[...] = jnp.broadcast_to(jnp.sum(total, axis=1, keepdims=True), count_ref.shape)


def gather_rows(slots_ref, expert, pairs, rows_ref):
    capacity = rows_ref.shape[0] // len(pairs)
    width = rows_ref.shape[1]
    for group, (mine, other) in enumerate(pairs):
        span = mine.shape[0]
        slot = slots_ref[group, pl.ds(expert, 1), :]
        picked = picks(slot, capacity).astype(bfloat)
        rows = dot(picked[:, :span], mine[:, :width]) + dot(picked[:, span:], other[:, :width])
        rows_ref[group * capacity : (group + 1) * capacity, :] = rows.astype(bfloat)


def slot_gates(expert, tails, count):
    lane = lax.broadcasted_iota(jnp.int32, tails.shape, 1)
    chosen = (lane == expert) | (lane == expert + count) | (lane == expert + 2 * count)
    return jnp.sum(jnp.where(chosen, tails.astype(single), 0.0), axis=1, keepdims=True)


def half_columns(place_ref, width):
    return pl.ds(pl.multiple_of(place_ref[1] * width, 128), width)


def return_order(groups):
    rest = list(range(1, groups)) + [0]
    return [[3], [1, 2, 0]] if groups == 4 else [rest]


def forward_kernel(count, top_count, amount, halved, start, with_out, place_ref, gate_w, up_w, *refs):
    if with_out:
        down_w, refs = refs[0], refs[1:]
    parts, refs = refs[:amount], refs[amount:]
    parts, pins = parts[:-1], parts[-1:]
    gate_ref, up_ref, half_ref, tail_ref, slots_ref, count_ref = refs[:6]
    refs = refs[6:]
    step = pl.program_id(0)
    joined_ref = refs[-1] if halved else None
    rows_ref = refs[-2] if halved else refs[-1]
    width = gate_w.shape[1]
    pairs = group_parts(parts, joined_ref)

    @pl.when(step == 0)
    def _():
        find_slots(place_ref, top_count, pairs, slots_ref, count_ref)

    gather_rows(slots_ref, start + step, pairs, rows_ref)
    half_ref[0] = rows_ref[:, half_columns(place_ref, half_ref.shape[2])]
    tails = rows_ref[:, width:]
    tail_ref[0] = tails
    rows = rows_ref[:, :width]
    gate_pre = dot(rows, gate_w[0])
    up_pre = dot(rows, up_w[0])
    gate_ref[0] = gate_pre.astype(bfloat)
    up_ref[0] = up_pre.astype(bfloat)
    if with_out:
        gates = slot_gates(place_ref[0] + start + step, tails, count)
        hidden = (gate_pre * jax.nn.sigmoid(gate_pre) * up_pre * gates).astype(bfloat)
        refs[0][0] = dot(hidden, down_w[0]).astype(bfloat)


def hidden_grads(gate_pre, up_pre, gates, grad_hidden):
    sig = jax.nn.sigmoid(gate_pre)
    silu = gate_pre * sig
    hidden = silu * up_pre
    scaled = grad_hidden * gates
    grad_gate_pre = (scaled * up_pre * sig * (1.0 + gate_pre * (1.0 - sig))).astype(bfloat)
    grad_up_pre = (scaled * silu).astype(bfloat)
    return hidden, (hidden * gates).astype(bfloat), grad_gate_pre, grad_up_pre


def backward_kernel(count, amount, halved, place_ref, slots_ref, gate_w, up_w, down_w, gate_ref, up_ref, tail_ref, *refs):
    parts, refs = refs[:amount], refs[amount:]
    hidden_ref, grad_gate_ref, grad_up_ref, half_ref, refs = refs[0], refs[1], refs[2], refs[3], refs[4:]
    back_ref, rows_ref = refs[:2]
    joined_ref = refs[2] if halved else None
    width = gate_w.shape[1]
    step = pl.program_id(0)
    expert = place_ref[0] + step
    gather_rows(slots_ref, step, group_parts(parts, joined_ref), rows_ref)
    half_ref[0] = rows_ref[:, half_columns(place_ref, half_ref.shape[2])]
    gates = slot_gates(expert, tail_ref[0], count)
    grad_hidden = dot_nt(rows_ref[:, :width], down_w[0])
    hidden, hidden_low, grad_gate_pre, grad_up_pre = hidden_grads(
        gate_ref[0].astype(single), up_ref[0].astype(single), gates, grad_hidden
    )
    hidden_ref[0] = hidden_low
    grad_gate_ref[0] = grad_gate_pre
    grad_up_ref[0] = grad_up_pre
    back = dot_nt(grad_gate_pre, gate_w[0]) + dot_nt(grad_up_pre, up_w[0])
    back_ref[0, :, :width] = back.astype(bfloat)
    tails = rows_ref[:, width:].astype(single)
    lane = lax.broadcasted_iota(jnp.int32, tails.shape, 1)
    inner = jnp.sum(jnp.where(lane < 3, tails, 0.0), axis=1, keepdims=True)
    inner = inner * (place_ref[2] == 0).astype(single)
    grad_logit = gates * (jnp.sum(hidden * grad_hidden, axis=1, keepdims=True) - inner)
    back_ref[0, :, width:] = jnp.where(lane == expert, grad_logit, 0.0).astype(bfloat)


def weights_kernel(count, groups, start, place_ref, slots_ref, down_w, gate_ref, up_ref, tail_ref, *refs):
    hidden_near, gate_near, up_near, near_x, near_g, far_x = refs[:6]
    parts, refs = refs[6 : 6 + 2 * groups], refs[6 + 2 * groups :]
    shards, (rows_ref, full_ref) = refs[:-2], refs[-2:]
    expert = start + pl.program_id(0)
    gather_rows(slots_ref, expert, group_parts(parts, None), rows_ref)
    gates = slot_gates(place_ref[0] + expert, tail_ref[0], count)
    grad_hidden = dot_nt(rows_ref[...], down_w[0])
    _, hidden, grad_gate_pre, grad_up_pre = hidden_grads(
        gate_ref[0].astype(single), up_ref[0].astype(single), gates, grad_hidden
    )
    far_g = rows_ref[:, half_columns(place_ref, full_ref.shape[1])]
    far, near = far_x[0], near_x[0]
    sums = (
        dot_tn(far, grad_gate_pre) + dot_tn(near, gate_near[0]),
        dot_tn(far, grad_up_pre) + dot_tn(near, up_near[0]),
        dot_tn(far_g, hidden) + dot_tn(near_g[0], hidden_near[0]),
    )
    for i, value in enumerate(sums):
        full_ref[i] = value.astype(bfloat)
    size = shards[0].shape[2]
    for step, shard in enumerate(shards):
        at = pl.multiple_of((place_ref[3] ^ step) * size, size)
        for i in range(3):
            shard[0, i] = full_ref[i, pl.ds(at, size), :]


def finish_kernel(scale_ref, own_ref, *refs):
    arrived, (d_gate, d_up, d_down, done_ref) = refs[:-4], refs[-4:]
    scale = scale_ref[:1, :1]

    def total(i):
        value = own_ref[0, i].astype(single)
        for ref in arrived:
            value = value + ref[0, i].astype(single)
        return value * scale

    d_gate[0] = total(0)
    d_up[0] = total(1)
    d_down[0] = total(2).T
    done_ref[...] = scale_ref[...]


def finish_more_kernel(gate_in, up_in, down_in, scale_ref, *refs):
    finish_kernel(scale_ref, *refs)


def return_kernel(first, cycle, slots_ref, rows_ref, mine, other, picked_ref):
    experts, capacity, width = rows_ref.shape
    span = mine.shape[1]
    group = (pl.program_id(0) + first) % cycle

    @pl.when(pl.program_id(1) == 0)
    def _():
        for e in range(experts):
            slot = slots_ref[group, e : e + 1, :]
            picked_ref[e * capacity : (e + 1) * capacity, :] = picks(slot, capacity).astype(bfloat)

    back = dot_tn(picked_ref[...], rows_ref[...].reshape(experts * capacity, width)).astype(bfloat)
    mine[0] = back[:span]
    other[0] = back[span:]


def kernel_call(kernel, name, grid, in_specs, out_specs, out_shape, scratch, flops, moved, args, prefetch=0, aliases=None):
    return pl.pallas_call(
        kernel,
        name=name,
        grid_spec=pltpu.PrefetchScalarGridSpec(
            num_scalar_prefetch=prefetch,
            grid=grid,
            in_specs=in_specs,
            out_specs=out_specs,
            scratch_shapes=scratch,
        ),
        out_shape=out_shape,
        input_output_aliases=aliases or {},
        compiler_params=pltpu.CompilerParams(
            dimension_semantics=("arbitrary",) * len(grid), vmem_limit_bytes=VMEM_LIMIT
        ),
        cost_estimate=pl.CostEstimate(flops=flops, bytes_accessed=moved, transcendentals=0),
    )(*args)


def per_expert(*shape, start=0):
    return pl.BlockSpec((1,) + shape, lambda e, *_: (e + start,) + (0,) * len(shape))


def once(*shape):
    return pl.BlockSpec(
        shape, lambda e, *_: (0,) * len(shape), pipeline_mode=pl.Buffered(buffer_count=1)
    )


def return_rows(slots, rows, order, capacity, span):
    groups, _, tokens = slots.shape
    experts, _, width = rows.shape
    amount, first = len(order), order[0]
    cycle = amount if amount > 1 else groups
    cuts = 2 if width % 256 == 0 else 1
    cut = width // cuts
    part = pl.BlockSpec((1, span, cut), lambda g, n: (g, 0, n))
    return kernel_call(
        functools.partial(return_kernel, first, cycle),
        "return_rows",
        (amount, cuts),
        [
            pl.BlockSpec(slots.shape, lambda g, n: (0, 0, 0)),
            pl.BlockSpec((experts, capacity, cut), lambda g, n: (0, (g + first) % cycle, n)),
        ],
        [part, part],
        [jax.ShapeDtypeStruct((amount, span, width), bfloat)] * 2,
        [pltpu.VMEM((experts * capacity, tokens), bfloat)],
        2 * amount * experts * capacity * tokens * width,
        2 * amount * (experts * capacity + tokens) * width,
        (slots, rows),
    )


def expert_forward(place, count, top_count, pin, weights, parts, groups, capacity, start, experts):
    span, whole = parts[0].shape
    tokens = 2 * span
    width, hidden = weights[0].shape[1:]
    with_out = len(weights) == 3
    total = groups * capacity
    halved = len(parts) > 2 * groups
    specs = [per_expert(width, hidden, start=start)] * 2
    outs = [per_expert(total, hidden)] * 2
    outs += [per_expert(total, width // 2), per_expert(total, whole - width)]
    shapes = [jax.ShapeDtypeStruct((experts, total, hidden), bfloat)] * 2
    shapes += [jax.ShapeDtypeStruct((experts, total, width // 2), bfloat)]
    shapes += [jax.ShapeDtypeStruct((experts, total, whole - width), bfloat)]
    listed = (groups, -(-weights[0].shape[0] // 8) * 8, tokens)
    outs += [pl.BlockSpec(listed, lambda e, *_: (0, 0, 0)), pl.BlockSpec((8, 128), lambda e, *_: (0, 0))]
    shapes += [jax.ShapeDtypeStruct(listed, jnp.int32), jax.ShapeDtypeStruct((8, 128), single)]
    scratch = [pltpu.VMEM((total, whole), bfloat)]
    if halved:
        scratch += [pltpu.VMEM((2, span, whole), bfloat)]
    if with_out:
        specs += [per_expert(hidden, width, start=start)]
        outs += [per_expert(total, width)]
        shapes += [jax.ShapeDtypeStruct((experts, total, width), bfloat)]
    specs += [once(*part.shape) for part in parts] + [pl.BlockSpec(memory_space=pl.ANY)]
    return kernel_call(
        functools.partial(forward_kernel, count, top_count, len(parts) + 1, halved, start, with_out),
        "expert_forward" if with_out else "expert_forward_far",
        (experts,), specs, outs, shapes, scratch,
        2 * experts * total * (width * hidden * len(weights) + tokens * whole),
        2 * experts * (len(weights) * width * hidden + total * width + 4 * total * hidden),
        (place,) + tuple(weights) + tuple(parts) + (pin,),
        prefetch=1,
    )


def expert_backward(place, count, slots, weights, gate_pre, up_pre, tails, parts, capacity):
    groups, _, tokens = slots.shape
    experts = weights[0].shape[0]
    span, whole = parts[0].shape
    width, hidden = weights[0].shape[1:]
    total = groups * capacity
    thin = per_expert(total, hidden)
    specs = [once(*slots.shape)] + [per_expert(width, hidden)] * 2
    specs += [per_expert(hidden, width), thin, thin, per_expert(total, tails.shape[2])]
    outs = [thin] * 3 + [per_expert(total, width // 2), per_expert(total, whole)]
    shapes = [jax.ShapeDtypeStruct((experts, total, hidden), bfloat)] * 3
    shapes += [jax.ShapeDtypeStruct((experts, total, width // 2), bfloat)]
    shapes += [jax.ShapeDtypeStruct((experts, total, whole), bfloat)]
    return kernel_call(
        functools.partial(backward_kernel, count, len(parts), len(parts) > 2 * groups),
        "expert_backward",
        (experts,), specs + [once(*part.shape) for part in parts], outs, shapes,
        [pltpu.VMEM((total, whole), bfloat)]
        + ([pltpu.VMEM((2, span, whole), bfloat)] if len(parts) > 2 * groups else []),
        2 * experts * total * width * (hidden * 3 + tokens),
        2 * experts * (3 * width * hidden + 3 * total * width // 2 + 7 * total * hidden),
        (place, slots) + tuple(weights) + (gate_pre, up_pre, tails) + tuple(parts),
        prefetch=1,
    )


def expert_weights(place, count, slots, down_w, far, near, parts, capacity, start, far_start, experts, shards):
    groups, _, tokens = slots.shape
    hidden, width = down_w.shape[1:]
    total = groups * capacity
    far_pre, (far_tails, far_half) = far[:2], far[2:]
    thin = per_expert(total, hidden, start=far_start)
    wide = per_expert(total, width // 2, start=far_start)
    thin_at = per_expert(total, hidden, start=start)
    wide_at = per_expert(total, width // 2, start=start)
    specs = [once(*slots.shape), per_expert(hidden, width, start=start)]
    specs += [thin, thin, per_expert(total, far_tails.shape[2], start=far_start)] + [thin_at] * 3
    specs += [wide_at, wide_at, wide]
    size = width // (2 * shards)
    return kernel_call(
        functools.partial(weights_kernel, count, groups, start),
        "expert_weights",
        (experts,), specs + [once(*part.shape) for part in parts],
        [per_expert(3, size, hidden)] * shards,
        [jax.ShapeDtypeStruct((experts, 3, size, hidden), bfloat)] * shards,
        [pltpu.VMEM((total, width), bfloat), pltpu.VMEM((3, width // 2, hidden), bfloat)],
        2 * experts * total * width * (hidden * 4 + tokens),
        2 * experts * (5 * width * hidden // 2 + 3 * total * width // 2 + 7 * total * hidden),
        (place, slots, down_w) + tuple(far_pre) + (far_tails,) + tuple(near) + (far_half,) + tuple(parts),
        prefetch=1,
    )


def finish_weights(experts, start, scale, own, arrived, before):
    some, _, size, hidden = own.shape
    ready = [per_expert(3, size, hidden)] * (1 + len(arrived))
    kernel = finish_kernel if before is None else finish_more_kernel
    kept = [] if before is None else [pl.BlockSpec(memory_space=pl.ANY)] * 3
    small = pl.BlockSpec((8, 128), lambda e, *_: (0, 0))
    *grads, done = kernel_call(
        kernel,
        "finish_weights",
        (some,),
        kept + [small] + ready,
        [per_expert(size, hidden, start=start)] * 2 + [per_expert(hidden, size, start=start), small],
        [jax.ShapeDtypeStruct((experts, size, hidden), single)] * 2
        + [jax.ShapeDtypeStruct((experts, hidden, size), single), jax.ShapeDtypeStruct((8, 128), single)],
        [],
        3 * some * size * hidden,
        12 * some * size * hidden,
        tuple(before or ()) + (scale, own) + tuple(arrived),
        aliases={} if before is None else {0: 0, 1: 1, 2: 2},
    )
    return grads, done


def rotate(value, cosines, sines, back):
    pieces = []
    for at in range(0, value.shape[1], 128):
        piece = value[:, at : at + 128]
        lane = lax.broadcasted_iota(jnp.int32, piece.shape, 1)
        later, sooner = pltpu.roll(piece, 96, 1), pltpu.roll(piece, 32, 1)
        if back:
            turned = jnp.where(lane % 64 < 32, later, -sooner)
        else:
            turned = jnp.where(lane % 64 < 32, -later, sooner)
        pieces.append(piece * cosines + turned * sines)
    return pieces[0] if len(pieces) == 1 else jnp.concatenate(pieces, axis=1)


def query_blocks(length):
    return [(at, at + ABLK) for at in range(0, length, ABLK)]


def attend_kernel(place_ref, tokens_ref, gain_ref, query_w, key_w, value_w, out_w, cos_ref, sin_ref,
                  normed_ref, queries_ref, keys_ref, values_ref, mixed_ref, lse_ref, stay_ref, leave_ref, total_ref):
    step = pl.program_id(0)
    length = tokens_ref.shape[0]
    group = query_w.shape[1] // key_w.shape[1]

    @pl.when(step == 0)
    def _():
        inputs = tokens_ref[...].astype(single)
        inverse = lax.rsqrt(jnp.mean(inputs * inputs, axis=1, keepdims=True) + EPS)
        normed_ref[...] = (inputs * inverse * gain_ref[...]).astype(bfloat)

    normed = normed_ref[...]
    cosines, sines = cos_ref[...], sin_ref[...]
    queries = rotate(dot(normed, query_w[...]), cosines, sines, False) * HEAD_DIMENSION ** (-0.5)
    keys = rotate(dot(normed, key_w[...]), cosines, sines, False)
    values = dot(normed, value_w[...])
    size = HEAD_DIMENSION
    mixed = []
    for kv in range(key_w.shape[1] // size):
        key = keys[:, kv * size : (kv + 1) * size].astype(bfloat)
        value = values[:, kv * size : (kv + 1) * size].astype(bfloat)
        keys_ref[kv] = key
        values_ref[kv] = value
        for head in range(kv * group, (kv + 1) * group):
            query = queries[:, head * size : (head + 1) * size].astype(bfloat)
            queries_ref[head] = query
            outs, sums = [], []
            for start, seen in query_blocks(length):
                scores = dot_nt(key[:seen], query[start : start + ABLK])
                peak = jnp.max(scores, axis=0, keepdims=True)
                weights = jnp.exp(scores - peak)
                total = jnp.sum(weights, axis=0, keepdims=True)
                probs = (weights / total).astype(bfloat)
                outs.append(dot_tn(value[:seen], probs))
                sums.append(peak + jnp.log(total))
            mixed.append(jnp.concatenate(outs, axis=1))
            lse_ref[0, head : head + 1, :] = jnp.concatenate(sums, axis=1)
    mixed = jnp.concatenate(mixed, axis=0).T.astype(bfloat)
    mixed_ref[...] = mixed
    part = dot(mixed, out_w[...])

    @pl.when(step == 0)
    def _():
        total_ref[...] = part

    @pl.when(step > 0)
    def _():
        total_ref[...] += part

    @pl.when(step == pl.num_programs(0) - 1)
    def _():
        span = stay_ref.shape[0]
        core = place_ref[2]
        mine = pl.ds(pl.multiple_of(core * span, span), span)
        other = pl.ds(pl.multiple_of((1 - core) * span, span), span)
        stay_ref[...] = total_ref[mine, :] + tokens_ref[mine, :].astype(single)
        leave_ref[...] = total_ref[other, :]


def attend_back_kernel(place_ref, mine_ref, other_ref, tokens_ref, query_w, key_w, value_w, out_w, cos_ref, sin_ref,
                       queries_ref, keys_ref, values_ref, lse_ref,
                       raw_query_ref, raw_key_ref, raw_value_ref, stay_ref, leave_ref, gain_ref, low_ref, total_ref):
    step = pl.program_id(0)
    length = tokens_ref.shape[0]
    span = mine_ref.shape[0]
    core = place_ref[2]
    mine = pl.ds(pl.multiple_of(core * span, span), span)
    other = pl.ds(pl.multiple_of((1 - core) * span, span), span)
    low_ref[mine, :] = dot_nt(mine_ref[...], out_w[...]).astype(bfloat)
    low_ref[other, :] = dot_nt(other_ref[...], out_w[...]).astype(bfloat)
    grads = low_ref[...].astype(single)
    size = HEAD_DIMENSION
    group = query_w.shape[1] // key_w.shape[1]
    grad_queries, grad_keys, grad_values = [], [], []
    for kv in range(key_w.shape[1] // size):
        key, value = keys_ref[kv], values_ref[kv]
        key_parts = [[] for _ in query_blocks(length)]
        value_parts = [[] for _ in query_blocks(length)]
        for head in range(kv * group, (kv + 1) * group):
            query = queries_ref[head]
            grad = grads[:, head * size : (head + 1) * size].astype(bfloat)
            outs = []
            for block, (start, seen) in enumerate(query_blocks(length)):
                rows = slice(start, start + ABLK)
                scores = dot_nt(key[:seen], query[rows])
                probs = jnp.exp(scores - lse_ref[0, head : head + 1, rows])
                grad_probs = dot_nt(value[:seen], grad[rows])
                inner = jnp.sum(probs * grad_probs, axis=0, keepdims=True)
                grad_scores = (probs * (grad_probs - inner)).astype(bfloat)
                outs.append(dot_tn(grad_scores, key[:seen]))
                key_parts[block].append(dot(grad_scores, query[rows]))
                value_parts[block].append(dot(probs.astype(bfloat), grad[rows]))
            grad_queries.append(jnp.concatenate(outs, axis=0))

        def whole(parts):
            rows = []
            for at in range(len(parts)):
                here = slice(at * ABLK, (at + 1) * ABLK)
                rows.append(sum(one[here] for block in parts[at:] for one in block))
            return jnp.concatenate(rows, axis=0)

        grad_keys.append(whole(key_parts))
        grad_values.append(whole(value_parts))
    cosines, sines = cos_ref[...], sin_ref[...]
    grad_query = jnp.concatenate(grad_queries, axis=1) * HEAD_DIMENSION ** (-0.5)
    raw_query = rotate(grad_query, cosines, sines, True).astype(bfloat)
    raw_key = rotate(jnp.concatenate(grad_keys, axis=1), cosines, sines, True).astype(bfloat)
    raw_value = jnp.concatenate(grad_values, axis=1).astype(bfloat)
    raw_query_ref[...] = raw_query
    raw_key_ref[...] = raw_key
    raw_value_ref[...] = raw_value
    part = dot_nt(raw_query, query_w[...]) + dot_nt(raw_key, key_w[...]) + dot_nt(raw_value, value_w[...])

    @pl.when(step == 0)
    def _():
        total_ref[...] = part

    @pl.when(step > 0)
    def _():
        total_ref[...] += part

    @pl.when(step == pl.num_programs(0) - 1)
    def _():
        stay_ref[...] = total_ref[mine, :]
        leave_ref[...] = total_ref[other, :].astype(bfloat)
        inputs = tokens_ref[...].astype(single)
        inverse = lax.rsqrt(jnp.mean(inputs * inputs, axis=1, keepdims=True) + EPS)
        gain = jnp.sum(total_ref[...] * inputs * inverse, axis=0, keepdims=True)
        first = lax.broadcasted_iota(jnp.int32, gain_ref.shape, 0) == 0
        gain_ref[...] = jnp.where(first, gain, 0.0)


def attend(place, tokens, gain, query_w, key_w, value_w, out_w, tables):
    length, width = tokens.shape
    span, size = length // 2, HEAD_DIMENSION
    steps = key_w.shape[1] // 128
    wide, thin = query_w.shape[1] // steps, 128
    heads, kv_heads = query_w.shape[1] // size, key_w.shape[1] // size
    whole = lambda *shape: pl.BlockSpec(shape, lambda i, *_: (0,) * len(shape))
    across = lambda rows, columns: pl.BlockSpec((rows, columns), lambda i, *_: (0, i))
    split = lambda *shape: pl.BlockSpec(shape, lambda i, *_: (i,) + (0,) * (len(shape) - 1))
    low = lambda *shape: jax.ShapeDtypeStruct(shape, bfloat)
    high = lambda *shape: jax.ShapeDtypeStruct(shape, single)
    return kernel_call(
        attend_kernel,
        "attend",
        (steps,),
        [whole(length, width), whole(1, width), across(width, wide), across(width, thin), across(width, thin),
         split(wide, width), whole(length, 128), whole(length, 128)],
        [whole(length, width), split(heads // steps, length, size), split(kv_heads // steps, length, size),
         split(kv_heads // steps, length, size), across(length, wide), split(1, 8, length),
         whole(span, width), whole(span, width)],
        [low(length, width), low(heads, length, size), low(kv_heads, length, size), low(kv_heads, length, size),
         low(length, heads * size), high(steps, 8, length), high(span, width), high(span, width)],
        [pltpu.VMEM((length, width), single)],
        2 * length * width * (2 * heads + 2 * kv_heads) * size,
        2 * (length * width * 6 + 2 * width * (heads + kv_heads) * size),
        (place, tokens, gain, query_w, key_w, value_w, out_w) + tuple(tables),
        prefetch=1,
    )


def attend_back(place, mine, other, tokens, query_w, key_w, value_w, out_w, tables, saved):
    length, width = tokens.shape
    span, size = length // 2, HEAD_DIMENSION
    steps = key_w.shape[1] // 128
    wide, thin = query_w.shape[1] // steps, 128
    heads, kv_heads = query_w.shape[1] // size, key_w.shape[1] // size
    whole = lambda *shape: pl.BlockSpec(shape, lambda i, *_: (0,) * len(shape))
    across = lambda rows, columns: pl.BlockSpec((rows, columns), lambda i, *_: (0, i))
    split = lambda *shape: pl.BlockSpec(shape, lambda i, *_: (i,) + (0,) * (len(shape) - 1))
    low = lambda *shape: jax.ShapeDtypeStruct(shape, bfloat)
    high = lambda *shape: jax.ShapeDtypeStruct(shape, single)
    return kernel_call(
        attend_back_kernel,
        "attend_back",
        (steps,),
        [whole(span, width), whole(span, width), whole(length, width),
         across(width, wide), across(width, thin), across(width, thin), split(wide, width),
         whole(length, 128), whole(length, 128), split(heads // steps, length, size),
         split(kv_heads // steps, length, size), split(kv_heads // steps, length, size), split(1, 8, length)],
        [across(length, wide), across(length, thin), across(length, thin),
         whole(span, width), whole(span, width), whole(8, width)],
        [low(length, heads * size), low(length, kv_heads * size), low(length, kv_heads * size),
         high(span, width), low(span, width), high(8, width)],
        [pltpu.VMEM((length, wide), bfloat), pltpu.VMEM((length, width), single)],
        6 * length * width * (heads + kv_heads) * size,
        2 * (length * width * 6 + 2 * width * (heads + kv_heads) * size),
        (place, mine, other, tokens, query_w, key_w, value_w, out_w) + tuple(tables) + tuple(saved),
        prefetch=1,
    )


def three_lanes(value, starts, lanes):
    total = None
    for start in starts:
        low = value.astype(bfloat).astype(single)
        value = value - low
        moved = pltpu.roll(low, start, 1) if start else low
        total = moved if total is None else total + moved
    return total


def token_kernel(count, place_ref, stay_ref, came_ref, routes_ref, valid_ref, gain_ref, router_ref, hidden_ref, token_ref):
    width = stay_ref.shape[1]
    hidden = stay_ref[...] + came_ref[...]
    hidden_ref[...] = hidden
    inverse = lax.rsqrt(jnp.mean(hidden * hidden, axis=1, keepdims=True) + EPS)
    moe_in = (hidden * inverse * gain_ref[...]).astype(bfloat)
    token_ref[:, :width] = moe_in
    logits = dot(moe_in, router_ref[...])
    logits = jnp.concatenate([logits, jnp.zeros((logits.shape[0], 128 - count), single)], axis=1)
    lane = lax.broadcasted_iota(jnp.int32, logits.shape, 1)
    picked = lane == routes_ref[:, :1]
    for k in range(1, routes_ref.shape[1]):
        picked = picked | (lane == routes_ref[:, k : k + 1])
    peak = jnp.max(jnp.where(picked, logits, -1e30), axis=1, keepdims=True)
    weights = jnp.where(picked, jnp.exp(jnp.where(picked, logits, peak) - peak), 0.0)
    gates = weights / jnp.sum(weights, axis=1, keepdims=True)
    tail = three_lanes(gates, (0, count, 2 * count), 128)
    routes = routes_ref[...].astype(single)
    first = lax.broadcasted_iota(jnp.int32, routes.shape, 1) == 0
    routes = routes + jnp.where(first, 64.0 * valid_ref[...].astype(single), 0.0)
    blank = jnp.zeros((routes.shape[0], 128 - routes.shape[1]), single)
    token_ref[:, width:] = (tail + jnp.concatenate([blank, routes], axis=1)).astype(bfloat)


def layer_kernel(addends, place_ref, hidden_ref, target_ref, valid_ref, *refs):
    parts, (layer_ref, grad_ref, token_ref) = refs[:addends], refs[addends:]
    width = hidden_ref.shape[1]
    moe = sum_of(parts)
    layer = hidden_ref[...] + moe
    layer_ref[...] = layer.astype(bfloat)
    valid = valid_ref[...].astype(single)
    grad = valid * (layer - target_ref[...].astype(single))
    grad_ref[...] = grad
    token_ref[:, :width] = grad.astype(bfloat)
    inner = jnp.sum(grad * moe, axis=1, keepdims=True)
    lane = lax.broadcasted_iota(jnp.int32, (inner.shape[0], 128), 1)
    inner = jnp.where(lane == 0, inner, 0.0)
    token_ref[:, width:] = three_lanes(inner, (0, 1, 2), 128).astype(bfloat)


def sum_of(parts):
    total = None
    for part in parts:
        value = (part[0] if len(part.shape) == 3 else part[...]).astype(single)
        total = value if total is None else total + value
    return total


def norm_kernel(addends, place_ref, hidden_ref, grad_layer_ref, *refs):
    parts, (gain_ref, router_ref, grad_ref, low_ref, logits_ref, sum_ref) = refs[:addends], refs[addends:]
    width = hidden_ref.shape[1]
    wide = sum_of(parts)
    logits = wide[:, width:].astype(bfloat)
    logits_ref[...] = logits
    count = router_ref.shape[1]
    grad_in = wide[:, :width] + dot_nt(logits[:, :count], router_ref[...])
    hidden = hidden_ref[...]
    inverse = lax.rsqrt(jnp.mean(hidden * hidden, axis=1, keepdims=True) + EPS)
    scaled = grad_in * gain_ref[...]
    inner = jnp.mean(scaled * hidden, axis=1, keepdims=True)
    grad = grad_layer_ref[...] + inverse * scaled - hidden * (inverse * inverse * inverse * inner)
    grad_ref[...] = grad
    low_ref[...] = grad.astype(bfloat)
    gain = jnp.sum(grad_in * hidden * inverse, axis=0, keepdims=True)
    first = lax.broadcasted_iota(jnp.int32, sum_ref.shape, 0) == 0
    gain = jnp.where(first, gain, 0.0)

    @pl.when(pl.program_id(0) == 0)
    def _():
        sum_ref[...] = gain

    @pl.when(pl.program_id(0) > 0)
    def _():
        sum_ref[...] += gain


def token_rows(kernel, name, steps, place, rowwise, others, outs, kept=()):
    block = outs[0].shape[0] // steps

    def spec(array):
        if isinstance(array, tuple) and array[1] is None:
            return pl.BlockSpec(
                (block, array[0].shape[1]), lambda i, place: (place[2] * steps + i, 0)
            )
        if isinstance(array, tuple):
            array, index = array
            return pl.BlockSpec((1, block, array.shape[2]), lambda i, place: (index, i, 0))
        return pl.BlockSpec((block, array.shape[1]), lambda i, place: (i, 0))

    bare = [array[0] if isinstance(array, tuple) else array for array in rowwise]
    return kernel_call(
        kernel,
        name,
        (steps,),
        [spec(array) for array in rowwise]
        + [pl.BlockSpec(array.shape, lambda i, place: (0, 0)) for array in others],
        [pl.BlockSpec((block, out.shape[1]), lambda i, place: (i, 0)) for out in outs]
        + [pl.BlockSpec(out.shape, lambda i, place: (0, 0)) for out in kept],
        list(outs) + list(kept),
        [],
        1,
        8 * sum(out.shape[0] * out.shape[1] for out in outs),
        (place,) + tuple(bare) + tuple(others),
        prefetch=1,
    )


def pack_kernel(lane_at, terms, cut, place_ref, sums_ref, *refs):
    lefts, rights, refs = refs[:terms], refs[terms : 2 * terms], refs[2 * terms :]
    outs, full_ref = refs[:-1], refs[-1]
    span = lefts[0].shape[0]
    at = 0
    for term in range(terms):
        left, right = lefts[term], rights[term]
        rows = left.shape[0]
        columns = right.shape[1]
        if right.shape[0] == rows:
            value = dot_tn(left[...], right[...])
        else:
            core = place_ref[2] if term == 0 else 1 - place_ref[2]
            value = dot_tn(left[...], right[pl.ds(pl.multiple_of(core * rows, rows), rows), :])
        if term == 1 and lefts[0].shape[0] != rights[0].shape[0]:
            full_ref[:, :columns] += value
        else:
            full_ref[:, at : at + columns] = value
            at += columns
    sums = sums_ref[...]
    high = sums.astype(bfloat)
    low = (sums - high.astype(single)).astype(bfloat)
    lane = lax.broadcasted_iota(jnp.int32, (sums.shape[0], 128), 1)
    chosen = (lane == lane_at).astype(bfloat)
    column = dot_tn(high, chosen) + dot_tn(low, chosen)
    width = full_ref.shape[1]
    if at < width:
        full_ref[:, width - 128 :] = column
    else:
        full_ref[:, width - 128 :] += column
    some, block = outs[0].shape[:2]

    def blocks(step, i):
        start = (i * cut + (place_ref[4] ^ step)) * block
        return full_ref[pl.ds(pl.multiple_of(start, block), block), :].astype(bfloat)

    for step in range(min(cut, len(outs))):
        if len(outs) > cut and step == cut - 1:
            early = pl.program_id(0) < pl.num_programs(0) // 2

            @pl.when(early)
            def _():
                outs[-2][0] = blocks(step, 0)

            @pl.when(jnp.logical_not(early))
            def _():
                outs[-1][0] = blocks(step, 0)

        else:
            for i in range(some):
                outs[step][i] = blocks(step, i)


def pack_sums(place, lefts, rights, sums, lane_at, columns, count_dp, owners):
    width = sums.shape[1]
    block = width // (count_dp * owners)
    steps = count_dp if (width // count_dp) % 128 == 0 else 1
    tall = lambda array: pl.BlockSpec((array.shape[0], width // steps), lambda i, *_: (0, i))
    whole = lambda array: pl.BlockSpec(array.shape, lambda i, *_: (0, 0))
    some = count_dp // steps
    halved = owners == 4 and steps == count_dp
    specs = [pl.BlockSpec((some, block, columns), lambda i, *_: (i, 0, 0))] * owners
    shapes = [jax.ShapeDtypeStruct((count_dp, block, columns), bfloat)] * owners
    if halved:
        half = count_dp // 2
        specs[3:] = [
            pl.BlockSpec((1, block, columns), lambda i, *_: (jnp.minimum(i, half - 1), 0, 0)),
            pl.BlockSpec((1, block, columns), lambda i, *_: (jnp.maximum(i - half, 0), 0, 0)),
        ]
        shapes[3:] = [jax.ShapeDtypeStruct((half, block, columns), bfloat)] * 2
    outs = kernel_call(
        functools.partial(pack_kernel, lane_at, len(lefts), owners),
        "pack_sums",
        (steps,),
        [tall(sums)] + [tall(left) for left in lefts] + [whole(right) for right in rights],
        specs,
        shapes,
        [pltpu.VMEM((width // steps, columns), single)],
        2 * sum(left.shape[0] * width * columns for left in lefts),
        2 * width * columns,
        (place, sums) + tuple(lefts) + tuple(rights),
        prefetch=1,
    )
    outs = list(outs)
    if halved:
        return outs[:3] + [(outs[3], outs[4])]
    if owners == 4:
        half = count_dp // 2
        return outs[:3] + [(outs[3][:half], outs[3][half:])]
    return outs


def rope_tables(length, head_size):
    half_size = head_size // 2
    frequency = THETA ** (-jnp.arange(half_size, dtype=jnp.float32) * 2.0 / head_size)
    angles = jnp.arange(length, dtype=jnp.float32)[:, None] * frequency[None, :]
    return (jnp.cos(angles), jnp.sin(angles))


def rms_backward(value_matrix, inverse, gain, grad_normed):
    scaled = grad_normed * gain
    grad_gain = jnp.sum(grad_normed * value_matrix * inverse, axis=0)
    grad_values = inverse * scaled - value_matrix * inverse**3 * jnp.mean(
        scaled * value_matrix, axis=-1, keepdims=True
    )
    return (grad_values, grad_gain)


def assemble(mine, other):
    first = lax.axis_index("tensor") == 0
    return jnp.concatenate([jnp.where(first, mine, other), jnp.where(first, other, mine)], axis=0)


def combine_groups(slots, rows, capacity, span, between):
    owners = slots.shape[0]
    orders = return_order(owners)
    if len(orders) == 1:
        mine, other = return_rows(slots, after(rows, *between(())), orders[0], capacity, span)
        other = swap(other)
        sent = [
            (mine[i].astype(single) + other[i].astype(single)).astype(bfloat)
            for i in range(owners - 1)
        ]
        came = [to_peer(part, "expert", i) for i, part in enumerate(sent, 1)]
    else:
        mine, other = return_rows(slots, rows, orders[0], capacity, span)
        other = after(swap(other), *hold(other))
        came, sent = send_farthest(mine, other)
        done = between(sent)
        came[0] = after(came[0], *hold(sent[0]), *done)
        mine, other = return_rows(slots, after(rows, *done), orders[1], capacity, span)
        other = after(swap(other), *hold(other))
        came, sent = send_nearer(mine, other, came)
    own = len(orders[-1]) - 1
    return [(mine, own), (other, own)] + came, sent


def on_device(
    tokens,
    teacher,
    routes,
    valid,
    teacher_rows,
    norm_attn,
    norm_moe,
    w_query,
    key_projection_weight,
    value_projection_weight,
    w_out,
    w_router,
    w_gate,
    w_up,
    w_down,
):
    rows_dev, model_width = tokens.shape
    seq_count = rows_dev // SEQUENCE_LENGTH
    heads_local = w_query.shape[1] // HEAD_DIMENSION
    kv_local = key_projection_weight.shape[1] // HEAD_DIMENSION
    query_width = w_query.shape[1]
    key_width = key_projection_weight.shape[1]
    experts_local = w_gate.shape[0]
    owners = lax.axis_size("expert")
    count_dp = lax.axis_size("dp")
    groups = count_dp * owners
    all_experts = experts_local * owners
    top_count = routes.shape[1]
    capacity = rows_dev * top_count * 5 // (4 * all_experts)
    at_dp, at_ex, core = lax.axis_index("dp"), lax.axis_index("expert"), lax.axis_index("tensor")
    span = rows_dev // 2
    shards = count_dp // 2
    place = [at_ex * experts_local, at_dp // shards, core, at_dp % shards, at_ex]
    place = jnp.stack(place).astype(jnp.int32)

    def mine_of(value, axis=0):
        return lax.dynamic_slice_in_dim(value, core * span, span, axis)

    def other_of(value, axis=0):
        return lax.dynamic_slice_in_dim(value, (1 - core) * span, span, axis)

    tables = [jnp.tile(table, (1, 4)) for table in rope_tables(SEQUENCE_LENGTH, HEAD_DIMENSION)]
    gain_attn, gain_moe = norm_attn.reshape(1, model_width), norm_moe.reshape(1, model_width)

    def tokens_like(columns, kind):
        return jax.ShapeDtypeStruct((span, columns), kind)

    weights = (w_query, key_projection_weight, value_projection_weight, w_out)
    normed, queries, keys, values, mixed, log_sums, staying, leaving = attend(
        place, tokens, gain_attn, *weights, tables
    )
    came = after(swap(leaving), *hold(leaving))
    wide = model_width + 128
    hidden_first, token = token_rows(
        functools.partial(token_kernel, all_experts),
        "token",
        4,
        place,
        [staying, came, (routes, None), (valid[:, None], None)],
        [gain_moe, w_router],
        [tokens_like(model_width, single), tokens_like(wide, bfloat)],
    )

    some = experts_local // 2
    pieces = ((0, some), (some, experts_local - some))
    few = max(1, experts_local // 5)

    def interleave(mine, other):
        return [part for pair in zip(mine, other) for part in pair]

    def far_forward(parts, start, amount, pin):
        return expert_forward(
            place, all_experts, top_count, pin, (w_gate, w_up), parts, owners, capacity, start, amount
        )

    wanted, valid_rows = after_all([teacher_rows, valid[:, None]], token)
    wanted = mine_of(wanted[0])
    chooser = (wanted[:, None] == jnp.arange(rows_dev, dtype=jnp.int32)).astype(bfloat)
    target = jnp.dot(chooser, teacher, preferred_element_type=bfloat)

    mirror = to_mirror(token)
    near_parts = spread(token, (target,))
    mirror = after(mirror, *near_parts)
    peers = from_peers(mirror)
    mirror_other = swap(mirror)
    gate_pre, up_pre, near_half, near_tails, slots, valid_count, results = expert_forward(
        place, all_experts, top_count, mirror, (w_gate, w_up, w_down), near_parts, owners, capacity, 0, experts_local
    )
    results = after(results, mirror_other)
    peers_other = []

    def swap_peers(sent):
        peers[:] = after_all(peers, *sent)
        peers_other.extend(swap(peer) for peer in peers)
        return sent

    addends, sent = combine_groups(slots, results, capacity, span, swap_peers)
    far_tokens = interleave([mirror] + peers, [mirror_other] + peers_other)
    far = [far_forward(far_tokens, *pieces[0], sent[0])]
    addends[-1] = after(addends[-1], far[0][0], *hold(sent[0]))
    layer_low, grad_layer, token_grad = token_rows(
        functools.partial(layer_kernel, len(addends)),
        "layer",
        4,
        place,
        [hidden_first, target, (valid_rows, None)] + addends,
        [],
        [tokens_like(model_width, bfloat), tokens_like(model_width, single), tokens_like(wide, bfloat)],
    )

    far.append(far_forward(far_tokens, *pieces[1], token_grad))
    mirror = to_mirror(token_grad)
    near_parts = spread(token_grad, (far[1][0],))
    mirror = after(mirror, *near_parts)
    peers = from_peers(mirror)
    mirror_other = swap(mirror)
    hidden_low, grad_gate_pre, grad_up_pre, near_grad_half, results = expert_backward(
        place, all_experts, after(slots, mirror), (w_gate, w_up, w_down), gate_pre, up_pre, near_tails, near_parts, capacity
    )
    results = after(results, mirror_other)
    weight_parts, far_grads = [], []

    def weights_of(start, amount, others=()):
        piece = 0 if start < some else 1
        far_gate, far_up, far_half, far_tails, far_slots, _ = far[piece]
        values = expert_weights(
            place,
            all_experts,
            after(far_slots, *others),
            w_down,
            (far_gate, far_up, far_tails, far_half),
            (hidden_low, grad_gate_pre, grad_up_pre, near_half, near_grad_half),
            far_grads,
            capacity,
            start,
            start - pieces[piece][0],
            amount,
            shards,
        )
        came = [to_peer(values[step], "dp", step) for step in range(1, shards)]
        weight_parts.append((start, values[0], came))
        return values

    def first_weights(sent):
        peers[:] = after_all(peers, *sent)
        peers_other = [swap(peer) for peer in peers]
        far_grads.extend(interleave([mirror] + peers, [mirror_other] + peers_other))
        return weights_of(0, few)

    addends, sent = combine_groups(slots, results, capacity, span, first_weights)
    layer_low = after(layer_low, *sent)
    layer_other = swap(layer_low)
    block_out = assemble(layer_low, layer_other)
    done = weights_of(few, some - few, sent)
    addends[-1] = after(addends[-1], *done, layer_other, *hold(sent[0]))
    grad_hidden, grad_attn, grad_logits, gain_sums = token_rows(
        functools.partial(norm_kernel, len(addends)),
        "norm",
        4,
        place,
        [hidden_first, grad_layer] + addends,
        [gain_moe, w_router],
        [tokens_like(model_width, single), tokens_like(model_width, bfloat), tokens_like(128, bfloat)],
        [jax.ShapeDtypeStruct((8, model_width), single)],
    )
    grad_attn_other = after(swap(grad_attn), *hold(grad_attn), *weight_parts[0][2])
    first_parts = pack_sums(
        place,
        [grad_attn, grad_attn_other, token],
        [mixed, mixed, grad_logits],
        gain_sums,
        all_experts,
        query_width + 128,
        count_dp,
        owners,
    )
    first_sum = start_sum(first_parts)
    done = weights_of(some, experts_local - some, first_parts[-1] if owners == 4 else first_parts)
    first_sum, sent = go_on(first_sum, *done)
    grad_attn = after(grad_attn, *sent)
    raw_query, raw_key, raw_value, staying, leaving, gain_sums = attend_back(
        place, grad_attn, grad_attn_other, tokens, *weights, tables, (queries, keys, values, log_sums)
    )
    gain_sums = after(gain_sums, *first_sum[1:], *weight_parts[1][2])
    second_parts = pack_sums(
        place,
        [normed] * 3,
        [raw_query, raw_key, raw_value],
        gain_sums,
        0,
        query_width + 2 * key_width + 128,
        count_dp,
        owners,
    )
    first_total = add_up(first_sum[0], first_sum[1:])
    second_sum = start_sum(second_parts)
    step = 1
    while step < count_dp:
        valid_count = valid_count + to_peer(valid_count, "dp", step)
        step *= 2
    scale = float(rows_dev * groups) / valid_count
    second_sum, sent = go_on(second_sum, scale)
    first_dense = over_dp(after(first_total, *sent))
    weight_grads, done = None, []
    for start, values, came in weight_parts[:2]:
        came = [after(part, sent[0]) for part in came]
        weight_grads, finished = finish_weights(experts_local, start, scale, values, came, weight_grads)
        done.append(finished)
    inputs_mine = mine_of(tokens).astype(single)
    inverse_mine = lax.rsqrt(jnp.mean(inputs_mine * inputs_mine, axis=-1, keepdims=True) + EPS)
    grad_first, _ = rms_backward(
        inputs_mine, inverse_mine, norm_attn, staying + swap(leaving).astype(single)
    )
    grad_tokens_mine = (grad_hidden + grad_first) * scale[0, 0]
    grad_tokens = assemble(grad_tokens_mine, swap(grad_tokens_mine))
    second_total = add_up(second_sum[0], second_sum[1:])
    second_dense = over_dp(after(second_total, grad_tokens, first_dense, *done)) * scale[0, 0]
    first_dense = first_dense * scale[0, 0]
    for start, values, came in weight_parts[2:]:
        came = [after(part, second_total) for part in came]
        weight_grads, _ = finish_weights(experts_local, start, scale, values, came, weight_grads)
    shared = jnp.concatenate([first_dense[:, query_width:], second_dense[:, -128:]], axis=1)
    shared = shared + swap(shared)

    key_at = query_width
    return (
        block_out,
        grad_tokens,
        shared[:, -128],
        shared[:, all_experts],
        second_dense[:, :key_at],
        second_dense[:, key_at : key_at + key_width],
        second_dense[:, key_at + key_width : key_at + 2 * key_width],
        first_dense[:, :query_width].T,
        shared[:, :all_experts],
        weight_grads[0],
        weight_grads[1],
        weight_grads[2],
    )


def solution(mesh):
    placed = (
        P(("dp", "expert"), None),
        P(("dp", "expert"), None),
        P(("dp", "expert"), None),
        P(("dp", "expert")),
        P(("dp", "expert"), None),
        P(),
        P(),
        P(None, "tensor"),
        P(None, "tensor"),
        P(None, "tensor"),
        P("tensor", None),
        P(),
        P("expert", None, "tensor"),
        P("expert", None, "tensor"),
        P("expert", "tensor", None),
    )
    return jax.shard_map(
        on_device,
        mesh=mesh,
        in_specs=placed,
        out_specs=(
            P(("dp", "expert"), None),
            P(("dp", "expert"), None),
            P(("dp", "expert")),
            P(("dp", "expert")),
            P(("dp", "expert"), "tensor"),
            P(("dp", "expert"), "tensor"),
            P(("dp", "expert"), "tensor"),
            P("tensor", ("dp", "expert")),
            P(("dp", "expert"), None),
            P("expert", "dp", "tensor"),
            P("expert", "dp", "tensor"),
            P("expert", "tensor", "dp"),
        ),
        check_vma=False,
    )
```

```python
import functools

import jax
import jax.numpy as jnp
import numpy as np
from jax import lax
from jax.experimental import pallas as pl
from jax.experimental.pallas import tpu as pltpu
from jax.sharding import PartitionSpec as P

HEAD_DIMENSION = 64
SEQUENCE_LENGTH = 512
ABLK = 256


EPS = 1e-06
VMEM_LIMIT = 56 * 1024 * 1024
COST = 100
THETA = 10000.0
bfloat = jnp.bfloat16
single = jnp.float32


def pass_kernel(*refs):
    pass


def after_all(values, *others):
    anywhere = pl.BlockSpec(memory_space=pl.ANY)
    return pl.pallas_call(
        pass_kernel,
        name="after",
        in_specs=[anywhere] * (len(values) + len(others)),
        out_specs=[anywhere] * len(values),
        out_shape=[jax.ShapeDtypeStruct(value.shape, value.dtype) for value in values],
        input_output_aliases={i: i for i in range(len(values))},
        cost_estimate=pl.CostEstimate(flops=0, bytes_accessed=0, transcendentals=0),
    )(*values, *others)


def after(value, *others):
    return after_all([value], *others)[0] if others else value


def hold(value):
    anywhere = pl.BlockSpec(memory_space=pl.ANY)
    return [
        pl.pallas_call(
            pass_kernel,
            name="hold",
            in_specs=[anywhere],
            out_specs=anywhere,
            out_shape=jax.ShapeDtypeStruct((8, 128), single),
            cost_estimate=pl.CostEstimate(flops=10**12, bytes_accessed=10**9, transcendentals=0),
        )(value)
    ]


def swap(value):
    return lax.ppermute(value, "tensor", [(0, 1), (1, 0)])


def to_peer(value, axis, step):
    return lax.ppermute(value, axis, [(i, i ^ step) for i in range(lax.axis_size(axis))])


def to_mirror(value):
    count = lax.axis_size("dp")
    return lax.ppermute(value, "dp", [(i, count - 1 - i) for i in range(count)])


def from_peers(value):
    return [to_peer(value, "expert", s) for s in range(1, lax.axis_size("expert"))]


def halves_kernel(low_ref, high_ref, *refs):
    refs[-2][...] = low_ref[...]
    refs[-1][...] = high_ref[...]


def low_and_high(low, high, *others):
    rows, width = low.shape
    half = jax.ShapeDtypeStruct((rows // 2, width), low.dtype)
    return pl.pallas_call(
        halves_kernel,
        name="halves",
        grid=(1,),
        in_specs=[
            pl.BlockSpec((rows // 2, width), lambda i: (0, 0)),
            pl.BlockSpec((rows // 2, width), lambda i: (1, 0)),
        ]
        + [pl.BlockSpec(memory_space=pl.ANY)] * len(others),
        out_specs=[pl.BlockSpec((rows // 2, width), lambda i: (0, 0))] * 2,
        out_shape=[half, half],
        cost_estimate=pl.CostEstimate(flops=0, bytes_accessed=2**20, transcendentals=0),
    )(low, high, *others)


def spread(value, pause=()):
    own_other = swap(value)
    if lax.axis_size("expert") != 4:
        near = from_peers(value)
        near[0] = after(near[0], own_other, *hold(value), *pause)
        return [value, own_other] + [part for mine in near for part in (mine, swap(mine))]
    first, second = to_peer(value, "expert", 1), to_peer(value, "expert", 2)
    for_first, for_second = low_and_high(second, first, own_other, *hold(value), *pause)
    low, high = to_peer(for_first, "expert", 1), to_peer(for_second, "expert", 2)
    first_other, second_other = swap(first), swap(second)
    low = after(low, *hold(for_first), first_other, second_other)
    return [value, own_other, first, first_other, second, second_other, low, high, swap(low), swap(high)]


def farther_kernel(mine_ref, other_ref, low_ref, high_ref):
    cut = low_ref.shape[0]
    total = (mine_ref[0].astype(single) + other_ref[0].astype(single)).astype(bfloat)
    low_ref[...] = total[:cut]
    high_ref[...] = total[cut:]


def nearer_kernel(mine_first, other_first, mine_second, other_second, low_ref, high_ref, first_ref, second_ref):
    step = pl.program_id(0)
    low = jnp.where(step == 0, low_ref[...].astype(single), 0.0)
    high = jnp.where(step == 0, 0.0, high_ref[...].astype(single))
    first = mine_first[0].astype(single) + other_first[0].astype(single) + high
    second = mine_second[0].astype(single) + other_second[0].astype(single) + low
    first_ref[...] = first.astype(bfloat)
    second_ref[...] = second.astype(bfloat)


def send_farthest(mine, other):
    _, span, width = mine.shape
    half = jax.ShapeDtypeStruct((span // 2, width), bfloat)
    low, high = pl.pallas_call(
        farther_kernel,
        name="farther",
        out_shape=[half, half],
        cost_estimate=pl.CostEstimate(flops=0, bytes_accessed=2**21, transcendentals=0),
    )(mine, other)
    return [to_peer(low, "expert", 1), to_peer(high, "expert", 2)], (low, high)


def send_nearer(mine, other, came):
    _, span, width = mine.shape
    half = pl.BlockSpec((span // 2, width), lambda i: (i, 0))
    only = pl.BlockSpec((span // 2, width), lambda i: (0, 0))
    stacked = lambda index: pl.BlockSpec((1, span // 2, width), lambda i: (index, i, 0))
    whole = jax.ShapeDtypeStruct((span, width), bfloat)
    first, second = pl.pallas_call(
        nearer_kernel,
        name="nearer",
        grid=(2,),
        in_specs=[stacked(0), stacked(0), stacked(1), stacked(1), only, only],
        out_specs=[half, half],
        out_shape=[whole, whole],
        cost_estimate=pl.CostEstimate(flops=0, bytes_accessed=2**22, transcendentals=0),
    )(mine, other, mine, other, *came)
    return [to_peer(first, "expert", 1), to_peer(second, "expert", 2)], (first, second)


def start_sum(parts):
    if len(parts) != 4:
        return parts, None
    low, high = parts[3]
    return parts, [to_peer(low, "expert", 1), to_peer(high, "expert", 2)]


def dense_kernel(first_in, second_in, low_ref, high_ref, *refs):
    first_ref, second_ref = refs[-2:]
    step = pl.program_id(0)
    low = jnp.where(step == 0, low_ref[...].astype(single), 0.0)
    high = jnp.where(step == 0, 0.0, high_ref[...].astype(single))
    first_ref[...] = (first_in[...].astype(single) + high).astype(bfloat)
    second_ref[...] = (second_in[...].astype(single) + low).astype(bfloat)


def go_on(state, *others):
    parts, came = state
    if came is None:
        sent = [after(part, *others) for part in parts[1:]]
        return [parts[0]] + [to_peer(part, "expert", i) for i, part in enumerate(sent, 1)], sent
    low = after(came[0], *hold(parts[3][0]))
    shape = parts[1].shape
    half = pl.BlockSpec((shape[0] // 2,) + shape[1:], lambda i: (i, 0, 0))
    only = pl.BlockSpec((shape[0] // 2,) + shape[1:], lambda i: (0, 0, 0))
    whole = jax.ShapeDtypeStruct(shape, bfloat)
    first, second = pl.pallas_call(
        dense_kernel,
        name="dense_nearer",
        grid=(2,),
        in_specs=[half, half, only, only] + [pl.BlockSpec(memory_space=pl.ANY)] * len(others),
        out_specs=[half, half],
        out_shape=[whole, whole],
        cost_estimate=pl.CostEstimate(flops=0, bytes_accessed=2**22, transcendentals=0),
    )(parts[1], parts[2], low, came[1], *others)
    came = to_peer(first, "expert", 1), to_peer(second, "expert", 2)
    return [parts[0], after(came[0], *hold(first)), came[1]], [first, second]


def add_up(own, arrived):
    total = own.astype(single)
    for part in arrived:
        total = total + part.astype(single)
    return total


def sum_all(value, axes):
    for axis in axes:
        step = 1
        while step < lax.axis_size(axis):
            value = value + to_peer(value, axis, step)
            step *= 2
    return value


def over_dp_start(total):
    at_dp, count = lax.axis_index("dp"), lax.axis_size("dp")
    parts = {r: lax.dynamic_index_in_dim(total, at_dp ^ r, 0, keepdims=False) for r in range(count)}
    return over_dp_send(parts, 1)


def over_dp_send(parts, step):
    if step >= lax.axis_size("dp"):
        return parts, None, step
    return parts, jnp.concatenate([parts[r].astype(bfloat) for r in parts if r & step], axis=0), step


def over_dp_step(state, *others):
    parts, sent, step = state
    parts = dict(parts)
    leaving = [r for r in parts if r & step]
    came = after(to_peer(sent, "dp", step), *hold(sent), *others).astype(single)
    rows = came.shape[0] // len(leaving)
    for i, r in enumerate(leaving):
        parts[r ^ step] = parts[r ^ step] + came[i * rows : (i + 1) * rows]
        del parts[r]
    return over_dp_send(parts, 2 * step)


def over_dp_end(state, *others):
    while state[1] is not None:
        state, others = over_dp_step(state, *others), ()
    return state[0][0]


def over_dp_at_once(total):
    at_dp = lax.axis_index("dp")

    def row(step):
        return lax.dynamic_index_in_dim(total, at_dp ^ step, 0, keepdims=False)

    sent = [row(step).astype(bfloat) for step in range(1, lax.axis_size("dp"))]
    return row(0), [to_peer(part, "dp", step) for step, part in enumerate(sent, 1)], sent


def scaled_sum_kernel(amount, widths, scale_ref, *refs):
    parts, outs = refs[:amount], refs[amount:]
    total = None
    for part in parts:
        value = part[...].astype(single)
        total = value if total is None else total + value
    total = total * scale_ref[:1, :1]
    at = 0
    for out, width in zip(outs, widths):
        out[...] = total[:, at : at + width]
        at += width


def scaled_sum(scale, parts, widths):
    rows = parts[0].shape[0]
    return pl.pallas_call(
        functools.partial(scaled_sum_kernel, len(parts), widths),
        name="scaled_sum",
        out_shape=[jax.ShapeDtypeStruct((rows, width), single) for width in widths],
        cost_estimate=pl.CostEstimate(flops=0, bytes_accessed=2**21, transcendentals=0),
    )(scale, *parts)


def dot(left, right):
    return lax.dot_general(left, right, (((1,), (0,)), ((), ())), preferred_element_type=single)


def dot_nt(left, right):
    return lax.dot_general(left, right, (((1,), (1,)), ((), ())), preferred_element_type=single)


def dot_tn(left, right):
    return lax.dot_general(left, right, (((0,), (0,)), ((), ())), preferred_element_type=single)


def picks(slot, capacity):
    return slot == lax.broadcasted_iota(jnp.int32, (capacity, slot.shape[1]), 0)


def group_parts(parts, joined_ref):
    if joined_ref is None:
        return [(parts[i], parts[i + 1]) for i in range(0, len(parts), 2)]
    cut = parts[-1].shape[0]

    @pl.when(pl.program_id(0) == 0)
    def _():
        for i in range(2):
            for j in range(2):
                joined_ref[i, j * cut : (j + 1) * cut, :] = parts[-4 + 2 * i + j][...]

    pairs = [(parts[i], parts[i + 1]) for i in range(0, len(parts) - 4, 2)]
    return pairs + [(joined_ref.at[0], joined_ref.at[1])]


def find_slots(first_ref, top_count, pairs, slots_ref):
    groups, experts, tokens = slots_ref.shape
    row = lax.broadcasted_iota(jnp.int32, (tokens, tokens), 0)
    earlier = (row < lax.broadcasted_iota(jnp.int32, (tokens, tokens), 1)).astype(bfloat)
    ids = lax.broadcasted_iota(jnp.int32, (experts, tokens), 0)
    ids = (ids + first_ref[0]).astype(single)
    for group, pair in enumerate(pairs):
        tails = [part[:, part.shape[1] - 128 :].astype(single).T for part in pair]
        routes = jnp.concatenate(tails, axis=1)[128 - top_count :]
        mask = ids == routes[:1]
        for k in range(1, top_count):
            mask = mask | (ids == routes[k : k + 1])
        before = dot(mask.astype(single).astype(bfloat), earlier)
        slots_ref[group] = jnp.where(mask, before, -1.0).astype(jnp.int32)


def gather_rows(slots_ref, expert, pairs, rows_ref):
    capacity = rows_ref.shape[0] // len(pairs)
    width = rows_ref.shape[1]
    for group, (mine, other) in enumerate(pairs):
        span = mine.shape[0]
        slot = slots_ref[group, pl.ds(expert, 1), :]
        picked = picks(slot, capacity).astype(bfloat)
        rows = dot(picked[:, :span], mine[:, :width]) + dot(picked[:, span:], other[:, :width])
        rows_ref[group * capacity : (group + 1) * capacity, :] = rows.astype(bfloat)


def slot_gates(expert, tails, count):
    lane = lax.broadcasted_iota(jnp.int32, tails.shape, 1)
    chosen = (lane == expert) | (lane == expert + count) | (lane == expert + 2 * count)
    return jnp.sum(jnp.where(chosen, tails.astype(single), 0.0), axis=1, keepdims=True)


def half_columns(place_ref, width):
    return pl.ds(pl.multiple_of(place_ref[1] * width, 128), width)


def return_order(groups):
    rest = list(range(1, groups)) + [0]
    return [[3], [1, 2], [0]] if groups == 4 else [rest]


def forward_kernel(count, top_count, amount, halved, start, with_out, place_ref, gate_w, up_w, *refs):
    if with_out:
        down_w, refs = refs[0], refs[1:]
    parts, refs = refs[:amount], refs[amount:]
    parts, pins = parts[:-1], parts[-1:]
    gate_ref, up_ref, half_ref, tail_ref, slots_ref = refs[:5]
    refs = refs[5:]
    step = pl.program_id(0)
    joined_ref = refs[-1] if halved else None
    rows_ref = refs[-2] if halved else refs[-1]
    width = gate_w.shape[1]
    pairs = group_parts(parts, joined_ref)

    @pl.when(step == 0)
    def _():
        find_slots(place_ref, top_count, pairs, slots_ref)

    gather_rows(slots_ref, start + step, pairs, rows_ref)
    half_ref[0] = rows_ref[:, half_columns(place_ref, half_ref.shape[2])]
    tails = rows_ref[:, width:]
    tail_ref[0] = tails
    rows = rows_ref[:, :width]
    gate_pre = dot(rows, gate_w[0])
    up_pre = dot(rows, up_w[0])
    gate_ref[0] = gate_pre.astype(bfloat)
    up_ref[0] = up_pre.astype(bfloat)
    if with_out:
        gates = slot_gates(place_ref[0] + start + step, tails, count)
        hidden = (gate_pre * jax.nn.sigmoid(gate_pre) * up_pre * gates).astype(bfloat)
        refs[0][0] = dot(hidden, down_w[0]).astype(bfloat)


def hidden_grads(gate_pre, up_pre, gates, grad_hidden):
    sig = jax.nn.sigmoid(gate_pre)
    silu = gate_pre * sig
    hidden = silu * up_pre
    scaled = grad_hidden * gates
    grad_gate_pre = (scaled * up_pre * sig * (1.0 + gate_pre * (1.0 - sig))).astype(bfloat)
    grad_up_pre = (scaled * silu).astype(bfloat)
    return hidden, (hidden * gates).astype(bfloat), grad_gate_pre, grad_up_pre


def backward_kernel(count, amount, halved, pins, place_ref, slots_ref, gate_w, up_w, down_w, gate_ref, up_ref, tail_ref, *refs):
    parts, refs = refs[:amount], refs[amount + pins :]
    hidden_ref, grad_gate_ref, grad_up_ref, half_ref, refs = refs[0], refs[1], refs[2], refs[3], refs[4:]
    back_ref, rows_ref = refs[:2]
    joined_ref = refs[2] if halved else None
    width = gate_w.shape[1]
    step = pl.program_id(0)
    expert = place_ref[0] + step
    gather_rows(slots_ref, step, group_parts(parts, joined_ref), rows_ref)
    half_ref[0] = rows_ref[:, half_columns(place_ref, half_ref.shape[2])]
    gates = slot_gates(expert, tail_ref[0], count)
    grad_hidden = dot_nt(rows_ref[:, :width], down_w[0])
    hidden, hidden_low, grad_gate_pre, grad_up_pre = hidden_grads(
        gate_ref[0].astype(single), up_ref[0].astype(single), gates, grad_hidden
    )
    hidden_ref[0] = hidden_low
    grad_gate_ref[0] = grad_gate_pre
    grad_up_ref[0] = grad_up_pre
    back = dot_nt(grad_gate_pre, gate_w[0]) + dot_nt(grad_up_pre, up_w[0])
    back_ref[0, :, :width] = back.astype(bfloat)
    tails = rows_ref[:, width:].astype(single)
    lane = lax.broadcasted_iota(jnp.int32, tails.shape, 1)
    inner = jnp.sum(jnp.where(lane < 3, tails, 0.0), axis=1, keepdims=True)
    inner = inner * (place_ref[2] == 0).astype(single)
    grad_logit = gates * (jnp.sum(hidden * grad_hidden, axis=1, keepdims=True) - inner)
    back_ref[0, :, width:] = jnp.where(lane == expert, grad_logit, 0.0).astype(bfloat)


def weights_kernel(count, groups, start, pins, place_ref, slots_ref, down_w, gate_ref, up_ref, tail_ref, *refs):
    hidden_near, gate_near, up_near, near_x, near_g, far_x = refs[:6]
    parts, refs = refs[6 : 6 + 2 * groups], refs[6 + 2 * groups + pins :]
    shards, (rows_ref, full_ref) = refs[:-2], refs[-2:]
    expert = start + pl.program_id(0)
    gather_rows(slots_ref, expert, group_parts(parts, None), rows_ref)
    gates = slot_gates(place_ref[0] + expert, tail_ref[0], count)
    grad_hidden = dot_nt(rows_ref[...], down_w[0])
    _, hidden, grad_gate_pre, grad_up_pre = hidden_grads(
        gate_ref[0].astype(single), up_ref[0].astype(single), gates, grad_hidden
    )
    far_g = rows_ref[:, half_columns(place_ref, full_ref.shape[1])]
    far, near = far_x[0], near_x[0]
    sums = (
        dot_tn(far, grad_gate_pre) + dot_tn(near, gate_near[0]),
        dot_tn(far, grad_up_pre) + dot_tn(near, up_near[0]),
        dot_tn(far_g, hidden) + dot_tn(near_g[0], hidden_near[0]),
    )
    for i, value in enumerate(sums):
        full_ref[i] = value.astype(bfloat)
    size = shards[0].shape[2]
    for step, shard in enumerate(shards):
        at = pl.multiple_of((place_ref[3] ^ step) * size, size)
        for i in range(3):
            shard[0, i] = full_ref[i, pl.ds(at, size), :]


def finish_kernel(scale_ref, own_ref, *refs):
    arrived, (d_gate, d_up, d_down, done_ref) = refs[:-4], refs[-4:]
    scale = scale_ref[:1, :1]

    def total(i):
        value = own_ref[0, i].astype(single)
        for ref in arrived:
            value = value + ref[0, i].astype(single)
        return value * scale

    d_gate[0] = total(0)
    d_up[0] = total(1)
    d_down[0] = total(2).T
    done_ref[...] = scale_ref[...]


def finish_more_kernel(gate_in, up_in, down_in, scale_ref, *refs):
    finish_kernel(scale_ref, *refs)


def return_kernel(first, cycle, slots_ref, rows_ref, mine, other, picked_ref):
    experts, capacity, width = rows_ref.shape
    span = mine.shape[1]
    group = (pl.program_id(0) + first) % cycle

    @pl.when(pl.program_id(1) == 0)
    def _():
        for e in range(experts):
            slot = slots_ref[group, e : e + 1, :]
            picked_ref[e * capacity : (e + 1) * capacity, :] = picks(slot, capacity).astype(bfloat)

    back = dot_tn(picked_ref[...], rows_ref[...].reshape(experts * capacity, width)).astype(bfloat)
    mine[0] = back[:span]
    other[0] = back[span:]


def kernel_call(kernel, name, grid, in_specs, out_specs, out_shape, scratch, flops, moved, args, prefetch=0, aliases=None):
    return pl.pallas_call(
        kernel,
        name=name,
        grid_spec=pltpu.PrefetchScalarGridSpec(
            num_scalar_prefetch=prefetch,
            grid=grid,
            in_specs=in_specs,
            out_specs=out_specs,
            scratch_shapes=scratch,
        ),
        out_shape=out_shape,
        input_output_aliases=aliases or {},
        compiler_params=pltpu.CompilerParams(
            dimension_semantics=("arbitrary",) * len(grid), vmem_limit_bytes=VMEM_LIMIT
        ),
        cost_estimate=pl.CostEstimate(flops=COST * flops, bytes_accessed=moved, transcendentals=0),
    )(*args)


def per_expert(*shape, start=0):
    return pl.BlockSpec((1,) + shape, lambda e, *_: (e + start,) + (0,) * len(shape))


def anywhere(pins):
    return [pl.BlockSpec(memory_space=pl.ANY) for _ in pins]


def once(*shape):
    return pl.BlockSpec(
        shape, lambda e, *_: (0,) * len(shape), pipeline_mode=pl.Buffered(buffer_count=1)
    )


def return_rows(slots, rows, order, capacity, span):
    groups, _, tokens = slots.shape
    experts, _, width = rows.shape
    amount, first = len(order), order[0]
    cycle = groups
    cuts = 2 if width % 256 == 0 else 1
    cut = width // cuts
    part = pl.BlockSpec((1, span, cut), lambda g, n: (g, 0, n))
    return kernel_call(
        functools.partial(return_kernel, first, cycle),
        "return_rows",
        (amount, cuts),
        [
            pl.BlockSpec(slots.shape, lambda g, n: (0, 0, 0)),
            pl.BlockSpec((experts, capacity, cut), lambda g, n: (0, (g + first) % cycle, n)),
        ],
        [part, part],
        [jax.ShapeDtypeStruct((amount, span, width), bfloat)] * 2,
        [pltpu.VMEM((experts * capacity, tokens), bfloat)],
        2 * amount * experts * capacity * tokens * width,
        2 * amount * (experts * capacity + tokens) * width,
        (slots, rows),
    )


def expert_forward(place, count, top_count, pin, weights, parts, groups, capacity, start, experts):
    span, whole = parts[0].shape
    tokens = 2 * span
    width, hidden = weights[0].shape[1:]
    with_out = len(weights) == 3
    total = groups * capacity
    halved = len(parts) > 2 * groups
    specs = [per_expert(width, hidden, start=start)] * 2
    outs = [per_expert(total, hidden)] * 2
    outs += [per_expert(total, width // 2), per_expert(total, whole - width)]
    shapes = [jax.ShapeDtypeStruct((experts, total, hidden), bfloat)] * 2
    shapes += [jax.ShapeDtypeStruct((experts, total, width // 2), bfloat)]
    shapes += [jax.ShapeDtypeStruct((experts, total, whole - width), bfloat)]
    listed = (groups, -(-weights[0].shape[0] // 8) * 8, tokens)
    outs += [pl.BlockSpec(listed, lambda e, *_: (0, 0, 0))]
    shapes += [jax.ShapeDtypeStruct(listed, jnp.int32)]
    scratch = [pltpu.VMEM((total, whole), bfloat)]
    if halved:
        scratch += [pltpu.VMEM((2, span, whole), bfloat)]
    if with_out:
        specs += [per_expert(hidden, width, start=start)]
        outs += [per_expert(total, width)]
        shapes += [jax.ShapeDtypeStruct((experts, total, width), bfloat)]
    specs += [once(*part.shape) for part in parts] + [pl.BlockSpec(memory_space=pl.ANY)]
    return kernel_call(
        functools.partial(forward_kernel, count, top_count, len(parts) + 1, halved, start, with_out),
        "expert_forward" if with_out else "expert_forward_far",
        (experts,), specs, outs, shapes, scratch,
        2 * experts * total * (width * hidden * len(weights) + tokens * whole),
        2 * experts * (len(weights) * width * hidden + total * width + 4 * total * hidden),
        (place,) + tuple(weights) + tuple(parts) + (pin,),
        prefetch=1,
    )


def expert_backward(place, count, slots, weights, gate_pre, up_pre, tails, parts, capacity, pins):
    groups, _, tokens = slots.shape
    experts = weights[0].shape[0]
    span, whole = parts[0].shape
    width, hidden = weights[0].shape[1:]
    total = groups * capacity
    thin = per_expert(total, hidden)
    specs = [once(*slots.shape)] + [per_expert(width, hidden)] * 2
    specs += [per_expert(hidden, width), thin, thin, per_expert(total, tails.shape[2])]
    outs = [thin] * 3 + [per_expert(total, width // 2), per_expert(total, whole)]
    shapes = [jax.ShapeDtypeStruct((experts, total, hidden), bfloat)] * 3
    shapes += [jax.ShapeDtypeStruct((experts, total, width // 2), bfloat)]
    shapes += [jax.ShapeDtypeStruct((experts, total, whole), bfloat)]
    return kernel_call(
        functools.partial(backward_kernel, count, len(parts), len(parts) > 2 * groups, len(pins)),
        "expert_backward",
        (experts,), specs + [once(*part.shape) for part in parts] + anywhere(pins), outs, shapes,
        [pltpu.VMEM((total, whole), bfloat)]
        + ([pltpu.VMEM((2, span, whole), bfloat)] if len(parts) > 2 * groups else []),
        2 * experts * total * width * (hidden * 3 + tokens),
        2 * experts * (3 * width * hidden + 3 * total * width // 2 + 7 * total * hidden),
        (place, slots) + tuple(weights) + (gate_pre, up_pre, tails) + tuple(parts) + tuple(pins),
        prefetch=1,
    )


def expert_weights(place, count, slots, down_w, far, near, parts, capacity, start, far_start, experts, shards, pins):
    groups, _, tokens = slots.shape
    hidden, width = down_w.shape[1:]
    total = groups * capacity
    far_pre, (far_tails, far_half) = far[:2], far[2:]
    thin = per_expert(total, hidden, start=far_start)
    wide = per_expert(total, width // 2, start=far_start)
    thin_at = per_expert(total, hidden, start=start)
    wide_at = per_expert(total, width // 2, start=start)
    specs = [once(*slots.shape), per_expert(hidden, width, start=start)]
    specs += [thin, thin, per_expert(total, far_tails.shape[2], start=far_start)] + [thin_at] * 3
    specs += [wide_at, wide_at, wide]
    size = width // (2 * shards)
    return kernel_call(
        functools.partial(weights_kernel, count, groups, start, len(pins)),
        "expert_weights",
        (experts,), specs + [once(*part.shape) for part in parts] + anywhere(pins),
        [per_expert(3, size, hidden)] * shards,
        [jax.ShapeDtypeStruct((experts, 3, size, hidden), bfloat)] * shards,
        [pltpu.VMEM((total, width), bfloat), pltpu.VMEM((3, width // 2, hidden), bfloat)],
        2 * experts * total * width * (hidden * 4 + tokens),
        2 * experts * (5 * width * hidden // 2 + 3 * total * width // 2 + 7 * total * hidden),
        (place, slots, down_w) + tuple(far_pre) + (far_tails,) + tuple(near) + (far_half,) + tuple(parts) + tuple(pins),
        prefetch=1,
    )


def finish_weights(experts, start, scale, own, arrived, before):
    some, _, size, hidden = own.shape
    ready = [per_expert(3, size, hidden)] * (1 + len(arrived))
    kernel = finish_kernel if before is None else finish_more_kernel
    kept = [] if before is None else [pl.BlockSpec(memory_space=pl.ANY)] * 3
    small = pl.BlockSpec((8, 128), lambda e, *_: (0, 0))
    *grads, done = kernel_call(
        kernel,
        "finish_weights",
        (some,),
        kept + [small] + ready,
        [per_expert(size, hidden, start=start)] * 2 + [per_expert(hidden, size, start=start), small],
        [jax.ShapeDtypeStruct((experts, size, hidden), single)] * 2
        + [jax.ShapeDtypeStruct((experts, hidden, size), single), jax.ShapeDtypeStruct((8, 128), single)],
        [],
        3 * some * size * hidden,
        12 * some * size * hidden,
        tuple(before or ()) + (scale, own) + tuple(arrived),
        aliases={} if before is None else {0: 0, 1: 1, 2: 2},
    )
    return grads, done


def rotate(value, cosines, sines, back):
    pieces = []
    for at in range(0, value.shape[1], 128):
        piece = value[:, at : at + 128]
        lane = lax.broadcasted_iota(jnp.int32, piece.shape, 1)
        later, sooner = pltpu.roll(piece, 96, 1), pltpu.roll(piece, 32, 1)
        if back:
            turned = jnp.where(lane % 64 < 32, later, -sooner)
        else:
            turned = jnp.where(lane % 64 < 32, -later, sooner)
        pieces.append(piece * cosines + turned * sines)
    return pieces[0] if len(pieces) == 1 else jnp.concatenate(pieces, axis=1)


def query_blocks(length):
    return [(at, at + ABLK) for at in range(0, length, ABLK)]


def attend_kernel(place_ref, tokens_ref, gain_ref, query_w, key_w, value_w, out_w, cos_ref, sin_ref,
                  normed_ref, queries_ref, keys_ref, values_ref, mixed_ref, lse_ref, stay_ref, leave_ref, total_ref):
    step = pl.program_id(0)
    length = tokens_ref.shape[0]
    group = query_w.shape[1] // key_w.shape[1]

    @pl.when(step == 0)
    def _():
        inputs = tokens_ref[...].astype(single)
        inverse = lax.rsqrt(jnp.mean(inputs * inputs, axis=1, keepdims=True) + EPS)
        normed_ref[...] = (inputs * inverse * gain_ref[...]).astype(bfloat)

    normed = normed_ref[...]
    cosines, sines = cos_ref[...], sin_ref[...]
    queries = rotate(dot(normed, query_w[...]), cosines, sines, False) * HEAD_DIMENSION ** (-0.5)
    keys = rotate(dot(normed, key_w[...]), cosines, sines, False)
    values = dot(normed, value_w[...])
    size = HEAD_DIMENSION
    mixed = []
    for kv in range(key_w.shape[1] // size):
        key = keys[:, kv * size : (kv + 1) * size].astype(bfloat)
        value = values[:, kv * size : (kv + 1) * size].astype(bfloat)
        keys_ref[kv] = key
        values_ref[kv] = value
        for head in range(kv * group, (kv + 1) * group):
            query = queries[:, head * size : (head + 1) * size].astype(bfloat)
            queries_ref[head] = query
            outs, sums = [], []
            for start, seen in query_blocks(length):
                scores = dot_nt(key[:seen], query[start : start + ABLK])
                peak = jnp.max(scores, axis=0, keepdims=True)
                weights = jnp.exp(scores - peak)
                total = jnp.sum(weights, axis=0, keepdims=True)
                probs = (weights / total).astype(bfloat)
                outs.append(dot_tn(value[:seen], probs))
                sums.append(peak + jnp.log(total))
            mixed.append(jnp.concatenate(outs, axis=1))
            lse_ref[0, head : head + 1, :] = jnp.concatenate(sums, axis=1)
    mixed = jnp.concatenate(mixed, axis=0).T.astype(bfloat)
    mixed_ref[...] = mixed
    part = dot(mixed, out_w[...])

    @pl.when(step == 0)
    def _():
        total_ref[...] = part

    @pl.when(step > 0)
    def _():
        total_ref[...] += part

    @pl.when(step == pl.num_programs(0) - 1)
    def _():
        span = stay_ref.shape[0]
        core = place_ref[2]
        mine = pl.ds(pl.multiple_of(core * span, span), span)
        other = pl.ds(pl.multiple_of((1 - core) * span, span), span)
        stay_ref[...] = total_ref[mine, :] + tokens_ref[mine, :].astype(single)
        leave_ref[...] = total_ref[other, :]


def attend_back_kernel(place_ref, mine_ref, other_ref, tokens_ref, query_w, key_w, value_w, out_w, cos_ref, sin_ref,
                       queries_ref, keys_ref, values_ref, lse_ref,
                       raw_query_ref, raw_key_ref, raw_value_ref, stay_ref, leave_ref, gain_ref, low_ref, total_ref):
    step = pl.program_id(0)
    length = tokens_ref.shape[0]
    span = mine_ref.shape[0]
    core = place_ref[2]
    mine = pl.ds(pl.multiple_of(core * span, span), span)
    other = pl.ds(pl.multiple_of((1 - core) * span, span), span)
    low_ref[mine, :] = dot_nt(mine_ref[...], out_w[...]).astype(bfloat)
    low_ref[other, :] = dot_nt(other_ref[...], out_w[...]).astype(bfloat)
    grads = low_ref[...].astype(single)
    size = HEAD_DIMENSION
    group = query_w.shape[1] // key_w.shape[1]
    grad_queries, grad_keys, grad_values = [], [], []
    for kv in range(key_w.shape[1] // size):
        key, value = keys_ref[kv], values_ref[kv]
        key_parts = [[] for _ in query_blocks(length)]
        value_parts = [[] for _ in query_blocks(length)]
        for head in range(kv * group, (kv + 1) * group):
            query = queries_ref[head]
            grad = grads[:, head * size : (head + 1) * size].astype(bfloat)
            outs = []
            for block, (start, seen) in enumerate(query_blocks(length)):
                rows = slice(start, start + ABLK)
                scores = dot_nt(key[:seen], query[rows])
                probs = jnp.exp(scores - lse_ref[0, head : head + 1, rows])
                grad_probs = dot_nt(value[:seen], grad[rows])
                inner = jnp.sum(probs * grad_probs, axis=0, keepdims=True)
                grad_scores = (probs * (grad_probs - inner)).astype(bfloat)
                outs.append(dot_tn(grad_scores, key[:seen]))
                key_parts[block].append(dot(grad_scores, query[rows]))
                value_parts[block].append(dot(probs.astype(bfloat), grad[rows]))
            grad_queries.append(jnp.concatenate(outs, axis=0))

        def whole(parts):
            rows = []
            for at in range(len(parts)):
                here = slice(at * ABLK, (at + 1) * ABLK)
                rows.append(sum(one[here] for block in parts[at:] for one in block))
            return jnp.concatenate(rows, axis=0)

        grad_keys.append(whole(key_parts))
        grad_values.append(whole(value_parts))
    cosines, sines = cos_ref[...], sin_ref[...]
    grad_query = jnp.concatenate(grad_queries, axis=1) * HEAD_DIMENSION ** (-0.5)
    raw_query = rotate(grad_query, cosines, sines, True).astype(bfloat)
    raw_key = rotate(jnp.concatenate(grad_keys, axis=1), cosines, sines, True).astype(bfloat)
    raw_value = jnp.concatenate(grad_values, axis=1).astype(bfloat)
    raw_query_ref[...] = raw_query
    raw_key_ref[...] = raw_key
    raw_value_ref[...] = raw_value
    part = dot_nt(raw_query, query_w[...]) + dot_nt(raw_key, key_w[...]) + dot_nt(raw_value, value_w[...])

    @pl.when(step == 0)
    def _():
        total_ref[...] = part

    @pl.when(step > 0)
    def _():
        total_ref[...] += part

    @pl.when(step == pl.num_programs(0) - 1)
    def _():
        stay_ref[...] = total_ref[mine, :]
        leave_ref[...] = total_ref[other, :].astype(bfloat)
        inputs = tokens_ref[...].astype(single)
        inverse = lax.rsqrt(jnp.mean(inputs * inputs, axis=1, keepdims=True) + EPS)
        gain = jnp.sum(total_ref[...] * inputs * inverse, axis=0, keepdims=True)
        first = lax.broadcasted_iota(jnp.int32, gain_ref.shape, 0) == 0
        gain_ref[...] = jnp.where(first, gain, 0.0)


def attend(place, tokens, gain, query_w, key_w, value_w, out_w, tables):
    length, width = tokens.shape
    span, size = length // 2, HEAD_DIMENSION
    steps = key_w.shape[1] // 128
    wide, thin = query_w.shape[1] // steps, 128
    heads, kv_heads = query_w.shape[1] // size, key_w.shape[1] // size
    whole = lambda *shape: pl.BlockSpec(shape, lambda i, *_: (0,) * len(shape))
    across = lambda rows, columns: pl.BlockSpec((rows, columns), lambda i, *_: (0, i))
    split = lambda *shape: pl.BlockSpec(shape, lambda i, *_: (i,) + (0,) * (len(shape) - 1))
    low = lambda *shape: jax.ShapeDtypeStruct(shape, bfloat)
    high = lambda *shape: jax.ShapeDtypeStruct(shape, single)
    return kernel_call(
        attend_kernel,
        "attend",
        (steps,),
        [whole(length, width), whole(1, width), across(width, wide), across(width, thin), across(width, thin),
         split(wide, width), whole(length, 128), whole(length, 128)],
        [whole(length, width), split(heads // steps, length, size), split(kv_heads // steps, length, size),
         split(kv_heads // steps, length, size), across(length, wide), split(1, 8, length),
         whole(span, width), whole(span, width)],
        [low(length, width), low(heads, length, size), low(kv_heads, length, size), low(kv_heads, length, size),
         low(length, heads * size), high(steps, 8, length), high(span, width), high(span, width)],
        [pltpu.VMEM((length, width), single)],
        2 * length * width * (2 * heads + 2 * kv_heads) * size,
        2 * (length * width * 6 + 2 * width * (heads + kv_heads) * size),
        (place, tokens, gain, query_w, key_w, value_w, out_w) + tuple(tables),
        prefetch=1,
    )


def attend_back(place, mine, other, tokens, query_w, key_w, value_w, out_w, tables, saved):
    length, width = tokens.shape
    span, size = length // 2, HEAD_DIMENSION
    steps = key_w.shape[1] // 128
    wide, thin = query_w.shape[1] // steps, 128
    heads, kv_heads = query_w.shape[1] // size, key_w.shape[1] // size
    whole = lambda *shape: pl.BlockSpec(shape, lambda i, *_: (0,) * len(shape))
    across = lambda rows, columns: pl.BlockSpec((rows, columns), lambda i, *_: (0, i))
    split = lambda *shape: pl.BlockSpec(shape, lambda i, *_: (i,) + (0,) * (len(shape) - 1))
    low = lambda *shape: jax.ShapeDtypeStruct(shape, bfloat)
    high = lambda *shape: jax.ShapeDtypeStruct(shape, single)
    return kernel_call(
        attend_back_kernel,
        "attend_back",
        (steps,),
        [whole(span, width), whole(span, width), whole(length, width),
         across(width, wide), across(width, thin), across(width, thin), split(wide, width),
         whole(length, 128), whole(length, 128), split(heads // steps, length, size),
         split(kv_heads // steps, length, size), split(kv_heads // steps, length, size), split(1, 8, length)],
        [across(length, wide), across(length, thin), across(length, thin),
         whole(span, width), whole(span, width), whole(8, width)],
        [low(length, heads * size), low(length, kv_heads * size), low(length, kv_heads * size),
         high(span, width), low(span, width), high(8, width)],
        [pltpu.VMEM((length, wide), bfloat), pltpu.VMEM((length, width), single)],
        6 * length * width * (heads + kv_heads) * size,
        2 * (length * width * 6 + 2 * width * (heads + kv_heads) * size),
        (place, mine, other, tokens, query_w, key_w, value_w, out_w) + tuple(tables) + tuple(saved),
        prefetch=1,
    )


def three_lanes(value, starts, lanes):
    total = None
    for start in starts:
        low = value.astype(bfloat).astype(single)
        value = value - low
        moved = pltpu.roll(low, start, 1) if start else low
        total = moved if total is None else total + moved
    return total


def token_kernel(count, place_ref, stay_ref, came_ref, routes_ref, gain_ref, router_ref, hidden_ref, token_ref):
    width = stay_ref.shape[1]
    hidden = stay_ref[...] + came_ref[...]
    hidden_ref[...] = hidden
    inverse = lax.rsqrt(jnp.mean(hidden * hidden, axis=1, keepdims=True) + EPS)
    moe_in = (hidden * inverse * gain_ref[...]).astype(bfloat)
    token_ref[:, :width] = moe_in
    logits = dot_nt(moe_in, router_ref[...])
    logits = jnp.concatenate([logits, jnp.zeros((logits.shape[0], 128 - count), single)], axis=1)
    lane = lax.broadcasted_iota(jnp.int32, logits.shape, 1)
    picked = lane == routes_ref[:, :1]
    for k in range(1, routes_ref.shape[1]):
        picked = picked | (lane == routes_ref[:, k : k + 1])
    peak = jnp.max(jnp.where(picked, logits, -1e30), axis=1, keepdims=True)
    weights = jnp.where(picked, jnp.exp(jnp.where(picked, logits, peak) - peak), 0.0)
    gates = weights / jnp.sum(weights, axis=1, keepdims=True)
    tail = three_lanes(gates, (0, count, 2 * count), 128)
    routes = routes_ref[...].astype(single)
    blank = jnp.zeros((routes.shape[0], 128 - routes.shape[1]), single)
    token_ref[:, width:] = (tail + jnp.concatenate([blank, routes], axis=1)).astype(bfloat)


def layer_kernel(addends, place_ref, hidden_ref, target_ref, valid_ref, *refs):
    parts, (layer_ref, grad_ref, low_ref, token_ref) = refs[:addends], refs[addends:]
    width = hidden_ref.shape[1]
    moe = sum_of(parts)
    layer = hidden_ref[...] + moe
    layer_ref[...] = layer.astype(bfloat)
    valid = valid_ref[:, :1].astype(single)
    grad = valid * (layer - target_ref[...].astype(single))
    grad_ref[...] = grad
    low_ref[...] = grad.astype(bfloat)
    token_ref[:, :width] = grad.astype(bfloat)
    inner = jnp.sum(grad * moe, axis=1, keepdims=True)
    lane = lax.broadcasted_iota(jnp.int32, (inner.shape[0], 128), 1)
    inner = jnp.where(lane == 0, inner, 0.0)
    token_ref[:, width:] = three_lanes(inner, (0, 1, 2), 128).astype(bfloat)


def sum_of(parts):
    total = None
    for part in parts:
        value = (part[0] if len(part.shape) == 3 else part[...]).astype(single)
        total = value if total is None else total + value
    return total


def norm_kernel(addends, place_ref, hidden_ref, grad_layer_ref, *refs):
    parts, (gain_ref, router_ref, digits_ref, grad_ref, low_ref, logits_ref, sum_ref) = refs[:addends], refs[addends:]
    width = hidden_ref.shape[1]
    wide = sum_of(parts)
    logits = wide[:, width:].astype(bfloat)
    logits_ref[...] = logits
    count = router_ref.shape[0]
    grad_in = wide[:, :width] + dot(logits[:, :count], router_ref[...])
    hidden = hidden_ref[...]
    inverse = lax.rsqrt(jnp.mean(hidden * hidden, axis=1, keepdims=True) + EPS)
    scaled = grad_in * gain_ref[...]
    inner = jnp.mean(scaled * hidden, axis=1, keepdims=True)
    grad = grad_layer_ref[...] + inverse * scaled - hidden * (inverse * inverse * inverse * inner)
    grad_ref[...] = grad
    low_ref[...] = grad.astype(bfloat)
    gain = jnp.sum(grad_in * hidden * inverse, axis=0, keepdims=True)
    first = lax.broadcasted_iota(jnp.int32, sum_ref.shape, 0) == 0
    gain = jnp.where(first, gain, 0.0)

    @pl.when(pl.program_id(0) == 0)
    def _():
        sum_ref[...] = gain + digits_ref[:, :1]

    @pl.when(pl.program_id(0) > 0)
    def _():
        sum_ref[...] += gain


def token_rows(kernel, name, steps, place, rowwise, others, outs, kept=()):
    block = outs[0].shape[0] // steps

    def spec(array):
        if isinstance(array, tuple) and array[1] is None:
            return pl.BlockSpec(
                (block, array[0].shape[1]), lambda i, place: (place[2] * steps + i, 0)
            )
        if isinstance(array, tuple):
            array, index = array
            return pl.BlockSpec((1, block, array.shape[2]), lambda i, place: (index, i, 0))
        return pl.BlockSpec((block, array.shape[1]), lambda i, place: (i, 0))

    bare = [array[0] if isinstance(array, tuple) else array for array in rowwise]
    return kernel_call(
        kernel,
        name,
        (steps,),
        [spec(array) for array in rowwise]
        + [pl.BlockSpec(array.shape, lambda i, place: (0, 0)) for array in others],
        [pl.BlockSpec((block, out.shape[1]), lambda i, place: (i, 0)) for out in outs]
        + [pl.BlockSpec(out.shape, lambda i, place: (0, 0)) for out in kept],
        list(outs) + list(kept),
        [],
        1,
        8 * sum(out.shape[0] * out.shape[1] for out in outs),
        (place,) + tuple(bare) + tuple(others),
        prefetch=1,
    )


def pack_kernel(lane_at, terms, cut, place_ref, sums_ref, *refs):
    lefts, rights, refs = refs[:terms], refs[terms : 2 * terms], refs[2 * terms :]
    outs, full_ref = refs[:-1], refs[-1]
    span = lefts[0].shape[0]
    at = 0
    for term in range(terms):
        left, right = lefts[term], rights[term]
        rows = left.shape[0]
        columns = right.shape[1]
        if right.shape[0] == rows:
            value = dot_tn(left[...], right[...])
        else:
            core = place_ref[2] if term == 0 else 1 - place_ref[2]
            value = dot_tn(left[...], right[pl.ds(pl.multiple_of(core * rows, rows), rows), :])
        if term == 1 and lefts[0].shape[0] != rights[0].shape[0]:
            full_ref[:, :columns] += value
        else:
            full_ref[:, at : at + columns] = value
            at += columns
    sums = sums_ref[...]
    high = sums.astype(bfloat)
    low = (sums - high.astype(single)).astype(bfloat)
    lane = lax.broadcasted_iota(jnp.int32, (sums.shape[0], 128), 1)
    chosen = (lane == lane_at + lax.broadcasted_iota(jnp.int32, lane.shape, 0)).astype(bfloat)
    column = dot_tn(high, chosen) + dot_tn(low, chosen)
    width = full_ref.shape[1]
    if at < width:
        full_ref[:, width - 128 :] = column
    else:
        full_ref[:, width - 128 :] += column
    some, block = outs[0].shape[:2]

    def blocks(step, i):
        start = (i * cut + (place_ref[4] ^ step)) * block
        return full_ref[pl.ds(pl.multiple_of(start, block), block), :].astype(bfloat)

    for step in range(min(cut, len(outs))):
        if len(outs) > cut and step == cut - 1:
            early = pl.program_id(0) < pl.num_programs(0) // 2

            @pl.when(early)
            def _():
                outs[-2][0] = blocks(step, 0)

            @pl.when(jnp.logical_not(early))
            def _():
                outs[-1][0] = blocks(step, 0)

        else:
            for i in range(some):
                outs[step][i] = blocks(step, i)


def pack_sums(place, lefts, rights, sums, lane_at, columns, count_dp, owners):
    width = sums.shape[1]
    block = width // (count_dp * owners)
    steps = count_dp if (width // count_dp) % 128 == 0 else 1
    tall = lambda array: pl.BlockSpec((array.shape[0], width // steps), lambda i, *_: (0, i))
    whole = lambda array: pl.BlockSpec(array.shape, lambda i, *_: (0, 0))
    some = count_dp // steps
    halved = owners == 4 and steps == count_dp
    specs = [pl.BlockSpec((some, block, columns), lambda i, *_: (i, 0, 0))] * owners
    shapes = [jax.ShapeDtypeStruct((count_dp, block, columns), bfloat)] * owners
    if halved:
        half = count_dp // 2
        specs[3:] = [
            pl.BlockSpec((1, block, columns), lambda i, *_: (jnp.minimum(i, half - 1), 0, 0)),
            pl.BlockSpec((1, block, columns), lambda i, *_: (jnp.maximum(i - half, 0), 0, 0)),
        ]
        shapes[3:] = [jax.ShapeDtypeStruct((half, block, columns), bfloat)] * 2
    outs = kernel_call(
        functools.partial(pack_kernel, lane_at, len(lefts), owners),
        "pack_sums",
        (steps,),
        [tall(sums)] + [tall(left) for left in lefts] + [whole(right) for right in rights],
        specs,
        shapes,
        [pltpu.VMEM((width // steps, columns), single)],
        2 * sum(left.shape[0] * width * columns for left in lefts),
        2 * width * columns,
        (place, sums) + tuple(lefts) + tuple(rights),
        prefetch=1,
    )
    outs = list(outs)
    if halved:
        return outs[:3] + [(outs[3], outs[4])]
    if owners == 4:
        half = count_dp // 2
        return outs[:3] + [(outs[3][:half], outs[3][half:])]
    return outs


def rope_tables(length, head_size):
    half_size = head_size // 2
    frequency = np.float32(THETA) ** (-np.arange(half_size, dtype=np.float32) * np.float32(2.0) / np.float32(head_size))
    angles = np.arange(length, dtype=np.float32)[:, None] * frequency.astype(np.float32)[None, :]
    return [jnp.asarray(np.tile(f(angles).astype(np.float32), (1, 128 // half_size))) for f in (np.cos, np.sin)]


def rms_backward(value_matrix, inverse, gain, grad_normed):
    scaled = grad_normed * gain
    grad_gain = jnp.sum(grad_normed * value_matrix * inverse, axis=0)
    grad_values = inverse * scaled - value_matrix * inverse**3 * jnp.mean(
        scaled * value_matrix, axis=-1, keepdims=True
    )
    return (grad_values, grad_gain)


def assemble(mine, other):
    first = lax.axis_index("tensor") == 0
    return jnp.concatenate([jnp.where(first, mine, other), jnp.where(first, other, mine)], axis=0)


def combine_groups(slots, rows, capacity, span, between, later=None):
    owners = slots.shape[0]
    orders = return_order(owners)
    if len(orders) == 1:
        mine, other = return_rows(slots, after(rows, *between(())), orders[0], capacity, span)
        other = swap(other)
        sent = [
            (mine[i].astype(single) + other[i].astype(single)).astype(bfloat)
            for i in range(owners - 1)
        ]
        came = [to_peer(part, "expert", i) for i, part in enumerate(sent, 1)]
    else:
        mine, other = return_rows(slots, rows, orders[0], capacity, span)
        other = after(swap(other), *hold(other))
        came, sent = send_farthest(mine, other)
        done = between(sent)
        came[0] = after(came[0], *hold(sent[0]), *done)
        rows = after(rows, *done, *hold(sent[0]), *hold(sent[1]))
        mine, other = return_rows(slots, rows, orders[1], capacity, span)
        other = after(swap(other), *hold(other))
        came, sent = send_nearer(mine, other, came)
        rows = after(rows, *sent, *hold(sent[0]), *hold(sent[1]))
        done = later(sent) if later else ()
        mine, other = return_rows(slots, rows, orders[2], capacity, span)
        other = swap(after(other, *done))
    own = len(orders[-1]) - 1
    return [(mine, own), (other, own)] + came, sent


def on_device(
    tokens,
    teacher,
    routes,
    valid,
    teacher_rows,
    norm_attn,
    norm_moe,
    w_query,
    key_projection_weight,
    value_projection_weight,
    w_out,
    w_router,
    w_gate,
    w_up,
    w_down,
):
    rows_dev, model_width = tokens.shape
    seq_count = rows_dev // SEQUENCE_LENGTH
    heads_local = w_query.shape[1] // HEAD_DIMENSION
    kv_local = key_projection_weight.shape[1] // HEAD_DIMENSION
    query_width = w_query.shape[1]
    key_width = key_projection_weight.shape[1]
    experts_local = w_gate.shape[0]
    owners = lax.axis_size("expert")
    count_dp = lax.axis_size("dp")
    groups = count_dp * owners
    all_experts = experts_local * owners
    top_count = routes.shape[1]
    capacity = rows_dev * top_count * 5 // (4 * all_experts)
    at_dp, at_ex, core = lax.axis_index("dp"), lax.axis_index("expert"), lax.axis_index("tensor")
    span = rows_dev // 2
    shards = count_dp // 2
    place = [at_ex * experts_local, at_dp // shards, core, at_dp % shards, at_ex]
    place = jnp.stack(place).astype(jnp.int32)

    def mine_of(value, axis=0):
        return lax.dynamic_slice_in_dim(value, core * span, span, axis)

    def other_of(value, axis=0):
        return lax.dynamic_slice_in_dim(value, (1 - core) * span, span, axis)

    tables = rope_tables(SEQUENCE_LENGTH, HEAD_DIMENSION)
    gain_attn, gain_moe = norm_attn.reshape(1, model_width), norm_moe.reshape(1, model_width)

    def tokens_like(columns, kind):
        return jax.ShapeDtypeStruct((span, columns), kind)

    weights = (w_query, key_projection_weight, value_projection_weight, w_out)
    normed, queries, keys, values, mixed, log_sums, staying, leaving = attend(
        place, tokens, gain_attn, *weights, tables
    )
    came = after(swap(leaving), *hold(leaving))
    wide = model_width + 128
    hidden_first, token = token_rows(
        functools.partial(token_kernel, all_experts),
        "token",
        4,
        place,
        [staying, came, (routes, None)],
        [gain_moe, w_router.T],
        [tokens_like(model_width, single), tokens_like(wide, bfloat)],
    )

    some = experts_local // 2
    few = max(1, some - some // 2)
    pieces = ((0, some), (some, experts_local - some))

    def interleave(mine, other):
        return [part for pair in zip(mine, other) for part in pair]

    def far_forward(parts, start, amount, pin):
        return expert_forward(
            place, all_experts, top_count, pin, (w_gate, w_up), parts, owners, capacity, start, amount
        )

    (wanted,) = after_all([mine_of(teacher_rows, 1)], token)
    (valid_rows,) = after_all([mine_of(valid)[:, None] + jnp.zeros((span, 128), jnp.int32)], token)
    chooser = (wanted[0][:, None] == jnp.arange(rows_dev, dtype=jnp.int32)).astype(bfloat)
    target = jnp.dot(chooser, teacher, preferred_element_type=bfloat)

    mirror = to_mirror(token)
    (counted,) = after_all([jnp.broadcast_to(valid[None, :], (8, rows_dev))], token)
    count = jnp.sum(counted[0])
    digits = jnp.stack([jnp.zeros((), jnp.int32), count // 64, count // 8 % 8, count % 8] + [jnp.zeros((), jnp.int32)] * 4)
    digits = jnp.broadcast_to(digits.astype(single)[:, None], (8, 128))
    near_parts = spread(token, (target, digits))
    mirror = after(mirror, *near_parts)
    peers = from_peers(mirror)
    mirror_other = swap(mirror)
    gate_pre, up_pre, near_half, near_tails, slots, results = expert_forward(
        place, all_experts, top_count, mirror, (w_gate, w_up, w_down), near_parts, owners, capacity, 0, experts_local
    )
    results = after(results, mirror_other)
    peers_other = []

    def swap_peers(sent):
        peers[:] = after_all(peers, *sent)
        peers_other.extend(swap(peer) for peer in peers)
        return sent

    addends, sent = combine_groups(slots, results, capacity, span, swap_peers)
    far_tokens = interleave([mirror] + peers, [mirror_other] + peers_other)
    far = [far_forward(far_tokens, *pieces[0], sent[0])]
    addends[-1] = after(addends[-1], far[0][0], *hold(sent[0]))
    layer_low, grad_layer, layer_grad, token_grad = token_rows(
        functools.partial(layer_kernel, len(addends)),
        "layer",
        4,
        place,
        [hidden_first, target, valid_rows] + addends,
        [],
        [tokens_like(model_width, bfloat), tokens_like(model_width, single), tokens_like(model_width, bfloat), tokens_like(wide, bfloat)],
    )

    far.append(far_forward(far_tokens, *pieces[1], token_grad))
    mirror = to_mirror(after(layer_grad, *hold(token_grad)))
    near_parts = spread(token_grad, (far[1][0],))
    mirror = after(mirror, *near_parts)
    peers = from_peers(mirror)
    mirror_other = swap(mirror)
    hidden_low, grad_gate_pre, grad_up_pre, near_grad_half, results = expert_backward(
        place, all_experts, slots, (w_gate, w_up, w_down), gate_pre, up_pre, near_tails, near_parts, capacity, (mirror,)
    )
    results = after(results, mirror_other)
    weight_parts, far_grads = [], []

    def weights_of(start, amount, others=()):
        piece = 0 if start < some else 1
        far_gate, far_up, far_half, far_tails, far_slots = far[piece]
        values = expert_weights(
            place,
            all_experts,
            far_slots,
            w_down,
            (far_gate, far_up, far_tails, far_half),
            (hidden_low, grad_gate_pre, grad_up_pre, near_half, near_grad_half),
            far_grads,
            capacity,
            start,
            start - pieces[piece][0],
            amount,
            shards,
            tuple(others),
        )
        came = [to_peer(values[step], "dp", step) for step in range(1, shards)]
        weight_parts.append((start, values[0], came))
        return (*values, *[pin for value in values[1:] for pin in hold(value)])

    def swap_far(sent):
        peers[:] = after_all(peers, *sent)
        peers_other = [swap(peer) for peer in peers]
        far_grads.extend(interleave([mirror] + peers, [mirror_other] + peers_other))
        return peers_other

    results = after(results, *peers)
    addends, sent = combine_groups(slots, results, capacity, span, lambda sent: sent, swap_far)
    if owners != 4:
        swap_far(sent)
    done = weights_of(0, few, sent)
    addends[-1] = after(addends[-1], *done, *hold(sent[0]))
    grad_hidden, grad_attn, grad_logits, gain_sums = token_rows(
        functools.partial(norm_kernel, len(addends)),
        "norm",
        4,
        place,
        [hidden_first, grad_layer] + addends,
        [gain_moe, w_router.T, digits],
        [tokens_like(model_width, single), tokens_like(model_width, bfloat), tokens_like(128, bfloat)],
        [jax.ShapeDtypeStruct((8, model_width), single)],
    )
    grad_attn_other = after(swap(grad_attn), *hold(grad_attn))
    first_parts = pack_sums(
        place,
        [grad_attn, grad_attn_other, token],
        [mixed, mixed, grad_logits],
        gain_sums,
        all_experts,
        query_width + 128,
        count_dp,
        owners,
    )
    first_sum = start_sum(first_parts)
    done = weights_of(some, experts_local - some, first_parts[-1] if owners == 4 else first_parts)
    first_sum, sent = go_on(first_sum, *done)
    grad_attn, layer_low = after_all([grad_attn, layer_low], *sent, *weight_parts[0][2])
    layer_other = swap(layer_low)
    raw_query, raw_key, raw_value, staying, leaving, gain_sums = attend_back(
        place, grad_attn, grad_attn_other, tokens, *weights, tables, (queries, keys, values, log_sums)
    )
    second_parts = pack_sums(
        place,
        [normed] * 3,
        [raw_query, raw_key, raw_value],
        after(gain_sums, *first_sum[1:], layer_other),
        0,
        query_width + 2 * key_width + 128,
        count_dp,
        owners,
    )
    second_sum = start_sum(second_parts)
    last = second_parts[-1] if owners == 4 else second_parts
    leaving = swap(leaving)
    first_total = add_up(first_sum[0], after_all(first_sum[1:], *last, leaving))
    first_dense = over_dp_start(first_total)
    pins = [] if first_dense[1] is None else [first_dense[1], *hold(first_dense[1])]
    done = weights_of(few, some - few, (*last, *hold(last[0]), *pins))
    second_sum, sent = go_on(second_sum, *done)
    first_dense = over_dp_step(first_dense, *sent, *weight_parts[1][2])
    leaving = after(leaving, *sent)
    inputs_mine = mine_of(tokens).astype(single)
    inverse_mine = lax.rsqrt(jnp.mean(inputs_mine * inputs_mine, axis=-1, keepdims=True) + EPS)
    grad_first, _ = rms_backward(
        inputs_mine, inverse_mine, norm_attn, staying + leaving.astype(single)
    )
    grad_tokens_mine = grad_hidden + grad_first
    pins = [] if first_dense[1] is None else [first_dense[1], *hold(first_dense[1])]
    second_total = add_up(second_sum[0], after_all(second_sum[1:], grad_tokens_mine, *pins))
    own, arrived, sent = over_dp_at_once(second_total)
    first_dense = over_dp_end(first_dense, *sent)
    tail = first_dense[:, query_width:]
    tail = tail + after(swap(tail), *hold(tail))
    counted = tail[:1, all_experts + 1 : all_experts + 4] * jnp.asarray([[32.0, 4.0, 0.5]], single)
    scale = jnp.broadcast_to(rows_dev * groups / jnp.sum(counted, axis=1, keepdims=True), (8, 128))
    first_dense, tail = first_dense * scale[0, 0], tail * scale[0, 0]
    grad_tokens_mine = grad_tokens_mine * scale[0, 0]
    grad_tokens_other = after(swap(grad_tokens_mine), *hold(grad_tokens_mine))
    grad_tokens = assemble(grad_tokens_mine, grad_tokens_other)
    layer_low = after(layer_low, *sent)
    block_out = assemble(layer_low, layer_other)
    weight_grads, finished = None, ()
    for start, values, came in weight_parts:
        came = [after(part, *sent, grad_tokens_other) for part in came]
        weight_grads, finished = finish_weights(experts_local, start, scale, values, came, weight_grads)
    arrived[0] = after(arrived[0], *hold(sent[0]), finished, grad_tokens, tail)
    grad_query, grad_key, grad_value, second_tail = scaled_sum(
        scale, [own] + arrived, (query_width, key_width, key_width, 128)
    )
    second_tail = second_tail + swap(second_tail)
    return (
        block_out,
        grad_tokens,
        second_tail[:, 0],
        tail[:, all_experts],
        grad_query,
        grad_key,
        grad_value,
        first_dense[:, :query_width].T,
        tail[:, :all_experts],
        weight_grads[0],
        weight_grads[1],
        weight_grads[2],
    )


def solution(mesh):
    placed = (
        P(("dp", "expert"), None),
        P(("dp", "expert"), None),
        P(("dp", "expert"), None),
        P(("dp", "expert")),
        P(("dp", "expert"), None),
        P(),
        P(),
        P(None, "tensor"),
        P(None, "tensor"),
        P(None, "tensor"),
        P("tensor", None),
        P(),
        P("expert", None, "tensor"),
        P("expert", None, "tensor"),
        P("expert", "tensor", None),
    )
    return jax.shard_map(
        on_device,
        mesh=mesh,
        in_specs=placed,
        out_specs=(
            P(("dp", "expert"), None),
            P(("dp", "expert"), None),
            P(("dp", "expert")),
            P(("dp", "expert")),
            P(("dp", "expert"), "tensor"),
            P(("dp", "expert"), "tensor"),
            P(("dp", "expert"), "tensor"),
            P("tensor", ("dp", "expert")),
            P(("dp", "expert"), None),
            P("expert", "dp", "tensor"),
            P("expert", "dp", "tensor"),
            P("expert", "tensor", "dp"),
        ),
        check_vma=False,
    )
```

```python
import functools
import math

import jax
import jax.numpy as jnp
import numpy as np
from jax import lax
from jax.experimental import pallas as pl
from jax.experimental.pallas import tpu as pltpu
from jax.sharding import PartitionSpec as P

HEAD_DIMENSION = 64
SEQUENCE_LENGTH = 512
ABLK = 256


EPS = 1e-06
VMEM_LIMIT = 56 * 1024 * 1024
CHUNK_OWN = 2
CHUNK_OTHERS = 1
COST = 100
THETA = 10000.0
bfloat = jnp.bfloat16
single = jnp.float32


def pass_kernel(*refs):
    pass


def after_all(values, *others):
    anywhere = pl.BlockSpec(memory_space=pl.ANY)
    return pl.pallas_call(
        pass_kernel,
        name="after",
        in_specs=[anywhere] * (len(values) + len(others)),
        out_specs=[anywhere] * len(values),
        out_shape=[jax.ShapeDtypeStruct(value.shape, value.dtype) for value in values],
        input_output_aliases={i: i for i in range(len(values))},
        cost_estimate=pl.CostEstimate(flops=0, bytes_accessed=0, transcendentals=0),
    )(*values, *others)


def after(value, *others):
    return after_all([value], *others)[0] if others else value


def hold(value):
    anywhere = pl.BlockSpec(memory_space=pl.ANY)
    return [
        pl.pallas_call(
            pass_kernel,
            name="hold",
            in_specs=[anywhere],
            out_specs=anywhere,
            out_shape=jax.ShapeDtypeStruct((8, 128), single),
            cost_estimate=pl.CostEstimate(flops=10**12, bytes_accessed=10**9, transcendentals=0),
        )(value)
    ]


def swap(value):
    return lax.ppermute(value, "tensor", [(0, 1), (1, 0)])


def to_peer(value, axis, step):
    return lax.ppermute(value, axis, [(i, i ^ step) for i in range(lax.axis_size(axis))])


def to_mirror(value):
    count = lax.axis_size("dp")
    return lax.ppermute(value, "dp", [(i, count - 1 - i) for i in range(count)])


def from_peers(value):
    return [to_peer(value, "expert", s) for s in range(1, lax.axis_size("expert"))]


def halves_kernel(low_ref, high_ref, *refs):
    refs[-2][...] = low_ref[...]
    refs[-1][...] = high_ref[...]


def low_and_high(low, high, *others):
    rows, width = low.shape
    half = jax.ShapeDtypeStruct((rows // 2, width), low.dtype)
    return pl.pallas_call(
        halves_kernel,
        name="halves",
        grid=(1,),
        in_specs=[
            pl.BlockSpec((rows // 2, width), lambda i: (0, 0)),
            pl.BlockSpec((rows // 2, width), lambda i: (1, 0)),
        ]
        + [pl.BlockSpec(memory_space=pl.ANY)] * len(others),
        out_specs=[pl.BlockSpec((rows // 2, width), lambda i: (0, 0))] * 2,
        out_shape=[half, half],
        cost_estimate=pl.CostEstimate(flops=0, bytes_accessed=2**20, transcendentals=0),
    )(low, high, *others)


def spread(value, own_other, pause=(), more_pause=()):
    if lax.axis_size("expert") != 4:
        near = from_peers(value)
        near[0] = after(near[0], own_other, *hold(value), *pause, *more_pause)
        return [part for mine in near for part in (mine, swap(mine))]
    first, second = to_peer(value, "expert", 1), to_peer(value, "expert", 2)
    for_first, for_second = low_and_high(second, first, own_other, *hold(value), *pause)
    low, high = to_peer(for_first, "expert", 1), to_peer(for_second, "expert", 2)
    first_other, second_other = swap(first), swap(second)
    low = after(low, *hold(for_first), first_other, second_other, *more_pause)
    return [first, first_other, second, second_other, low, high, swap(low), swap(high)]


def farther_kernel(mine_ref, other_ref, low_ref, high_ref):
    cut = low_ref.shape[0]
    total = (mine_ref[0].astype(single) + other_ref[0].astype(single)).astype(bfloat)
    low_ref[...] = total[:cut]
    high_ref[...] = total[cut:]


def nearer_kernel(mine_first, other_first, mine_second, other_second, low_ref, high_ref, first_ref, second_ref):
    step = pl.program_id(0)
    low = jnp.where(step == 0, low_ref[...].astype(single), 0.0)
    high = jnp.where(step == 0, 0.0, high_ref[...].astype(single))
    first = mine_first[0].astype(single) + other_first[0].astype(single) + high
    second = mine_second[0].astype(single) + other_second[0].astype(single) + low
    first_ref[...] = first.astype(bfloat)
    second_ref[...] = second.astype(bfloat)


def send_farthest(mine, other):
    _, span, width = mine.shape
    half = jax.ShapeDtypeStruct((span // 2, width), bfloat)
    low, high = pl.pallas_call(
        farther_kernel,
        name="farther",
        out_shape=[half, half],
        cost_estimate=pl.CostEstimate(flops=0, bytes_accessed=2**21, transcendentals=0),
    )(mine, other)
    return [to_peer(low, "expert", 1), to_peer(high, "expert", 2)], (low, high)


def send_nearer(mine, other, came):
    _, span, width = mine.shape
    half = pl.BlockSpec((span // 2, width), lambda i: (i, 0))
    only = pl.BlockSpec((span // 2, width), lambda i: (0, 0))
    stacked = lambda index: pl.BlockSpec((1, span // 2, width), lambda i: (index, i, 0))
    whole = jax.ShapeDtypeStruct((span, width), bfloat)
    first, second = pl.pallas_call(
        nearer_kernel,
        name="nearer",
        grid=(2,),
        in_specs=[stacked(0), stacked(0), stacked(1), stacked(1), only, only],
        out_specs=[half, half],
        out_shape=[whole, whole],
        cost_estimate=pl.CostEstimate(flops=0, bytes_accessed=2**22, transcendentals=0),
    )(mine, other, mine, other, *came)
    return [to_peer(first, "expert", 1), to_peer(second, "expert", 2)], (first, second)


def start_sum(parts):
    if len(parts) != 4:
        return parts, None
    low, high = parts[3]
    return parts, [to_peer(low, "expert", 1), to_peer(high, "expert", 2)]


def dense_kernel(first_in, second_in, low_ref, high_ref, *refs):
    first_ref, second_ref = refs[-2:]
    step = pl.program_id(0)
    low = jnp.where(step == 0, low_ref[...].astype(single), 0.0)
    high = jnp.where(step == 0, 0.0, high_ref[...].astype(single))
    first_ref[...] = (first_in[...].astype(single) + high).astype(bfloat)
    second_ref[...] = (second_in[...].astype(single) + low).astype(bfloat)


def go_on(state, *others):
    parts, came = state
    if came is None:
        sent = [after(part, *others) for part in parts[1:]]
        return [parts[0]] + [to_peer(part, "expert", i) for i, part in enumerate(sent, 1)], sent
    low = after(came[0], *hold(parts[3][0]))
    shape = parts[1].shape
    half = pl.BlockSpec((shape[0] // 2,) + shape[1:], lambda i: (i, 0, 0))
    only = pl.BlockSpec((shape[0] // 2,) + shape[1:], lambda i: (0, 0, 0))
    whole = jax.ShapeDtypeStruct(shape, bfloat)
    first, second = pl.pallas_call(
        dense_kernel,
        name="dense_nearer",
        grid=(2,),
        in_specs=[half, half, only, only] + [pl.BlockSpec(memory_space=pl.ANY)] * len(others),
        out_specs=[half, half],
        out_shape=[whole, whole],
        cost_estimate=pl.CostEstimate(flops=0, bytes_accessed=2**22, transcendentals=0),
    )(parts[1], parts[2], low, came[1], *others)
    came = to_peer(first, "expert", 1), to_peer(second, "expert", 2)
    return [parts[0], after(came[0], *hold(first)), came[1]], [first, second]


def add_up(own, arrived):
    total = own.astype(single)
    for part in arrived:
        total = total + part.astype(single)
    return total


def sum_all(value, axes):
    for axis in axes:
        step = 1
        while step < lax.axis_size(axis):
            value = value + to_peer(value, axis, step)
            step *= 2
    return value


def over_dp_start(total):
    at_dp, count = lax.axis_index("dp"), lax.axis_size("dp")
    parts = {r: lax.dynamic_index_in_dim(total, at_dp ^ r, 0, keepdims=False) for r in range(count)}
    return over_dp_send(parts, 1)


def over_dp_send(parts, step):
    if step >= lax.axis_size("dp"):
        return parts, None, step
    return parts, jnp.concatenate([parts[r].astype(bfloat) for r in parts if r & step], axis=0), step


def over_dp_step(state, *others):
    parts, sent, step = state
    parts = dict(parts)
    leaving = [r for r in parts if r & step]
    came = after(to_peer(sent, "dp", step), *hold(sent), *others).astype(single)
    rows = came.shape[0] // len(leaving)
    for i, r in enumerate(leaving):
        parts[r ^ step] = parts[r ^ step] + came[i * rows : (i + 1) * rows]
        del parts[r]
    return over_dp_send(parts, 2 * step)


def over_dp_end(state, *others):
    while state[1] is not None:
        state, others = over_dp_step(state, *others), ()
    return state[0][0]


def over_dp_at_once(total):
    at_dp = lax.axis_index("dp")

    def row(step):
        return lax.dynamic_index_in_dim(total, at_dp ^ step, 0, keepdims=False)

    sent = [row(step).astype(bfloat) for step in range(1, lax.axis_size("dp"))]
    return row(0), [to_peer(part, "dp", step) for step, part in enumerate(sent, 1)], sent


def scaled_sum_kernel(amount, widths, scale_ref, *refs):
    parts, outs = refs[:amount], refs[amount:]
    total = None
    for part in parts:
        value = part[...].astype(single)
        total = value if total is None else total + value
    total = total * scale_ref[:1, :1]
    at = 0
    for out, width in zip(outs, widths):
        out[...] = total[:, at : at + width]
        at += width


def scaled_sum(scale, parts, widths):
    rows = parts[0].shape[0]
    return pl.pallas_call(
        functools.partial(scaled_sum_kernel, len(parts), widths),
        name="scaled_sum",
        out_shape=[jax.ShapeDtypeStruct((rows, width), single) for width in widths],
        cost_estimate=pl.CostEstimate(flops=0, bytes_accessed=2**21, transcendentals=0),
    )(scale, *parts)


def dot(left, right):
    return lax.dot_general(left, right, (((1,), (0,)), ((), ())), preferred_element_type=single)


def dot_nt(left, right):
    return lax.dot_general(left, right, (((1,), (1,)), ((), ())), preferred_element_type=single)


def dot_tn(left, right):
    return lax.dot_general(left, right, (((0,), (0,)), ((), ())), preferred_element_type=single)


def picks(slot, capacity):
    return slot == lax.broadcasted_iota(jnp.int32, (capacity, slot.shape[1]), 0)


def group_parts(parts, joined_ref):
    if joined_ref is None:
        return [(parts[i], parts[i + 1]) for i in range(0, len(parts), 2)]
    cut = parts[-1].shape[0]

    @pl.when(pl.program_id(0) == 0)
    def _():
        for i in range(2):
            for j in range(2):
                joined_ref[i, j * cut : (j + 1) * cut, :] = parts[-4 + 2 * i + j][...]

    pairs = [(parts[i], parts[i + 1]) for i in range(0, len(parts) - 4, 2)]
    return pairs + [(joined_ref.at[0], joined_ref.at[1])]


def find_slots(first_ref, top_count, pairs, slots_ref):
    groups, experts, tokens = slots_ref.shape
    row = lax.broadcasted_iota(jnp.int32, (tokens, tokens), 0)
    earlier = (row < lax.broadcasted_iota(jnp.int32, (tokens, tokens), 1)).astype(bfloat)
    ids = lax.broadcasted_iota(jnp.int32, (experts, tokens), 0)
    ids = (ids + first_ref[0]).astype(single)
    for group, pair in enumerate(pairs):
        tails = [part[:, part.shape[1] - 128 :].astype(single).T for part in pair]
        routes = jnp.concatenate(tails, axis=1)[128 - top_count :]
        mask = ids == routes[:1]
        for k in range(1, top_count):
            mask = mask | (ids == routes[k : k + 1])
        before = dot(mask.astype(single).astype(bfloat), earlier)
        slots_ref[group] = jnp.where(mask, before, -1.0).astype(jnp.int32)


def gather_rows(slots_ref, expert, pairs, rows_ref):
    capacity = rows_ref.shape[0] // len(pairs)
    width = rows_ref.shape[1]
    for group, (mine, other) in enumerate(pairs):
        span = mine.shape[0]
        slot = slots_ref[group, pl.ds(expert, 1), :]
        picked = picks(slot, capacity).astype(bfloat)
        rows = dot(picked[:, :span], mine[:, :width]) + dot(picked[:, span:], other[:, :width])
        rows_ref[group * capacity : (group + 1) * capacity, :] = rows.astype(bfloat)


def slot_gates(expert, tails, count):
    lane = lax.broadcasted_iota(jnp.int32, tails.shape, 1)
    chosen = (lane == expert) | (lane == expert + count) | (lane == expert + 2 * count)
    return jnp.sum(jnp.where(chosen, tails.astype(single), 0.0), axis=1, keepdims=True)


def half_columns(place_ref, width):
    return pl.ds(pl.multiple_of(place_ref[1] * width, 128), width)


def return_order(groups):
    rest = list(range(1, groups)) + [0]
    return [[3], [1, 2], [0]] if groups == 4 else [rest]


def forward_kernel(count, top_count, amount, halved, start, chunk, with_out, place_ref, gate_w, up_w, *refs):
    if with_out:
        down_w, refs = refs[0], refs[1:]
    parts, refs = refs[:amount], refs[amount:]
    parts, pins = parts[:-1], parts[-1:]
    gate_ref, up_ref, half_ref, tail_ref, slots_ref = refs[:5]
    refs = refs[5:]
    step = pl.program_id(0)
    joined_ref = refs[-1] if halved else None
    rows_ref = refs[-2] if halved else refs[-1]
    width = gate_w.shape[1]
    pairs = group_parts(parts, joined_ref)

    @pl.when(step == 0)
    def _():
        find_slots(place_ref, top_count, pairs, slots_ref)

    for i in range(chunk):
        expert = start + step * chunk + i
        gather_rows(slots_ref, expert, pairs, rows_ref)
        half_ref[i] = rows_ref[:, half_columns(place_ref, half_ref.shape[2])]
        tails = rows_ref[:, width:]
        tail_ref[i] = tails
        rows = rows_ref[:, :width]
        gate_pre = dot(rows, gate_w[i])
        up_pre = dot(rows, up_w[i])
        gate_ref[i] = gate_pre.astype(bfloat)
        up_ref[i] = up_pre.astype(bfloat)
        if with_out:
            gates = slot_gates(place_ref[0] + expert, tails, count)
            hidden = (gate_pre * jax.nn.sigmoid(gate_pre) * up_pre * gates).astype(bfloat)
            refs[0][i] = dot(hidden, down_w[i]).astype(bfloat)


def hidden_grads(gate_pre, up_pre, gates, grad_hidden):
    sig = jax.nn.sigmoid(gate_pre)
    silu = gate_pre * sig
    hidden = silu * up_pre
    scaled = grad_hidden * gates
    grad_gate_pre = (scaled * up_pre * sig * (1.0 + gate_pre * (1.0 - sig))).astype(bfloat)
    grad_up_pre = (scaled * silu).astype(bfloat)
    return hidden, (hidden * gates).astype(bfloat), grad_gate_pre, grad_up_pre


def joined(refs):
    return refs[0][0] if len(refs) == 1 else jnp.concatenate([ref[0] for ref in refs], axis=0)


def backward_kernel(count, amount, halved, pins, pieces, place_ref, slots_ref, gate_w, up_w, down_w, *refs):
    gate_refs, up_refs, tail_refs = (refs[i * pieces : (i + 1) * pieces] for i in range(3))
    refs = refs[3 * pieces :]
    parts, refs = refs[:amount], refs[amount + pins :]
    hidden_ref, grad_gate_ref, grad_up_ref, half_ref, refs = refs[0], refs[1], refs[2], refs[3], refs[4:]
    back_ref, rows_ref = refs[:2]
    joined_ref = refs[2] if halved else None
    width = gate_w.shape[1]
    step = pl.program_id(0)
    expert = place_ref[0] + step
    gather_rows(slots_ref, step, group_parts(parts, joined_ref), rows_ref)
    half_ref[0] = rows_ref[:, half_columns(place_ref, half_ref.shape[2])]
    gates = slot_gates(expert, joined(tail_refs), count)
    grad_hidden = dot_nt(rows_ref[:, :width], down_w[0])
    hidden, hidden_low, grad_gate_pre, grad_up_pre = hidden_grads(
        joined(gate_refs).astype(single), joined(up_refs).astype(single), gates, grad_hidden
    )
    hidden_ref[0] = hidden_low
    grad_gate_ref[0] = grad_gate_pre
    grad_up_ref[0] = grad_up_pre
    back = dot_nt(grad_gate_pre, gate_w[0]) + dot_nt(grad_up_pre, up_w[0])
    back_ref[0, :, :width] = back.astype(bfloat)
    tails = rows_ref[:, width:].astype(single)
    lane = lax.broadcasted_iota(jnp.int32, tails.shape, 1)
    inner = jnp.sum(jnp.where(lane < 3, tails, 0.0), axis=1, keepdims=True)
    inner = inner * (place_ref[2] == 0).astype(single)
    grad_logit = gates * (jnp.sum(hidden * grad_hidden, axis=1, keepdims=True) - inner)
    back_ref[0, :, width:] = jnp.where(lane == expert, grad_logit, 0.0).astype(bfloat)


def weights_kernel(count, groups, start, pins, pieces, place_ref, slots_ref, down_w, gate_ref, up_ref, tail_ref, *refs):
    hidden_near, gate_near, up_near, near_g, far_x = refs[:5]
    near_x, refs = refs[5 : 5 + pieces], refs[5 + pieces :]
    parts, refs = refs[: 2 * groups], refs[2 * groups + pins :]
    shards, (rows_ref, full_ref) = refs[:-2], refs[-2:]
    expert = start + pl.program_id(0)
    gather_rows(slots_ref, expert, group_parts(parts, None), rows_ref)
    gates = slot_gates(place_ref[0] + expert, tail_ref[0], count)
    grad_hidden = dot_nt(rows_ref[...], down_w[0])
    _, hidden, grad_gate_pre, grad_up_pre = hidden_grads(
        gate_ref[0].astype(single), up_ref[0].astype(single), gates, grad_hidden
    )
    far_g = rows_ref[:, half_columns(place_ref, full_ref.shape[1])]
    far, near = far_x[0], joined(near_x)
    sums = (
        dot_tn(far, grad_gate_pre) + dot_tn(near, gate_near[0]),
        dot_tn(far, grad_up_pre) + dot_tn(near, up_near[0]),
        dot_tn(far_g, hidden) + dot_tn(near_g[0], hidden_near[0]),
    )
    for i, value in enumerate(sums):
        full_ref[i] = value.astype(bfloat)
    size = shards[0].shape[2]
    for step, shard in enumerate(shards):
        at = pl.multiple_of((place_ref[3] ^ step) * size, size)
        for i in range(3):
            shard[0, i] = full_ref[i, pl.ds(at, size), :]


def finish_kernel(scale_ref, own_ref, *refs):
    arrived, (d_gate, d_up, d_down, done_ref) = refs[:-4], refs[-4:]
    scale = scale_ref[:1, :1]
    for e in range(own_ref.shape[0]):

        def total(i):
            value = own_ref[e, i].astype(single)
            for ref in arrived:
                value = value + ref[e, i].astype(single)
            return value * scale

        d_gate[e] = total(0)
        d_up[e] = total(1)
        d_down[e] = total(2).T
    done_ref[...] = scale_ref[...]


def finish_more_kernel(gate_in, up_in, down_in, scale_ref, *refs):
    finish_kernel(scale_ref, *refs)


def return_kernel(first, cycle, slots_ref, rows_ref, mine, other, picked_ref):
    experts, capacity, width = rows_ref.shape
    span = mine.shape[1]
    group = (pl.program_id(0) + first) % cycle

    @pl.when(pl.program_id(1) == 0)
    def _():
        for e in range(experts):
            slot = slots_ref[group, e : e + 1, :]
            picked_ref[e * capacity : (e + 1) * capacity, :] = picks(slot, capacity).astype(bfloat)

    back = dot_tn(picked_ref[...], rows_ref[...].reshape(experts * capacity, width)).astype(bfloat)
    mine[0] = back[:span]
    other[0] = back[span:]


def kernel_call(kernel, name, grid, in_specs, out_specs, out_shape, scratch, flops, moved, args, prefetch=0, aliases=None):
    return pl.pallas_call(
        kernel,
        name=name,
        grid_spec=pltpu.PrefetchScalarGridSpec(
            num_scalar_prefetch=prefetch,
            grid=grid,
            in_specs=in_specs,
            out_specs=out_specs,
            scratch_shapes=scratch,
        ),
        out_shape=out_shape,
        input_output_aliases=aliases or {},
        compiler_params=pltpu.CompilerParams(
            dimension_semantics=("arbitrary",) * len(grid), vmem_limit_bytes=VMEM_LIMIT
        ),
        cost_estimate=pl.CostEstimate(flops=COST * flops, bytes_accessed=moved, transcendentals=0),
    )(*args)


def per_expert(*shape, start=0):
    return pl.BlockSpec((1,) + shape, lambda e, *_: (e + start,) + (0,) * len(shape))


def anywhere(pins):
    return [pl.BlockSpec(memory_space=pl.ANY) for _ in pins]


def once(*shape):
    return pl.BlockSpec(
        shape, lambda e, *_: (0,) * len(shape), pipeline_mode=pl.Buffered(buffer_count=1)
    )


def return_rows(slots, rows, order, capacity, span):
    groups, _, tokens = slots.shape
    experts, _, width = rows.shape
    amount, first = len(order), order[0]
    cycle = groups
    cuts = 2 if width % 256 == 0 and amount == 1 else 1
    cut = width // cuts
    part = pl.BlockSpec((1, span, cut), lambda g, n: (g, 0, n))
    return kernel_call(
        functools.partial(return_kernel, first, cycle),
        "return_rows",
        (amount, cuts),
        [
            pl.BlockSpec(slots.shape, lambda g, n: (0, 0, 0)),
            pl.BlockSpec((experts, capacity, cut), lambda g, n: (0, (g + first) % cycle, n)),
        ],
        [part, part],
        [jax.ShapeDtypeStruct((amount, span, width), bfloat)] * 2,
        [pltpu.VMEM((experts * capacity, tokens), bfloat)],
        2 * amount * experts * capacity * tokens * width,
        2 * amount * (experts * capacity + tokens) * width,
        (slots, rows),
    )


def expert_forward(place, count, top_count, pin, weights, parts, groups, capacity, start, experts, chunk=1):
    if experts % chunk or start % chunk:
        chunk = 1

    def per_expert(*shape, start=0):
        return pl.BlockSpec((chunk,) + shape, lambda e, *_: (e + start // chunk,) + (0,) * len(shape))

    span, whole = parts[0].shape
    tokens = 2 * span
    width, hidden = weights[0].shape[1:]
    with_out = len(weights) == 3
    total = groups * capacity
    halved = len(parts) > 2 * groups
    specs = [per_expert(width, hidden, start=start)] * 2
    outs = [per_expert(total, hidden)] * 2
    outs += [per_expert(total, width // 2), per_expert(total, whole - width)]
    shapes = [jax.ShapeDtypeStruct((experts, total, hidden), bfloat)] * 2
    shapes += [jax.ShapeDtypeStruct((experts, total, width // 2), bfloat)]
    shapes += [jax.ShapeDtypeStruct((experts, total, whole - width), bfloat)]
    listed = (groups, -(-weights[0].shape[0] // 8) * 8, tokens)
    outs += [pl.BlockSpec(listed, lambda e, *_: (0, 0, 0))]
    shapes += [jax.ShapeDtypeStruct(listed, jnp.int32)]
    scratch = [pltpu.VMEM((total, whole), bfloat)]
    if halved:
        scratch += [pltpu.VMEM((2, span, whole), bfloat)]
    if with_out:
        specs += [per_expert(hidden, width, start=start)]
        outs += [per_expert(total, width)]
        shapes += [jax.ShapeDtypeStruct((experts, total, width), bfloat)]
    specs += [once(*part.shape) for part in parts] + [pl.BlockSpec(memory_space=pl.ANY)]
    return kernel_call(
        functools.partial(forward_kernel, count, top_count, len(parts) + 1, halved, start, chunk, with_out),
        "expert_forward" if with_out else "expert_forward_far",
        (experts // chunk,), specs, outs, shapes, scratch,
        2 * experts * total * (width * hidden * len(weights) + tokens * whole),
        2 * experts * (len(weights) * width * hidden + total * width + 4 * total * hidden),
        (place,) + tuple(weights) + tuple(parts) + (pin,),
        prefetch=1,
    )


def expert_backward(place, count, slots, weights, gate_pre, up_pre, tails, parts, capacity, pins):
    groups, _, tokens = slots.shape
    experts = weights[0].shape[0]
    span, whole = parts[0].shape
    width, hidden = weights[0].shape[1:]
    total = groups * capacity
    thin = per_expert(total, hidden)
    specs = [once(*slots.shape)] + [per_expert(width, hidden)] * 2
    specs += [per_expert(hidden, width)]
    specs += [per_expert(*piece.shape[1:]) for piece in (*gate_pre, *up_pre, *tails)]
    outs = [thin] * 3 + [per_expert(total, width // 2), per_expert(total, whole)]
    shapes = [jax.ShapeDtypeStruct((experts, total, hidden), bfloat)] * 3
    shapes += [jax.ShapeDtypeStruct((experts, total, width // 2), bfloat)]
    shapes += [jax.ShapeDtypeStruct((experts, total, whole), bfloat)]
    return kernel_call(
        functools.partial(backward_kernel, count, len(parts), len(parts) > 2 * groups, len(pins), len(tails)),
        "expert_backward",
        (experts,), specs + [once(*part.shape) for part in parts] + anywhere(pins), outs, shapes,
        [pltpu.VMEM((total, whole), bfloat)]
        + ([pltpu.VMEM((2, span, whole), bfloat)] if len(parts) > 2 * groups else []),
        2 * experts * total * width * (hidden * 3 + tokens),
        2 * experts * (3 * width * hidden + 3 * total * width // 2 + 7 * total * hidden),
        (place, slots) + tuple(weights) + tuple(gate_pre) + tuple(up_pre) + tuple(tails) + tuple(parts) + tuple(pins),
        prefetch=1,
    )


def expert_weights(place, count, slots, down_w, far, near, near_x, parts, capacity, start, far_start, experts, shards, pins):
    groups, _, tokens = slots.shape
    hidden, width = down_w.shape[1:]
    total = groups * capacity
    far_pre, (far_tails, far_half) = far[:2], far[2:]
    thin = per_expert(total, hidden, start=far_start)
    wide = per_expert(total, width // 2, start=far_start)
    thin_at = per_expert(total, hidden, start=start)
    wide_at = per_expert(total, width // 2, start=start)
    specs = [once(*slots.shape), per_expert(hidden, width, start=start)]
    specs += [thin, thin, per_expert(total, far_tails.shape[2], start=far_start)] + [thin_at] * 3
    specs += [wide_at, wide]
    specs += [per_expert(*piece.shape[1:], start=start) for piece in near_x]
    size = width // (2 * shards)
    return kernel_call(
        functools.partial(weights_kernel, count, groups, start, len(pins), len(near_x)),
        "expert_weights",
        (experts,), specs + [once(*part.shape) for part in parts] + anywhere(pins),
        [per_expert(3, size, hidden)] * shards,
        [jax.ShapeDtypeStruct((experts, 3, size, hidden), bfloat)] * shards,
        [pltpu.VMEM((total, width), bfloat), pltpu.VMEM((3, width // 2, hidden), bfloat)],
        2 * experts * total * width * (hidden * 4 + tokens),
        2 * experts * (5 * width * hidden // 2 + 3 * total * width // 2 + 7 * total * hidden),
        (place, slots, down_w) + tuple(far_pre) + (far_tails,) + tuple(near) + (far_half,) + tuple(near_x) + tuple(parts) + tuple(pins),
        prefetch=1,
    )


def finish_weights(experts, start, scale, own, arrived, before):
    some, _, size, hidden = own.shape
    chunk = math.gcd(some, start) if start else some

    def block(*shape, at=0):
        return pl.BlockSpec((chunk,) + shape, lambda e, *_: (e + at // chunk,) + (0,) * len(shape))

    ready = [block(3, size, hidden)] * (1 + len(arrived))
    kernel = finish_kernel if before is None else finish_more_kernel
    kept = [] if before is None else [pl.BlockSpec(memory_space=pl.ANY)] * 3
    small = pl.BlockSpec((8, 128), lambda e, *_: (0, 0))
    *grads, done = kernel_call(
        kernel,
        "finish_weights",
        (some // chunk,),
        kept + [small] + ready,
        [block(size, hidden, at=start)] * 2 + [block(hidden, size, at=start), small],
        [jax.ShapeDtypeStruct((experts, size, hidden), single)] * 2
        + [jax.ShapeDtypeStruct((experts, hidden, size), single), jax.ShapeDtypeStruct((8, 128), single)],
        [],
        3 * some * size * hidden,
        12 * some * size * hidden,
        tuple(before or ()) + (scale, own) + tuple(arrived),
        aliases={} if before is None else {0: 0, 1: 1, 2: 2},
    )
    return grads, done


def rotate(value, cosines, sines, back):
    pieces = []
    for at in range(0, value.shape[1], 128):
        piece = value[:, at : at + 128]
        lane = lax.broadcasted_iota(jnp.int32, piece.shape, 1)
        later, sooner = pltpu.roll(piece, 96, 1), pltpu.roll(piece, 32, 1)
        if back:
            turned = jnp.where(lane % 64 < 32, later, -sooner)
        else:
            turned = jnp.where(lane % 64 < 32, -later, sooner)
        pieces.append(piece * cosines + turned * sines)
    return pieces[0] if len(pieces) == 1 else jnp.concatenate(pieces, axis=1)


def query_blocks(length):
    return [(at, at + ABLK) for at in range(0, length, ABLK)]


def attend_kernel(place_ref, tokens_ref, gain_ref, query_w, key_w, value_w, out_w, cos_ref, sin_ref,
                  normed_ref, queries_ref, keys_ref, values_ref, mixed_ref, lse_ref, stay_ref, leave_ref, total_ref):
    step = pl.program_id(0)
    length = tokens_ref.shape[0]
    group = query_w.shape[1] // key_w.shape[1]

    @pl.when(step == 0)
    def _():
        inputs = tokens_ref[...].astype(single)
        inverse = lax.rsqrt(jnp.mean(inputs * inputs, axis=1, keepdims=True) + EPS)
        normed_ref[...] = (inputs * inverse * gain_ref[...]).astype(bfloat)

    normed = normed_ref[...]
    cosines, sines = cos_ref[...], sin_ref[...]
    queries = rotate(dot(normed, query_w[...]), cosines, sines, False) * HEAD_DIMENSION ** (-0.5)
    keys = rotate(dot(normed, key_w[...]), cosines, sines, False)
    values = dot(normed, value_w[...])
    size = HEAD_DIMENSION
    mixed = []
    for kv in range(key_w.shape[1] // size):
        key = keys[:, kv * size : (kv + 1) * size].astype(bfloat)
        value = values[:, kv * size : (kv + 1) * size].astype(bfloat)
        keys_ref[kv] = key
        values_ref[kv] = value
        for head in range(kv * group, (kv + 1) * group):
            query = queries[:, head * size : (head + 1) * size].astype(bfloat)
            queries_ref[head] = query
            outs, sums = [], []
            for start, seen in query_blocks(length):
                scores = dot_nt(key[:seen], query[start : start + ABLK])
                peak = jnp.max(scores, axis=0, keepdims=True)
                weights = jnp.exp(scores - peak)
                total = jnp.sum(weights, axis=0, keepdims=True)
                probs = (weights / total).astype(bfloat)
                outs.append(dot_tn(value[:seen], probs))
                sums.append(peak + jnp.log(total))
            mixed.append(jnp.concatenate(outs, axis=1))
            lse_ref[0, head : head + 1, :] = jnp.concatenate(sums, axis=1)
    mixed = jnp.concatenate(mixed, axis=0).T.astype(bfloat)
    mixed_ref[...] = mixed
    part = dot(mixed, out_w[...])

    @pl.when(step == 0)
    def _():
        total_ref[...] = part

    @pl.when(step > 0)
    def _():
        total_ref[...] += part

    @pl.when(step == pl.num_programs(0) - 1)
    def _():
        span = stay_ref.shape[0]
        core = place_ref[2]
        mine = pl.ds(pl.multiple_of(core * span, span), span)
        other = pl.ds(pl.multiple_of((1 - core) * span, span), span)
        stay_ref[...] = total_ref[mine, :] + tokens_ref[mine, :].astype(single)
        leave_ref[...] = total_ref[other, :]


def attend_back_kernel(place_ref, mine_ref, other_ref, tokens_ref, query_w, key_w, value_w, out_w, cos_ref, sin_ref,
                       queries_ref, keys_ref, values_ref, lse_ref,
                       raw_query_ref, raw_key_ref, raw_value_ref, stay_ref, leave_ref, gain_ref, low_ref, total_ref):
    step = pl.program_id(0)
    length = tokens_ref.shape[0]
    span = mine_ref.shape[0]
    core = place_ref[2]
    mine = pl.ds(pl.multiple_of(core * span, span), span)
    other = pl.ds(pl.multiple_of((1 - core) * span, span), span)
    low_ref[mine, :] = dot_nt(mine_ref[...], out_w[...]).astype(bfloat)
    low_ref[other, :] = dot_nt(other_ref[...], out_w[...]).astype(bfloat)
    grads = low_ref[...].astype(single)
    size = HEAD_DIMENSION
    group = query_w.shape[1] // key_w.shape[1]
    grad_queries, grad_keys, grad_values = [], [], []
    for kv in range(key_w.shape[1] // size):
        key, value = keys_ref[kv], values_ref[kv]
        key_parts = [[] for _ in query_blocks(length)]
        value_parts = [[] for _ in query_blocks(length)]
        for head in range(kv * group, (kv + 1) * group):
            query = queries_ref[head]
            grad = grads[:, head * size : (head + 1) * size].astype(bfloat)
            outs = []
            for block, (start, seen) in enumerate(query_blocks(length)):
                rows = slice(start, start + ABLK)
                scores = dot_nt(key[:seen], query[rows])
                probs = jnp.exp(scores - lse_ref[0, head : head + 1, rows])
                grad_probs = dot_nt(value[:seen], grad[rows])
                inner = jnp.sum(probs * grad_probs, axis=0, keepdims=True)
                grad_scores = (probs * (grad_probs - inner)).astype(bfloat)
                outs.append(dot_tn(grad_scores, key[:seen]))
                key_parts[block].append(dot(grad_scores, query[rows]))
                value_parts[block].append(dot(probs.astype(bfloat), grad[rows]))
            grad_queries.append(jnp.concatenate(outs, axis=0))

        def whole(parts):
            rows = []
            for at in range(len(parts)):
                here = slice(at * ABLK, (at + 1) * ABLK)
                rows.append(sum(one[here] for block in parts[at:] for one in block))
            return jnp.concatenate(rows, axis=0)

        grad_keys.append(whole(key_parts))
        grad_values.append(whole(value_parts))
    cosines, sines = cos_ref[...], sin_ref[...]
    grad_query = jnp.concatenate(grad_queries, axis=1) * HEAD_DIMENSION ** (-0.5)
    raw_query = rotate(grad_query, cosines, sines, True).astype(bfloat)
    raw_key = rotate(jnp.concatenate(grad_keys, axis=1), cosines, sines, True).astype(bfloat)
    raw_value = jnp.concatenate(grad_values, axis=1).astype(bfloat)
    raw_query_ref[...] = raw_query
    raw_key_ref[...] = raw_key
    raw_value_ref[...] = raw_value
    part = dot_nt(raw_query, query_w[...]) + dot_nt(raw_key, key_w[...]) + dot_nt(raw_value, value_w[...])

    @pl.when(step == 0)
    def _():
        total_ref[...] = part

    @pl.when(step > 0)
    def _():
        total_ref[...] += part

    @pl.when(step == pl.num_programs(0) - 1)
    def _():
        stay_ref[...] = total_ref[mine, :]
        leave_ref[...] = total_ref[other, :].astype(bfloat)
        inputs = tokens_ref[...].astype(single)
        inverse = lax.rsqrt(jnp.mean(inputs * inputs, axis=1, keepdims=True) + EPS)
        gain = jnp.sum(total_ref[...] * inputs * inverse, axis=0, keepdims=True)
        first = lax.broadcasted_iota(jnp.int32, gain_ref.shape, 0) == 0
        gain_ref[...] = jnp.where(first, gain, 0.0)


def attend(place, tokens, gain, query_w, key_w, value_w, out_w, tables):
    length, width = tokens.shape
    span, size = length // 2, HEAD_DIMENSION
    steps = key_w.shape[1] // 128
    wide, thin = query_w.shape[1] // steps, 128
    heads, kv_heads = query_w.shape[1] // size, key_w.shape[1] // size
    whole = lambda *shape: pl.BlockSpec(shape, lambda i, *_: (0,) * len(shape))
    across = lambda rows, columns: pl.BlockSpec((rows, columns), lambda i, *_: (0, i))
    split = lambda *shape: pl.BlockSpec(shape, lambda i, *_: (i,) + (0,) * (len(shape) - 1))
    low = lambda *shape: jax.ShapeDtypeStruct(shape, bfloat)
    high = lambda *shape: jax.ShapeDtypeStruct(shape, single)
    return kernel_call(
        attend_kernel,
        "attend",
        (steps,),
        [whole(length, width), pl.BlockSpec((width,), lambda i, *_: (0,)), across(width, wide), across(width, thin), across(width, thin),
         split(wide, width), whole(length, 128), whole(length, 128)],
        [whole(length, width), split(heads // steps, length, size), split(kv_heads // steps, length, size),
         split(kv_heads // steps, length, size), across(length, wide), split(1, 8, length),
         whole(span, width), whole(span, width)],
        [low(length, width), low(heads, length, size), low(kv_heads, length, size), low(kv_heads, length, size),
         low(length, heads * size), high(steps, 8, length), high(span, width), high(span, width)],
        [pltpu.VMEM((length, width), single)],
        2 * length * width * (2 * heads + 2 * kv_heads) * size,
        2 * (length * width * 6 + 2 * width * (heads + kv_heads) * size),
        (place, tokens, gain, query_w, key_w, value_w, out_w) + tuple(tables),
        prefetch=1,
    )


def attend_back(place, mine, other, tokens, query_w, key_w, value_w, out_w, tables, saved):
    length, width = tokens.shape
    span, size = length // 2, HEAD_DIMENSION
    steps = key_w.shape[1] // 128
    wide, thin = query_w.shape[1] // steps, 128
    heads, kv_heads = query_w.shape[1] // size, key_w.shape[1] // size
    whole = lambda *shape: pl.BlockSpec(shape, lambda i, *_: (0,) * len(shape))
    across = lambda rows, columns: pl.BlockSpec((rows, columns), lambda i, *_: (0, i))
    split = lambda *shape: pl.BlockSpec(shape, lambda i, *_: (i,) + (0,) * (len(shape) - 1))
    low = lambda *shape: jax.ShapeDtypeStruct(shape, bfloat)
    high = lambda *shape: jax.ShapeDtypeStruct(shape, single)
    return kernel_call(
        attend_back_kernel,
        "attend_back",
        (steps,),
        [whole(span, width), whole(span, width), whole(length, width),
         across(width, wide), across(width, thin), across(width, thin), split(wide, width),
         whole(length, 128), whole(length, 128), split(heads // steps, length, size),
         split(kv_heads // steps, length, size), split(kv_heads // steps, length, size), split(1, 8, length)],
        [across(length, wide), across(length, thin), across(length, thin),
         whole(span, width), whole(span, width), whole(8, width)],
        [low(length, heads * size), low(length, kv_heads * size), low(length, kv_heads * size),
         high(span, width), low(span, width), high(8, width)],
        [pltpu.VMEM((length, wide), bfloat), pltpu.VMEM((length, width), single)],
        6 * length * width * (heads + kv_heads) * size,
        2 * (length * width * 6 + 2 * width * (heads + kv_heads) * size),
        (place, mine, other, tokens, query_w, key_w, value_w, out_w) + tuple(tables) + tuple(saved),
        prefetch=1,
    )


def three_lanes(value, starts, lanes):
    total = None
    for start in starts:
        low = value.astype(bfloat).astype(single)
        value = value - low
        moved = pltpu.roll(low, start, 1) if start else low
        total = moved if total is None else total + moved
    return total


def token_kernel(count, place_ref, stay_ref, came_ref, routes_ref, gain_ref, router_ref, hidden_ref, token_ref):
    width = stay_ref.shape[1]
    hidden = stay_ref[...] + came_ref[...]
    hidden_ref[...] = hidden
    inverse = lax.rsqrt(jnp.mean(hidden * hidden, axis=1, keepdims=True) + EPS)
    moe_in = (hidden * inverse * gain_ref[...]).astype(bfloat)
    token_ref[:, :width] = moe_in
    logits = dot_nt(moe_in, router_ref[...])
    logits = jnp.concatenate([logits, jnp.zeros((logits.shape[0], 128 - count), single)], axis=1)
    lane = lax.broadcasted_iota(jnp.int32, logits.shape, 1)
    routes = routes_ref[...].astype(single).T
    lanes = lane.astype(single)
    picked = lanes == routes[:, :1]
    for k in range(1, routes.shape[1]):
        picked = picked | (lanes == routes[:, k : k + 1])
    peak = jnp.max(jnp.where(picked, logits, -1e30), axis=1, keepdims=True)
    weights = jnp.where(picked, jnp.exp(jnp.where(picked, logits, peak) - peak), 0.0)
    gates = weights / jnp.sum(weights, axis=1, keepdims=True)
    tail = three_lanes(gates, (0, count, 2 * count), 128)
    blank = jnp.zeros((routes.shape[0], 128 - routes.shape[1]), single)
    token_ref[:, width:] = (tail + jnp.concatenate([blank, routes], axis=1)).astype(bfloat)


def layer_kernel(addends, place_ref, hidden_ref, target_ref, valid_ref, *refs):
    parts, (layer_ref, grad_ref, low_ref, token_ref) = refs[:addends], refs[addends:]
    width = hidden_ref.shape[1]
    moe = sum_of(parts)
    layer = hidden_ref[...] + moe
    layer_ref[...] = layer.astype(bfloat)
    valid = valid_ref[:, :1].astype(single)
    grad = valid * (layer - target_ref[...].astype(single))
    grad_ref[...] = grad
    low_ref[...] = grad.astype(bfloat)
    token_ref[:, :width] = grad.astype(bfloat)
    inner = jnp.sum(grad * moe, axis=1, keepdims=True)
    lane = lax.broadcasted_iota(jnp.int32, (inner.shape[0], 128), 1)
    inner = jnp.where(lane == 0, inner, 0.0)
    token_ref[:, width:] = three_lanes(inner, (0, 1, 2), 128).astype(bfloat)


def sum_of(parts):
    total = None
    for part in parts:
        value = (part[0] if len(part.shape) == 3 else part[...]).astype(single)
        total = value if total is None else total + value
    return total


def norm_kernel(addends, place_ref, hidden_ref, grad_layer_ref, *refs):
    parts, (gain_ref, router_ref, digits_ref, grad_ref, low_ref, logits_ref, sum_ref) = refs[:addends], refs[addends:]
    width = hidden_ref.shape[1]
    wide = sum_of(parts)
    logits = wide[:, width:].astype(bfloat)
    logits_ref[...] = logits
    count = router_ref.shape[0]
    grad_in = wide[:, :width] + dot(logits[:, :count], router_ref[...])
    hidden = hidden_ref[...]
    inverse = lax.rsqrt(jnp.mean(hidden * hidden, axis=1, keepdims=True) + EPS)
    scaled = grad_in * gain_ref[...]
    inner = jnp.mean(scaled * hidden, axis=1, keepdims=True)
    grad = grad_layer_ref[...] + inverse * scaled - hidden * (inverse * inverse * inverse * inner)
    grad_ref[...] = grad
    low_ref[...] = grad.astype(bfloat)
    gain = jnp.sum(grad_in * hidden * inverse, axis=0, keepdims=True)
    first = lax.broadcasted_iota(jnp.int32, sum_ref.shape, 0) == 0
    gain = jnp.where(first, gain, 0.0)

    @pl.when(pl.program_id(0) == 0)
    def _():
        sum_ref[...] = gain + digits_ref[:, :1]

    @pl.when(pl.program_id(0) > 0)
    def _():
        sum_ref[...] += gain


def digits_kernel(valid_ref, pin_ref, digits_ref):
    count = jnp.sum(valid_ref[:1, :].astype(single), axis=1, keepdims=True)
    high = jnp.floor(count * (1.0 / 64.0))
    middle = jnp.floor((count - 64.0 * high) * 0.125)
    low = count - 64.0 * high - 8.0 * middle
    row = lax.broadcasted_iota(jnp.int32, digits_ref.shape, 0)
    digits_ref[...] = jnp.where(row == 1, high, jnp.where(row == 2, middle, jnp.where(row == 3, low, 0.0)))


def count_digits(valid, pin):
    return pl.pallas_call(
        digits_kernel,
        name="digits",
        grid=(1,),
        in_specs=[pl.BlockSpec(valid.shape, lambda i: (0, 0)), pl.BlockSpec(memory_space=pl.ANY)],
        out_specs=pl.BlockSpec((8, 128), lambda i: (0, 0)),
        out_shape=jax.ShapeDtypeStruct((8, 128), single),
        cost_estimate=pl.CostEstimate(flops=0, bytes_accessed=2**14, transcendentals=0),
    )(valid, pin)


def token_rows(kernel, name, steps, place, rowwise, others, outs, kept=()):
    block = outs[0].shape[0] // steps

    def spec(array):
        if isinstance(array, tuple) and array[1] is None:
            return pl.BlockSpec(
                (array[0].shape[0], block), lambda i, place: (0, place[2] * steps + i)
            )
        if isinstance(array, tuple):
            array, index = array
            return pl.BlockSpec((1, block, array.shape[2]), lambda i, place: (index, i, 0))
        return pl.BlockSpec((block, array.shape[1]), lambda i, place: (i, 0))

    bare = [array[0] if isinstance(array, tuple) else array for array in rowwise]
    return kernel_call(
        kernel,
        name,
        (steps,),
        [spec(array) for array in rowwise]
        + [pl.BlockSpec(array.shape, lambda i, place, n=array.ndim: (0,) * n) for array in others],
        [pl.BlockSpec((block, out.shape[1]), lambda i, place: (i, 0)) for out in outs]
        + [pl.BlockSpec(out.shape, lambda i, place: (0, 0)) for out in kept],
        list(outs) + list(kept),
        [],
        1,
        8 * sum(out.shape[0] * out.shape[1] for out in outs),
        (place,) + tuple(bare) + tuple(others),
        prefetch=1,
    )


def pack_kernel(lane_at, terms, cut, place_ref, sums_ref, *refs):
    lefts, rights, refs = refs[:terms], refs[terms : 2 * terms], refs[2 * terms :]
    outs, full_ref = refs[:-1], refs[-1]
    span = lefts[0].shape[0]
    at = 0
    for term in range(terms):
        left, right = lefts[term], rights[term]
        rows = left.shape[0]
        columns = right.shape[1]
        if right.shape[0] == rows:
            value = dot_tn(left[...], right[...])
        else:
            core = place_ref[2] if term == 0 else 1 - place_ref[2]
            value = dot_tn(left[...], right[pl.ds(pl.multiple_of(core * rows, rows), rows), :])
        if term == 1 and lefts[0].shape[0] != rights[0].shape[0]:
            full_ref[:, :columns] += value
        else:
            full_ref[:, at : at + columns] = value
            at += columns
    sums = sums_ref[...]
    high = sums.astype(bfloat)
    low = (sums - high.astype(single)).astype(bfloat)
    lane = lax.broadcasted_iota(jnp.int32, (sums.shape[0], 128), 1)
    chosen = (lane == lane_at + lax.broadcasted_iota(jnp.int32, lane.shape, 0)).astype(bfloat)
    column = dot_tn(high, chosen) + dot_tn(low, chosen)
    width = full_ref.shape[1]
    if at < width:
        full_ref[:, width - 128 :] = column
    else:
        full_ref[:, width - 128 :] += column
    some, block = outs[0].shape[:2]

    def blocks(step, i):
        start = (i * cut + (place_ref[4] ^ step)) * block
        return full_ref[pl.ds(pl.multiple_of(start, block), block), :].astype(bfloat)

    for step in range(min(cut, len(outs))):
        if len(outs) > cut and step == cut - 1:
            early = pl.program_id(0) < pl.num_programs(0) // 2

            @pl.when(early)
            def _():
                outs[-2][0] = blocks(step, 0)

            @pl.when(jnp.logical_not(early))
            def _():
                outs[-1][0] = blocks(step, 0)

        else:
            for i in range(some):
                outs[step][i] = blocks(step, i)


def pack_sums(place, lefts, rights, sums, lane_at, columns, count_dp, owners):
    width = sums.shape[1]
    block = width // (count_dp * owners)
    steps = count_dp if (width // count_dp) % 128 == 0 else 1
    tall = lambda array: pl.BlockSpec((array.shape[0], width // steps), lambda i, *_: (0, i))
    whole = lambda array: pl.BlockSpec(array.shape, lambda i, *_: (0, 0))
    some = count_dp // steps
    halved = owners == 4 and steps == count_dp
    specs = [pl.BlockSpec((some, block, columns), lambda i, *_: (i, 0, 0))] * owners
    shapes = [jax.ShapeDtypeStruct((count_dp, block, columns), bfloat)] * owners
    if halved:
        half = count_dp // 2
        specs[3:] = [
            pl.BlockSpec((1, block, columns), lambda i, *_: (jnp.minimum(i, half - 1), 0, 0)),
            pl.BlockSpec((1, block, columns), lambda i, *_: (jnp.maximum(i - half, 0), 0, 0)),
        ]
        shapes[3:] = [jax.ShapeDtypeStruct((half, block, columns), bfloat)] * 2
    outs = kernel_call(
        functools.partial(pack_kernel, lane_at, len(lefts), owners),
        "pack_sums",
        (steps,),
        [tall(sums)] + [tall(left) for left in lefts] + [whole(right) for right in rights],
        specs,
        shapes,
        [pltpu.VMEM((width // steps, columns), single)],
        2 * sum(left.shape[0] * width * columns for left in lefts),
        2 * width * columns,
        (place, sums) + tuple(lefts) + tuple(rights),
        prefetch=1,
    )
    outs = list(outs)
    if halved:
        return outs[:3] + [(outs[3], outs[4])]
    if owners == 4:
        half = count_dp // 2
        return outs[:3] + [(outs[3][:half], outs[3][half:])]
    return outs


def rope_tables(length, head_size):
    half_size = head_size // 2
    frequency = np.float32(THETA) ** (-np.arange(half_size, dtype=np.float32) * np.float32(2.0) / np.float32(head_size))
    angles = np.arange(length, dtype=np.float32)[:, None] * frequency.astype(np.float32)[None, :]
    return [jnp.asarray(np.tile(f(angles).astype(np.float32), (1, 128 // half_size))) for f in (np.cos, np.sin)]


def rms_backward(value_matrix, inverse, gain, grad_normed):
    scaled = grad_normed * gain
    grad_gain = jnp.sum(grad_normed * value_matrix * inverse, axis=0)
    grad_values = inverse * scaled - value_matrix * inverse**3 * jnp.mean(
        scaled * value_matrix, axis=-1, keepdims=True
    )
    return (grad_values, grad_gain)


def assemble(mine, other):
    first = lax.axis_index("tensor") == 0
    return jnp.concatenate([jnp.where(first, mine, other), jnp.where(first, other, mine)], axis=0)


def combine_groups(slots, rows, capacity, span, between, later=None, own=None):
    owners = lax.axis_size("expert")
    orders = return_order(owners)
    if own is not None:
        orders = [[group - 1 for group in order if group] for order in orders]
    if len(orders) == 1:
        mine, other = return_rows(slots, after(rows, *between(())), orders[0], capacity, span)
        other = swap(other)
        sent = [
            (mine[i].astype(single) + other[i].astype(single)).astype(bfloat)
            for i in range(owners - 1)
        ]
        came = [to_peer(part, "expert", i) for i, part in enumerate(sent, 1)]
    else:
        mine, other = return_rows(slots, rows, orders[0], capacity, span)
        other = after(swap(other), *hold(other))
        came, sent = send_farthest(mine, other)
        done = between(sent)
        came[0] = after(came[0], *hold(sent[0]), *done)
        rows = after(rows, *done, *hold(sent[0]), *hold(sent[1]))
        mine, other = return_rows(slots, rows, orders[1], capacity, span)
        other = after(swap(other), *hold(other))
        came, sent = send_nearer(mine, other, came)
        done = later(sent) if later else ()
        if own is None:
            rows = after(rows, *sent, *hold(sent[0]), *hold(sent[1]))
            mine, other = return_rows(slots, rows, orders[2], capacity, span)
            other = swap(after(other, *done))
    if own is not None:
        return [(own[0], 0), (own[1], 0)] + came, sent
    at = len(orders[-1]) - 1
    return [(mine, at), (other, at)] + came, sent


def on_device(
    tokens,
    teacher,
    routes,
    valid,
    teacher_rows,
    norm_attn,
    norm_moe,
    w_query,
    key_projection_weight,
    value_projection_weight,
    w_out,
    w_router,
    w_gate,
    w_up,
    w_down,
):
    rows_dev, model_width = tokens.shape
    seq_count = rows_dev // SEQUENCE_LENGTH
    heads_local = w_query.shape[1] // HEAD_DIMENSION
    kv_local = key_projection_weight.shape[1] // HEAD_DIMENSION
    query_width = w_query.shape[1]
    key_width = key_projection_weight.shape[1]
    experts_local = w_gate.shape[0]
    owners = lax.axis_size("expert")
    count_dp = lax.axis_size("dp")
    groups = count_dp * owners
    all_experts = experts_local * owners
    top_count = routes.shape[1]
    capacity = rows_dev * top_count * 5 // (4 * all_experts)
    at_dp, at_ex, core = lax.axis_index("dp"), lax.axis_index("expert"), lax.axis_index("tensor")
    span = rows_dev // 2
    shards = count_dp // 2
    place = [at_ex * experts_local, at_dp // shards, core, at_dp % shards, at_ex]
    place = jnp.stack(place).astype(jnp.int32)

    def mine_of(value, axis=0):
        return lax.dynamic_slice_in_dim(value, core * span, span, axis)

    def other_of(value, axis=0):
        return lax.dynamic_slice_in_dim(value, (1 - core) * span, span, axis)

    tables = rope_tables(SEQUENCE_LENGTH, HEAD_DIMENSION)
    gain_attn, gain_moe = norm_attn, norm_moe

    def tokens_like(columns, kind):
        return jax.ShapeDtypeStruct((span, columns), kind)

    weights = (w_query, key_projection_weight, value_projection_weight, w_out)
    normed, queries, keys, values, mixed, log_sums, staying, leaving = attend(
        place, tokens, gain_attn, *weights, tables
    )
    came = after(swap(leaving), *hold(leaving))
    wide = model_width + 128
    hidden_first, token = token_rows(
        functools.partial(token_kernel, all_experts),
        "token",
        2,
        place,
        [staying, came, (routes.T, None)],
        [gain_moe, w_router.T],
        [tokens_like(model_width, single), tokens_like(wide, bfloat)],
    )

    some = experts_local // 2
    few = max(1, some - some // 2)
    pieces = ((0, some), (some, experts_local - some))

    def interleave(mine, other):
        return [part for pair in zip(mine, other) for part in pair]

    def far_forward(parts, start, amount, pin):
        return expert_forward(
            place, all_experts, top_count, pin, (w_gate, w_up), parts, owners, capacity, start, amount
        )

    mirror = to_mirror(token)
    own_other = swap(token)
    def forward(parts, groups, pin, chunk):
        return expert_forward(
            place, all_experts, top_count, pin, (w_gate, w_up, w_down), parts, groups, capacity, 0, experts_local, chunk
        )

    own = forward([token, own_other], 1, token, CHUNK_OWN)
    own_mine, own_leaving = return_rows(own[4], own[5], [0], capacity, span)
    (wanted,) = after_all([mine_of(teacher_rows, 1)], own[5])
    (valid_rows,) = after_all([mine_of(valid)[:, None] + jnp.zeros((span, 128), jnp.int32)], own[5])
    chooser = (wanted[0][:, None] == jnp.arange(rows_dev, dtype=jnp.int32)).astype(bfloat)
    target = jnp.dot(chooser, teacher, preferred_element_type=bfloat)
    near_parts = spread(token, own_other, (own[5],), (own_mine, target, valid_rows))
    mirror = after(mirror, *near_parts)
    peers = from_peers(mirror)
    mirror_other = swap(mirror)
    own_came = swap(after(own_leaving, mirror))
    others = forward(near_parts, owners - 1, mirror, CHUNK_OTHERS)
    gate_pre, up_pre, near_half, near_tails = zip(own[:4], others[:4])
    slots = jnp.concatenate([own[4], others[4]], axis=0)
    results = after(others[5], mirror_other, own_came)
    peers_other = []

    def swap_peers(sent):
        peers[:] = after_all(peers, *sent)
        peers_other.extend(swap(peer) for peer in peers)
        return sent

    addends, sent = combine_groups(
        others[4], results, capacity, span, swap_peers, own=(own_mine, own_came)
    )
    far_tokens = interleave([mirror] + peers, [mirror_other] + peers_other)
    far = [far_forward(far_tokens, *pieces[0], sent[0])]
    addends[-1] = after(addends[-1], far[0][0], *hold(sent[0]))
    layer_low, grad_layer, layer_grad, token_grad = token_rows(
        functools.partial(layer_kernel, len(addends)),
        "layer",
        2,
        place,
        [hidden_first, target, valid_rows] + addends,
        [],
        [tokens_like(model_width, bfloat), tokens_like(model_width, single), tokens_like(model_width, bfloat), tokens_like(wide, bfloat)],
    )

    leaving = after(layer_grad, *hold(token_grad))
    mirror = to_mirror(leaving)
    far.append(far_forward(far_tokens, *pieces[1], hold(leaving)[0]))
    own_other = swap(token_grad)
    digits = count_digits(jnp.broadcast_to(valid[None, :], (8, rows_dev)), far[1][0])
    near_parts = [token_grad, own_other] + spread(token_grad, own_other, (far[1][0],), (digits,))
    mirror = after(mirror, *near_parts)
    peers = from_peers(mirror)
    mirror_other = swap(mirror)
    hidden_low, grad_gate_pre, grad_up_pre, near_grad_half, results = expert_backward(
        place, all_experts, slots, (w_gate, w_up, w_down), gate_pre, up_pre, near_tails, near_parts, capacity, (mirror,)
    )
    results = after(results, mirror_other)
    weight_parts, far_grads = [], []

    def weights_of(start, amount, others=()):
        piece = 0 if start < some else 1
        far_gate, far_up, far_half, far_tails, far_slots = far[piece]
        values = expert_weights(
            place,
            all_experts,
            far_slots,
            w_down,
            (far_gate, far_up, far_tails, far_half),
            (hidden_low, grad_gate_pre, grad_up_pre, near_grad_half),
            near_half,
            far_grads,
            capacity,
            start,
            start - pieces[piece][0],
            amount,
            shards,
            tuple(others),
        )
        came = [to_peer(values[step], "dp", step) for step in range(1, shards)]
        weight_parts.append((start, values[0], came))
        return (*values, *[pin for value in values[1:] for pin in hold(value)])

    def swap_far(sent):
        peers[:] = after_all(peers, *sent)
        peers_other = [swap(peer) for peer in peers]
        far_grads.extend(interleave([mirror] + peers, [mirror_other] + peers_other))
        return peers_other

    results = after(results, *peers)
    addends, sent = combine_groups(slots, results, capacity, span, lambda sent: sent, swap_far)
    if owners != 4:
        swap_far(sent)
    done = weights_of(0, few, sent)
    addends[-1] = after(addends[-1], *done, *hold(sent[0]))
    grad_hidden, grad_attn, grad_logits, gain_sums = token_rows(
        functools.partial(norm_kernel, len(addends)),
        "norm",
        2,
        place,
        [hidden_first, grad_layer] + addends,
        [gain_moe, w_router.T, digits],
        [tokens_like(model_width, single), tokens_like(model_width, bfloat), tokens_like(128, bfloat)],
        [jax.ShapeDtypeStruct((8, model_width), single)],
    )
    grad_attn_other = after(swap(grad_attn), *hold(grad_attn))
    first_parts = pack_sums(
        place,
        [grad_attn, grad_attn_other, token],
        [mixed, mixed, grad_logits],
        gain_sums,
        all_experts,
        query_width + 128,
        count_dp,
        owners,
    )
    first_sum = start_sum(first_parts)
    done = weights_of(some, experts_local - some, first_parts[-1] if owners == 4 else first_parts)
    first_sum, sent = go_on(first_sum, *done)
    grad_attn, layer_low = after_all([grad_attn, layer_low], *sent, *weight_parts[0][2])
    layer_other = swap(layer_low)
    raw_query, raw_key, raw_value, staying, leaving, gain_sums = attend_back(
        place, grad_attn, grad_attn_other, tokens, *weights, tables, (queries, keys, values, log_sums)
    )
    second_parts = pack_sums(
        place,
        [normed] * 3,
        [raw_query, raw_key, raw_value],
        after(gain_sums, *first_sum[1:], layer_other),
        0,
        query_width + 2 * key_width + 128,
        count_dp,
        owners,
    )
    second_sum = start_sum(second_parts)
    last = second_parts[-1] if owners == 4 else second_parts
    leaving = swap(leaving)
    first_total = add_up(first_sum[0], after_all(first_sum[1:], *last, leaving))
    first_dense = over_dp_start(first_total)
    pins = [] if first_dense[1] is None else [first_dense[1], *hold(first_dense[1])]
    done = weights_of(few, some - few, (*last, *hold(last[0]), *pins))
    second_sum, sent = go_on(second_sum, *done)
    first_dense = over_dp_step(first_dense, *sent, *weight_parts[1][2])
    leaving = after(leaving, *sent)
    inputs_mine = mine_of(tokens).astype(single)
    inverse_mine = lax.rsqrt(jnp.mean(inputs_mine * inputs_mine, axis=-1, keepdims=True) + EPS)
    grad_first, _ = rms_backward(
        inputs_mine, inverse_mine, norm_attn, staying + leaving.astype(single)
    )
    grad_tokens_mine = grad_hidden + grad_first
    pins = [] if first_dense[1] is None else [first_dense[1], *hold(first_dense[1])]
    second_total = add_up(second_sum[0], after_all(second_sum[1:], grad_tokens_mine, *pins))
    own, arrived, sent = over_dp_at_once(second_total)
    first_dense = over_dp_end(first_dense, *sent)
    tail = first_dense[:, query_width:]
    tail = tail + after(swap(tail), *hold(tail))
    counted = tail[:1, all_experts + 1 : all_experts + 4] * jnp.asarray([[32.0, 4.0, 0.5]], single)
    scale = jnp.broadcast_to(rows_dev * groups / jnp.sum(counted, axis=1, keepdims=True), (8, 128))
    first_dense, tail = first_dense * scale[0, 0], tail * scale[0, 0]
    grad_tokens_mine = grad_tokens_mine * scale[0, 0]
    grad_tokens_other = after(swap(grad_tokens_mine), *hold(grad_tokens_mine))
    grad_tokens = assemble(grad_tokens_mine, grad_tokens_other)
    layer_low = after(layer_low, *sent)
    block_out = assemble(layer_low, layer_other)
    weight_grads, finished = None, ()
    for start, values, came in weight_parts:
        came = [after(part, *sent, grad_tokens_other) for part in came]
        weight_grads, finished = finish_weights(experts_local, start, scale, values, came, weight_grads)
    arrived[0] = after(arrived[0], *hold(sent[0]), finished, grad_tokens, tail)
    grad_query, grad_key, grad_value, second_tail = scaled_sum(
        scale, [own] + arrived, (query_width, key_width, key_width, 128)
    )
    second_tail = second_tail + swap(second_tail)
    return (
        block_out,
        grad_tokens,
        second_tail[:, 0],
        tail[:, all_experts],
        grad_query,
        grad_key,
        grad_value,
        first_dense[:, :query_width].T,
        tail[:, :all_experts],
        weight_grads[0],
        weight_grads[1],
        weight_grads[2],
    )


def solution(mesh):
    placed = (
        P(("dp", "expert"), None),
        P(("dp", "expert"), None),
        P(("dp", "expert"), None),
        P(("dp", "expert")),
        P(("dp", "expert"), None),
        P(),
        P(),
        P(None, "tensor"),
        P(None, "tensor"),
        P(None, "tensor"),
        P("tensor", None),
        P(),
        P("expert", None, "tensor"),
        P("expert", None, "tensor"),
        P("expert", "tensor", None),
    )
    return jax.shard_map(
        on_device,
        mesh=mesh,
        in_specs=placed,
        out_specs=(
            P(("dp", "expert"), None),
            P(("dp", "expert"), None),
            P(("dp", "expert")),
            P(("dp", "expert")),
            P(("dp", "expert"), "tensor"),
            P(("dp", "expert"), "tensor"),
            P(("dp", "expert"), "tensor"),
            P("tensor", ("dp", "expert")),
            P(("dp", "expert"), None),
            P("expert", "dp", "tensor"),
            P("expert", "dp", "tensor"),
            P("expert", "tensor", "dp"),
        ),
        check_vma=False,
    )
```

```python
import functools
import math

import jax
import jax.numpy as jnp
import numpy as np
from jax import lax
from jax.experimental import pallas as pl
from jax.experimental.pallas import tpu as pltpu
from jax.sharding import PartitionSpec as P

HEAD_DIMENSION = 64
SEQUENCE_LENGTH = 512
ABLK = 256


EPS = 1e-06
VMEM_LIMIT = 56 * 1024 * 1024
CHUNK_OWN = 2
CHUNK_OTHERS = 1
COST = 100
THETA = 10000.0
bfloat = jnp.bfloat16
single = jnp.float32


def pass_kernel(*refs):
    pass


def after_all(values, *others):
    anywhere = pl.BlockSpec(memory_space=pl.ANY)
    return pl.pallas_call(
        pass_kernel,
        name="after",
        in_specs=[anywhere] * (len(values) + len(others)),
        out_specs=[anywhere] * len(values),
        out_shape=[jax.ShapeDtypeStruct(value.shape, value.dtype) for value in values],
        input_output_aliases={i: i for i in range(len(values))},
        cost_estimate=pl.CostEstimate(flops=0, bytes_accessed=0, transcendentals=0),
    )(*values, *others)


def after(value, *others):
    return after_all([value], *others)[0] if others else value


def hold(value):
    anywhere = pl.BlockSpec(memory_space=pl.ANY)
    return [
        pl.pallas_call(
            pass_kernel,
            name="hold",
            in_specs=[anywhere],
            out_specs=anywhere,
            out_shape=jax.ShapeDtypeStruct((8, 128), single),
            cost_estimate=pl.CostEstimate(flops=10**12, bytes_accessed=10**9, transcendentals=0),
        )(value)
    ]


def swap(value):
    return lax.ppermute(value, "tensor", [(0, 1), (1, 0)])


def to_peer(value, axis, step):
    return lax.ppermute(value, axis, [(i, i ^ step) for i in range(lax.axis_size(axis))])


def to_mirror(value):
    count = lax.axis_size("dp")
    return lax.ppermute(value, "dp", [(i, count - 1 - i) for i in range(count)])


def from_peers(value):
    return [to_peer(value, "expert", s) for s in range(1, lax.axis_size("expert"))]


def halves_kernel(low_ref, high_ref, *refs):
    refs[-2][...] = low_ref[...]
    refs[-1][...] = high_ref[...]


def low_and_high(low, high, *others):
    rows, width = low.shape
    half = jax.ShapeDtypeStruct((rows // 2, width), low.dtype)
    return pl.pallas_call(
        halves_kernel,
        name="halves",
        grid=(1,),
        in_specs=[
            pl.BlockSpec((rows // 2, width), lambda i: (0, 0)),
            pl.BlockSpec((rows // 2, width), lambda i: (1, 0)),
        ]
        + [pl.BlockSpec(memory_space=pl.ANY)] * len(others),
        out_specs=[pl.BlockSpec((rows // 2, width), lambda i: (0, 0))] * 2,
        out_shape=[half, half],
        cost_estimate=pl.CostEstimate(flops=0, bytes_accessed=2**20, transcendentals=0),
    )(low, high, *others)


def spread(value, own_other, pause=(), more_pause=()):
    if lax.axis_size("expert") != 4:
        near = from_peers(value)
        near[0] = after(near[0], own_other, *hold(value), *pause, *more_pause)
        return [part for mine in near for part in (mine, swap(mine))]
    first, second = to_peer(value, "expert", 1), to_peer(value, "expert", 2)
    for_first, for_second = low_and_high(second, first, own_other, *hold(value), *pause)
    low, high = to_peer(for_first, "expert", 1), to_peer(for_second, "expert", 2)
    first_other, second_other = swap(first), swap(second)
    low = after(low, *hold(for_first), first_other, second_other, *more_pause)
    return [first, first_other, second, second_other, low, high, swap(low), swap(high)]


def farther_kernel(mine_ref, other_ref, low_ref, high_ref):
    cut = low_ref.shape[0]
    total = (mine_ref[0].astype(single) + other_ref[0].astype(single)).astype(bfloat)
    low_ref[...] = total[:cut]
    high_ref[...] = total[cut:]


def nearer_kernel(mine_first, other_first, mine_second, other_second, low_ref, high_ref, first_ref, second_ref):
    step = pl.program_id(0)
    low = jnp.where(step == 0, low_ref[...].astype(single), 0.0)
    high = jnp.where(step == 0, 0.0, high_ref[...].astype(single))
    first = mine_first[0].astype(single) + other_first[0].astype(single) + high
    second = mine_second[0].astype(single) + other_second[0].astype(single) + low
    first_ref[...] = first.astype(bfloat)
    second_ref[...] = second.astype(bfloat)


def send_farthest(mine, other):
    _, span, width = mine.shape
    half = jax.ShapeDtypeStruct((span // 2, width), bfloat)
    low, high = pl.pallas_call(
        farther_kernel,
        name="farther",
        out_shape=[half, half],
        cost_estimate=pl.CostEstimate(flops=0, bytes_accessed=2**21, transcendentals=0),
    )(mine, other)
    return [to_peer(low, "expert", 1), to_peer(high, "expert", 2)], (low, high)


def send_nearer(mine, other, came):
    _, span, width = mine.shape
    half = pl.BlockSpec((span // 2, width), lambda i: (i, 0))
    only = pl.BlockSpec((span // 2, width), lambda i: (0, 0))
    stacked = lambda index: pl.BlockSpec((1, span // 2, width), lambda i: (index, i, 0))
    whole = jax.ShapeDtypeStruct((span, width), bfloat)
    first, second = pl.pallas_call(
        nearer_kernel,
        name="nearer",
        grid=(2,),
        in_specs=[stacked(0), stacked(0), stacked(1), stacked(1), only, only],
        out_specs=[half, half],
        out_shape=[whole, whole],
        cost_estimate=pl.CostEstimate(flops=0, bytes_accessed=2**22, transcendentals=0),
    )(mine, other, mine, other, *came)
    return [to_peer(first, "expert", 1), to_peer(second, "expert", 2)], (first, second)


def start_sum(parts):
    if len(parts) != 4:
        return parts, None
    low, high = parts[3]
    return parts, [to_peer(low, "expert", 1), to_peer(high, "expert", 2)]


def dense_kernel(first_in, second_in, low_ref, high_ref, *refs):
    first_ref, second_ref = refs[-2:]
    step = pl.program_id(0)
    low = jnp.where(step == 0, low_ref[...].astype(single), 0.0)
    high = jnp.where(step == 0, 0.0, high_ref[...].astype(single))
    first_ref[...] = (first_in[...].astype(single) + high).astype(bfloat)
    second_ref[...] = (second_in[...].astype(single) + low).astype(bfloat)


def go_on(state, *others):
    parts, came = state
    if came is None:
        sent = [after(part, *others) for part in parts[1:]]
        return [parts[0]] + [to_peer(part, "expert", i) for i, part in enumerate(sent, 1)], sent
    low = after(came[0], *hold(parts[3][0]))
    shape = parts[1].shape
    half = pl.BlockSpec((shape[0] // 2,) + shape[1:], lambda i: (i, 0, 0))
    only = pl.BlockSpec((shape[0] // 2,) + shape[1:], lambda i: (0, 0, 0))
    whole = jax.ShapeDtypeStruct(shape, bfloat)
    first, second = pl.pallas_call(
        dense_kernel,
        name="dense_nearer",
        grid=(2,),
        in_specs=[half, half, only, only] + [pl.BlockSpec(memory_space=pl.ANY)] * len(others),
        out_specs=[half, half],
        out_shape=[whole, whole],
        cost_estimate=pl.CostEstimate(flops=0, bytes_accessed=2**22, transcendentals=0),
    )(parts[1], parts[2], low, came[1], *others)
    came = to_peer(first, "expert", 1), to_peer(second, "expert", 2)
    return [parts[0], after(came[0], *hold(first)), came[1]], [first, second]


def add_up(own, arrived):
    total = own.astype(single)
    for part in arrived:
        total = total + part.astype(single)
    return total


def sum_all(value, axes):
    for axis in axes:
        step = 1
        while step < lax.axis_size(axis):
            value = value + to_peer(value, axis, step)
            step *= 2
    return value


def over_dp_start(total):
    at_dp, count = lax.axis_index("dp"), lax.axis_size("dp")
    parts = {r: lax.dynamic_index_in_dim(total, at_dp ^ r, 0, keepdims=False) for r in range(count)}
    return over_dp_send(parts, 1)


def over_dp_send(parts, step):
    if step >= lax.axis_size("dp"):
        return parts, None, step
    return parts, jnp.concatenate([parts[r].astype(bfloat) for r in parts if r & step], axis=0), step


def over_dp_step(state, *others):
    parts, sent, step = state
    parts = dict(parts)
    leaving = [r for r in parts if r & step]
    came = after(to_peer(sent, "dp", step), *hold(sent), *others).astype(single)
    rows = came.shape[0] // len(leaving)
    for i, r in enumerate(leaving):
        parts[r ^ step] = parts[r ^ step] + came[i * rows : (i + 1) * rows]
        del parts[r]
    return over_dp_send(parts, 2 * step)


def over_dp_end(state, *others):
    while state[1] is not None:
        state, others = over_dp_step(state, *others), ()
    return state[0][0]


def over_dp_at_once(total):
    at_dp = lax.axis_index("dp")
    sent = [
        lax.dynamic_index_in_dim(total, at_dp ^ step, 0, keepdims=False).astype(bfloat)
        for step in range(1, lax.axis_size("dp"))
    ]
    return [to_peer(part, "dp", step) for step, part in enumerate(sent, 1)], sent


def scaled_sum_kernel(amount, widths, place_ref, scale_ref, total_ref, *refs):
    parts, outs = refs[:amount], refs[amount:]
    total = total_ref[0]
    for part in parts:
        total = total + part[...].astype(single)
    total = total * scale_ref[:1, :1]
    at = 0
    for out, width in zip(outs, widths):
        out[...] = total[:, at : at + width]
        at += width


def scaled_sum(place, scale, total, parts, widths):
    _, rows, columns = total.shape
    whole = lambda *shape: pl.BlockSpec(shape, lambda i, place: (0,) * len(shape))
    return kernel_call(
        functools.partial(scaled_sum_kernel, len(parts), widths),
        "scaled_sum",
        (1,),
        [whole(8, 128), pl.BlockSpec((1, rows, columns), lambda i, place: (place[5], 0, 0))]
        + [whole(rows, columns)] * len(parts),
        [whole(rows, width) for width in widths],
        [jax.ShapeDtypeStruct((rows, width), single) for width in widths],
        [],
        1,
        2**21,
        (place, scale, total) + tuple(parts),
        prefetch=1,
    )


def dot(left, right):
    return lax.dot_general(left, right, (((1,), (0,)), ((), ())), preferred_element_type=single)


def dot_nt(left, right):
    return lax.dot_general(left, right, (((1,), (1,)), ((), ())), preferred_element_type=single)


def dot_tn(left, right):
    return lax.dot_general(left, right, (((0,), (0,)), ((), ())), preferred_element_type=single)


def picks(slot, capacity):
    return slot == lax.broadcasted_iota(jnp.int32, (capacity, slot.shape[1]), 0)


def group_parts(parts, joined_ref):
    if joined_ref is None:
        return [(parts[i], parts[i + 1]) for i in range(0, len(parts), 2)]
    cut = parts[-1].shape[0]

    @pl.when(pl.program_id(0) == 0)
    def _():
        for i in range(2):
            for j in range(2):
                joined_ref[i, j * cut : (j + 1) * cut, :] = parts[-4 + 2 * i + j][...]

    pairs = [(parts[i], parts[i + 1]) for i in range(0, len(parts) - 4, 2)]
    return pairs + [(joined_ref.at[0], joined_ref.at[1])]


def find_slots(first_ref, top_count, pairs, slots_ref):
    groups, experts, tokens = slots_ref.shape
    row = lax.broadcasted_iota(jnp.int32, (tokens, tokens), 0)
    earlier = (row < lax.broadcasted_iota(jnp.int32, (tokens, tokens), 1)).astype(bfloat)
    ids = lax.broadcasted_iota(jnp.int32, (experts, tokens), 0)
    ids = (ids + first_ref[0]).astype(single)
    for group, pair in enumerate(pairs):
        tails = [part[:, part.shape[1] - 128 :].astype(single).T for part in pair]
        routes = jnp.concatenate(tails, axis=1)[128 - top_count :]
        mask = ids == routes[:1]
        for k in range(1, top_count):
            mask = mask | (ids == routes[k : k + 1])
        before = dot(mask.astype(single).astype(bfloat), earlier)
        slots_ref[group] = jnp.where(mask, before, -1.0).astype(jnp.int32)


def gather_rows(slots_ref, expert, pairs, rows_ref):
    capacity = rows_ref.shape[0] // len(pairs)
    width = rows_ref.shape[1]
    for group, (mine, other) in enumerate(pairs):
        span = mine.shape[0]
        slot = slots_ref[group, pl.ds(expert, 1), :]
        picked = picks(slot, capacity).astype(bfloat)
        rows = dot(picked[:, :span], mine[:, :width]) + dot(picked[:, span:], other[:, :width])
        rows_ref[group * capacity : (group + 1) * capacity, :] = rows.astype(bfloat)


def slot_gates(expert, tails, count):
    lane = lax.broadcasted_iota(jnp.int32, tails.shape, 1)
    chosen = (lane == expert) | (lane == expert + count) | (lane == expert + 2 * count)
    return jnp.sum(jnp.where(chosen, tails.astype(single), 0.0), axis=1, keepdims=True)


def half_columns(place_ref, width):
    return pl.ds(pl.multiple_of(place_ref[1] * width, 128), width)


def return_order(groups):
    rest = list(range(1, groups)) + [0]
    return [[3], [1, 2], [0]] if groups == 4 else [rest]


def forward_kernel(count, top_count, amount, halved, start, chunk, with_out, place_ref, gate_w, up_w, *refs):
    if with_out:
        down_w, refs = refs[0], refs[1:]
    parts, refs = refs[:amount], refs[amount:]
    parts, pins = parts[:-1], parts[-1:]
    gate_ref, up_ref, half_ref, tail_ref, slots_ref = refs[:5]
    refs = refs[5:]
    step = pl.program_id(0)
    joined_ref = refs[-1] if halved else None
    rows_ref = refs[-2] if halved else refs[-1]
    width = gate_w.shape[1]
    pairs = group_parts(parts, joined_ref)

    @pl.when(step == 0)
    def _():
        find_slots(place_ref, top_count, pairs, slots_ref)

    for i in range(chunk):
        expert = start + step * chunk + i
        gather_rows(slots_ref, expert, pairs, rows_ref)
        half_ref[i] = rows_ref[:, half_columns(place_ref, half_ref.shape[2])]
        tails = rows_ref[:, width:]
        tail_ref[i] = tails
        rows = rows_ref[:, :width]
        gate_pre = dot(rows, gate_w[i])
        up_pre = dot(rows, up_w[i])
        gate_ref[i] = gate_pre.astype(bfloat)
        up_ref[i] = up_pre.astype(bfloat)
        if with_out:
            gates = slot_gates(place_ref[0] + expert, tails, count)
            hidden = (gate_pre * jax.nn.sigmoid(gate_pre) * up_pre * gates).astype(bfloat)
            refs[0][i] = dot(hidden, down_w[i]).astype(bfloat)


def hidden_grads(gate_pre, up_pre, gates, grad_hidden):
    sig = jax.nn.sigmoid(gate_pre)
    silu = gate_pre * sig
    hidden = silu * up_pre
    scaled = grad_hidden * gates
    grad_gate_pre = (scaled * up_pre * sig * (1.0 + gate_pre * (1.0 - sig))).astype(bfloat)
    grad_up_pre = (scaled * silu).astype(bfloat)
    return hidden, (hidden * gates).astype(bfloat), grad_gate_pre, grad_up_pre


def joined(refs):
    return refs[0][0] if len(refs) == 1 else jnp.concatenate([ref[0] for ref in refs], axis=0)


def backward_kernel(count, amount, halved, pins, pieces, place_ref, slots_ref, gate_w, up_w, down_w, *refs):
    gate_refs, up_refs, tail_refs = (refs[i * pieces : (i + 1) * pieces] for i in range(3))
    refs = refs[3 * pieces :]
    parts, refs = refs[:amount], refs[amount + pins :]
    hidden_ref, grad_gate_ref, grad_up_ref, half_ref, refs = refs[0], refs[1], refs[2], refs[3], refs[4:]
    back_ref, rows_ref = refs[:2]
    joined_ref = refs[2] if halved else None
    width = gate_w.shape[1]
    step = pl.program_id(0)
    expert = place_ref[0] + step
    gather_rows(slots_ref, step, group_parts(parts, joined_ref), rows_ref)
    half_ref[0] = rows_ref[:, half_columns(place_ref, half_ref.shape[2])]
    gates = slot_gates(expert, joined(tail_refs), count)
    grad_hidden = dot_nt(rows_ref[:, :width], down_w[0])
    hidden, hidden_low, grad_gate_pre, grad_up_pre = hidden_grads(
        joined(gate_refs).astype(single), joined(up_refs).astype(single), gates, grad_hidden
    )
    hidden_ref[0] = hidden_low
    grad_gate_ref[0] = grad_gate_pre
    grad_up_ref[0] = grad_up_pre
    back = dot_nt(grad_gate_pre, gate_w[0]) + dot_nt(grad_up_pre, up_w[0])
    back_ref[0, :, :width] = back.astype(bfloat)
    tails = rows_ref[:, width:].astype(single)
    lane = lax.broadcasted_iota(jnp.int32, tails.shape, 1)
    inner = jnp.sum(jnp.where(lane < 3, tails, 0.0), axis=1, keepdims=True)
    inner = inner * (place_ref[2] == 0).astype(single)
    grad_logit = gates * (jnp.sum(hidden * grad_hidden, axis=1, keepdims=True) - inner)
    back_ref[0, :, width:] = jnp.where(lane == expert, grad_logit, 0.0).astype(bfloat)


def weights_kernel(count, groups, start, pins, pieces, place_ref, slots_ref, down_w, gate_ref, up_ref, tail_ref, *refs):
    hidden_near, gate_near, up_near, near_g, far_x = refs[:5]
    near_x, refs = refs[5 : 5 + pieces], refs[5 + pieces :]
    parts, refs = refs[: 2 * groups], refs[2 * groups + pins :]
    shards, (rows_ref, full_ref) = refs[:-2], refs[-2:]
    expert = start + pl.program_id(0)
    gather_rows(slots_ref, expert, group_parts(parts, None), rows_ref)
    gates = slot_gates(place_ref[0] + expert, tail_ref[0], count)
    grad_hidden = dot_nt(rows_ref[...], down_w[0])
    _, hidden, grad_gate_pre, grad_up_pre = hidden_grads(
        gate_ref[0].astype(single), up_ref[0].astype(single), gates, grad_hidden
    )
    far_g = rows_ref[:, half_columns(place_ref, full_ref.shape[1])]
    far, near = far_x[0], joined(near_x)
    sums = (
        dot_tn(far, grad_gate_pre) + dot_tn(near, gate_near[0]),
        dot_tn(far, grad_up_pre) + dot_tn(near, up_near[0]),
        dot_tn(far_g, hidden) + dot_tn(near_g[0], hidden_near[0]),
    )
    for i, value in enumerate(sums):
        full_ref[i] = value.astype(bfloat)
    size = shards[0].shape[2]
    for step, shard in enumerate(shards):
        at = pl.multiple_of((place_ref[3] ^ step) * size, size)
        for i in range(3):
            shard[0, i] = full_ref[i, pl.ds(at, size), :]


def finish_kernel(scale_ref, own_ref, *refs):
    arrived, (d_gate, d_up, d_down, done_ref) = refs[:-4], refs[-4:]
    scale = scale_ref[:1, :1]
    for e in range(own_ref.shape[0]):

        def total(i):
            value = own_ref[e, i].astype(single)
            for ref in arrived:
                value = value + ref[e, i].astype(single)
            return value * scale

        d_gate[e] = total(0)
        d_up[e] = total(1)
        d_down[e] = total(2).T
    done_ref[...] = scale_ref[...]


def finish_more_kernel(gate_in, up_in, down_in, scale_ref, *refs):
    finish_kernel(scale_ref, *refs)


def return_kernel(first, cycle, slots_ref, rows_ref, mine, other, picked_ref):
    experts, capacity, width = rows_ref.shape
    span = mine.shape[1]
    group = (pl.program_id(0) + first) % cycle

    @pl.when(pl.program_id(1) == 0)
    def _():
        for e in range(experts):
            slot = slots_ref[group, e : e + 1, :]
            picked_ref[e * capacity : (e + 1) * capacity, :] = picks(slot, capacity).astype(bfloat)

    back = dot_tn(picked_ref[...], rows_ref[...].reshape(experts * capacity, width)).astype(bfloat)
    mine[0] = back[:span]
    other[0] = back[span:]


def kernel_call(kernel, name, grid, in_specs, out_specs, out_shape, scratch, flops, moved, args, prefetch=0, aliases=None):
    return pl.pallas_call(
        kernel,
        name=name,
        grid_spec=pltpu.PrefetchScalarGridSpec(
            num_scalar_prefetch=prefetch,
            grid=grid,
            in_specs=in_specs,
            out_specs=out_specs,
            scratch_shapes=scratch,
        ),
        out_shape=out_shape,
        input_output_aliases=aliases or {},
        compiler_params=pltpu.CompilerParams(
            dimension_semantics=("arbitrary",) * len(grid), vmem_limit_bytes=VMEM_LIMIT
        ),
        cost_estimate=pl.CostEstimate(flops=COST * flops, bytes_accessed=moved, transcendentals=0),
    )(*args)


def per_expert(*shape, start=0):
    return pl.BlockSpec((1,) + shape, lambda e, *_: (e + start,) + (0,) * len(shape))


def anywhere(pins):
    return [pl.BlockSpec(memory_space=pl.ANY) for _ in pins]


def once(*shape):
    return pl.BlockSpec(
        shape, lambda e, *_: (0,) * len(shape), pipeline_mode=pl.Buffered(buffer_count=1)
    )


def return_rows(slots, rows, order, capacity, span):
    groups, _, tokens = slots.shape
    experts, _, width = rows.shape
    amount, first = len(order), order[0]
    cycle = groups
    cuts = 2 if width % 256 == 0 and amount == 1 else 1
    cut = width // cuts
    part = pl.BlockSpec((1, span, cut), lambda g, n: (g, 0, n))
    return kernel_call(
        functools.partial(return_kernel, first, cycle),
        "return_rows",
        (amount, cuts),
        [
            pl.BlockSpec(slots.shape, lambda g, n: (0, 0, 0)),
            pl.BlockSpec((experts, capacity, cut), lambda g, n: (0, (g + first) % cycle, n)),
        ],
        [part, part],
        [jax.ShapeDtypeStruct((amount, span, width), bfloat)] * 2,
        [pltpu.VMEM((experts * capacity, tokens), bfloat)],
        2 * amount * experts * capacity * tokens * width,
        2 * amount * (experts * capacity + tokens) * width,
        (slots, rows),
    )


def expert_forward(place, count, top_count, pin, weights, parts, groups, capacity, start, experts, chunk=1):
    if experts % chunk or start % chunk:
        chunk = 1

    def per_expert(*shape, start=0):
        return pl.BlockSpec((chunk,) + shape, lambda e, *_: (e + start // chunk,) + (0,) * len(shape))

    span, whole = parts[0].shape
    tokens = 2 * span
    width, hidden = weights[0].shape[1:]
    with_out = len(weights) == 3
    total = groups * capacity
    halved = len(parts) > 2 * groups
    specs = [per_expert(width, hidden, start=start)] * 2
    outs = [per_expert(total, hidden)] * 2
    outs += [per_expert(total, width // 2), per_expert(total, whole - width)]
    shapes = [jax.ShapeDtypeStruct((experts, total, hidden), bfloat)] * 2
    shapes += [jax.ShapeDtypeStruct((experts, total, width // 2), bfloat)]
    shapes += [jax.ShapeDtypeStruct((experts, total, whole - width), bfloat)]
    listed = (groups, -(-weights[0].shape[0] // 8) * 8, tokens)
    outs += [pl.BlockSpec(listed, lambda e, *_: (0, 0, 0))]
    shapes += [jax.ShapeDtypeStruct(listed, jnp.int32)]
    scratch = [pltpu.VMEM((total, whole), bfloat)]
    if halved:
        scratch += [pltpu.VMEM((2, span, whole), bfloat)]
    if with_out:
        specs += [per_expert(hidden, width, start=start)]
        outs += [per_expert(total, width)]
        shapes += [jax.ShapeDtypeStruct((experts, total, width), bfloat)]
    specs += [once(*part.shape) for part in parts] + [pl.BlockSpec(memory_space=pl.ANY)]
    return kernel_call(
        functools.partial(forward_kernel, count, top_count, len(parts) + 1, halved, start, chunk, with_out),
        "expert_forward" if with_out else "expert_forward_far",
        (experts // chunk,), specs, outs, shapes, scratch,
        2 * experts * total * (width * hidden * len(weights) + tokens * whole),
        2 * experts * (len(weights) * width * hidden + total * width + 4 * total * hidden),
        (place,) + tuple(weights) + tuple(parts) + (pin,),
        prefetch=1,
    )


def expert_backward(place, count, slots, weights, gate_pre, up_pre, tails, parts, capacity, pins):
    groups, _, tokens = slots.shape
    experts = weights[0].shape[0]
    span, whole = parts[0].shape
    width, hidden = weights[0].shape[1:]
    total = groups * capacity
    thin = per_expert(total, hidden)
    specs = [once(*slots.shape)] + [per_expert(width, hidden)] * 2
    specs += [per_expert(hidden, width)]
    specs += [per_expert(*piece.shape[1:]) for piece in (*gate_pre, *up_pre, *tails)]
    outs = [thin] * 3 + [per_expert(total, width // 2), per_expert(total, whole)]
    shapes = [jax.ShapeDtypeStruct((experts, total, hidden), bfloat)] * 3
    shapes += [jax.ShapeDtypeStruct((experts, total, width // 2), bfloat)]
    shapes += [jax.ShapeDtypeStruct((experts, total, whole), bfloat)]
    return kernel_call(
        functools.partial(backward_kernel, count, len(parts), len(parts) > 2 * groups, len(pins), len(tails)),
        "expert_backward",
        (experts,), specs + [once(*part.shape) for part in parts] + anywhere(pins), outs, shapes,
        [pltpu.VMEM((total, whole), bfloat)]
        + ([pltpu.VMEM((2, span, whole), bfloat)] if len(parts) > 2 * groups else []),
        2 * experts * total * width * (hidden * 3 + tokens),
        2 * experts * (3 * width * hidden + 3 * total * width // 2 + 7 * total * hidden),
        (place, slots) + tuple(weights) + tuple(gate_pre) + tuple(up_pre) + tuple(tails) + tuple(parts) + tuple(pins),
        prefetch=1,
    )


def expert_weights(place, count, slots, down_w, far, near, near_x, parts, capacity, start, far_start, experts, shards, pins):
    groups, _, tokens = slots.shape
    hidden, width = down_w.shape[1:]
    total = groups * capacity
    far_pre, (far_tails, far_half) = far[:2], far[2:]
    thin = per_expert(total, hidden, start=far_start)
    wide = per_expert(total, width // 2, start=far_start)
    thin_at = per_expert(total, hidden, start=start)
    wide_at = per_expert(total, width // 2, start=start)
    specs = [once(*slots.shape), per_expert(hidden, width, start=start)]
    specs += [thin, thin, per_expert(total, far_tails.shape[2], start=far_start)] + [thin_at] * 3
    specs += [wide_at, wide]
    specs += [per_expert(*piece.shape[1:], start=start) for piece in near_x]
    size = width // (2 * shards)
    return kernel_call(
        functools.partial(weights_kernel, count, groups, start, len(pins), len(near_x)),
        "expert_weights",
        (experts,), specs + [once(*part.shape) for part in parts] + anywhere(pins),
        [per_expert(3, size, hidden)] * shards,
        [jax.ShapeDtypeStruct((experts, 3, size, hidden), bfloat)] * shards,
        [pltpu.VMEM((total, width), bfloat), pltpu.VMEM((3, width // 2, hidden), bfloat)],
        2 * experts * total * width * (hidden * 4 + tokens),
        2 * experts * (5 * width * hidden // 2 + 3 * total * width // 2 + 7 * total * hidden),
        (place, slots, down_w) + tuple(far_pre) + (far_tails,) + tuple(near) + (far_half,) + tuple(near_x) + tuple(parts) + tuple(pins),
        prefetch=1,
    )


def finish_weights(experts, start, scale, own, arrived, before):
    some, _, size, hidden = own.shape
    chunk = math.gcd(some, start) if start else some

    def block(*shape, at=0):
        return pl.BlockSpec((chunk,) + shape, lambda e, *_: (e + at // chunk,) + (0,) * len(shape))

    ready = [block(3, size, hidden)] * (1 + len(arrived))
    kernel = finish_kernel if before is None else finish_more_kernel
    kept = [] if before is None else [pl.BlockSpec(memory_space=pl.ANY)] * 3
    small = pl.BlockSpec((8, 128), lambda e, *_: (0, 0))
    *grads, done = kernel_call(
        kernel,
        "finish_weights",
        (some // chunk,),
        kept + [small] + ready,
        [block(size, hidden, at=start)] * 2 + [block(hidden, size, at=start), small],
        [jax.ShapeDtypeStruct((experts, size, hidden), single)] * 2
        + [jax.ShapeDtypeStruct((experts, hidden, size), single), jax.ShapeDtypeStruct((8, 128), single)],
        [],
        3 * some * size * hidden,
        12 * some * size * hidden,
        tuple(before or ()) + (scale, own) + tuple(arrived),
        aliases={} if before is None else {0: 0, 1: 1, 2: 2},
    )
    return grads, done


def rotate(value, cosines, sines, back):
    pieces = []
    for at in range(0, value.shape[1], 128):
        piece = value[:, at : at + 128]
        lane = lax.broadcasted_iota(jnp.int32, piece.shape, 1)
        later, sooner = pltpu.roll(piece, 96, 1), pltpu.roll(piece, 32, 1)
        if back:
            turned = jnp.where(lane % 64 < 32, later, -sooner)
        else:
            turned = jnp.where(lane % 64 < 32, -later, sooner)
        pieces.append(piece * cosines + turned * sines)
    return pieces[0] if len(pieces) == 1 else jnp.concatenate(pieces, axis=1)


def query_blocks(length):
    return [(at, at + ABLK) for at in range(0, length, ABLK)]


def attend_kernel(place_ref, tokens_ref, gain_ref, query_w, key_w, value_w, out_w, cos_ref, sin_ref,
                  normed_ref, queries_ref, keys_ref, values_ref, mixed_ref, lse_ref, stay_ref, leave_ref, total_ref):
    step = pl.program_id(0)
    length = tokens_ref.shape[0]
    group = query_w.shape[1] // key_w.shape[1]

    @pl.when(step == 0)
    def _():
        inputs = tokens_ref[...].astype(single)
        inverse = lax.rsqrt(jnp.mean(inputs * inputs, axis=1, keepdims=True) + EPS)
        normed_ref[...] = (inputs * inverse * gain_ref[...]).astype(bfloat)

    normed = normed_ref[...]
    cosines, sines = cos_ref[...], sin_ref[...]
    queries = rotate(dot(normed, query_w[...]), cosines, sines, False) * HEAD_DIMENSION ** (-0.5)
    keys = rotate(dot(normed, key_w[...]), cosines, sines, False)
    values = dot(normed, value_w[...])
    size = HEAD_DIMENSION
    mixed = []
    for kv in range(key_w.shape[1] // size):
        key = keys[:, kv * size : (kv + 1) * size].astype(bfloat)
        value = values[:, kv * size : (kv + 1) * size].astype(bfloat)
        keys_ref[kv] = key
        values_ref[kv] = value
        for head in range(kv * group, (kv + 1) * group):
            query = queries[:, head * size : (head + 1) * size].astype(bfloat)
            queries_ref[head] = query
            outs, sums = [], []
            for start, seen in query_blocks(length):
                scores = dot_nt(key[:seen], query[start : start + ABLK])
                peak = jnp.max(scores, axis=0, keepdims=True)
                weights = jnp.exp(scores - peak)
                total = jnp.sum(weights, axis=0, keepdims=True)
                probs = (weights / total).astype(bfloat)
                outs.append(dot_tn(value[:seen], probs))
                sums.append(peak + jnp.log(total))
            mixed.append(jnp.concatenate(outs, axis=1))
            lse_ref[0, head : head + 1, :] = jnp.concatenate(sums, axis=1)
    mixed = jnp.concatenate(mixed, axis=0).T.astype(bfloat)
    mixed_ref[...] = mixed
    part = dot(mixed, out_w[...])

    @pl.when(step == 0)
    def _():
        total_ref[...] = part

    @pl.when(step > 0)
    def _():
        total_ref[...] += part

    @pl.when(step == pl.num_programs(0) - 1)
    def _():
        span = stay_ref.shape[0]
        core = place_ref[2]
        mine = pl.ds(pl.multiple_of(core * span, span), span)
        other = pl.ds(pl.multiple_of((1 - core) * span, span), span)
        stay_ref[...] = total_ref[mine, :] + tokens_ref[mine, :].astype(single)
        leave_ref[...] = total_ref[other, :]


def attend_back_kernel(place_ref, mine_ref, other_ref, tokens_ref, query_w, key_w, value_w, out_w, cos_ref, sin_ref,
                       queries_ref, keys_ref, values_ref, lse_ref,
                       raw_query_ref, raw_key_ref, raw_value_ref, stay_ref, leave_ref, gain_ref, low_ref, total_ref):
    step = pl.program_id(0)
    length = tokens_ref.shape[0]
    span = mine_ref.shape[0]
    core = place_ref[2]
    mine = pl.ds(pl.multiple_of(core * span, span), span)
    other = pl.ds(pl.multiple_of((1 - core) * span, span), span)
    low_ref[mine, :] = dot_nt(mine_ref[...], out_w[...]).astype(bfloat)
    low_ref[other, :] = dot_nt(other_ref[...], out_w[...]).astype(bfloat)
    grads = low_ref[...].astype(single)
    size = HEAD_DIMENSION
    group = query_w.shape[1] // key_w.shape[1]
    grad_queries, grad_keys, grad_values = [], [], []
    for kv in range(key_w.shape[1] // size):
        key, value = keys_ref[kv], values_ref[kv]
        key_parts = [[] for _ in query_blocks(length)]
        value_parts = [[] for _ in query_blocks(length)]
        for head in range(kv * group, (kv + 1) * group):
            query = queries_ref[head]
            grad = grads[:, head * size : (head + 1) * size].astype(bfloat)
            outs = []
            for block, (start, seen) in enumerate(query_blocks(length)):
                rows = slice(start, start + ABLK)
                scores = dot_nt(key[:seen], query[rows])
                probs = jnp.exp(scores - lse_ref[0, head : head + 1, rows])
                grad_probs = dot_nt(value[:seen], grad[rows])
                inner = jnp.sum(probs * grad_probs, axis=0, keepdims=True)
                grad_scores = (probs * (grad_probs - inner)).astype(bfloat)
                outs.append(dot_tn(grad_scores, key[:seen]))
                key_parts[block].append(dot(grad_scores, query[rows]))
                value_parts[block].append(dot(probs.astype(bfloat), grad[rows]))
            grad_queries.append(jnp.concatenate(outs, axis=0))

        def whole(parts):
            rows = []
            for at in range(len(parts)):
                here = slice(at * ABLK, (at + 1) * ABLK)
                rows.append(sum(one[here] for block in parts[at:] for one in block))
            return jnp.concatenate(rows, axis=0)

        grad_keys.append(whole(key_parts))
        grad_values.append(whole(value_parts))
    cosines, sines = cos_ref[...], sin_ref[...]
    grad_query = jnp.concatenate(grad_queries, axis=1) * HEAD_DIMENSION ** (-0.5)
    raw_query = rotate(grad_query, cosines, sines, True).astype(bfloat)
    raw_key = rotate(jnp.concatenate(grad_keys, axis=1), cosines, sines, True).astype(bfloat)
    raw_value = jnp.concatenate(grad_values, axis=1).astype(bfloat)
    raw_query_ref[...] = raw_query
    raw_key_ref[...] = raw_key
    raw_value_ref[...] = raw_value
    part = dot_nt(raw_query, query_w[...]) + dot_nt(raw_key, key_w[...]) + dot_nt(raw_value, value_w[...])

    @pl.when(step == 0)
    def _():
        total_ref[...] = part

    @pl.when(step > 0)
    def _():
        total_ref[...] += part

    @pl.when(step == pl.num_programs(0) - 1)
    def _():
        stay_ref[...] = total_ref[mine, :]
        leave_ref[...] = total_ref[other, :].astype(bfloat)
        inputs = tokens_ref[...].astype(single)
        inverse = lax.rsqrt(jnp.mean(inputs * inputs, axis=1, keepdims=True) + EPS)
        gain = jnp.sum(total_ref[...] * inputs * inverse, axis=0, keepdims=True)
        first = lax.broadcasted_iota(jnp.int32, gain_ref.shape, 0) == 0
        gain_ref[...] = jnp.where(first, gain, 0.0)


def attend(place, tokens, gain, query_w, key_w, value_w, out_w, tables):
    length, width = tokens.shape
    span, size = length // 2, HEAD_DIMENSION
    steps = key_w.shape[1] // 128
    wide, thin = query_w.shape[1] // steps, 128
    heads, kv_heads = query_w.shape[1] // size, key_w.shape[1] // size
    whole = lambda *shape: pl.BlockSpec(shape, lambda i, *_: (0,) * len(shape))
    across = lambda rows, columns: pl.BlockSpec((rows, columns), lambda i, *_: (0, i))
    split = lambda *shape: pl.BlockSpec(shape, lambda i, *_: (i,) + (0,) * (len(shape) - 1))
    low = lambda *shape: jax.ShapeDtypeStruct(shape, bfloat)
    high = lambda *shape: jax.ShapeDtypeStruct(shape, single)
    return kernel_call(
        attend_kernel,
        "attend",
        (steps,),
        [whole(length, width), pl.BlockSpec((width,), lambda i, *_: (0,)), across(width, wide), across(width, thin), across(width, thin),
         split(wide, width), whole(length, 128), whole(length, 128)],
        [whole(length, width), split(heads // steps, length, size), split(kv_heads // steps, length, size),
         split(kv_heads // steps, length, size), across(length, wide), split(1, 8, length),
         whole(span, width), whole(span, width)],
        [low(length, width), low(heads, length, size), low(kv_heads, length, size), low(kv_heads, length, size),
         low(length, heads * size), high(steps, 8, length), high(span, width), high(span, width)],
        [pltpu.VMEM((length, width), single)],
        2 * length * width * (2 * heads + 2 * kv_heads) * size,
        2 * (length * width * 6 + 2 * width * (heads + kv_heads) * size),
        (place, tokens, gain, query_w, key_w, value_w, out_w) + tuple(tables),
        prefetch=1,
    )


def attend_back(place, mine, other, tokens, query_w, key_w, value_w, out_w, tables, saved):
    length, width = tokens.shape
    span, size = length // 2, HEAD_DIMENSION
    steps = key_w.shape[1] // 128
    wide, thin = query_w.shape[1] // steps, 128
    heads, kv_heads = query_w.shape[1] // size, key_w.shape[1] // size
    whole = lambda *shape: pl.BlockSpec(shape, lambda i, *_: (0,) * len(shape))
    across = lambda rows, columns: pl.BlockSpec((rows, columns), lambda i, *_: (0, i))
    split = lambda *shape: pl.BlockSpec(shape, lambda i, *_: (i,) + (0,) * (len(shape) - 1))
    low = lambda *shape: jax.ShapeDtypeStruct(shape, bfloat)
    high = lambda *shape: jax.ShapeDtypeStruct(shape, single)
    return kernel_call(
        attend_back_kernel,
        "attend_back",
        (steps,),
        [whole(span, width), whole(span, width), whole(length, width),
         across(width, wide), across(width, thin), across(width, thin), split(wide, width),
         whole(length, 128), whole(length, 128), split(heads // steps, length, size),
         split(kv_heads // steps, length, size), split(kv_heads // steps, length, size), split(1, 8, length)],
        [across(length, wide), across(length, thin), across(length, thin),
         whole(span, width), whole(span, width), whole(8, width)],
        [low(length, heads * size), low(length, kv_heads * size), low(length, kv_heads * size),
         high(span, width), low(span, width), high(8, width)],
        [pltpu.VMEM((length, wide), bfloat), pltpu.VMEM((length, width), single)],
        6 * length * width * (heads + kv_heads) * size,
        2 * (length * width * 6 + 2 * width * (heads + kv_heads) * size),
        (place, mine, other, tokens, query_w, key_w, value_w, out_w) + tuple(tables) + tuple(saved),
        prefetch=1,
    )


def three_lanes(value, starts, lanes):
    total = None
    for start in starts:
        low = value.astype(bfloat).astype(single)
        value = value - low
        moved = pltpu.roll(low, start, 1) if start else low
        total = moved if total is None else total + moved
    return total


def token_kernel(count, place_ref, stay_ref, came_ref, routes_ref, gain_ref, router_ref, hidden_ref, token_ref):
    width = stay_ref.shape[1]
    hidden = stay_ref[...] + came_ref[...]
    hidden_ref[...] = hidden
    inverse = lax.rsqrt(jnp.mean(hidden * hidden, axis=1, keepdims=True) + EPS)
    moe_in = (hidden * inverse * gain_ref[...]).astype(bfloat)
    token_ref[:, :width] = moe_in
    logits = dot_nt(moe_in, router_ref[...])
    logits = jnp.concatenate([logits, jnp.zeros((logits.shape[0], 128 - count), single)], axis=1)
    lane = lax.broadcasted_iota(jnp.int32, logits.shape, 1)
    routes = routes_ref[...].astype(single).T
    lanes = lane.astype(single)
    picked = lanes == routes[:, :1]
    for k in range(1, routes.shape[1]):
        picked = picked | (lanes == routes[:, k : k + 1])
    peak = jnp.max(jnp.where(picked, logits, -1e30), axis=1, keepdims=True)
    weights = jnp.where(picked, jnp.exp(jnp.where(picked, logits, peak) - peak), 0.0)
    gates = weights / jnp.sum(weights, axis=1, keepdims=True)
    tail = three_lanes(gates, (0, count, 2 * count), 128)
    blank = jnp.zeros((routes.shape[0], 128 - routes.shape[1]), single)
    token_ref[:, width:] = (tail + jnp.concatenate([blank, routes], axis=1)).astype(bfloat)


def layer_kernel(addends, place_ref, hidden_ref, target_ref, valid_ref, *refs):
    parts, (layer_ref, grad_ref, low_ref, token_ref) = refs[:addends], refs[addends:]
    width = hidden_ref.shape[1]
    moe = sum_of(parts)
    layer = hidden_ref[...] + moe
    layer_ref[...] = layer.astype(bfloat)
    valid = valid_ref[:, :1].astype(single)
    grad = valid * (layer - target_ref[...].astype(single))
    grad_ref[...] = grad
    low_ref[...] = grad.astype(bfloat)
    token_ref[:, :width] = grad.astype(bfloat)
    inner = jnp.sum(grad * moe, axis=1, keepdims=True)
    lane = lax.broadcasted_iota(jnp.int32, (inner.shape[0], 128), 1)
    inner = jnp.where(lane == 0, inner, 0.0)
    token_ref[:, width:] = three_lanes(inner, (0, 1, 2), 128).astype(bfloat)


def sum_of(parts):
    total = None
    for part in parts:
        value = (part[0] if len(part.shape) == 3 else part[...]).astype(single)
        total = value if total is None else total + value
    return total


def norm_kernel(addends, place_ref, hidden_ref, grad_layer_ref, *refs):
    parts, (gain_ref, router_ref, digits_ref, grad_ref, low_ref, logits_ref, sum_ref) = refs[:addends], refs[addends:]
    width = hidden_ref.shape[1]
    wide = sum_of(parts)
    logits = wide[:, width:].astype(bfloat)
    logits_ref[...] = logits
    count = router_ref.shape[0]
    grad_in = wide[:, :width] + dot(logits[:, :count], router_ref[...])
    hidden = hidden_ref[...]
    inverse = lax.rsqrt(jnp.mean(hidden * hidden, axis=1, keepdims=True) + EPS)
    scaled = grad_in * gain_ref[...]
    inner = jnp.mean(scaled * hidden, axis=1, keepdims=True)
    grad = grad_layer_ref[...] + inverse * scaled - hidden * (inverse * inverse * inverse * inner)
    grad_ref[...] = grad
    low_ref[...] = grad.astype(bfloat)
    gain = jnp.sum(grad_in * hidden * inverse, axis=0, keepdims=True)
    first = lax.broadcasted_iota(jnp.int32, sum_ref.shape, 0) == 0
    gain = jnp.where(first, gain, 0.0)

    @pl.when(pl.program_id(0) == 0)
    def _():
        sum_ref[...] = gain + digits_ref[:, :1]

    @pl.when(pl.program_id(0) > 0)
    def _():
        sum_ref[...] += gain


def digits_kernel(valid_ref, pin_ref, digits_ref):
    count = jnp.sum(valid_ref[:1, :].astype(single), axis=1, keepdims=True)
    high = jnp.floor(count * (1.0 / 64.0))
    middle = jnp.floor((count - 64.0 * high) * 0.125)
    low = count - 64.0 * high - 8.0 * middle
    row = lax.broadcasted_iota(jnp.int32, digits_ref.shape, 0)
    digits_ref[...] = jnp.where(row == 1, high, jnp.where(row == 2, middle, jnp.where(row == 3, low, 0.0)))


def count_digits(valid, pin):
    return pl.pallas_call(
        digits_kernel,
        name="digits",
        grid=(1,),
        in_specs=[pl.BlockSpec(valid.shape, lambda i: (0, 0)), pl.BlockSpec(memory_space=pl.ANY)],
        out_specs=pl.BlockSpec((8, 128), lambda i: (0, 0)),
        out_shape=jax.ShapeDtypeStruct((8, 128), single),
        cost_estimate=pl.CostEstimate(flops=0, bytes_accessed=2**14, transcendentals=0),
    )(valid, pin)


def token_rows(kernel, name, steps, place, rowwise, others, outs, kept=()):
    block = outs[0].shape[0] // steps

    def spec(array):
        if isinstance(array, tuple) and array[1] is None:
            return pl.BlockSpec(
                (array[0].shape[0], block), lambda i, place: (0, place[2] * steps + i)
            )
        if isinstance(array, tuple):
            array, index = array
            return pl.BlockSpec((1, block, array.shape[2]), lambda i, place: (index, i, 0))
        return pl.BlockSpec((block, array.shape[1]), lambda i, place: (i, 0))

    bare = [array[0] if isinstance(array, tuple) else array for array in rowwise]
    return kernel_call(
        kernel,
        name,
        (steps,),
        [spec(array) for array in rowwise]
        + [pl.BlockSpec(array.shape, lambda i, place, n=array.ndim: (0,) * n) for array in others],
        [pl.BlockSpec((block, out.shape[1]), lambda i, place: (i, 0)) for out in outs]
        + [pl.BlockSpec(out.shape, lambda i, place: (0, 0)) for out in kept],
        list(outs) + list(kept),
        [],
        1,
        8 * sum(out.shape[0] * out.shape[1] for out in outs),
        (place,) + tuple(bare) + tuple(others),
        prefetch=1,
    )


def pack_kernel(lane_at, terms, cut, place_ref, sums_ref, *refs):
    lefts, rights, refs = refs[:terms], refs[terms : 2 * terms], refs[2 * terms :]
    outs, full_ref = refs[:-1], refs[-1]
    span = lefts[0].shape[0]
    at = 0
    for term in range(terms):
        left, right = lefts[term], rights[term]
        rows = left.shape[0]
        columns = right.shape[1]
        if right.shape[0] == rows:
            value = dot_tn(left[...], right[...])
        else:
            core = place_ref[2] if term == 0 else 1 - place_ref[2]
            value = dot_tn(left[...], right[pl.ds(pl.multiple_of(core * rows, rows), rows), :])
        if term == 1 and lefts[0].shape[0] != rights[0].shape[0]:
            full_ref[:, :columns] += value
        else:
            full_ref[:, at : at + columns] = value
            at += columns
    sums = sums_ref[...]
    high = sums.astype(bfloat)
    low = (sums - high.astype(single)).astype(bfloat)
    lane = lax.broadcasted_iota(jnp.int32, (sums.shape[0], 128), 1)
    chosen = (lane == lane_at + lax.broadcasted_iota(jnp.int32, lane.shape, 0)).astype(bfloat)
    column = dot_tn(high, chosen) + dot_tn(low, chosen)
    width = full_ref.shape[1]
    if at < width:
        full_ref[:, width - 128 :] = column
    else:
        full_ref[:, width - 128 :] += column
    some, block = outs[0].shape[:2]

    def blocks(step, i):
        start = (i * cut + (place_ref[4] ^ step)) * block
        return full_ref[pl.ds(pl.multiple_of(start, block), block), :].astype(bfloat)

    for step in range(min(cut, len(outs))):
        if len(outs) > cut and step == cut - 1:
            early = pl.program_id(0) < pl.num_programs(0) // 2

            @pl.when(early)
            def _():
                outs[-2][0] = blocks(step, 0)

            @pl.when(jnp.logical_not(early))
            def _():
                outs[-1][0] = blocks(step, 0)

        else:
            for i in range(some):
                outs[step][i] = blocks(step, i)


def pack_sums(place, lefts, rights, sums, lane_at, columns, count_dp, owners):
    width = sums.shape[1]
    block = width // (count_dp * owners)
    steps = count_dp if (width // count_dp) % 128 == 0 else 1
    tall = lambda array: pl.BlockSpec((array.shape[0], width // steps), lambda i, *_: (0, i))
    whole = lambda array: pl.BlockSpec(array.shape, lambda i, *_: (0, 0))
    some = count_dp // steps
    halved = owners == 4 and steps == count_dp
    specs = [pl.BlockSpec((some, block, columns), lambda i, *_: (i, 0, 0))] * owners
    shapes = [jax.ShapeDtypeStruct((count_dp, block, columns), bfloat)] * owners
    if halved:
        half = count_dp // 2
        specs[3:] = [
            pl.BlockSpec((1, block, columns), lambda i, *_: (jnp.minimum(i, half - 1), 0, 0)),
            pl.BlockSpec((1, block, columns), lambda i, *_: (jnp.maximum(i - half, 0), 0, 0)),
        ]
        shapes[3:] = [jax.ShapeDtypeStruct((half, block, columns), bfloat)] * 2
    outs = kernel_call(
        functools.partial(pack_kernel, lane_at, len(lefts), owners),
        "pack_sums",
        (steps,),
        [tall(sums)] + [tall(left) for left in lefts] + [whole(right) for right in rights],
        specs,
        shapes,
        [pltpu.VMEM((width // steps, columns), single)],
        2 * sum(left.shape[0] * width * columns for left in lefts),
        2 * width * columns,
        (place, sums) + tuple(lefts) + tuple(rights),
        prefetch=1,
    )
    outs = list(outs)
    if halved:
        return outs[:3] + [(outs[3], outs[4])]
    if owners == 4:
        half = count_dp // 2
        return outs[:3] + [(outs[3][:half], outs[3][half:])]
    return outs


def rope_tables(length, head_size):
    half_size = head_size // 2
    frequency = np.float32(THETA) ** (-np.arange(half_size, dtype=np.float32) * np.float32(2.0) / np.float32(head_size))
    angles = np.arange(length, dtype=np.float32)[:, None] * frequency.astype(np.float32)[None, :]
    return [jnp.asarray(np.tile(f(angles).astype(np.float32), (1, 128 // half_size))) for f in (np.cos, np.sin)]


def rms_backward(value_matrix, inverse, gain, grad_normed):
    scaled = grad_normed * gain
    grad_gain = jnp.sum(grad_normed * value_matrix * inverse, axis=0)
    grad_values = inverse * scaled - value_matrix * inverse**3 * jnp.mean(
        scaled * value_matrix, axis=-1, keepdims=True
    )
    return (grad_values, grad_gain)


def assemble(mine, other):
    first = lax.axis_index("tensor") == 0
    return jnp.concatenate([jnp.where(first, mine, other), jnp.where(first, other, mine)], axis=0)


def combine_groups(slots, rows, capacity, span, between, later=None, own=None):
    owners = lax.axis_size("expert")
    orders = return_order(owners)
    if own is not None:
        orders = [[group - 1 for group in order if group] for order in orders]
    if len(orders) == 1:
        mine, other = return_rows(slots, after(rows, *between(())), orders[0], capacity, span)
        other = swap(other)
        sent = [
            (mine[i].astype(single) + other[i].astype(single)).astype(bfloat)
            for i in range(owners - 1)
        ]
        came = [to_peer(part, "expert", i) for i, part in enumerate(sent, 1)]
    else:
        mine, other = return_rows(slots, rows, orders[0], capacity, span)
        other = after(swap(other), *hold(other))
        came, sent = send_farthest(mine, other)
        done = between(sent)
        came[0] = after(came[0], *hold(sent[0]), *done)
        rows = after(rows, *done, *hold(sent[0]), *hold(sent[1]))
        mine, other = return_rows(slots, rows, orders[1], capacity, span)
        other = after(swap(other), *hold(other))
        came, sent = send_nearer(mine, other, came)
        done = later(sent) if later else ()
        if own is None:
            rows = after(rows, *sent, *hold(sent[0]), *hold(sent[1]))
            mine, other = return_rows(slots, rows, orders[2], capacity, span)
            other = swap(after(other, *done))
    if own is not None:
        return [(own[0], 0), (own[1], 0)] + came, sent
    at = len(orders[-1]) - 1
    return [(mine, at), (other, at)] + came, sent


def on_device(
    tokens,
    teacher,
    routes,
    valid,
    teacher_rows,
    norm_attn,
    norm_moe,
    w_query,
    key_projection_weight,
    value_projection_weight,
    w_out,
    w_router,
    w_gate,
    w_up,
    w_down,
):
    rows_dev, model_width = tokens.shape
    seq_count = rows_dev // SEQUENCE_LENGTH
    heads_local = w_query.shape[1] // HEAD_DIMENSION
    kv_local = key_projection_weight.shape[1] // HEAD_DIMENSION
    query_width = w_query.shape[1]
    key_width = key_projection_weight.shape[1]
    experts_local = w_gate.shape[0]
    owners = lax.axis_size("expert")
    count_dp = lax.axis_size("dp")
    groups = count_dp * owners
    all_experts = experts_local * owners
    top_count = routes.shape[1]
    capacity = rows_dev * top_count * 5 // (4 * all_experts)
    at_dp, at_ex, core = lax.axis_index("dp"), lax.axis_index("expert"), lax.axis_index("tensor")
    span = rows_dev // 2
    shards = count_dp // 2
    place = [at_ex * experts_local, at_dp // shards, core, at_dp % shards, at_ex, at_dp]
    place = jnp.stack(place).astype(jnp.int32)

    def mine_of(value, axis=0):
        return lax.dynamic_slice_in_dim(value, core * span, span, axis)

    def other_of(value, axis=0):
        return lax.dynamic_slice_in_dim(value, (1 - core) * span, span, axis)

    tables = rope_tables(SEQUENCE_LENGTH, HEAD_DIMENSION)
    gain_attn, gain_moe = norm_attn, norm_moe

    def tokens_like(columns, kind):
        return jax.ShapeDtypeStruct((span, columns), kind)

    weights = (w_query, key_projection_weight, value_projection_weight, w_out)
    normed, queries, keys, values, mixed, log_sums, staying, leaving = attend(
        place, tokens, gain_attn, *weights, tables
    )
    came = after(swap(leaving), *hold(leaving))
    wide = model_width + 128
    hidden_first, token = token_rows(
        functools.partial(token_kernel, all_experts),
        "token",
        2,
        place,
        [staying, came, (routes.T, None)],
        [gain_moe, w_router.T],
        [tokens_like(model_width, single), tokens_like(wide, bfloat)],
    )

    some = experts_local // 2
    few = max(1, some - some // 2)
    pieces = ((0, some), (some, experts_local - some))

    def interleave(mine, other):
        return [part for pair in zip(mine, other) for part in pair]

    def far_forward(parts, start, amount, pin):
        return expert_forward(
            place, all_experts, top_count, pin, (w_gate, w_up), parts, owners, capacity, start, amount
        )

    mirror = to_mirror(token)
    own_other = swap(token)
    def forward(parts, groups, pin, chunk):
        return expert_forward(
            place, all_experts, top_count, pin, (w_gate, w_up, w_down), parts, groups, capacity, 0, experts_local, chunk
        )

    own = forward([token, own_other], 1, token, CHUNK_OWN)
    own_mine, own_leaving = return_rows(own[4], own[5], [0], capacity, span)
    (wanted,) = after_all([mine_of(teacher_rows, 1)], own[5])
    (valid_rows,) = after_all([mine_of(valid)[:, None] + jnp.zeros((span, 128), jnp.int32)], own[5])
    chooser = (wanted[0][:, None] == jnp.arange(rows_dev, dtype=jnp.int32)).astype(bfloat)
    target = jnp.dot(chooser, teacher, preferred_element_type=bfloat)
    near_parts = spread(token, own_other, (own[5],), (own_mine, target, valid_rows))
    mirror = after(mirror, *near_parts)
    peers = from_peers(mirror)
    mirror_other = swap(mirror)
    own_came = swap(after(own_leaving, mirror))
    others = forward(near_parts, owners - 1, mirror, CHUNK_OTHERS)
    gate_pre, up_pre, near_half, near_tails = zip(own[:4], others[:4])
    slots = jnp.concatenate([own[4], others[4]], axis=0)
    results = after(others[5], mirror_other, own_came)
    peers_other = []

    def swap_peers(sent):
        peers[:] = after_all(peers, *sent)
        peers_other.extend(swap(peer) for peer in peers)
        return sent

    addends, sent = combine_groups(
        others[4], results, capacity, span, swap_peers, own=(own_mine, own_came)
    )
    far_tokens = interleave([mirror] + peers, [mirror_other] + peers_other)
    far = [far_forward(far_tokens, *pieces[0], sent[0])]
    addends[-1] = after(addends[-1], far[0][0], *hold(sent[0]))
    layer_low, grad_layer, layer_grad, token_grad = token_rows(
        functools.partial(layer_kernel, len(addends)),
        "layer",
        2,
        place,
        [hidden_first, target, valid_rows] + addends,
        [],
        [tokens_like(model_width, bfloat), tokens_like(model_width, single), tokens_like(model_width, bfloat), tokens_like(wide, bfloat)],
    )

    leaving = after(layer_grad, *hold(token_grad))
    mirror = to_mirror(leaving)
    far.append(far_forward(far_tokens, *pieces[1], hold(leaving)[0]))
    own_other = swap(token_grad)
    digits = count_digits(jnp.broadcast_to(valid[None, :], (8, rows_dev)), far[1][0])
    near_parts = [token_grad, own_other] + spread(token_grad, own_other, (far[1][0],), (digits,))
    mirror = after(mirror, *near_parts)
    peers = from_peers(mirror)
    mirror_other = swap(mirror)
    hidden_low, grad_gate_pre, grad_up_pre, near_grad_half, results = expert_backward(
        place, all_experts, slots, (w_gate, w_up, w_down), gate_pre, up_pre, near_tails, near_parts, capacity, (mirror,)
    )
    results = after(results, mirror_other)
    weight_parts, far_grads = [], []

    def weights_of(start, amount, others=()):
        piece = 0 if start < some else 1
        far_gate, far_up, far_half, far_tails, far_slots = far[piece]
        values = expert_weights(
            place,
            all_experts,
            far_slots,
            w_down,
            (far_gate, far_up, far_tails, far_half),
            (hidden_low, grad_gate_pre, grad_up_pre, near_grad_half),
            near_half,
            far_grads,
            capacity,
            start,
            start - pieces[piece][0],
            amount,
            shards,
            tuple(others),
        )
        came = [to_peer(values[step], "dp", step) for step in range(1, shards)]
        weight_parts.append((start, values[0], came))
        return (*values, *[pin for value in values[1:] for pin in hold(value)])

    def swap_far(sent):
        peers[:] = after_all(peers, *sent)
        peers_other = [swap(peer) for peer in peers]
        far_grads.extend(interleave([mirror] + peers, [mirror_other] + peers_other))
        return peers_other

    results = after(results, *peers)
    addends, sent = combine_groups(slots, results, capacity, span, lambda sent: sent, swap_far)
    if owners != 4:
        swap_far(sent)
    done = weights_of(0, few, sent)
    addends[-1] = after(addends[-1], *done, *hold(sent[0]))
    grad_hidden, grad_attn, grad_logits, gain_sums = token_rows(
        functools.partial(norm_kernel, len(addends)),
        "norm",
        2,
        place,
        [hidden_first, grad_layer] + addends,
        [gain_moe, w_router.T, digits],
        [tokens_like(model_width, single), tokens_like(model_width, bfloat), tokens_like(128, bfloat)],
        [jax.ShapeDtypeStruct((8, model_width), single)],
    )
    grad_attn_other = after(swap(grad_attn), *hold(grad_attn))
    first_parts = pack_sums(
        place,
        [grad_attn, grad_attn_other, token],
        [mixed, mixed, grad_logits],
        gain_sums,
        all_experts,
        query_width + 128,
        count_dp,
        owners,
    )
    first_sum = start_sum(first_parts)
    done = weights_of(some, experts_local - some, first_parts[-1] if owners == 4 else first_parts)
    first_sum, sent = go_on(first_sum, *done)
    grad_attn, layer_low = after_all([grad_attn, layer_low], *sent, *weight_parts[0][2])
    layer_other = swap(layer_low)
    raw_query, raw_key, raw_value, staying, leaving, gain_sums = attend_back(
        place, grad_attn, grad_attn_other, tokens, *weights, tables, (queries, keys, values, log_sums)
    )
    second_parts = pack_sums(
        place,
        [normed] * 3,
        [raw_query, raw_key, raw_value],
        after(gain_sums, *first_sum[1:], layer_other),
        0,
        query_width + 2 * key_width + 128,
        count_dp,
        owners,
    )
    second_sum = start_sum(second_parts)
    last = second_parts[-1] if owners == 4 else second_parts
    leaving = swap(leaving)
    first_total = add_up(first_sum[0], after_all(first_sum[1:], *last, leaving))
    first_dense = over_dp_start(first_total)
    pins = [] if first_dense[1] is None else [first_dense[1], *hold(first_dense[1])]
    done = weights_of(few, some - few, (*last, *hold(last[0]), *pins))
    second_sum, sent = go_on(second_sum, *done)
    first_dense = over_dp_step(first_dense, *sent, *weight_parts[1][2])
    leaving = after(leaving, *sent)
    inputs_mine = mine_of(tokens).astype(single)
    inverse_mine = lax.rsqrt(jnp.mean(inputs_mine * inputs_mine, axis=-1, keepdims=True) + EPS)
    grad_first, _ = rms_backward(
        inputs_mine, inverse_mine, norm_attn, staying + leaving.astype(single)
    )
    layer_low = after(layer_low, *sent)
    block_out = assemble(layer_low, layer_other)
    pins = [] if first_dense[1] is None else [first_dense[1], *hold(first_dense[1])]
    grad_tokens_mine = after(grad_hidden + grad_first, *pins, block_out)
    grad_tokens_other = after(swap(grad_tokens_mine), *hold(grad_tokens_mine))
    second_total = add_up(second_sum[0], after_all(second_sum[1:], grad_tokens_other, block_out, *pins))
    arrived, sent = over_dp_at_once(second_total)
    first_dense = over_dp_end(first_dense, *sent)
    tail = first_dense[:, query_width:]
    counted = tail[:1, all_experts + 1 : all_experts + 4] * jnp.asarray([[64.0, 8.0, 1.0]], single)
    tail = tail + after(swap(tail), *hold(tail))
    scale = jnp.broadcast_to(rows_dev * groups / jnp.sum(counted, axis=1, keepdims=True), (8, 128))
    first_dense, tail = first_dense * scale[0, 0], tail * scale[0, 0]
    grad_tokens = assemble(grad_tokens_mine, grad_tokens_other) * scale[0, 0]
    weight_grads, finished = None, ()
    for start, values, came in weight_parts:
        came = [after(part, *sent) for part in came]
        weight_grads, finished = finish_weights(experts_local, start, scale, values, came, weight_grads)
    arrived[0] = after(arrived[0], *hold(sent[0]), finished, grad_tokens, tail)
    grad_query, grad_key, grad_value, second_tail = scaled_sum(
        place, scale, second_total, arrived, (query_width, key_width, key_width, 128)
    )
    second_tail = second_tail + swap(second_tail)
    return (
        block_out,
        grad_tokens,
        second_tail[:, 0],
        tail[:, all_experts],
        grad_query,
        grad_key,
        grad_value,
        first_dense[:, :query_width].T,
        tail[:, :all_experts],
        weight_grads[0],
        weight_grads[1],
        weight_grads[2],
    )


def solution(mesh):
    placed = (
        P(("dp", "expert"), None),
        P(("dp", "expert"), None),
        P(("dp", "expert"), None),
        P(("dp", "expert")),
        P(("dp", "expert"), None),
        P(),
        P(),
        P(None, "tensor"),
        P(None, "tensor"),
        P(None, "tensor"),
        P("tensor", None),
        P(),
        P("expert", None, "tensor"),
        P("expert", None, "tensor"),
        P("expert", "tensor", None),
    )
    return jax.shard_map(
        on_device,
        mesh=mesh,
        in_specs=placed,
        out_specs=(
            P(("dp", "expert"), None),
            P(("dp", "expert"), None),
            P(("dp", "expert")),
            P(("dp", "expert")),
            P(("dp", "expert"), "tensor"),
            P(("dp", "expert"), "tensor"),
            P(("dp", "expert"), "tensor"),
            P("tensor", ("dp", "expert")),
            P(("dp", "expert"), None),
            P("expert", "dp", "tensor"),
            P("expert", "dp", "tensor"),
            P("expert", "tensor", "dp"),
        ),
        check_vma=False,
    )
```

```python
import functools
import math

import jax
import jax.numpy as jnp
import numpy as np
from jax import lax
from jax.experimental import pallas as pl
from jax.experimental.pallas import tpu as pltpu
from jax.sharding import PartitionSpec as P

HEAD_DIMENSION = 64
SEQUENCE_LENGTH = 512
ABLK = 256


EPS = 1e-06
VMEM_LIMIT = 56 * 1024 * 1024
CHUNK_OWN = 2
CHUNK_OTHERS = 1
COST = 100
THETA = 10000.0
bfloat = jnp.bfloat16
single = jnp.float32


def pass_kernel(*refs):
    pass


def after_all(values, *others):
    anywhere = pl.BlockSpec(memory_space=pl.ANY)
    return pl.pallas_call(
        pass_kernel,
        name="after",
        in_specs=[anywhere] * (len(values) + len(others)),
        out_specs=[anywhere] * len(values),
        out_shape=[jax.ShapeDtypeStruct(value.shape, value.dtype) for value in values],
        input_output_aliases={i: i for i in range(len(values))},
        cost_estimate=pl.CostEstimate(flops=0, bytes_accessed=0, transcendentals=0),
    )(*values, *others)


def after(value, *others):
    return after_all([value], *others)[0] if others else value


def hold(value):
    anywhere = pl.BlockSpec(memory_space=pl.ANY)
    return [
        pl.pallas_call(
            pass_kernel,
            name="hold",
            in_specs=[anywhere],
            out_specs=anywhere,
            out_shape=jax.ShapeDtypeStruct((8, 128), single),
            cost_estimate=pl.CostEstimate(flops=10**12, bytes_accessed=10**9, transcendentals=0),
        )(value)
    ]


def swap(value):
    return lax.ppermute(value, "tensor", [(0, 1), (1, 0)])


def to_peer(value, axis, step):
    return lax.ppermute(value, axis, [(i, i ^ step) for i in range(lax.axis_size(axis))])


def to_mirror(value):
    count = lax.axis_size("dp")
    return lax.ppermute(value, "dp", [(i, count - 1 - i) for i in range(count)])


def from_peers(value):
    return [to_peer(value, "expert", s) for s in range(1, lax.axis_size("expert"))]


def halves_kernel(low_ref, high_ref, *refs):
    refs[-2][...] = low_ref[...]
    refs[-1][...] = high_ref[...]


def low_and_high(low, high, *others):
    rows, width = low.shape
    half = jax.ShapeDtypeStruct((rows // 2, width), low.dtype)
    return pl.pallas_call(
        halves_kernel,
        name="halves",
        grid=(1,),
        in_specs=[
            pl.BlockSpec((rows // 2, width), lambda i: (0, 0)),
            pl.BlockSpec((rows // 2, width), lambda i: (1, 0)),
        ]
        + [pl.BlockSpec(memory_space=pl.ANY)] * len(others),
        out_specs=[pl.BlockSpec((rows // 2, width), lambda i: (0, 0))] * 2,
        out_shape=[half, half],
        cost_estimate=pl.CostEstimate(flops=0, bytes_accessed=2**20, transcendentals=0),
    )(low, high, *others)


def spread(value, own_other, pause=(), more_pause=()):
    if lax.axis_size("expert") != 4:
        near = from_peers(value)
        near[0] = after(near[0], own_other, *hold(value), *pause, *more_pause)
        return [part for mine in near for part in (mine, swap(mine))]
    first, second = to_peer(value, "expert", 1), to_peer(value, "expert", 2)
    for_first, for_second = low_and_high(second, first, own_other, *hold(value), *pause)
    low, high = to_peer(for_first, "expert", 1), to_peer(for_second, "expert", 2)
    first_other, second_other = swap(first), swap(second)
    low = after(low, *hold(for_first), first_other, second_other, *more_pause)
    return [first, first_other, second, second_other, low, high, swap(low), swap(high)]


def farther_kernel(mine_ref, other_ref, low_ref, high_ref):
    cut = low_ref.shape[0]
    total = (mine_ref[0].astype(single) + other_ref[0].astype(single)).astype(bfloat)
    low_ref[...] = total[:cut]
    high_ref[...] = total[cut:]


def nearer_kernel(mine_first, other_first, mine_second, other_second, low_ref, high_ref, first_ref, second_ref):
    step = pl.program_id(0)
    low = jnp.where(step == 0, low_ref[...].astype(single), 0.0)
    high = jnp.where(step == 0, 0.0, high_ref[...].astype(single))
    first = mine_first[0].astype(single) + other_first[0].astype(single) + high
    second = mine_second[0].astype(single) + other_second[0].astype(single) + low
    first_ref[...] = first.astype(bfloat)
    second_ref[...] = second.astype(bfloat)


def send_farthest(mine, other):
    _, span, width = mine.shape
    half = jax.ShapeDtypeStruct((span // 2, width), bfloat)
    low, high = pl.pallas_call(
        farther_kernel,
        name="farther",
        out_shape=[half, half],
        cost_estimate=pl.CostEstimate(flops=0, bytes_accessed=2**21, transcendentals=0),
    )(mine, other)
    return [to_peer(low, "expert", 1), to_peer(high, "expert", 2)], (low, high)


def send_nearer(mine, other, came):
    _, span, width = mine.shape
    half = pl.BlockSpec((span // 2, width), lambda i: (i, 0))
    only = pl.BlockSpec((span // 2, width), lambda i: (0, 0))
    stacked = lambda index: pl.BlockSpec((1, span // 2, width), lambda i: (index, i, 0))
    whole = jax.ShapeDtypeStruct((span, width), bfloat)
    first, second = pl.pallas_call(
        nearer_kernel,
        name="nearer",
        grid=(2,),
        in_specs=[stacked(0), stacked(0), stacked(1), stacked(1), only, only],
        out_specs=[half, half],
        out_shape=[whole, whole],
        cost_estimate=pl.CostEstimate(flops=0, bytes_accessed=2**22, transcendentals=0),
    )(mine, other, mine, other, *came)
    return [to_peer(first, "expert", 1), to_peer(second, "expert", 2)], (first, second)


def start_sum(parts):
    if len(parts) != 4:
        return parts, None
    low, high = parts[3]
    return parts, [to_peer(low, "expert", 1), to_peer(high, "expert", 2)]


def dense_kernel(first_in, second_in, low_ref, high_ref, *refs):
    first_ref, second_ref = refs[-2:]
    step = pl.program_id(0)
    low = jnp.where(step == 0, low_ref[...].astype(single), 0.0)
    high = jnp.where(step == 0, 0.0, high_ref[...].astype(single))
    first_ref[...] = (first_in[...].astype(single) + high).astype(bfloat)
    second_ref[...] = (second_in[...].astype(single) + low).astype(bfloat)


def go_on(state, *others):
    parts, came = state
    if came is None:
        sent = [after(part, *others) for part in parts[1:]]
        return [parts[0]] + [to_peer(part, "expert", i) for i, part in enumerate(sent, 1)], sent
    low = after(came[0], *hold(parts[3][0]))
    shape = parts[1].shape
    half = pl.BlockSpec((shape[0] // 2,) + shape[1:], lambda i: (i, 0, 0))
    only = pl.BlockSpec((shape[0] // 2,) + shape[1:], lambda i: (0, 0, 0))
    whole = jax.ShapeDtypeStruct(shape, bfloat)
    first, second = pl.pallas_call(
        dense_kernel,
        name="dense_nearer",
        grid=(2,),
        in_specs=[half, half, only, only] + [pl.BlockSpec(memory_space=pl.ANY)] * len(others),
        out_specs=[half, half],
        out_shape=[whole, whole],
        cost_estimate=pl.CostEstimate(flops=0, bytes_accessed=2**22, transcendentals=0),
    )(parts[1], parts[2], low, came[1], *others)
    came = to_peer(first, "expert", 1), to_peer(second, "expert", 2)
    return [parts[0], after(came[0], *hold(first)), came[1]], [first, second]


def add_up(own, arrived):
    total = own.astype(single)
    for part in arrived:
        total = total + part.astype(single)
    return total


def sum_all(value, axes):
    for axis in axes:
        step = 1
        while step < lax.axis_size(axis):
            value = value + to_peer(value, axis, step)
            step *= 2
    return value


def over_dp_start(total):
    at_dp, count = lax.axis_index("dp"), lax.axis_size("dp")
    parts = {r: lax.dynamic_index_in_dim(total, at_dp ^ r, 0, keepdims=False) for r in range(count)}
    return over_dp_send(parts, 1)


def over_dp_send(parts, step):
    if step >= lax.axis_size("dp"):
        return parts, None, step
    return parts, jnp.concatenate([parts[r].astype(bfloat) for r in parts if r & step], axis=0), step


def over_dp_step(state, *others):
    parts, sent, step = state
    parts = dict(parts)
    leaving = [r for r in parts if r & step]
    came = after(to_peer(sent, "dp", step), *hold(sent), *others).astype(single)
    rows = came.shape[0] // len(leaving)
    for i, r in enumerate(leaving):
        parts[r ^ step] = parts[r ^ step] + came[i * rows : (i + 1) * rows]
        del parts[r]
    return over_dp_send(parts, 2 * step)


def over_dp_end(state, *others):
    while state[1] is not None:
        state, others = over_dp_step(state, *others), ()
    return state[0][0]


def over_dp_at_once(total):
    at_dp = lax.axis_index("dp")
    sent = [
        lax.dynamic_index_in_dim(total, at_dp ^ step, 0, keepdims=False).astype(bfloat)
        for step in range(1, lax.axis_size("dp"))
    ]
    return [to_peer(part, "dp", step) for step, part in enumerate(sent, 1)], sent


def scaled_sum_kernel(amount, widths, place_ref, scale_ref, total_ref, *refs):
    parts, outs = refs[:amount], refs[amount:]
    total = total_ref[0]
    for part in parts:
        total = total + part[...].astype(single)
    total = total * scale_ref[:1, :1]
    at = 0
    for out, width in zip(outs, widths):
        out[...] = total[:, at : at + width]
        at += width


def scaled_sum(place, scale, total, parts, widths):
    _, rows, columns = total.shape
    whole = lambda *shape: pl.BlockSpec(shape, lambda i, place: (0,) * len(shape))
    return kernel_call(
        functools.partial(scaled_sum_kernel, len(parts), widths),
        "scaled_sum",
        (1,),
        [whole(8, 128), pl.BlockSpec((1, rows, columns), lambda i, place: (place[5], 0, 0))]
        + [whole(rows, columns)] * len(parts),
        [whole(rows, width) for width in widths],
        [jax.ShapeDtypeStruct((rows, width), single) for width in widths],
        [],
        1,
        2**21,
        (place, scale, total) + tuple(parts),
        prefetch=1,
    )


def dot(left, right):
    return lax.dot_general(left, right, (((1,), (0,)), ((), ())), preferred_element_type=single)


def dot_nt(left, right):
    return lax.dot_general(left, right, (((1,), (1,)), ((), ())), preferred_element_type=single)


def dot_tn(left, right):
    return lax.dot_general(left, right, (((0,), (0,)), ((), ())), preferred_element_type=single)


def picks(slot, capacity):
    return slot == lax.broadcasted_iota(jnp.int32, (capacity, slot.shape[1]), 0)


def group_parts(parts, joined_ref):
    if joined_ref is None:
        return [(parts[i], parts[i + 1]) for i in range(0, len(parts), 2)]
    cut = parts[-1].shape[0]

    @pl.when(pl.program_id(0) == 0)
    def _():
        for i in range(2):
            for j in range(2):
                joined_ref[i, j * cut : (j + 1) * cut, :] = parts[-4 + 2 * i + j][...]

    pairs = [(parts[i], parts[i + 1]) for i in range(0, len(parts) - 4, 2)]
    return pairs + [(joined_ref.at[0], joined_ref.at[1])]


def find_slots(first_ref, top_count, pairs, slots_ref):
    groups, experts, tokens = slots_ref.shape
    row = lax.broadcasted_iota(jnp.int32, (tokens, tokens), 0)
    earlier = (row < lax.broadcasted_iota(jnp.int32, (tokens, tokens), 1)).astype(bfloat)
    ids = lax.broadcasted_iota(jnp.int32, (experts, tokens), 0)
    ids = (ids + first_ref[0]).astype(single)
    for group, pair in enumerate(pairs):
        tails = [part[:, part.shape[1] - 128 :].astype(single).T for part in pair]
        routes = jnp.concatenate(tails, axis=1)[128 - top_count :]
        mask = ids == routes[:1]
        for k in range(1, top_count):
            mask = mask | (ids == routes[k : k + 1])
        before = dot(mask.astype(single).astype(bfloat), earlier)
        slots_ref[group] = jnp.where(mask, before, -1.0).astype(jnp.int32)


def gather_rows(slots_ref, expert, pairs, rows_ref):
    capacity = rows_ref.shape[0] // len(pairs)
    width = rows_ref.shape[1]
    for group, (mine, other) in enumerate(pairs):
        span = mine.shape[0]
        slot = slots_ref[group, pl.ds(expert, 1), :]
        picked = picks(slot, capacity).astype(bfloat)
        rows = dot(picked[:, :span], mine[:, :width]) + dot(picked[:, span:], other[:, :width])
        rows_ref[group * capacity : (group + 1) * capacity, :] = rows.astype(bfloat)


def slot_gates(expert, tails, count):
    lane = lax.broadcasted_iota(jnp.int32, tails.shape, 1)
    chosen = (lane == expert) | (lane == expert + count) | (lane == expert + 2 * count)
    return jnp.sum(jnp.where(chosen, tails.astype(single), 0.0), axis=1, keepdims=True)


def half_columns(place_ref, width):
    return pl.ds(pl.multiple_of(place_ref[1] * width, 128), width)


def return_order(groups):
    rest = list(range(1, groups)) + [0]
    return [[3], [1, 2], [0]] if groups == 4 else [rest]


def forward_kernel(count, top_count, amount, halved, start, chunk, with_out, place_ref, gate_w, up_w, *refs):
    if with_out:
        down_w, refs = refs[0], refs[1:]
    parts, refs = refs[:amount], refs[amount:]
    parts, pins = parts[:-1], parts[-1:]
    gate_ref, up_ref, half_ref, tail_ref, slots_ref = refs[:5]
    refs = refs[5:]
    step = pl.program_id(0)
    joined_ref = refs[-1] if halved else None
    rows_ref = refs[-2] if halved else refs[-1]
    width = gate_w.shape[1]
    pairs = group_parts(parts, joined_ref)

    @pl.when(step == 0)
    def _():
        find_slots(place_ref, top_count, pairs, slots_ref)

    for i in range(chunk):
        expert = start + step * chunk + i
        gather_rows(slots_ref, expert, pairs, rows_ref)
        half_ref[i] = rows_ref[:, half_columns(place_ref, half_ref.shape[2])]
        tails = rows_ref[:, width:]
        tail_ref[i] = tails
        rows = rows_ref[:, :width]
        gate_pre = dot(rows, gate_w[i])
        up_pre = dot(rows, up_w[i])
        gate_ref[i] = gate_pre.astype(bfloat)
        up_ref[i] = up_pre.astype(bfloat)
        if with_out:
            gates = slot_gates(place_ref[0] + expert, tails, count)
            hidden = (gate_pre * jax.nn.sigmoid(gate_pre) * up_pre * gates).astype(bfloat)
            refs[0][i] = dot(hidden, down_w[i]).astype(bfloat)


def hidden_grads(gate_pre, up_pre, gates, grad_hidden):
    sig = jax.nn.sigmoid(gate_pre)
    silu = gate_pre * sig
    hidden = silu * up_pre
    scaled = grad_hidden * gates
    grad_gate_pre = (scaled * up_pre * sig * (1.0 + gate_pre * (1.0 - sig))).astype(bfloat)
    grad_up_pre = (scaled * silu).astype(bfloat)
    return hidden, (hidden * gates).astype(bfloat), grad_gate_pre, grad_up_pre


def joined(refs):
    return refs[0][0] if len(refs) == 1 else jnp.concatenate([ref[0] for ref in refs], axis=0)


def backward_kernel(count, amount, halved, pins, pieces, place_ref, slots_ref, gate_w, up_w, down_w, *refs):
    gate_refs, up_refs, tail_refs = (refs[i * pieces : (i + 1) * pieces] for i in range(3))
    refs = refs[3 * pieces :]
    parts, refs = refs[:amount], refs[amount + pins :]
    hidden_ref, grad_gate_ref, grad_up_ref, half_ref, refs = refs[0], refs[1], refs[2], refs[3], refs[4:]
    back_ref, rows_ref = refs[:2]
    joined_ref = refs[2] if halved else None
    width = gate_w.shape[1]
    step = pl.program_id(0)
    expert = place_ref[0] + step
    gather_rows(slots_ref, step, group_parts(parts, joined_ref), rows_ref)
    half_ref[0] = rows_ref[:, half_columns(place_ref, half_ref.shape[2])]
    gates = slot_gates(expert, joined(tail_refs), count)
    grad_hidden = dot_nt(rows_ref[:, :width], down_w[0])
    hidden, hidden_low, grad_gate_pre, grad_up_pre = hidden_grads(
        joined(gate_refs).astype(single), joined(up_refs).astype(single), gates, grad_hidden
    )
    hidden_ref[0] = hidden_low
    grad_gate_ref[0] = grad_gate_pre
    grad_up_ref[0] = grad_up_pre
    back = dot_nt(grad_gate_pre, gate_w[0]) + dot_nt(grad_up_pre, up_w[0])
    back_ref[0, :, :width] = back.astype(bfloat)
    tails = rows_ref[:, width:].astype(single)
    lane = lax.broadcasted_iota(jnp.int32, tails.shape, 1)
    inner = jnp.sum(jnp.where(lane < 3, tails, 0.0), axis=1, keepdims=True)
    inner = inner * (place_ref[2] == 0).astype(single)
    grad_logit = gates * (jnp.sum(hidden * grad_hidden, axis=1, keepdims=True) - inner)
    back_ref[0, :, width:] = jnp.where(lane == expert, grad_logit, 0.0).astype(bfloat)


def weights_kernel(count, groups, start, pins, pieces, place_ref, slots_ref, down_w, gate_ref, up_ref, tail_ref, *refs):
    hidden_near, gate_near, up_near, near_g, far_x = refs[:5]
    near_x, refs = refs[5 : 5 + pieces], refs[5 + pieces :]
    parts, refs = refs[: 2 * groups], refs[2 * groups + pins :]
    shards, (rows_ref, full_ref) = refs[:-2], refs[-2:]
    expert = start + pl.program_id(0)
    gather_rows(slots_ref, expert, group_parts(parts, None), rows_ref)
    gates = slot_gates(place_ref[0] + expert, tail_ref[0], count)
    grad_hidden = dot_nt(rows_ref[...], down_w[0])
    _, hidden, grad_gate_pre, grad_up_pre = hidden_grads(
        gate_ref[0].astype(single), up_ref[0].astype(single), gates, grad_hidden
    )
    far_g = rows_ref[:, half_columns(place_ref, full_ref.shape[1])]
    far, near = far_x[0], joined(near_x)
    sums = (
        dot_tn(far, grad_gate_pre) + dot_tn(near, gate_near[0]),
        dot_tn(far, grad_up_pre) + dot_tn(near, up_near[0]),
        dot_tn(far_g, hidden) + dot_tn(near_g[0], hidden_near[0]),
    )
    for i, value in enumerate(sums):
        full_ref[i] = value.astype(bfloat)
    size = shards[0].shape[2]
    for step, shard in enumerate(shards):
        at = pl.multiple_of((place_ref[3] ^ step) * size, size)
        for i in range(3):
            shard[0, i] = full_ref[i, pl.ds(at, size), :]


def finish_kernel(scale_ref, own_ref, *refs):
    arrived, (d_gate, d_up, d_down, done_ref) = refs[:-4], refs[-4:]
    scale = scale_ref[:1, :1]
    for e in range(own_ref.shape[0]):

        def total(i):
            value = own_ref[e, i].astype(single)
            for ref in arrived:
                value = value + ref[e, i].astype(single)
            return value * scale

        d_gate[e] = total(0)
        d_up[e] = total(1)
        d_down[e] = total(2).T
    done_ref[...] = scale_ref[...]


def finish_more_kernel(gate_in, up_in, down_in, scale_ref, *refs):
    finish_kernel(scale_ref, *refs)


def return_kernel(first, cycle, slots_ref, rows_ref, mine, other, picked_ref):
    experts, capacity, width = rows_ref.shape
    span = mine.shape[1]
    group = (pl.program_id(0) + first) % cycle

    @pl.when(pl.program_id(1) == 0)
    def _():
        for e in range(experts):
            slot = slots_ref[group, e : e + 1, :]
            picked_ref[e * capacity : (e + 1) * capacity, :] = picks(slot, capacity).astype(bfloat)

    back = dot_tn(picked_ref[...], rows_ref[...].reshape(experts * capacity, width)).astype(bfloat)
    mine[0] = back[:span]
    other[0] = back[span:]


def kernel_call(kernel, name, grid, in_specs, out_specs, out_shape, scratch, flops, moved, args, prefetch=0, aliases=None):
    return pl.pallas_call(
        kernel,
        name=name,
        grid_spec=pltpu.PrefetchScalarGridSpec(
            num_scalar_prefetch=prefetch,
            grid=grid,
            in_specs=in_specs,
            out_specs=out_specs,
            scratch_shapes=scratch,
        ),
        out_shape=out_shape,
        input_output_aliases=aliases or {},
        compiler_params=pltpu.CompilerParams(
            dimension_semantics=("arbitrary",) * len(grid), vmem_limit_bytes=VMEM_LIMIT
        ),
        cost_estimate=pl.CostEstimate(flops=COST * flops, bytes_accessed=moved, transcendentals=0),
    )(*args)


def per_expert(*shape, start=0):
    return pl.BlockSpec((1,) + shape, lambda e, *_: (e + start,) + (0,) * len(shape))


def anywhere(pins):
    return [pl.BlockSpec(memory_space=pl.ANY) for _ in pins]


def once(*shape):
    return pl.BlockSpec(
        shape, lambda e, *_: (0,) * len(shape), pipeline_mode=pl.Buffered(buffer_count=1)
    )


def return_rows(slots, rows, order, capacity, span):
    groups, _, tokens = slots.shape
    experts, _, width = rows.shape
    amount, first = len(order), order[0]
    cycle = groups
    cuts = 2 if width % 256 == 0 and amount == 1 else 1
    cut = width // cuts
    part = pl.BlockSpec((1, span, cut), lambda g, n: (g, 0, n))
    return kernel_call(
        functools.partial(return_kernel, first, cycle),
        "return_rows",
        (amount, cuts),
        [
            pl.BlockSpec(slots.shape, lambda g, n: (0, 0, 0)),
            pl.BlockSpec((experts, capacity, cut), lambda g, n: (0, (g + first) % cycle, n)),
        ],
        [part, part],
        [jax.ShapeDtypeStruct((amount, span, width), bfloat)] * 2,
        [pltpu.VMEM((experts * capacity, tokens), bfloat)],
        2 * amount * experts * capacity * tokens * width,
        2 * amount * (experts * capacity + tokens) * width,
        (slots, rows),
    )


def expert_forward(place, count, top_count, pin, weights, parts, groups, capacity, start, experts, chunk=1):
    if experts % chunk or start % chunk:
        chunk = 1

    def per_expert(*shape, start=0):
        return pl.BlockSpec((chunk,) + shape, lambda e, *_: (e + start // chunk,) + (0,) * len(shape))

    span, whole = parts[0].shape
    tokens = 2 * span
    width, hidden = weights[0].shape[1:]
    with_out = len(weights) == 3
    total = groups * capacity
    halved = len(parts) > 2 * groups
    specs = [per_expert(width, hidden, start=start)] * 2
    outs = [per_expert(total, hidden)] * 2
    outs += [per_expert(total, width // 2), per_expert(total, whole - width)]
    shapes = [jax.ShapeDtypeStruct((experts, total, hidden), bfloat)] * 2
    shapes += [jax.ShapeDtypeStruct((experts, total, width // 2), bfloat)]
    shapes += [jax.ShapeDtypeStruct((experts, total, whole - width), bfloat)]
    listed = (groups, -(-weights[0].shape[0] // 8) * 8, tokens)
    outs += [pl.BlockSpec(listed, lambda e, *_: (0, 0, 0))]
    shapes += [jax.ShapeDtypeStruct(listed, jnp.int32)]
    scratch = [pltpu.VMEM((total, whole), bfloat)]
    if halved:
        scratch += [pltpu.VMEM((2, span, whole), bfloat)]
    if with_out:
        specs += [per_expert(hidden, width, start=start)]
        outs += [per_expert(total, width)]
        shapes += [jax.ShapeDtypeStruct((experts, total, width), bfloat)]
    specs += [once(*part.shape) for part in parts] + [pl.BlockSpec(memory_space=pl.ANY)]
    return kernel_call(
        functools.partial(forward_kernel, count, top_count, len(parts) + 1, halved, start, chunk, with_out),
        "expert_forward" if with_out else "expert_forward_far",
        (experts // chunk,), specs, outs, shapes, scratch,
        2 * experts * total * (width * hidden * len(weights) + tokens * whole),
        2 * experts * (len(weights) * width * hidden + total * width + 4 * total * hidden),
        (place,) + tuple(weights) + tuple(parts) + (pin,),
        prefetch=1,
    )


def expert_backward(place, count, slots, weights, gate_pre, up_pre, tails, parts, capacity, pins):
    groups, _, tokens = slots.shape
    experts = weights[0].shape[0]
    span, whole = parts[0].shape
    width, hidden = weights[0].shape[1:]
    total = groups * capacity
    thin = per_expert(total, hidden)
    specs = [once(*slots.shape)] + [per_expert(width, hidden)] * 2
    specs += [per_expert(hidden, width)]
    specs += [per_expert(*piece.shape[1:]) for piece in (*gate_pre, *up_pre, *tails)]
    outs = [thin] * 3 + [per_expert(total, width // 2), per_expert(total, whole)]
    shapes = [jax.ShapeDtypeStruct((experts, total, hidden), bfloat)] * 3
    shapes += [jax.ShapeDtypeStruct((experts, total, width // 2), bfloat)]
    shapes += [jax.ShapeDtypeStruct((experts, total, whole), bfloat)]
    return kernel_call(
        functools.partial(backward_kernel, count, len(parts), len(parts) > 2 * groups, len(pins), len(tails)),
        "expert_backward",
        (experts,), specs + [once(*part.shape) for part in parts] + anywhere(pins), outs, shapes,
        [pltpu.VMEM((total, whole), bfloat)]
        + ([pltpu.VMEM((2, span, whole), bfloat)] if len(parts) > 2 * groups else []),
        2 * experts * total * width * (hidden * 3 + tokens),
        2 * experts * (3 * width * hidden + 3 * total * width // 2 + 7 * total * hidden),
        (place, slots) + tuple(weights) + tuple(gate_pre) + tuple(up_pre) + tuple(tails) + tuple(parts) + tuple(pins),
        prefetch=1,
    )


def expert_weights(place, count, slots, down_w, far, near, near_x, parts, capacity, start, far_start, experts, shards, pins):
    groups, _, tokens = slots.shape
    hidden, width = down_w.shape[1:]
    total = groups * capacity
    far_pre, (far_tails, far_half) = far[:2], far[2:]
    thin = per_expert(total, hidden, start=far_start)
    wide = per_expert(total, width // 2, start=far_start)
    thin_at = per_expert(total, hidden, start=start)
    wide_at = per_expert(total, width // 2, start=start)
    specs = [once(*slots.shape), per_expert(hidden, width, start=start)]
    specs += [thin, thin, per_expert(total, far_tails.shape[2], start=far_start)] + [thin_at] * 3
    specs += [wide_at, wide]
    specs += [per_expert(*piece.shape[1:], start=start) for piece in near_x]
    size = width // (2 * shards)
    return kernel_call(
        functools.partial(weights_kernel, count, groups, start, len(pins), len(near_x)),
        "expert_weights",
        (experts,), specs + [once(*part.shape) for part in parts] + anywhere(pins),
        [per_expert(3, size, hidden)] * shards,
        [jax.ShapeDtypeStruct((experts, 3, size, hidden), bfloat)] * shards,
        [pltpu.VMEM((total, width), bfloat), pltpu.VMEM((3, width // 2, hidden), bfloat)],
        2 * experts * total * width * (hidden * 4 + tokens),
        2 * experts * (5 * width * hidden // 2 + 3 * total * width // 2 + 7 * total * hidden),
        (place, slots, down_w) + tuple(far_pre) + (far_tails,) + tuple(near) + (far_half,) + tuple(near_x) + tuple(parts) + tuple(pins),
        prefetch=1,
    )


def finish_weights(experts, start, scale, own, arrived, before):
    some, _, size, hidden = own.shape
    chunk = math.gcd(some, start) if start else some

    def block(*shape, at=0):
        return pl.BlockSpec((chunk,) + shape, lambda e, *_: (e + at // chunk,) + (0,) * len(shape))

    ready = [block(3, size, hidden)] * (1 + len(arrived))
    kernel = finish_kernel if before is None else finish_more_kernel
    kept = [] if before is None else [pl.BlockSpec(memory_space=pl.ANY)] * 3
    small = pl.BlockSpec((8, 128), lambda e, *_: (0, 0))
    *grads, done = kernel_call(
        kernel,
        "finish_weights",
        (some // chunk,),
        kept + [small] + ready,
        [block(size, hidden, at=start)] * 2 + [block(hidden, size, at=start), small],
        [jax.ShapeDtypeStruct((experts, size, hidden), single)] * 2
        + [jax.ShapeDtypeStruct((experts, hidden, size), single), jax.ShapeDtypeStruct((8, 128), single)],
        [],
        3 * some * size * hidden,
        12 * some * size * hidden,
        tuple(before or ()) + (scale, own) + tuple(arrived),
        aliases={} if before is None else {0: 0, 1: 1, 2: 2},
    )
    return grads, done


def rotate(value, cosines, sines, back):
    pieces = []
    for at in range(0, value.shape[1], 128):
        piece = value[:, at : at + 128]
        lane = lax.broadcasted_iota(jnp.int32, piece.shape, 1)
        later, sooner = pltpu.roll(piece, 96, 1), pltpu.roll(piece, 32, 1)
        if back:
            turned = jnp.where(lane % 64 < 32, later, -sooner)
        else:
            turned = jnp.where(lane % 64 < 32, -later, sooner)
        pieces.append(piece * cosines + turned * sines)
    return pieces[0] if len(pieces) == 1 else jnp.concatenate(pieces, axis=1)


def query_blocks(length):
    return [(at, at + ABLK) for at in range(0, length, ABLK)]


def attend_kernel(place_ref, tokens_ref, gain_ref, query_w, key_w, value_w, out_w, cos_ref, sin_ref,
                  normed_ref, queries_ref, keys_ref, values_ref, mixed_ref, lse_ref, stay_ref, leave_ref, total_ref):
    step = pl.program_id(0)
    length = tokens_ref.shape[0]
    group = query_w.shape[1] // key_w.shape[1]

    @pl.when(step == 0)
    def _():
        inputs = tokens_ref[...].astype(single)
        inverse = lax.rsqrt(jnp.mean(inputs * inputs, axis=1, keepdims=True) + EPS)
        normed_ref[...] = (inputs * inverse * gain_ref[...]).astype(bfloat)

    normed = normed_ref[...]
    cosines, sines = cos_ref[...], sin_ref[...]
    queries = rotate(dot(normed, query_w[...]), cosines, sines, False) * HEAD_DIMENSION ** (-0.5)
    keys = rotate(dot(normed, key_w[...]), cosines, sines, False)
    values = dot(normed, value_w[...])
    size = HEAD_DIMENSION
    mixed = []
    for kv in range(key_w.shape[1] // size):
        key = keys[:, kv * size : (kv + 1) * size].astype(bfloat)
        value = values[:, kv * size : (kv + 1) * size].astype(bfloat)
        keys_ref[kv] = key
        values_ref[kv] = value
        for head in range(kv * group, (kv + 1) * group):
            query = queries[:, head * size : (head + 1) * size].astype(bfloat)
            queries_ref[head] = query
            outs, sums = [], []
            for start, seen in query_blocks(length):
                scores = dot_nt(key[:seen], query[start : start + ABLK])
                peak = jnp.max(scores, axis=0, keepdims=True)
                weights = jnp.exp(scores - peak)
                total = jnp.sum(weights, axis=0, keepdims=True)
                probs = (weights / total).astype(bfloat)
                outs.append(dot_tn(value[:seen], probs))
                sums.append(peak + jnp.log(total))
            mixed.append(jnp.concatenate(outs, axis=1))
            lse_ref[0, head : head + 1, :] = jnp.concatenate(sums, axis=1)
    mixed = jnp.concatenate(mixed, axis=0).T.astype(bfloat)
    mixed_ref[...] = mixed
    part = dot(mixed, out_w[...])

    @pl.when(step == 0)
    def _():
        total_ref[...] = part

    @pl.when(step > 0)
    def _():
        total_ref[...] += part

    @pl.when(step == pl.num_programs(0) - 1)
    def _():
        span = stay_ref.shape[0]
        core = place_ref[2]
        mine = pl.ds(pl.multiple_of(core * span, span), span)
        other = pl.ds(pl.multiple_of((1 - core) * span, span), span)
        stay_ref[...] = total_ref[mine, :] + tokens_ref[mine, :].astype(single)
        leave_ref[...] = total_ref[other, :]


def attend_back_kernel(place_ref, mine_ref, other_ref, tokens_ref, query_w, key_w, value_w, out_w, cos_ref, sin_ref,
                       queries_ref, keys_ref, values_ref, lse_ref,
                       raw_query_ref, raw_key_ref, raw_value_ref, stay_ref, leave_ref, gain_ref, low_ref, total_ref):
    step = pl.program_id(0)
    length = tokens_ref.shape[0]
    span = mine_ref.shape[0]
    core = place_ref[2]
    mine = pl.ds(pl.multiple_of(core * span, span), span)
    other = pl.ds(pl.multiple_of((1 - core) * span, span), span)
    low_ref[mine, :] = dot_nt(mine_ref[...], out_w[...]).astype(bfloat)
    low_ref[other, :] = dot_nt(other_ref[...], out_w[...]).astype(bfloat)
    grads = low_ref[...].astype(single)
    size = HEAD_DIMENSION
    group = query_w.shape[1] // key_w.shape[1]
    grad_queries, grad_keys, grad_values = [], [], []
    for kv in range(key_w.shape[1] // size):
        key, value = keys_ref[kv], values_ref[kv]
        key_parts = [[] for _ in query_blocks(length)]
        value_parts = [[] for _ in query_blocks(length)]
        for head in range(kv * group, (kv + 1) * group):
            query = queries_ref[head]
            grad = grads[:, head * size : (head + 1) * size].astype(bfloat)
            outs = []
            for block, (start, seen) in enumerate(query_blocks(length)):
                rows = slice(start, start + ABLK)
                scores = dot_nt(key[:seen], query[rows])
                probs = jnp.exp(scores - lse_ref[0, head : head + 1, rows])
                grad_probs = dot_nt(value[:seen], grad[rows])
                inner = jnp.sum(probs * grad_probs, axis=0, keepdims=True)
                grad_scores = (probs * (grad_probs - inner)).astype(bfloat)
                outs.append(dot_tn(grad_scores, key[:seen]))
                key_parts[block].append(dot(grad_scores, query[rows]))
                value_parts[block].append(dot(probs.astype(bfloat), grad[rows]))
            grad_queries.append(jnp.concatenate(outs, axis=0))

        def whole(parts):
            rows = []
            for at in range(len(parts)):
                here = slice(at * ABLK, (at + 1) * ABLK)
                rows.append(sum(one[here] for block in parts[at:] for one in block))
            return jnp.concatenate(rows, axis=0)

        grad_keys.append(whole(key_parts))
        grad_values.append(whole(value_parts))
    cosines, sines = cos_ref[...], sin_ref[...]
    grad_query = jnp.concatenate(grad_queries, axis=1) * HEAD_DIMENSION ** (-0.5)
    raw_query = rotate(grad_query, cosines, sines, True).astype(bfloat)
    raw_key = rotate(jnp.concatenate(grad_keys, axis=1), cosines, sines, True).astype(bfloat)
    raw_value = jnp.concatenate(grad_values, axis=1).astype(bfloat)
    raw_query_ref[...] = raw_query
    raw_key_ref[...] = raw_key
    raw_value_ref[...] = raw_value
    part = dot_nt(raw_query, query_w[...]) + dot_nt(raw_key, key_w[...]) + dot_nt(raw_value, value_w[...])

    @pl.when(step == 0)
    def _():
        total_ref[...] = part

    @pl.when(step > 0)
    def _():
        total_ref[...] += part

    @pl.when(step == pl.num_programs(0) - 1)
    def _():
        stay_ref[...] = total_ref[mine, :]
        leave_ref[...] = total_ref[other, :].astype(bfloat)
        inputs = tokens_ref[...].astype(single)
        inverse = lax.rsqrt(jnp.mean(inputs * inputs, axis=1, keepdims=True) + EPS)
        gain = jnp.sum(total_ref[...] * inputs * inverse, axis=0, keepdims=True)
        first = lax.broadcasted_iota(jnp.int32, gain_ref.shape, 0) == 0
        gain_ref[...] = jnp.where(first, gain, 0.0)


def attend(place, tokens, gain, query_w, key_w, value_w, out_w, tables):
    length, width = tokens.shape
    span, size = length // 2, HEAD_DIMENSION
    steps = key_w.shape[1] // 128
    wide, thin = query_w.shape[1] // steps, 128
    heads, kv_heads = query_w.shape[1] // size, key_w.shape[1] // size
    whole = lambda *shape: pl.BlockSpec(shape, lambda i, *_: (0,) * len(shape))
    across = lambda rows, columns: pl.BlockSpec((rows, columns), lambda i, *_: (0, i))
    split = lambda *shape: pl.BlockSpec(shape, lambda i, *_: (i,) + (0,) * (len(shape) - 1))
    low = lambda *shape: jax.ShapeDtypeStruct(shape, bfloat)
    high = lambda *shape: jax.ShapeDtypeStruct(shape, single)
    return kernel_call(
        attend_kernel,
        "attend",
        (steps,),
        [whole(length, width), pl.BlockSpec((width,), lambda i, *_: (0,)), across(width, wide), across(width, thin), across(width, thin),
         split(wide, width), whole(length, 128), whole(length, 128)],
        [whole(length, width), split(heads // steps, length, size), split(kv_heads // steps, length, size),
         split(kv_heads // steps, length, size), across(length, wide), split(1, 8, length),
         whole(span, width), whole(span, width)],
        [low(length, width), low(heads, length, size), low(kv_heads, length, size), low(kv_heads, length, size),
         low(length, heads * size), high(steps, 8, length), high(span, width), high(span, width)],
        [pltpu.VMEM((length, width), single)],
        2 * length * width * (2 * heads + 2 * kv_heads) * size,
        2 * (length * width * 6 + 2 * width * (heads + kv_heads) * size),
        (place, tokens, gain, query_w, key_w, value_w, out_w) + tuple(tables),
        prefetch=1,
    )


def attend_back(place, mine, other, tokens, query_w, key_w, value_w, out_w, tables, saved):
    length, width = tokens.shape
    span, size = length // 2, HEAD_DIMENSION
    steps = key_w.shape[1] // 128
    wide, thin = query_w.shape[1] // steps, 128
    heads, kv_heads = query_w.shape[1] // size, key_w.shape[1] // size
    whole = lambda *shape: pl.BlockSpec(shape, lambda i, *_: (0,) * len(shape))
    across = lambda rows, columns: pl.BlockSpec((rows, columns), lambda i, *_: (0, i))
    split = lambda *shape: pl.BlockSpec(shape, lambda i, *_: (i,) + (0,) * (len(shape) - 1))
    low = lambda *shape: jax.ShapeDtypeStruct(shape, bfloat)
    high = lambda *shape: jax.ShapeDtypeStruct(shape, single)
    return kernel_call(
        attend_back_kernel,
        "attend_back",
        (steps,),
        [whole(span, width), whole(span, width), whole(length, width),
         across(width, wide), across(width, thin), across(width, thin), split(wide, width),
         whole(length, 128), whole(length, 128), split(heads // steps, length, size),
         split(kv_heads // steps, length, size), split(kv_heads // steps, length, size), split(1, 8, length)],
        [across(length, wide), across(length, thin), across(length, thin),
         whole(span, width), whole(span, width), whole(8, width)],
        [low(length, heads * size), low(length, kv_heads * size), low(length, kv_heads * size),
         high(span, width), low(span, width), high(8, width)],
        [pltpu.VMEM((length, wide), bfloat), pltpu.VMEM((length, width), single)],
        6 * length * width * (heads + kv_heads) * size,
        2 * (length * width * 6 + 2 * width * (heads + kv_heads) * size),
        (place, mine, other, tokens, query_w, key_w, value_w, out_w) + tuple(tables) + tuple(saved),
        prefetch=1,
    )


def three_lanes(value, starts, lanes):
    total = None
    for start in starts:
        low = value.astype(bfloat).astype(single)
        value = value - low
        moved = pltpu.roll(low, start, 1) if start else low
        total = moved if total is None else total + moved
    return total


def token_kernel(count, place_ref, stay_ref, came_ref, routes_ref, gain_ref, router_ref, hidden_ref, token_ref):
    width = stay_ref.shape[1]
    hidden = stay_ref[...] + came_ref[...]
    hidden_ref[...] = hidden
    inverse = lax.rsqrt(jnp.mean(hidden * hidden, axis=1, keepdims=True) + EPS)
    moe_in = (hidden * inverse * gain_ref[...]).astype(bfloat)
    token_ref[:, :width] = moe_in
    logits = dot_nt(moe_in, router_ref[...])
    logits = jnp.concatenate([logits, jnp.zeros((logits.shape[0], 128 - count), single)], axis=1)
    lane = lax.broadcasted_iota(jnp.int32, logits.shape, 1)
    routes = routes_ref[...].astype(single).T
    lanes = lane.astype(single)
    picked = lanes == routes[:, :1]
    for k in range(1, routes.shape[1]):
        picked = picked | (lanes == routes[:, k : k + 1])
    peak = jnp.max(jnp.where(picked, logits, -1e30), axis=1, keepdims=True)
    weights = jnp.where(picked, jnp.exp(jnp.where(picked, logits, peak) - peak), 0.0)
    gates = weights / jnp.sum(weights, axis=1, keepdims=True)
    tail = three_lanes(gates, (0, count, 2 * count), 128)
    blank = jnp.zeros((routes.shape[0], 128 - routes.shape[1]), single)
    token_ref[:, width:] = (tail + jnp.concatenate([blank, routes], axis=1)).astype(bfloat)


def layer_kernel(addends, place_ref, hidden_ref, target_ref, valid_ref, *refs):
    parts, (layer_ref, grad_ref, low_ref, token_ref) = refs[:addends], refs[addends:]
    width = hidden_ref.shape[1]
    moe = sum_of(parts)
    layer = hidden_ref[...] + moe
    layer_ref[...] = layer.astype(bfloat)
    valid = valid_ref[:, :1].astype(single)
    grad = valid * (layer - target_ref[...].astype(single))
    grad_ref[...] = grad
    low_ref[...] = grad.astype(bfloat)
    token_ref[:, :width] = grad.astype(bfloat)
    inner = jnp.sum(grad * moe, axis=1, keepdims=True)
    lane = lax.broadcasted_iota(jnp.int32, (inner.shape[0], 128), 1)
    inner = jnp.where(lane == 0, inner, 0.0)
    token_ref[:, width:] = three_lanes(inner, (0, 1, 2), 128).astype(bfloat)


def sum_of(parts):
    total = None
    for part in parts:
        value = (part[0] if len(part.shape) == 3 else part[...]).astype(single)
        total = value if total is None else total + value
    return total


def norm_kernel(addends, place_ref, hidden_ref, grad_layer_ref, *refs):
    parts, (gain_ref, router_ref, digits_ref, grad_ref, low_ref, logits_ref, sum_ref) = refs[:addends], refs[addends:]
    width = hidden_ref.shape[1]
    wide = sum_of(parts)
    logits = wide[:, width:].astype(bfloat)
    logits_ref[...] = logits
    count = router_ref.shape[0]
    grad_in = wide[:, :width] + dot(logits[:, :count], router_ref[...])
    hidden = hidden_ref[...]
    inverse = lax.rsqrt(jnp.mean(hidden * hidden, axis=1, keepdims=True) + EPS)
    scaled = grad_in * gain_ref[...]
    inner = jnp.mean(scaled * hidden, axis=1, keepdims=True)
    grad = grad_layer_ref[...] + inverse * scaled - hidden * (inverse * inverse * inverse * inner)
    grad_ref[...] = grad
    low_ref[...] = grad.astype(bfloat)
    gain = jnp.sum(grad_in * hidden * inverse, axis=0, keepdims=True)
    first = lax.broadcasted_iota(jnp.int32, sum_ref.shape, 0) == 0
    gain = jnp.where(first, gain, 0.0)

    @pl.when(pl.program_id(0) == 0)
    def _():
        sum_ref[...] = gain + digits_ref[:, :1]

    @pl.when(pl.program_id(0) > 0)
    def _():
        sum_ref[...] += gain


def digits_kernel(valid_ref, pin_ref, digits_ref):
    count = jnp.sum(valid_ref[:1, :].astype(single), axis=1, keepdims=True)
    high = jnp.floor(count * (1.0 / 64.0))
    middle = jnp.floor((count - 64.0 * high) * 0.125)
    low = count - 64.0 * high - 8.0 * middle
    row = lax.broadcasted_iota(jnp.int32, digits_ref.shape, 0)
    digits_ref[...] = jnp.where(row == 1, high, jnp.where(row == 2, middle, jnp.where(row == 3, low, 0.0)))


def count_digits(valid, pin):
    return pl.pallas_call(
        digits_kernel,
        name="digits",
        grid=(1,),
        in_specs=[pl.BlockSpec(valid.shape, lambda i: (0, 0)), pl.BlockSpec(memory_space=pl.ANY)],
        out_specs=pl.BlockSpec((8, 128), lambda i: (0, 0)),
        out_shape=jax.ShapeDtypeStruct((8, 128), single),
        cost_estimate=pl.CostEstimate(flops=0, bytes_accessed=2**14, transcendentals=0),
    )(valid, pin)


def token_rows(kernel, name, steps, place, rowwise, others, outs, kept=()):
    block = outs[0].shape[0] // steps

    def spec(array):
        if isinstance(array, tuple) and array[1] is None:
            return pl.BlockSpec(
                (array[0].shape[0], block), lambda i, place: (0, place[2] * steps + i)
            )
        if isinstance(array, tuple):
            array, index = array
            return pl.BlockSpec((1, block, array.shape[2]), lambda i, place: (index, i, 0))
        return pl.BlockSpec((block, array.shape[1]), lambda i, place: (i, 0))

    bare = [array[0] if isinstance(array, tuple) else array for array in rowwise]
    return kernel_call(
        kernel,
        name,
        (steps,),
        [spec(array) for array in rowwise]
        + [pl.BlockSpec(array.shape, lambda i, place, n=array.ndim: (0,) * n) for array in others],
        [pl.BlockSpec((block, out.shape[1]), lambda i, place: (i, 0)) for out in outs]
        + [pl.BlockSpec(out.shape, lambda i, place: (0, 0)) for out in kept],
        list(outs) + list(kept),
        [],
        1,
        8 * sum(out.shape[0] * out.shape[1] for out in outs),
        (place,) + tuple(bare) + tuple(others),
        prefetch=1,
    )


def pack_kernel(lane_at, terms, cut, place_ref, sums_ref, *refs):
    lefts, rights, refs = refs[:terms], refs[terms : 2 * terms], refs[2 * terms :]
    outs, full_ref = refs[:-1], refs[-1]
    span = lefts[0].shape[0]
    at = 0
    for term in range(terms):
        left, right = lefts[term], rights[term]
        rows = left.shape[0]
        columns = right.shape[1]
        if right.shape[0] == rows:
            value = dot_tn(left[...], right[...])
        else:
            core = place_ref[2] if term == 0 else 1 - place_ref[2]
            value = dot_tn(left[...], right[pl.ds(pl.multiple_of(core * rows, rows), rows), :])
        if term == 1 and lefts[0].shape[0] != rights[0].shape[0]:
            full_ref[:, :columns] += value
        else:
            full_ref[:, at : at + columns] = value
            at += columns
    sums = sums_ref[...]
    high = sums.astype(bfloat)
    low = (sums - high.astype(single)).astype(bfloat)
    lane = lax.broadcasted_iota(jnp.int32, (sums.shape[0], 128), 1)
    chosen = (lane == lane_at + lax.broadcasted_iota(jnp.int32, lane.shape, 0)).astype(bfloat)
    column = dot_tn(high, chosen) + dot_tn(low, chosen)
    width = full_ref.shape[1]
    if at < width:
        full_ref[:, width - 128 :] = column
    else:
        full_ref[:, width - 128 :] += column
    some, block = outs[0].shape[:2]

    def blocks(step, i):
        start = (i * cut + (place_ref[4] ^ step)) * block
        return full_ref[pl.ds(pl.multiple_of(start, block), block), :].astype(bfloat)

    for step in range(min(cut, len(outs))):
        if len(outs) > cut and step == cut - 1:
            early = pl.program_id(0) < pl.num_programs(0) // 2

            @pl.when(early)
            def _():
                outs[-2][0] = blocks(step, 0)

            @pl.when(jnp.logical_not(early))
            def _():
                outs[-1][0] = blocks(step, 0)

        else:
            for i in range(some):
                outs[step][i] = blocks(step, i)


def pack_sums(place, lefts, rights, sums, lane_at, columns, count_dp, owners):
    width = sums.shape[1]
    block = width // (count_dp * owners)
    steps = count_dp if (width // count_dp) % 128 == 0 else 1
    tall = lambda array: pl.BlockSpec((array.shape[0], width // steps), lambda i, *_: (0, i))
    whole = lambda array: pl.BlockSpec(array.shape, lambda i, *_: (0, 0))
    some = count_dp // steps
    halved = owners == 4 and steps == count_dp
    specs = [pl.BlockSpec((some, block, columns), lambda i, *_: (i, 0, 0))] * owners
    shapes = [jax.ShapeDtypeStruct((count_dp, block, columns), bfloat)] * owners
    if halved:
        half = count_dp // 2
        specs[3:] = [
            pl.BlockSpec((1, block, columns), lambda i, *_: (jnp.minimum(i, half - 1), 0, 0)),
            pl.BlockSpec((1, block, columns), lambda i, *_: (jnp.maximum(i - half, 0), 0, 0)),
        ]
        shapes[3:] = [jax.ShapeDtypeStruct((half, block, columns), bfloat)] * 2
    outs = kernel_call(
        functools.partial(pack_kernel, lane_at, len(lefts), owners),
        "pack_sums",
        (steps,),
        [tall(sums)] + [tall(left) for left in lefts] + [whole(right) for right in rights],
        specs,
        shapes,
        [pltpu.VMEM((width // steps, columns), single)],
        2 * sum(left.shape[0] * width * columns for left in lefts),
        2 * width * columns,
        (place, sums) + tuple(lefts) + tuple(rights),
        prefetch=1,
    )
    outs = list(outs)
    if halved:
        return outs[:3] + [(outs[3], outs[4])]
    if owners == 4:
        half = count_dp // 2
        return outs[:3] + [(outs[3][:half], outs[3][half:])]
    return outs


def rope_tables(length, head_size):
    half_size = head_size // 2
    frequency = np.float32(THETA) ** (-np.arange(half_size, dtype=np.float32) * np.float32(2.0) / np.float32(head_size))
    angles = np.arange(length, dtype=np.float32)[:, None] * frequency.astype(np.float32)[None, :]
    return [jnp.asarray(np.tile(f(angles).astype(np.float32), (1, 128 // half_size))) for f in (np.cos, np.sin)]


def rms_backward(value_matrix, inverse, gain, grad_normed):
    scaled = grad_normed * gain
    grad_gain = jnp.sum(grad_normed * value_matrix * inverse, axis=0)
    grad_values = inverse * scaled - value_matrix * inverse**3 * jnp.mean(
        scaled * value_matrix, axis=-1, keepdims=True
    )
    return (grad_values, grad_gain)


def assemble(mine, other):
    first = lax.axis_index("tensor") == 0
    return jnp.concatenate([jnp.where(first, mine, other), jnp.where(first, other, mine)], axis=0)


def combine_groups(slots, rows, capacity, span, between, later=None, own=None):
    owners = lax.axis_size("expert")
    orders = return_order(owners)
    if own is not None:
        orders = [[group - 1 for group in order if group] for order in orders]
    if len(orders) == 1:
        mine, other = return_rows(slots, after(rows, *between(())), orders[0], capacity, span)
        other = swap(other)
        sent = [
            (mine[i].astype(single) + other[i].astype(single)).astype(bfloat)
            for i in range(owners - 1)
        ]
        came = [to_peer(part, "expert", i) for i, part in enumerate(sent, 1)]
    else:
        mine, other = return_rows(slots, rows, orders[0], capacity, span)
        other = after(swap(other), *hold(other))
        came, sent = send_farthest(mine, other)
        done = between(sent)
        came[0] = after(came[0], *hold(sent[0]), *done)
        rows = after(rows, *done, *hold(sent[0]), *hold(sent[1]))
        mine, other = return_rows(slots, rows, orders[1], capacity, span)
        other = after(swap(other), *hold(other))
        came, sent = send_nearer(mine, other, came)
        done = later(sent) if later else ()
        if own is None:
            rows = after(rows, *sent, *hold(sent[0]), *hold(sent[1]))
            mine, other = return_rows(slots, rows, orders[2], capacity, span)
            other = swap(after(other, *done))
    if own is not None:
        return [(own[0], 0), (own[1], 0)] + came, sent
    at = len(orders[-1]) - 1
    return [(mine, at), (other, at)] + came, sent


def on_device(
    tokens,
    teacher,
    routes,
    valid,
    teacher_rows,
    norm_attn,
    norm_moe,
    w_query,
    key_projection_weight,
    value_projection_weight,
    w_out,
    w_router,
    w_gate,
    w_up,
    w_down,
):
    rows_dev, model_width = tokens.shape
    seq_count = rows_dev // SEQUENCE_LENGTH
    heads_local = w_query.shape[1] // HEAD_DIMENSION
    kv_local = key_projection_weight.shape[1] // HEAD_DIMENSION
    query_width = w_query.shape[1]
    key_width = key_projection_weight.shape[1]
    experts_local = w_gate.shape[0]
    owners = lax.axis_size("expert")
    count_dp = lax.axis_size("dp")
    groups = count_dp * owners
    all_experts = experts_local * owners
    top_count = routes.shape[1]
    capacity = rows_dev * top_count * 5 // (4 * all_experts)
    at_dp, at_ex, core = lax.axis_index("dp"), lax.axis_index("expert"), lax.axis_index("tensor")
    span = rows_dev // 2
    shards = count_dp // 2
    place = [at_ex * experts_local, at_dp // shards, core, at_dp % shards, at_ex, at_dp]
    place = jnp.stack(place).astype(jnp.int32)

    def mine_of(value, axis=0):
        return lax.dynamic_slice_in_dim(value, core * span, span, axis)

    def other_of(value, axis=0):
        return lax.dynamic_slice_in_dim(value, (1 - core) * span, span, axis)

    tables = rope_tables(SEQUENCE_LENGTH, HEAD_DIMENSION)
    gain_attn, gain_moe = norm_attn, norm_moe

    def tokens_like(columns, kind):
        return jax.ShapeDtypeStruct((span, columns), kind)

    weights = (w_query, key_projection_weight, value_projection_weight, w_out)
    normed, queries, keys, values, mixed, log_sums, staying, leaving = attend(
        place, tokens, gain_attn, *weights, tables
    )
    came = after(swap(leaving), *hold(leaving))
    wide = model_width + 128
    hidden_first, token = token_rows(
        functools.partial(token_kernel, all_experts),
        "token",
        2,
        place,
        [staying, came, (routes.T, None)],
        [gain_moe, w_router.T],
        [tokens_like(model_width, single), tokens_like(wide, bfloat)],
    )

    some = experts_local // 2
    few = max(1, some - some // 2)
    pieces = ((0, some), (some, experts_local - some))

    def interleave(mine, other):
        return [part for pair in zip(mine, other) for part in pair]

    def far_forward(parts, start, amount, pin):
        return expert_forward(
            place, all_experts, top_count, pin, (w_gate, w_up), parts, owners, capacity, start, amount
        )

    mirror = to_mirror(token)
    own_other = swap(token)
    def forward(parts, groups, pin, chunk):
        return expert_forward(
            place, all_experts, top_count, pin, (w_gate, w_up, w_down), parts, groups, capacity, 0, experts_local, chunk
        )

    own = forward([token, own_other], 1, token, CHUNK_OWN)
    own_mine, own_leaving = return_rows(own[4], own[5], [0], capacity, span)
    (wanted,) = after_all([mine_of(teacher_rows, 1)], own[5])
    (valid_rows,) = after_all([mine_of(valid)[:, None] + jnp.zeros((span, 128), jnp.int32)], own[5])
    chooser = (wanted[0][:, None] == jnp.arange(rows_dev, dtype=jnp.int32)).astype(bfloat)
    target = jnp.dot(chooser, teacher, preferred_element_type=bfloat)
    near_parts = spread(token, own_other, (own[5],), (own_mine, target, valid_rows))
    mirror = after(mirror, *near_parts)
    peers = from_peers(mirror)
    mirror_other = swap(mirror)
    own_came = swap(after(own_leaving, mirror))
    others = forward(near_parts, owners - 1, mirror, CHUNK_OTHERS)
    gate_pre, up_pre, near_half, near_tails = zip(own[:4], others[:4])
    slots = jnp.concatenate([own[4], others[4]], axis=0)
    results = after(others[5], mirror_other, own_came)
    peers_other = []

    def swap_peers(sent):
        peers[:] = after_all(peers, *sent)
        peers_other.extend(swap(peer) for peer in peers)
        return sent

    addends, sent = combine_groups(
        others[4], results, capacity, span, swap_peers, own=(own_mine, own_came)
    )
    far_tokens = interleave([mirror] + peers, [mirror_other] + peers_other)
    far = [far_forward(far_tokens, *pieces[0], sent[0])]
    addends[-1] = after(addends[-1], far[0][0], *hold(sent[0]))
    layer_low, grad_layer, layer_grad, token_grad = token_rows(
        functools.partial(layer_kernel, len(addends)),
        "layer",
        2,
        place,
        [hidden_first, target, valid_rows] + addends,
        [],
        [tokens_like(model_width, bfloat), tokens_like(model_width, single), tokens_like(model_width, bfloat), tokens_like(wide, bfloat)],
    )

    leaving = after(layer_grad, *hold(token_grad))
    mirror = to_mirror(leaving)
    far.append(far_forward(far_tokens, *pieces[1], hold(leaving)[0]))
    own_other = swap(token_grad)
    digits = count_digits(jnp.broadcast_to(valid[None, :], (8, rows_dev)), far[1][0])
    near_parts = [token_grad, own_other] + spread(token_grad, own_other, (far[1][0],), (digits,))
    mirror = after(mirror, *near_parts)
    peers = from_peers(mirror)
    mirror_other = swap(mirror)
    hidden_low, grad_gate_pre, grad_up_pre, near_grad_half, results = expert_backward(
        place, all_experts, slots, (w_gate, w_up, w_down), gate_pre, up_pre, near_tails, near_parts, capacity, (mirror,)
    )
    results = after(results, mirror_other)
    weight_parts, far_grads = [], []

    def weights_of(start, amount, others=()):
        piece = 0 if start < some else 1
        far_gate, far_up, far_half, far_tails, far_slots = far[piece]
        values = expert_weights(
            place,
            all_experts,
            far_slots,
            w_down,
            (far_gate, far_up, far_tails, far_half),
            (hidden_low, grad_gate_pre, grad_up_pre, near_grad_half),
            near_half,
            far_grads,
            capacity,
            start,
            start - pieces[piece][0],
            amount,
            shards,
            tuple(others),
        )
        came = [to_peer(values[step], "dp", step) for step in range(1, shards)]
        weight_parts.append((start, values[0], came))
        return (*values, *[pin for value in values[1:] for pin in hold(value)])

    def swap_far(sent):
        peers[:] = after_all(peers, *sent)
        peers_other = [swap(peer) for peer in peers]
        far_grads.extend(interleave([mirror] + peers, [mirror_other] + peers_other))
        return peers_other

    results = after(results, *peers)
    addends, sent = combine_groups(slots, results, capacity, span, lambda sent: sent, swap_far)
    if owners != 4:
        swap_far(sent)
    done = weights_of(0, few, sent)
    addends[-1] = after(addends[-1], *done, *hold(sent[0]))
    grad_hidden, grad_attn, grad_logits, gain_sums = token_rows(
        functools.partial(norm_kernel, len(addends)),
        "norm",
        2,
        place,
        [hidden_first, grad_layer] + addends,
        [gain_moe, w_router.T, digits],
        [tokens_like(model_width, single), tokens_like(model_width, bfloat), tokens_like(128, bfloat)],
        [jax.ShapeDtypeStruct((8, model_width), single)],
    )
    grad_attn_other = after(swap(grad_attn), *hold(grad_attn))
    first_parts = pack_sums(
        place,
        [grad_attn, grad_attn_other, token],
        [mixed, mixed, grad_logits],
        gain_sums,
        all_experts,
        query_width + 128,
        count_dp,
        owners,
    )
    first_sum = start_sum(first_parts)
    done = weights_of(some, experts_local - some, first_parts[-1] if owners == 4 else first_parts)
    first_sum, sent = go_on(first_sum, *done)
    grad_attn, layer_low = after_all([grad_attn, layer_low], *sent, *weight_parts[0][2])
    layer_other = swap(layer_low)
    raw_query, raw_key, raw_value, staying, leaving, gain_sums = attend_back(
        place, grad_attn, grad_attn_other, tokens, *weights, tables, (queries, keys, values, log_sums)
    )
    second_parts = pack_sums(
        place,
        [normed] * 3,
        [raw_query, raw_key, raw_value],
        after(gain_sums, *first_sum[1:], layer_other),
        0,
        query_width + 2 * key_width + 128,
        count_dp,
        owners,
    )
    second_sum = start_sum(second_parts)
    last = second_parts[-1] if owners == 4 else second_parts
    leaving = swap(leaving)
    first_total = add_up(first_sum[0], after_all(first_sum[1:], *last, leaving))
    first_dense = over_dp_start(first_total)
    pins = [] if first_dense[1] is None else [first_dense[1], *hold(first_dense[1])]
    done = weights_of(few, some - few, (*last, *hold(last[0]), *pins))
    second_sum, sent = go_on(second_sum, *done)
    first_dense = over_dp_step(first_dense, *sent, *weight_parts[1][2])
    leaving = after(leaving, *sent)
    inputs_mine = mine_of(tokens).astype(single)
    inverse_mine = lax.rsqrt(jnp.mean(inputs_mine * inputs_mine, axis=-1, keepdims=True) + EPS)
    grad_first, _ = rms_backward(
        inputs_mine, inverse_mine, norm_attn, staying + leaving.astype(single)
    )
    layer_low = after(layer_low, *sent)
    block_out = assemble(layer_low, layer_other)
    pins = [] if first_dense[1] is None else [first_dense[1], *hold(first_dense[1])]
    grad_tokens_mine = after(grad_hidden + grad_first, *pins, block_out)
    grad_tokens_other = after(swap(grad_tokens_mine), *hold(grad_tokens_mine))
    second_total = add_up(second_sum[0], after_all(second_sum[1:], grad_tokens_other, block_out, *pins))
    arrived, sent = over_dp_at_once(second_total)
    first_dense = over_dp_end(first_dense, *sent)
    tail = first_dense[:, query_width:]
    counted = tail[:1, all_experts + 1 : all_experts + 4] * jnp.asarray([[64.0, 8.0, 1.0]], single)
    tail = tail + after(swap(tail), *hold(tail))
    scale = jnp.broadcast_to(rows_dev * groups / jnp.sum(counted, axis=1, keepdims=True), (8, 128))
    first_dense, tail = first_dense * scale[0, 0], tail * scale[0, 0]
    grad_tokens = assemble(grad_tokens_mine, grad_tokens_other) * scale[0, 0]
    weight_grads, finished = None, ()
    for start, values, came in weight_parts:
        came = [after(part, *sent) for part in came]
        weight_grads, finished = finish_weights(experts_local, start, scale, values, came, weight_grads)
    arrived = list(after_all(arrived, *hold(sent[0]), finished, grad_tokens, tail))
    grad_query, grad_key, grad_value, second_tail = scaled_sum(
        place, scale, second_total, arrived, (query_width, key_width, key_width, 128)
    )
    second_tail = second_tail + swap(second_tail)
    return (
        block_out,
        grad_tokens,
        second_tail[:, 0],
        tail[:, all_experts],
        grad_query,
        grad_key,
        grad_value,
        first_dense[:, :query_width].T,
        tail[:, :all_experts],
        weight_grads[0],
        weight_grads[1],
        weight_grads[2],
    )


def solution(mesh):
    placed = (
        P(("dp", "expert"), None),
        P(("dp", "expert"), None),
        P(("dp", "expert"), None),
        P(("dp", "expert")),
        P(("dp", "expert"), None),
        P(),
        P(),
        P(None, "tensor"),
        P(None, "tensor"),
        P(None, "tensor"),
        P("tensor", None),
        P(),
        P("expert", None, "tensor"),
        P("expert", None, "tensor"),
        P("expert", "tensor", None),
    )
    return jax.shard_map(
        on_device,
        mesh=mesh,
        in_specs=placed,
        out_specs=(
            P(("dp", "expert"), None),
            P(("dp", "expert"), None),
            P(("dp", "expert")),
            P(("dp", "expert")),
            P(("dp", "expert"), "tensor"),
            P(("dp", "expert"), "tensor"),
            P(("dp", "expert"), "tensor"),
            P("tensor", ("dp", "expert")),
            P(("dp", "expert"), None),
            P("expert", "dp", "tensor"),
            P("expert", "dp", "tensor"),
            P("expert", "tensor", "dp"),
        ),
        check_vma=False,
    )
```
